32 devices in a mesh: seq: 4 (over y, x), head: 8 (over z, core).
Axes of the slice: x: 2, y: 2, z: 4, core: 2. Of those that a mesh axis runs over, the one named last changes fastest.
Arguments:
- layer_input: bfloat16 [4096, 1024], P(('seq', 'head')), may hold values from -6 to 6
- lengths: int32 [5], replicated, may hold values from 128 to 3201, as said below
- gain_a1: bfloat16 [1024], P(('seq', 'head')), may hold values from 0.5 to 1.5
- lin_q: bfloat16 [1024, 256], P(('seq', 'head')), may hold values from -0.1875 to 0.1875
- lin_k: bfloat16 [1024, 256], P(('seq', 'head')), may hold values from -0.1875 to 0.1875
- lin_v: bfloat16 [1024, 1024], P(('seq', 'head')), may hold values from -0.1875 to 0.1875
- lin_out: bfloat16 [1024, 1024], P(('seq', 'head')), may hold values from -3 to 3
- gain_a2: bfloat16 [1024], P(('seq', 'head')), may hold values from 0.5 to 1.5
- mlp_a_gate: bfloat16 [1024, 2752], P(('seq', 'head')), may hold values from -0.1875 to 0.1875
- mlp_a_up: bfloat16 [1024, 2752], P(('seq', 'head')), may hold values from -0.1875 to 0.1875
- mlp_a_down: bfloat16 [2752, 1024], P(None, ('seq', 'head')), may hold values from -0.109375 to 0.109375
- gain_b1: bfloat16 [1024], P(('seq', 'head')), may hold values from 0.5 to 1.5
- win_q: bfloat16 [1024, 1024], P(('seq', 'head')), may hold values from -0.1875 to 0.1875
- win_k: bfloat16 [1024, 1024], P(('seq', 'head')), may hold values from -0.1875 to 0.1875
- win_v: bfloat16 [1024, 1024], P(('seq', 'head')), may hold values from -0.1875 to 0.1875
- win_out: bfloat16 [1024, 1024], P(('seq', 'head')), may hold values from -1.5 to 1.5
- gain_b2: bfloat16 [1024], P(('seq', 'head')), may hold values from 0.5 to 1.5
- mlp_b_gate: bfloat16 [1024, 2752], P(('seq', 'head')), may hold values from -0.1875 to 0.1875
- mlp_b_up: bfloat16 [1024, 2752], P(('seq', 'head')), may hold values from -0.1875 to 0.1875
- mlp_b_down: bfloat16 [2752, 1024], P(None, ('seq', 'head')), may hold values from -0.109375 to 0.109375
- cotangent: bfloat16 [4096, 1024], P(('seq', 'head')), may hold values from -6 to 6
Outputs:
- mixed: bfloat16 [4096, 1024], P(('seq', 'head'))
- grad_input: float32 [4096, 1024], P(('seq', 'head'))
- grad_gain_a1: float32 [1024], P(('seq', 'head'))
- grad_lin_q: float32 [1024, 256], P(('seq', 'head'))
- grad_lin_k: float32 [1024, 256], P(('seq', 'head'))
- grad_lin_v: float32 [1024, 1024], P(('seq', 'head'))
- grad_lin_out: float32 [1024, 1024], P(('seq', 'head'))
- grad_gain_a2: float32 [1024], P(('seq', 'head'))
- grad_mlp_a_gate: float32 [1024, 2752], P(('seq', 'head'))
- grad_mlp_a_up: float32 [1024, 2752], P(('seq', 'head'))
- grad_mlp_a_down: float32 [2752, 1024], P(None, ('seq', 'head'))
- grad_gain_b1: float32 [1024], P(('seq', 'head'))
- grad_win_q: float32 [1024, 1024], P(('seq', 'head'))
- grad_win_k: float32 [1024, 1024], P(('seq', 'head'))
- grad_win_v: float32 [1024, 1024], P(('seq', 'head'))
- grad_win_out: float32 [1024, 1024], P(('seq', 'head'))
- grad_gain_b2: float32 [1024], P(('seq', 'head'))
- grad_mlp_b_gate: float32 [1024, 2752], P(('seq', 'head'))
- grad_mlp_b_up: float32 [1024, 2752], P(('seq', 'head'))
- grad_mlp_b_down: float32 [2752, 1024], P(None, ('seq', 'head'))
The draws below stay inside these ranges and needn't reach their ends.
Inputs may be any that keep to these rules, and one draw needn't show every extreme that they name: 5 lengths in packing order summing to 4096: one sequence of 3201 tokens, and the others 128, 128, 256 and 383 in some order, some of them before the long one and the rest after it.
All inputs are finite; a program needn't handle non-finite values.
Results may differ from the reference program's by a relative error of at most 0.025.
Values may be sent and summed in bfloat16 or wider, within the bound.
A program may use at most 448 MiB of HBM per device.

```python
import jax
import jax.numpy as jnp
from jax import lax

D = 1024
HEADS = 16
FEAT = 16
FF = 2752
WINDOW = 64
MINLEN = 128
NSEQ = 5
TOKENS = 4096
VDIM = 64
FEATX = 273


def draw_lengths(key, part):
    pick_key = jax.random.fold_in(key, 11)
    order_key = jax.random.fold_in(key, 13)
    shorts = jnp.array([MINLEN, MINLEN, 2 * MINLEN, 3 * MINLEN - 1], jnp.int32)
    shorts = jax.random.permutation(order_key, shorts)
    longest = TOKENS - jnp.sum(shorts)
    position = jax.random.randint(pick_key, (), 0, NSEQ, dtype=jnp.int32)
    slots = jnp.arange(NSEQ, dtype=jnp.int32)
    before = shorts[jnp.clip(slots, 0, NSEQ - 2)]
    behind = shorts[jnp.clip(slots - 1, 0, NSEQ - 2)]
    return jnp.where(slots < position, before, jnp.where(slots == position, longest, behind)).astype(jnp.int32)


def steps_of(stream_key, extent, cuts, least, largest):
    level = 1.0
    for dim, shards_of in cuts:
        steps = jax.random.uniform(jax.random.fold_in(jax.random.fold_in(stream_key, 6), dim), (shards_of,), jnp.float32, least / len(cuts), largest / len(cuts))
        level = level * jnp.repeat(jnp.exp(steps), extent[dim] // shards_of).reshape((-1,) + (1,) * (len(extent) - 1 - dim))
    return level


def gaussian(stream_key, dims, deviation, reach, cuts=(), held_as=jnp.bfloat16):
    drawn = deviation * jax.random.normal(stream_key, dims, jnp.float32)
    if cuts:
        drawn = drawn * steps_of(stream_key, dims, cuts, -0.22, 0.18)
    return jnp.clip(drawn, -reach, reach).astype(held_as)


def setup_inputs(seed: int = 0) -> dict:
    arg_keys = jax.random.split(jax.random.key(seed), 22)
    layer_input = gaussian(arg_keys[0], (TOKENS, D), 1.0, 6.0, ((0, 32),))
    lengths = draw_lengths(jax.random.fold_in(arg_keys[21], 71), 0)
    gain_a1 = jnp.clip(1.0 + 0.1 * jax.random.normal(arg_keys[2], (D,), jnp.float32), 0.5, 1.5).astype(jnp.bfloat16)
    lin_q = gaussian(arg_keys[3], (D, HEADS * FEAT), D ** -0.5, 0.1875, ((0, 32),))
    lin_k = gaussian(arg_keys[4], (D, HEADS * FEAT), D ** -0.5, 0.1875, ((0, 32),))
    lin_v = gaussian(arg_keys[5], (D, D), D ** -0.5, 0.1875, ((0, 32),))
    lin_out = gaussian(arg_keys[6], (D, D), (D // 256) ** -0.5, 3.0, ((0, 32),))
    gain_a2 = jnp.clip(1.0 + 0.1 * jax.random.normal(arg_keys[7], (D,), jnp.float32), 0.5, 1.5).astype(jnp.bfloat16)
    mlp_a_gate = gaussian(arg_keys[8], (D, FF), D ** -0.5, 0.1875, ((0, 32),))
    mlp_a_up = gaussian(arg_keys[9], (D, FF), D ** -0.5, 0.1875, ((0, 32),))
    mlp_a_down = gaussian(arg_keys[10], (FF, D), FF ** -0.5, 0.109375, ((1, 32),))
    gain_b1 = jnp.clip(1.0 + 0.1 * jax.random.normal(arg_keys[11], (D,), jnp.float32), 0.5, 1.5).astype(jnp.bfloat16)
    win_q = gaussian(arg_keys[12], (D, D), D ** -0.5, 0.1875, ((0, 32),))
    win_k = gaussian(arg_keys[13], (D, D), D ** -0.5, 0.1875, ((0, 32),))
    win_v = gaussian(arg_keys[14], (D, D), D ** -0.5, 0.1875, ((0, 32),))
    win_out = gaussian(arg_keys[15], (D, D), (D // 64) ** -0.5, 1.5, ((0, 32),))
    gain_b2 = jnp.clip(1.0 + 0.1 * jax.random.normal(arg_keys[16], (D,), jnp.float32), 0.5, 1.5).astype(jnp.bfloat16)
    mlp_b_gate = gaussian(arg_keys[17], (D, FF), D ** -0.5, 0.1875, ((0, 32),))
    mlp_b_up = gaussian(arg_keys[18], (D, FF), D ** -0.5, 0.1875, ((0, 32),))
    mlp_b_down = gaussian(arg_keys[19], (FF, D), FF ** -0.5, 0.109375, ((1, 32),))
    cotangent = gaussian(arg_keys[20], (TOKENS, D), 1.0, 6.0, ((0, 32),))
    return dict(layer_input=layer_input, lengths=lengths, gain_a1=gain_a1, lin_q=lin_q, lin_k=lin_k, lin_v=lin_v, lin_out=lin_out, gain_a2=gain_a2, mlp_a_gate=mlp_a_gate, mlp_a_up=mlp_a_up, mlp_a_down=mlp_a_down, gain_b1=gain_b1, win_q=win_q, win_k=win_k, win_v=win_v, win_out=win_out, gain_b2=gain_b2, mlp_b_gate=mlp_b_gate, mlp_b_up=mlp_b_up, mlp_b_down=mlp_b_down, cotangent=cotangent)


@jax.custom_vjp
def low(v):
    return lax.optimization_barrier(v.astype(jnp.bfloat16)).astype(jnp.float32)

@jax.custom_vjp
def low_back(v):
    return v

def low_keep(v):
    return (low(v), None)

def low_pass(kept, grad):
    return (grad,)

def back_keep(v):
    return (v, None)

def back_low(kept, grad):
    return (low(grad),)
low.defvjp(low_keep, low_pass)
low_back.defvjp(back_keep, back_low)
EPSILON = 1e-05
PRECISE = lax.Precision.HIGHEST

def matmul_hi(left, right):
    return jnp.dot(left, right, precision=PRECISE, preferred_element_type=jnp.float32)

def rms_scale(values, gain_vec):
    inv_rms = lax.rsqrt(lax.optimization_barrier(jnp.mean(values * values, axis=-1, keepdims=True)) + EPSILON)
    return values * inv_rms * gain_vec

def features(vectors):
    leading = vectors.shape[:-1]
    linear = vectors * FEAT ** (-0.25)
    square = (vectors[..., :, None] * vectors[..., None, :]).reshape(leading + (FEAT * FEAT,)) * (2.0 * FEAT) ** (-0.5)
    return jnp.concatenate([jnp.ones(leading + (1,), jnp.float32), linear, square], axis=-1)

def segment_ids(lengths, positions):
    ends = jnp.cumsum(lengths).astype(jnp.int32)
    starts = (ends - lengths).astype(jnp.int32)
    counted = lax.optimization_barrier(jnp.sum((positions[:, None] >= starts[None, :]).astype(jnp.int32), axis=1)).astype(jnp.int32)
    return (counted - 1).astype(jnp.int32)

def by_rows(function, arrays):
    block_rows = min(4096, TOKENS)
    n_blocks = TOKENS // block_rows
    shaped = tuple((member.reshape((n_blocks, block_rows) + member.shape[1:]) for member in arrays))
    result = lax.map(jax.checkpoint(lambda pieces: function(*pieces)), shaped)
    return jax.tree.map(lambda member: member.reshape((TOKENS,) + member.shape[2:]), result)

def project_in(rows_in, gain_vec, w_query, w_key, w_value):
    normed = low(rms_scale(rows_in, gain_vec))
    return (low_back(low(matmul_hi(normed, w_query))), low_back(low(matmul_hi(normed, w_key))), low_back(low(matmul_hi(normed, w_value))))

def finish_layer(rows_in, attended, w_out, gain_vec, w_gate, w_up, w_down):
    mixed_rows = rows_in + low_back(matmul_hi(attended, w_out))
    normed = low(rms_scale(mixed_rows, gain_vec))
    gate_pre = low_back(matmul_hi(normed, w_gate))
    up_pre = low_back(matmul_hi(normed, w_up))
    hidden = low(jax.nn.silu(gate_pre) * up_pre)
    return mixed_rows + low_back(matmul_hi(hidden, w_down))

def taylor_attention(queries, keys_in, values_in, segment):
    block_rows = min(512, TOKENS)
    n_blocks = TOKENS // block_rows
    lin_coef = FEAT ** (-0.5)
    sq_coef = 0.5 / FEAT
    row_index = jnp.arange(block_rows, dtype=jnp.int32)
    causal = row_index[:, None] >= row_index[None, :]

    def run_block(carried, pieces):
        prefix_state, prefix_sum, seg_before = carried
        q_blk, k_blk, v_blk, seg_blk = pieces
        q_dot_k = jnp.einsum('thf,shf->hts', q_blk, k_blk, precision=PRECISE)
        allowed = (causal & (seg_blk[:, None] == seg_blk[None, :])).astype(jnp.float32)
        scores = (1.0 + lin_coef * q_dot_k + sq_coef * q_dot_k * q_dot_k) * allowed[None]
        q_feats = features(q_blk)
        continues = (seg_blk == seg_before).astype(jnp.float32)
        numerator = jnp.einsum('hts,shv->thv', scores, v_blk, precision=PRECISE) + continues[:, None, None] * jnp.einsum('thx,hxv->thv', q_feats, prefix_state, precision=PRECISE)
        denominator = lax.optimization_barrier(jnp.sum(scores, axis=2)).T + continues[:, None] * jnp.einsum('thx,hx->th', q_feats, prefix_sum, precision=PRECISE)
        seg_last = seg_blk[-1].astype(jnp.int32)
        in_tail = (seg_blk == seg_last).astype(jnp.float32)
        keeps = (seg_last == seg_before).astype(jnp.float32)
        k_feats = features(k_blk) * in_tail[:, None, None]
        prefix_state = keeps * prefix_state + jnp.einsum('thx,thv->hxv', k_feats, v_blk, precision=PRECISE)
        prefix_sum = keeps * prefix_sum + lax.optimization_barrier(jnp.sum(k_feats, axis=0))
        return ((prefix_state, prefix_sum, seg_last), numerator / denominator[:, :, None])
    initial = (jnp.zeros((HEADS, FEATX, VDIM), jnp.float32), jnp.zeros((HEADS, FEATX), jnp.float32), jnp.array(-1, jnp.int32))
    pieces = (queries.reshape(n_blocks, block_rows, HEADS, FEAT), keys_in.reshape(n_blocks, block_rows, HEADS, FEAT), values_in.reshape(n_blocks, block_rows, HEADS, VDIM), segment.reshape(n_blocks, block_rows).astype(jnp.int32))
    carried, result = lax.scan(jax.checkpoint(run_block), initial, pieces)
    return result.reshape(TOKENS, HEADS * VDIM)

def window_attention(queries, keys_in, values_in, segment):
    block_rows = min(512, TOKENS)
    n_blocks = TOKENS // block_rows
    rim = WINDOW - 1
    scaling = VDIM ** (-0.5)
    keys_pad = jnp.pad(keys_in, ((rim, 0), (0, 0), (0, 0)))
    values_pad = jnp.pad(values_in, ((rim, 0), (0, 0), (0, 0)))
    seg_pad = jnp.concatenate([jnp.full((rim,), -1, jnp.int32), segment.astype(jnp.int32)])
    offsets = jnp.arange(block_rows, dtype=jnp.int32)[:, None] - jnp.arange(block_rows + rim, dtype=jnp.int32)[None, :] + rim
    in_window = (offsets >= 0) & (offsets < WINDOW)

    def run_block(block_id):
        first_row = block_id * block_rows
        q_blk = lax.dynamic_slice_in_dim(queries, first_row, block_rows)
        k_blk = lax.dynamic_slice_in_dim(keys_pad, first_row, block_rows + rim)
        v_blk = lax.dynamic_slice_in_dim(values_pad, first_row, block_rows + rim)
        seg_q = lax.dynamic_slice_in_dim(segment, first_row, block_rows)
        seg_k = lax.dynamic_slice_in_dim(seg_pad, first_row, block_rows + rim)
        allowed = in_window & (seg_q[:, None] == seg_k[None, :])
        scores = low_back(jnp.einsum('thd,shd->hts', q_blk, k_blk, precision=PRECISE) * scaling)
        scores = jnp.where(allowed[None], scores, -1e+30)
        row_peak = lax.optimization_barrier(jnp.max(scores, axis=-1, keepdims=True))
        weights = jnp.exp(scores - row_peak)
        probs = weights / lax.optimization_barrier(jnp.sum(weights, axis=-1, keepdims=True))
        return jnp.einsum('hts,shd->thd', low(probs), v_blk, precision=PRECISE)
    result = lax.map(jax.checkpoint(run_block), jnp.arange(n_blocks, dtype=jnp.int32))
    return result.reshape(TOKENS, HEADS * VDIM)

def reference(layer_input, lengths, gain_a1, lin_q, lin_k, lin_v, lin_out, gain_a2, mlp_a_gate, mlp_a_up, mlp_a_down, gain_b1, win_q, win_k, win_v, win_out, gain_b2, mlp_b_gate, mlp_b_up, mlp_b_down, cotangent):
    positions = jnp.arange(TOKENS, dtype=jnp.int32)
    segment = segment_ids(lengths, positions)
    params = tuple((member.astype(jnp.float32) for member in (gain_a1, lin_q, lin_k, lin_v, lin_out, gain_a2, mlp_a_gate, mlp_a_up, mlp_a_down, gain_b1, win_q, win_k, win_v, win_out, gain_b2, mlp_b_gate, mlp_b_up, mlp_b_down)))

    def forward(rows_in, weights):
        queries, keys_in, values_in = by_rows(lambda row_block: project_in(row_block, weights[0], weights[1], weights[2], weights[3]), (rows_in,))
        taylor_out = taylor_attention(queries.reshape(TOKENS, HEADS, FEAT), keys_in.reshape(TOKENS, HEADS, FEAT), values_in.reshape(TOKENS, HEADS, VDIM), segment)
        attended = low_back(low(taylor_out))
        layer_a = by_rows(lambda row_block, att_block: finish_layer(row_block, att_block, weights[4], weights[5], weights[6], weights[7], weights[8]), (rows_in, attended))
        queries, keys_in, values_in = by_rows(lambda row_block: project_in(row_block, weights[9], weights[10], weights[11], weights[12]), (layer_a,))
        window_out = window_attention(queries.reshape(TOKENS, HEADS, VDIM), keys_in.reshape(TOKENS, HEADS, VDIM), values_in.reshape(TOKENS, HEADS, VDIM), segment)
        attended = low_back(low(window_out))
        return by_rows(lambda row_block, att_block: finish_layer(row_block, att_block, weights[13], weights[14], weights[15], weights[16], weights[17]), (layer_a, attended))
    output, pull_back = jax.vjp(forward, layer_input.astype(jnp.float32), params)
    grad_rows, grads = pull_back(cotangent.astype(jnp.float32))
    return (output.astype(jnp.bfloat16), grad_rows, grads[0], grads[1], grads[2], grads[3], grads[4], grads[5], grads[6], grads[7], grads[8], grads[9], grads[10], grads[11], grads[12], grads[13], grads[14], grads[15], grads[16], grads[17])
```

```python
import functools

import jax
import jax.numpy as jnp
import numpy as np
from jax import lax
from jax.experimental import pallas as pl
from jax.experimental.pallas import tpu as pltpu
from jax.sharding import Mesh
from jax.sharding import PartitionSpec as P

D = 1024
HEADS = 16
FEAT = 16
WINDOW = 64
NTP = 8
RIM = 64
SROWS = 160
EPSILON = 1e-05
AXES = ("sh", "sy", "sx", "hh", "hl")
TP = ("sy", "sx", "hl")
GROUP = ("sh", "hh")
MESH_ID = pl.DeviceIdType.MESH
F32 = jnp.float32
BF16 = jnp.bfloat16
VM = pltpu.VMEM
LIMIT = 56 * 1024 * 1024


def vmem_specs(count):
    return [pl.BlockSpec(memory_space=pltpu.VMEM)] * count


def matmul(left, right):
    return jnp.dot(left, right, preferred_element_type=F32)


def matmul_tn(left, right):
    return lax.dot_general(left, right, (((0,), (0,)), ((), ())), preferred_element_type=F32)


def matmul_nt(left, right):
    return lax.dot_general(left, right, (((1,), (1,)), ((), ())), preferred_element_type=F32)


def plane_place():
    sy, sx, c = lax.axis_index("sy"), lax.axis_index("sx"), lax.axis_index("hl")
    me = sy * 2 + sx
    xn = sy * 2 + (1 - sx)
    yn = (1 - sy) * 2 + sx
    dg = 3 - me
    return me, xn, yn, dg, c, {"sx": 1 - sx}, {"sy": 1 - sy}, {"hl": 1 - c}


def remote(src, dst, ssem, rsem, target):
    copy = pltpu.make_async_remote_copy(
        src_ref=src, dst_ref=dst, send_sem=ssem, recv_sem=rsem, device_id=target, device_id_type=MESH_ID
    )
    copy.start()
    return copy


AG_COPIES = 13
RS_COPIES = 10


def drain(stages):
    for _ in stages:
        pass


def gather_rows(full, ssem, rsem):
    me, xn, yn, dg, c, to_x, to_y, to_c = plane_place()

    def send(k, block, half, target):
        view = full.at[block, c, half]
        return remote(view, view, ssem.at[k], rsem.at[k], target)

    cps = {}
    cps[1] = send(1, me, 0, to_x)
    cps[3] = send(3, me, 1, to_y)
    cps[2] = send(2, me, 1, to_x)
    cps[4] = send(4, me, 0, to_y)
    own = full.at[me, c]
    cps[0] = remote(own, own, ssem.at[0], rsem.at[0], to_c)
    yield
    cps[1].wait_recv()
    cps[5] = send(5, xn, 0, to_y)
    cps[6] = send(6, xn, 0, to_c)
    cps[3].wait_recv()
    cps[7] = send(7, yn, 1, to_x)
    cps[8] = send(8, yn, 1, to_c)
    yield
    cps[2].wait_recv()
    cps[9] = send(9, xn, 1, to_c)
    cps[4].wait_recv()
    cps[10] = send(10, yn, 0, to_c)
    cps[5].wait_recv()
    cps[11] = send(11, dg, 0, to_c)
    cps[7].wait_recv()
    cps[12] = send(12, dg, 1, to_c)
    yield
    for k in (0, 6, 8, 9, 10, 11, 12):
        cps[k].wait_recv()
    for k in range(AG_COPIES):
        cps[k].wait_send()


def scatter_rows(part, own, cb, sb, keep, r1, r2, ssem, rsem):
    me, xn, yn, dg, c, to_x, to_y, to_c = plane_place()
    cps = {}
    for k, block in enumerate((dg, xn, yn, me)):
        cps[k] = remote(part.at[block, 1 - c], cb.at[k], ssem.at[k], rsem.at[k], to_c)

    def both(k, block, half):
        return part[block, c, half].astype(F32) + cb[k, half].astype(F32)

    yield
    cps[0].wait_recv()
    sb[0, 0] = both(0, dg, 0).astype(BF16)
    cps[4] = remote(sb.at[0, 0], r1.at[0, 0], ssem.at[4], rsem.at[4], to_x)
    sb[0, 1] = both(0, dg, 1).astype(BF16)
    cps[5] = remote(sb.at[0, 1], r1.at[1, 0], ssem.at[5], rsem.at[5], to_y)
    cps[1].wait_recv()
    sb[1, 0] = both(1, xn, 0).astype(BF16)
    cps[6] = remote(sb.at[1, 0], r1.at[0, 1], ssem.at[6], rsem.at[6], to_x)
    cps[2].wait_recv()
    sb[2, 1] = both(2, yn, 1).astype(BF16)
    cps[7] = remote(sb.at[2, 1], r1.at[1, 1], ssem.at[7], rsem.at[7], to_y)
    keep[0] = both(2, yn, 0)
    keep[1] = both(1, xn, 1)
    cps[3].wait_recv()
    own[0] = both(3, me, 0)
    own[1] = both(3, me, 1)
    yield
    cps[4].wait_recv()
    sb[2, 0] = (keep[0] + r1[0, 0].astype(F32)).astype(BF16)
    cps[8] = remote(sb.at[2, 0], r2.at[0], ssem.at[8], rsem.at[8], to_y)
    cps[5].wait_recv()
    sb[1, 1] = (keep[1] + r1[1, 0].astype(F32)).astype(BF16)
    cps[9] = remote(sb.at[1, 1], r2.at[1], ssem.at[9], rsem.at[9], to_x)
    yield
    cps[6].wait_recv()
    own[0] += r1[0, 1].astype(F32)
    cps[7].wait_recv()
    own[1] += r1[1, 1].astype(F32)
    cps[8].wait_recv()
    own[0] += r2[0].astype(F32)
    cps[9].wait_recv()
    own[1] += r2[1].astype(F32)
    for k in range(RS_COPIES):
        cps[k].wait_send()


def rs_scratch():
    return [
        VM((2, 64, D), F32),
        VM((4, 2, 64, D), BF16),
        VM((3, 2, 64, D), BF16),
        VM((2, 64, D), F32),
        VM((2, 2, 64, D), BF16),
        VM((2, 64, D), BF16),
        pltpu.SemaphoreType.DMA((RS_COPIES,)),
        pltpu.SemaphoreType.DMA((RS_COPIES,)),
    ]


def ag_scratch():
    return [pltpu.SemaphoreType.DMA((AG_COPIES,)), pltpu.SemaphoreType.DMA((AG_COPIES,))]


def cost(micros):
    return pl.CostEstimate(flops=0, bytes_accessed=int(micros * 3.0e6), transcendentals=0)


def group_place():
    return lax.axis_index("sh") * lax.axis_size("hh") + lax.axis_index("hh")


def group_peer(k, count):
    nhh = lax.axis_size("hh")
    other = lax.rem(group_place() + k, count)
    sh, hh = other // nhh, lax.rem(other, nhh)
    return other, sh, hh, {"sh": sh, "hh": hh}


def place_peer(k):
    coords = {}
    for bit, axis in enumerate(("hl", "sx", "sy")):
        here = lax.axis_index(axis)
        coords[axis] = 1 - here if (k >> bit) & 1 else here
    target = {axis: v for bit, (axis, v) in enumerate(coords.items()) if (k >> bit) & 1}
    return coords["sy"] * 2 + coords["sx"], coords["hl"], target


def barrier_of(plane, group, count):
    barrier = pltpu.get_barrier_semaphore()
    seen = 0
    for k in ((1, 2, 4) if plane == 3 else range(1, 8)) if plane else ():
        _, _, target = place_peer(k)
        pl.semaphore_signal(barrier, inc=1, device_id=target, device_id_type=MESH_ID)
        seen += 1
    if group:
        for k in range(1, count):
            target = group_peer(k, count)[3]
            pl.semaphore_signal(barrier, inc=1, device_id=target, device_id_type=MESH_ID)
            seen += 1
    pl.semaphore_wait(barrier, seen)


class Job:
    def __init__(self, kind, src, cols=None):
        self.kind, self.src, self.cols = kind, src, cols

    def out_shape(self):
        nsh, nhh = lax.axis_size("sh"), lax.axis_size("hh")
        shape = list(self.src.shape)
        if self.cols:
            shape[-1] = self.cols[1]
        if self.kind == "zg":
            shape = [nsh * 4, nhh] + shape[1:]
        if self.kind == "zr":
            shape = [nsh * nhh] + shape
        if self.kind == "zs":
            shape = [nsh * nhh, 4] + shape[2:]
        return jax.ShapeDtypeStruct(tuple(shape), self.src.dtype)


def job_start(kind, cols, src, out, ssem, rsem, lsem, count):
    sh, hh, g = lax.axis_index("sh"), lax.axis_index("hh"), group_place()
    cps = []
    local = None
    if kind == "zg":
        view = src.at[:, :, :, pl.ds(cols[0], cols[1])] if cols else src
        dst = out.at[pl.ds(sh * 4, 4), hh]
        for k in range(1, count):
            cps.append(remote(view, dst, ssem.at[k], rsem.at[k], group_peer(k, count)[3]))
        local = (view, dst)
    if kind == "zr":
        for k in range(1, count):
            cps.append(remote(src, out.at[g], ssem.at[k], rsem.at[k], group_peer(k, count)[3]))
        local = (src, out.at[g])
    if kind == "zs":
        part = lambda psh, phh: (
            src.at[pl.ds(psh * 4, 4), phh, :, :, pl.ds(cols[0], cols[1])]
            if cols
            else src.at[pl.ds(psh * 4, 4), phh]
        )
        for k in range(1, count):
            _, psh, phh, target = group_peer(k, count)
            cps.append(remote(part(psh, phh), out.at[g], ssem.at[k], rsem.at[k], target))
        local = (part(sh, hh), out.at[g])
    if kind == "zt":
        for k in range(1, count):
            other, _, _, target = group_peer(k, count)
            cps.append(remote(src.at[other], out.at[g], ssem.at[k], rsem.at[k], target))
        local = (src.at[g], out.at[g])
    if kind == "pa":
        s, c, _ = place_peer(0)
        for k in range(1, 8):
            ps, pc, target = place_peer(k)
            cps.append(remote(src.at[ps, pc], out.at[s, c], ssem.at[k], rsem.at[k], target))
        local = (src.at[s, c], out.at[s, c])
    cp = pltpu.make_async_copy(local[0], local[1], lsem)
    cp.start()
    return cps, cp


def job_wait(started):
    for cps, cp in started:
        for one in cps:
            one.wait()
        cp.wait()


ANY = pl.BlockSpec(memory_space=pl.ANY)
VMEM = pl.BlockSpec(memory_space=pltpu.VMEM)
SMEM = pl.BlockSpec(memory_space=pltpu.SMEM)


def step(body, ins, outs, scratch, jobs, plane, group, name, collective, micros):
    count = lax.axis_size(GROUP)
    n_in, n_out, n_job = len(ins), len(outs), len(jobs)
    kinds = [(job.kind, job.cols) for job in jobs]
    plane = 7 if any(job.kind == "pa" for job in jobs) else plane
    group = group or any(job.kind != "pa" for job in jobs)
    slots = max(count, 8)

    def kernel(*refs):
        in_refs, refs = refs[:n_in], refs[n_in:]
        sources, refs = refs[:n_job], refs[n_job:]
        out_refs, refs = refs[:n_out], refs[n_out:]
        results, refs = refs[:n_job], refs[n_job:]
        sems, own = (refs[-3:], refs[:-3]) if n_job else ((), refs)
        barrier_of(plane, group, count)
        started = []

        def begin():
            for i, (kind, cols) in enumerate(kinds):
                started.append(
                    job_start(
                        kind, cols, sources[i], results[i],
                        sems[0].at[i], sems[1].at[i], sems[2].at[i], count,
                    )
                )

        body(begin, *in_refs, *out_refs, *own)
        if n_job and not started:
            begin()
        job_wait(started)

    extra = [
        pltpu.SemaphoreType.DMA((n_job, slots)),
        pltpu.SemaphoreType.DMA((n_job, slots)),
        pltpu.SemaphoreType.DMA((n_job,)),
    ]
    result = pl.pallas_call(
        kernel,
        out_shape=tuple(o for o, _ in outs) + tuple(job.out_shape() for job in jobs),
        in_specs=[spec for _, spec in ins] + [ANY] * n_job,
        out_specs=tuple(spec for _, spec in outs) + (ANY,) * n_job,
        scratch_shapes=list(scratch) + (extra if n_job else []),
        compiler_params=pltpu.CompilerParams(
            collective_id=collective, has_side_effects=True, vmem_limit_bytes=LIMIT
        ),
        cost_estimate=cost(micros),
        name=name,
    )(*[v for v, _ in ins], *[job.src for job in jobs])
    return result[:n_out], result[n_out:]


FULL = jax.ShapeDtypeStruct((4, 2, 2, 64, D), BF16)
OWN = jax.ShapeDtypeStruct((2, 64, D), F32)


def flat(full):
    return full.reshape(1024, D)


def blocks(rows):
    return rows.reshape(4, 2, 2, 64, D)


def vmem(*values):
    return [(v, VMEM) for v in values]


def normed_half(u, gain):
    inv = lax.rsqrt(jnp.mean(u * u, axis=-1, keepdims=True) + EPSILON)
    return (u * inv * gain).astype(BF16)


def first(x, lin, jobs, collective):
    count = lax.axis_size(GROUP)
    nsh, nhh = lax.axis_size("sh"), lax.axis_size("hh")

    def body(begin, x_ref, lin_ref, full, mid, lin_full, s1, r1, s2, r2, l2):
        me, _, _, _, c, _, _, _ = plane_place()
        moved = job_start("pa", None, lin_ref, mid, s2.at[0], r2.at[0], l2.at[0], count)
        full[me, c] = x_ref[...]
        stages = gather_rows(full, s1, r1)
        next(stages)
        job_wait([moved])
        spread = job_start("zg", None, mid, lin_full, s2.at[1], r2.at[1], l2.at[1], count)
        next(stages)
        drain(stages)
        begin()
        job_wait([spread])

    slots = max(count, 8)
    return step(
        body,
        vmem(x) + [(lin, ANY)],
        [
            (FULL, VMEM),
            (jax.ShapeDtypeStruct(lin.shape, BF16), ANY),
            (jax.ShapeDtypeStruct((nsh * 4, nhh) + lin.shape[1:], BF16), ANY),
        ],
        ag_scratch()
        + [
            pltpu.SemaphoreType.DMA((2, slots)),
            pltpu.SemaphoreType.DMA((2, slots)),
            pltpu.SemaphoreType.DMA((2,)),
        ],
        jobs, 7, True, "first", collective, 25,
    )


def forward_step(part, u, gain, jobs, collective):
    def body(begin, part, u_ref, gain_ref, unew, full, own, cb, sb, keep, r1, r2, ss, rs, ags, agr):
        me, _, _, _, c, _, _, _ = plane_place()
        stages = scatter_rows(part, own, cb, sb, keep, r1, r2, ss, rs)
        next(stages)
        begin()
        drain(stages)
        for half in range(2):
            u = u_ref[half] + own[half]
            unew[half] = u
            full[me, c, half] = normed_half(u, gain_ref[...])
        drain(gather_rows(full, ags, agr))

    return step(
        body, vmem(blocks(part), u, gain), vmem(OWN, FULL), rs_scratch() + ag_scratch(),
        jobs, 3, False, "forward_step", collective, 28,
    )


def norm_back_half(dn, u, gain, upstream):
    inv = lax.rsqrt(jnp.mean(u * u, axis=-1, keepdims=True) + EPSILON)
    gained = dn * gain
    inner = jnp.mean(gained * u, axis=-1, keepdims=True)
    scaled = u * inv
    grad = upstream + inv * gained - scaled * (inv * inv * inner)
    return grad, jnp.sum(dn * scaled, axis=0, keepdims=True)


def backward_step(part, u, gain, upstream, jobs, collective, last=False):
    def body(begin, part, u_ref, gain_ref, up_ref, gnew, ggain, *rest):
        me, _, _, _, c, _, _, _ = plane_place()
        full, rest = (None, rest) if last else (rest[0], rest[1:])
        stages = scatter_rows(part, *rest[:8])
        next(stages)
        begin()
        drain(stages)
        own = rest[0]
        total = None
        for half in range(2):
            grad, gain_part = norm_back_half(
                own[half], u_ref[half].astype(F32), gain_ref[...], up_ref[half].astype(F32)
            )
            gnew[half] = grad
            total = gain_part if total is None else total + gain_part
            if not last:
                full[me, c, half] = grad.astype(BF16)
        ggain[...] = total
        if not last:
            drain(gather_rows(full, rest[8], rest[9]))

    outs = vmem(OWN, jax.ShapeDtypeStruct((1, D), F32)) + ([] if last else vmem(FULL))
    return step(
        body, vmem(blocks(part), u, gain, upstream), outs,
        rs_scratch() + ([] if last else ag_scratch()),
        jobs, 3, False, "last_backward" if last else "backward_step", collective, 16 if last else 28,
    )


def taylor_tables():
    pick = np.zeros((4, 2, 128, 256), np.float32)
    coef = np.zeros((8, 256), np.float32)
    pairs = [(i, j) for i in range(FEAT) for j in range(i, FEAT)]
    one = 4 * FEAT
    for x, (i, j) in enumerate(pairs):
        coef[:, x] = (2.0 * FEAT) ** -0.5 if i == j else FEAT**-0.5
        for t in range(4):
            pick[t, 0, t * FEAT + i, x] = 1.0
            pick[t, 1, t * FEAT + j, x] = 1.0
    for i in range(FEAT):
        x = len(pairs) + i
        coef[:, x] = FEAT**-0.25
        for t in range(4):
            pick[t, 0, t * FEAT + i, x] = 1.0
            pick[t, 1, one, x] = 1.0
    x = len(pairs) + FEAT
    coef[:, x] = 1.0
    pick[:, 0, one, x] = 1.0
    pick[:, 1, one, x] = 1.0
    shift = np.zeros((128, 128), np.float32)
    for i in range(2 * FEAT):
        shift[2 * FEAT + i, i] = 1.0
    return jnp.asarray(pick, BF16), jnp.asarray(coef, F32), jnp.asarray(shift, BF16)


def lanes(rows, width):
    return lax.broadcasted_iota(jnp.int32, (rows, width), 1)


def group_send(count, st, sm, ssem, rsem):
    g = group_place()
    nhh = lax.axis_size("hh")
    cps = []
    for k in range(1, count):
        other = lax.rem(g + k, count)
        target = {"sh": other // nhh, "hh": lax.rem(other, nhh)}
        cps.append(remote(st.at[g], st.at[g], ssem.at[0, k], rsem.at[0, k], target))
        cps.append(remote(sm.at[g], sm.at[g], ssem.at[1, k], rsem.at[1, k], target))
    return cps


def phi_of(x, pick, coef, t):
    left = matmul(x, pick[t, 0])
    right = matmul(x, pick[t, 1])
    return left, right, (left * right * coef).astype(BF16)


def taylor_forward_kernel(
    count, begin, qkv, seg_col, seg_row, last_ref, before_ref, pick, coef_ref, shift, cot_ref, mix,
    o_ref, y_ref, den_ref, pre_ref, psum_ref, cfull,
    st, sm, phis, ssem, rsem, ags, agr,
):
    g = group_place()
    me, _, _, _, c, _, _, _ = plane_place()
    cfull[me, c] = cot_ref[...]
    stages = gather_rows(cfull, ags, agr)
    next(stages)
    coef = coef_ref[0:1, :]
    left_half = lanes(256, 128) < 64

    def states(s, carry):
        rows = pl.ds(s * 256, 256)
        x = jnp.where(lanes(256, 128) == 4 * FEAT, jnp.ones((), BF16), qkv[rows, 0:128])
        v = qkv[rows, 128:256]
        tail = seg_col[rows, :] == last_ref[rows, :]
        v_tail = jnp.where(tail, v, jnp.zeros((), BF16))
        state = jnp.zeros((256, 128), F32)
        for h in range(2):
            _, _, phi_k = phi_of(x, pick, coef, 2 + h)
            side = left_half if h == 0 else jnp.logical_not(left_half)
            state += matmul_tn(phi_k, jnp.where(side, v_tail, jnp.zeros((), BF16)))
            total = jnp.sum(jnp.where(tail, phi_k.astype(F32), 0.0), axis=0, keepdims=True)
            sm[g, s, h : h + 1, :] = total
            _, _, phi_q = phi_of(x, pick, coef, h)
            phis[h, rows, :] = phi_q
        st[g, s] = state[:SROWS].astype(BF16)
        return carry

    sm[g] = jnp.zeros((4, 8, 256), F32)
    lax.fori_loop(0, 4, states, 0)
    cps = group_send(count, st, sm, ssem, rsem)
    begin()
    next(stages)

    def inner(s, carry):
        rows = pl.ds(s * 256, 256)
        x = qkv[rows, 0:128]
        v = qkv[rows, 128:256]
        k = matmul(x, shift[...]).astype(BF16)
        lane = lanes(256, 128)
        order = lax.broadcasted_iota(jnp.int32, (256, 256), 0) >= lanes(256, 256)
        allowed = order & (seg_col[rows, :] == seg_row[s])
        num = jnp.zeros((256, 128), F32)
        dens = []
        for h in range(2):
            q = jnp.where(lane // FEAT == h, x, jnp.zeros((), BF16))
            dot = matmul_nt(q, k)
            score = jnp.where(allowed, 1.0 + dot * FEAT**-0.5 + dot * dot * (0.5 / FEAT), 0.0)
            side = left_half if h == 0 else jnp.logical_not(left_half)
            num += matmul(score.astype(BF16), jnp.where(side, v, jnp.zeros((), BF16)))
            dens.append(jnp.sum(score, axis=1, keepdims=True))
        y_ref[rows, :] = num
        den_ref[rows, :] = jnp.where(left_half, dens[0], dens[1])
        return carry

    lax.fori_loop(0, 4, inner, 0)
    next(stages)
    for cp in cps:
        cp.wait_recv()

    def finish(s, carry):
        rows = pl.ds(s * 256, 256)

        def add(i, acc):
            state, total = acc
            m = mix[s, i]
            return (
                state + m * st[i // 4, lax.rem(i, 4)].astype(F32),
                total + m * sm[i // 4, lax.rem(i, 4)],
            )

        state, total = lax.fori_loop(
            0, 4 * count, add, (jnp.zeros((SROWS, 128), F32), jnp.zeros((8, 256), F32))
        )
        state = state.astype(BF16)
        pre_ref[s] = state
        psum_ref[s] = total
        cont = seg_col[rows, :] == before_ref[rows, :]
        num = jnp.zeros((256, 128), F32)
        dens = []
        for h in range(2):
            phi_q = phis[h, rows, :]
            side = left_half if h == 0 else jnp.logical_not(left_half)
            part = matmul(phi_q[:, :SROWS], state)
            num = jnp.where(side, part, num)
            dens.append(jnp.sum(phi_q.astype(F32) * total[h : h + 1], axis=1, keepdims=True))
        num = jnp.where(cont, num, 0.0) + y_ref[rows, :]
        den = jnp.where(cont, jnp.where(left_half, dens[0], dens[1]), 0.0) + den_ref[rows, :]
        y = num / den
        y_ref[rows, :] = y
        den_ref[rows, :] = den
        o_ref[rows, :] = y.astype(BF16)
        return carry

    lax.fori_loop(0, 4, finish, 0)
    drain(stages)
    for cp in cps:
        cp.wait_send()


def taylor_forward(qkv, seg, tables, cot, jobs, count, collective):
    return step(
        functools.partial(taylor_forward_kernel, count),
        vmem(qkv, seg["col"], seg["row"], seg["last"], seg["before"], *tables, cot)
        + [(seg["mix"], SMEM)],
        vmem(
            jax.ShapeDtypeStruct((1024, 128), BF16),
            jax.ShapeDtypeStruct((1024, 128), F32),
            jax.ShapeDtypeStruct((1024, 128), F32),
            jax.ShapeDtypeStruct((4, SROWS, 128), BF16),
            jax.ShapeDtypeStruct((4, 8, 256), F32),
            FULL,
        ),
        [
            VM((count, 4, SROWS, 128), BF16),
            VM((count, 4, 8, 256), F32),
            VM((2, 1024, 256), BF16),
            pltpu.SemaphoreType.DMA((2, count)),
            pltpu.SemaphoreType.DMA((2, count)),
        ]
        + ag_scratch(),
        jobs, 3, True, "taylor_forward", collective, 28,
    )


def taylor_backward_kernel(
    count, begin, qkv, do_ref, y_ref, den_ref, pre_ref, psum_ref,
    seg_col, seg_row, last_ref, before_ref, pick, coef_ref, shift, mix, out_ref,
    st, sm, acc, dnum_ref, ddens, ssem, rsem,
):
    g = group_place()
    coef = coef_ref[0:1, :]
    left_half = lanes(256, 128) < 64
    zero = jnp.zeros((), BF16)

    def sides(h):
        return left_half if h == 0 else jnp.logical_not(left_half)

    def feature_back(dphi, left, right, t):
        grad = dphi * coef
        return matmul_nt((grad * right).astype(BF16), pick[t, 0]) + matmul_nt(
            (grad * left).astype(BF16), pick[t, 1]
        )

    def states(s, carry):
        rows = pl.ds(s * 256, 256)
        x = jnp.where(lanes(256, 128) == 4 * FEAT, jnp.ones((), BF16), qkv[rows, 0:128])
        do = do_ref[rows, :].astype(F32)
        den = den_ref[rows, :]
        dnum = do / den
        dnum_low = dnum.astype(BF16)
        dnum_ref[rows, :] = dnum_low
        weighted = dnum * y_ref[rows, :]
        cont = seg_col[rows, :] == before_ref[rows, :]
        d_cont = jnp.where(cont, dnum_low, zero)
        pre = pre_ref[s]
        state = jnp.zeros((256, 128), F32)
        grad = jnp.zeros((256, 128), F32)
        for h in range(2):
            dden = -jnp.sum(jnp.where(sides(h), weighted, 0.0), axis=1, keepdims=True)
            ddens[h, rows, :] = jnp.broadcast_to(dden, (256, 128))
            left, right, phi_q = phi_of(x, pick, coef, h)
            d_side = jnp.where(sides(h), d_cont, zero)
            state += matmul_tn(phi_q, d_side)
            dden_cont = jnp.where(cont, dden, 0.0)
            sm[g, s, h : h + 1, :] = jnp.sum(
                phi_q.astype(F32) * dden_cont, axis=0, keepdims=True
            )
            dphi = jnp.concatenate(
                [matmul_nt(d_side, pre), jnp.zeros((256, 256 - SROWS), F32)], axis=1
            ) + dden_cont * psum_ref[s, h : h + 1, :]
            grad += feature_back(dphi, left, right, h)
        st[g, s] = state[:SROWS].astype(BF16)
        acc[0, rows, :] = grad
        return carry

    sm[g] = jnp.zeros((4, 8, 256), F32)
    lax.fori_loop(0, 4, states, 0)
    cps = group_send(count, st, sm, ssem, rsem)
    begin()

    def inner(s, carry):
        rows = pl.ds(s * 256, 256)
        x = qkv[rows, 0:128]
        v = qkv[rows, 128:256]
        dnum = dnum_ref[rows, :]
        k_low = matmul(x, shift[...]).astype(BF16)
        lane = lanes(256, 128)
        order = lax.broadcasted_iota(jnp.int32, (256, 256), 0) >= lanes(256, 256)
        allowed = order & (seg_col[rows, :] == seg_row[s])
        dq = jnp.zeros((256, 128), F32)
        dk = jnp.zeros((256, 128), F32)
        dv = jnp.zeros((256, 128), F32)
        for h in range(2):
            mine = lane // FEAT == h
            q = jnp.where(mine, x, zero)
            dot = matmul_nt(q, k_low)
            score = jnp.where(allowed, 1.0 + dot * FEAT**-0.5 + dot * dot * (0.5 / FEAT), 0.0)
            d_side = jnp.where(sides(h), dnum, zero)
            dscore = matmul_nt(d_side, v) + ddens[h, rows, 0:1]
            e = jnp.where(allowed, dscore * (FEAT**-0.5 + dot * (1.0 / FEAT)), 0.0).astype(BF16)
            dq += matmul(e, jnp.where(mine, k_low, zero))
            dk += matmul_tn(e, q)
            dv += matmul_tn(score.astype(BF16), d_side)
        acc[0, rows, :] += dq
        acc[1, rows, :] = dk
        acc[2, rows, :] = dv
        return carry

    lax.fori_loop(0, 4, inner, 0)
    for cp in cps:
        cp.wait_recv()

    def finish(s, carry):
        rows = pl.ds(s * 256, 256)

        def add(i, both):
            state, total = both
            m = mix[s, i]
            return (
                state + m * st[i // 4, lax.rem(i, 4)].astype(F32),
                total + m * sm[i // 4, lax.rem(i, 4)],
            )

        state, total = lax.fori_loop(
            0, 4 * count, add, (jnp.zeros((SROWS, 128), F32), jnp.zeros((8, 256), F32))
        )
        state = state.astype(BF16)
        x = jnp.where(lanes(256, 128) == 4 * FEAT, jnp.ones((), BF16), qkv[rows, 0:128])
        tail = seg_col[rows, :] == last_ref[rows, :]
        v_tail = jnp.where(tail, qkv[rows, 128:256], zero)
        grad = acc[0, rows, :]
        lane = lanes(256, 128)
        dv = jnp.zeros((256, 128), F32)
        for h in range(2):
            left, right, phi_k = phi_of(x, pick, coef, 2 + h)
            dphi = jnp.concatenate(
                [
                    matmul_nt(jnp.where(sides(h), v_tail, zero), state),
                    jnp.zeros((256, 256 - SROWS), F32),
                ],
                axis=1,
            ) + jnp.where(tail, total[h : h + 1], 0.0)
            grad += feature_back(dphi, left, right, 2 + h)
            dv = jnp.where(sides(h), matmul(phi_k[:, :SROWS], state), dv)
        grad += matmul_nt(acc[1, rows, :].astype(BF16), shift[...])
        dv = jnp.where(tail, dv, 0.0) + acc[2, rows, :]
        out_ref[rows, 0:128] = jnp.where(lane < 4 * FEAT, grad, 0.0).astype(BF16)
        out_ref[rows, 128:256] = dv.astype(BF16)
        return carry

    lax.fori_loop(0, 4, finish, 0)
    for cp in cps:
        cp.wait_send()


def taylor_backward(qkv, do, kept, seg, tables, jobs, count, collective):
    return step(
        functools.partial(taylor_backward_kernel, count),
        vmem(qkv, do, *kept, seg["col"], seg["row"], seg["last"], seg["before"], *tables)
        + [(seg["mix_back"], SMEM)],
        vmem(jax.ShapeDtypeStruct((1024, 256), BF16)),
        [
            VM((count, 4, SROWS, 128), BF16),
            VM((count, 4, 8, 256), F32),
            VM((3, 1024, 128), F32),
            VM((1024, 128), BF16),
            VM((2, 1024, 128), F32),
            pltpu.SemaphoreType.DMA((2, count)),
            pltpu.SemaphoreType.DMA((2, count)),
        ],
        jobs, 0, True, "taylor_backward", collective, 28,
    )


def rim_target(s, forward):
    hh, sh = lax.axis_index("hh"), lax.axis_index("sh")
    nhh, nsh = lax.axis_size("hh"), lax.axis_size("sh")
    if forward:
        wraps = jnp.where(hh == nhh - 1, 1, 0)
        slot = lax.rem(s + wraps, 4)
        leaves = wraps if s == 3 else 0
        return {"sh": lax.rem(sh + leaves, nsh), "hh": lax.rem(hh + 1, nhh)}, slot
    wraps = jnp.where(hh == 0, 1, 0)
    slot = lax.rem(s + 4 - wraps, 4)
    leaves = wraps if s == 0 else 0
    return {"sh": lax.rem(sh + nsh - leaves, nsh), "hh": lax.rem(hh + nhh - 1, nhh)}, slot


def window_mask(seg_col, seg_ext, rows, s):
    i = lax.broadcasted_iota(jnp.int32, (256, 256 + RIM), 0)
    j = lanes(256, 256 + RIM)
    return (j > i) & (j <= i + WINDOW) & (seg_col[rows, :] == seg_ext[s])


def window_probs(q, k, allowed):
    scores = jnp.where(allowed, matmul_nt(q, k) * 64**-0.5, -1e30)
    peak = jnp.max(scores, axis=1, keepdims=True)
    weights = jnp.exp(scores - peak)
    return weights / jnp.sum(weights, axis=1, keepdims=True)


def window_forward_kernel(begin, qkv, seg_col, seg_ext, o_ref, ext, rim, ssem, rsem):
    cps = []
    for s in range(4):
        target, slot = rim_target(s, True)
        src = qkv.at[pl.ds(s * 256 + 256 - RIM, RIM), pl.ds(128, 256)]
        cps.append(remote(src, rim.at[slot], ssem.at[s], rsem.at[slot], target))

    begin()

    def fill(s, carry):
        ext[s, RIM:, :] = qkv[pl.ds(s * 256, 256), 128:384]
        return carry

    lax.fori_loop(0, 4, fill, 0)
    for s in range(4):
        pltpu.make_async_copy(rim.at[s], rim.at[s], rsem.at[s]).wait()

    def run(s, carry):
        rows = pl.ds(s * 256, 256)
        ext[s, :RIM, :] = rim[s]
        q = qkv[rows, 0:128]
        k = ext[s, :, 0:128]
        v = ext[s, :, 128:256]
        left_half = lanes(256, 128) < 64
        allowed = window_mask(seg_col, seg_ext, rows, s)
        out = jnp.zeros((256, 128), F32)
        for h in range(2):
            side = left_half if h == 0 else jnp.logical_not(left_half)
            probs = window_probs(jnp.where(side, q, jnp.zeros((), BF16)), k, allowed)
            out = jnp.where(side, matmul(probs.astype(BF16), v), out)
        o_ref[rows, :] = out.astype(BF16)
        return carry

    lax.fori_loop(0, 4, run, 0)
    for cp in cps:
        cp.wait_send()


def window_forward(qkv, seg, jobs, collective):
    return step(
        window_forward_kernel,
        vmem(qkv, seg["col"], seg["ext"]),
        vmem(
            jax.ShapeDtypeStruct((1024, 128), BF16),
            jax.ShapeDtypeStruct((4, 256 + RIM, 256), BF16),
        ),
        [
            VM((4, RIM, 256), BF16),
            pltpu.SemaphoreType.DMA((4,)),
            pltpu.SemaphoreType.DMA((4,)),
        ],
        jobs, 0, True, "window_forward", collective, 14,
    )


def window_backward_kernel(
    begin, qkv, ext, do_ref, seg_col, seg_ext, part, u_ref, out_ref, mixed, acc, back, rim,
    ssem, rsem, own, cb, sb, keep, r1, r2, ss, rs,
):
    stages = scatter_rows(part, own, cb, sb, keep, r1, r2, ss, rs)
    next(stages)
    begin()
    zero = jnp.zeros((), BF16)

    def run(s, carry):
        rows = pl.ds(s * 256, 256)
        q = qkv[rows, 0:128]
        k = ext[s, :, 0:128]
        v = ext[s, :, 128:256]
        do = do_ref[rows, :]
        left_half = lanes(256, 128) < 64
        left_ext = lanes(256 + RIM, 128) < 64
        allowed = window_mask(seg_col, seg_ext, rows, s)
        dq = jnp.zeros((256, 128), F32)
        dk = jnp.zeros((256 + RIM, 128), F32)
        dv = jnp.zeros((256 + RIM, 128), F32)
        for h in range(2):
            side = left_half if h == 0 else jnp.logical_not(left_half)
            q_h = jnp.where(side, q, zero)
            do_h = jnp.where(side, do, zero)
            probs = window_probs(q_h, k, allowed)
            dprobs = matmul_nt(do_h, v)
            inner = jnp.sum(probs * dprobs, axis=1, keepdims=True)
            ds = (probs * (dprobs - inner)).astype(BF16)
            dq = jnp.where(side, matmul(ds, k), dq)
            dk += matmul_tn(ds, q_h)
            dv += matmul_tn(probs.astype(BF16), do_h)
        scale = 64**-0.5
        dk = dk * scale
        out_ref[rows, 0:128] = (dq * scale).astype(BF16)
        acc[rows, 0:128] = dk[RIM:]
        acc[rows, 128:256] = dv[RIM:]
        back[s, :, 0:128] = dk[:RIM].astype(BF16)
        back[s, :, 128:256] = dv[:RIM].astype(BF16)
        return carry

    lax.fori_loop(0, 4, run, 0)
    next(stages)
    cps = []
    for s in range(4):
        target, slot = rim_target(s, False)
        cps.append(remote(back.at[s], rim.at[slot], ssem.at[s], rsem.at[slot], target))
    next(stages)
    for s in range(4):
        pltpu.make_async_copy(rim.at[s], rim.at[s], rsem.at[s]).wait()

    def finish(s, carry):
        out_ref[pl.ds(s * 256, 256 - RIM), 128:384] = acc[pl.ds(s * 256, 256 - RIM), :].astype(BF16)
        rows = pl.ds(s * 256 + 256 - RIM, RIM)
        out_ref[rows, 128:384] = (acc[rows, :] + rim[s].astype(F32)).astype(BF16)
        return carry

    lax.fori_loop(0, 4, finish, 0)
    drain(stages)
    for half in range(2):
        mixed[half] = (u_ref[half] + own[half]).astype(BF16)
    for cp in cps:
        cp.wait_send()


def window_backward(qkv, ext, do, seg, part, u, jobs, collective):
    return step(
        window_backward_kernel,
        vmem(qkv, ext, do, seg["col"], seg["ext"], blocks(part), u),
        vmem(
            jax.ShapeDtypeStruct((1024, 384), BF16), jax.ShapeDtypeStruct((2, 64, D), BF16)
        ),
        [
            VM((1024, 256), F32),
            VM((4, RIM, 256), BF16),
            VM((4, RIM, 256), BF16),
            pltpu.SemaphoreType.DMA((4,)),
            pltpu.SemaphoreType.DMA((4,)),
        ]
        + rs_scratch(),
        jobs, 3, True, "window_backward", collective, 22,
    )


def row_routes():
    nsh, nhh = lax.axis_size("sh"), lax.axis_size("hh")
    groups = nsh * nhh
    routes = []
    for d in range(8 * groups):
        place, group = d // groups, d % groups
        s, c = place // 2, place % 2
        sh, hh = group // nhh, group % nhh
        routes.append((d, ((sh * 4 + s) * nhh + hh) * 2 + c))
    return routes


def segment_ids(lengths, positions):
    starts = jnp.cumsum(lengths) - lengths
    return jnp.sum((positions[..., None] >= starts).astype(jnp.int32), axis=-1) - 1


def segments(lengths, stretch):
    nsh, nhh = lax.axis_size("sh"), lax.axis_size("hh")
    sh, hh = lax.axis_index("sh"), lax.axis_index("hh")
    mine = (sh * 4 + jnp.arange(4, dtype=jnp.int32)) * nhh + hh
    first = mine * 256
    tokens = segment_ids(lengths, first[:, None] + jnp.arange(256, dtype=jnp.int32))
    ext = segment_ids(lengths, first[:, None] - RIM + jnp.arange(256 + RIM, dtype=jnp.int32))
    before = segment_ids(lengths, first - 1)
    last = tokens[:, -1]
    gsh, ghh, gs = jnp.meshgrid(
        jnp.arange(nsh), jnp.arange(nhh), jnp.arange(4), indexing="ij"
    )
    others = ((gsh * 4 + gs) * nhh + ghh).reshape(-1).astype(jnp.int32)
    others_last = segment_ids(lengths, others * 256 + 255)
    others_before = segment_ids(lengths, others * 256 - 1)
    mix = (others[None] < mine[:, None]) & (others_last[None] == before[:, None])
    mix_back = (others[None] > mine[:, None]) & (others_before[None] == last[:, None])
    wide = lambda a: jnp.broadcast_to(a[:, None], (4, 256)).reshape(1024, 1)
    return {
        "col": tokens.reshape(1024, 1),
        "row": tokens.reshape(4, 1, 256),
        "ext": ext.reshape(4, 1, 256 + RIM),
        "last": wide(last),
        "before": wide(before),
        "mix": mix.astype(F32),
        "mix_back": mix_back.astype(F32),
    }


def spread_ff(member):
    rows = member.shape[0]
    width = -(-member.shape[1] // (NTP * 128)) * 128
    padded = jnp.pad(member, ((0, 0), (0, NTP * width - member.shape[1])))
    return padded.reshape(rows, NTP, width)


def on_device(
    layer_input, lengths, gain_a1, lin_q, lin_k, lin_v, lin_out, gain_a2, mlp_a_gate, mlp_a_up,
    mlp_a_down, gain_b1, win_q, win_k, win_v, win_out, gain_b2, mlp_b_gate, mlp_b_up, mlp_b_down,
    cotangent,
):
    count = lax.axis_size(GROUP)
    rows = lin_q.shape[0]
    hidden_size = mlp_a_gate.shape[1]
    gains = jnp.pad(jnp.stack([gain_a1, gain_a2, gain_b1, gain_b2], axis=1), ((0, 0), (0, 60)))
    gains = jnp.broadcast_to(gains[:, None, :], (rows, NTP, 64))
    seg = segments(lengths, 0)
    tables = taylor_tables()

    split = lambda member: member.reshape(rows, NTP, -1)
    bundle_lin = jnp.concatenate(
        [split(lin_q), split(lin_k), gains, split(lin_v)], axis=-1
    ).transpose(1, 0, 2)
    bundle_a = jnp.concatenate(
        [spread_ff(mlp_a_gate), spread_ff(mlp_a_up), spread_ff(mlp_a_down.T)], axis=-1
    ).transpose(1, 0, 2)
    bundle_win = jnp.concatenate([split(win_q), split(win_k), split(win_v)], axis=-1).transpose(
        1, 0, 2
    )
    bundle_b = jnp.concatenate(
        [spread_ff(mlp_b_gate), spread_ff(mlp_b_up), spread_ff(mlp_b_down.T)], axis=-1
    ).transpose(1, 0, 2)
    ff = bundle_a.shape[-1] // 3
    width = bundle_lin.shape[-1]
    nsh, nhh = lax.axis_size("sh"), lax.axis_size("hh")
    places = lambda a: a.reshape(4, 2, rows, a.shape[-1])
    whole = lambda a: a.reshape(D, a.shape[-1])
    parts = lambda a: a.astype(BF16).reshape(nsh * 4, nhh, 2, rows, a.shape[-1])
    total = lambda a: jnp.sum(a.astype(F32), axis=0).astype(BF16)
    own_lin_out = lax.ppermute(lin_out, AXES, row_routes())
    own_win_out = lax.ppermute(win_out, AXES, row_routes())

    x_own = layer_input.reshape(2, 64, D)
    cot_own = cotangent.reshape(2, 64, D)
    (x_full, _, w_lin), (mid_a, mid_win, mid_b) = first(
        x_own, places(bundle_lin),
        [Job("pa", places(bundle_a)), Job("pa", places(bundle_win)), Job("pa", places(bundle_b))], 1,
    )
    w_lin = whole(w_lin)
    gains = w_lin[:, 64:68].astype(F32).T
    g_a1, g_a2, g_b1, g_b2 = (gains[i : i + 1] for i in range(4))
    w_lin = jnp.concatenate([w_lin[:, :64], jnp.zeros((D, 64), BF16), w_lin[:, 128:]], axis=1)
    n_a1 = normed_half(flat(x_full).astype(F32), g_a1)
    qkv_a = matmul(n_a1, w_lin).astype(BF16)
    (o_a, *kept, cot), (w_gate_a, w_lin_out) = taylor_forward(
        qkv_a, seg, tables, cot_own, [Job("zg", mid_a, (0, ff)), Job("zr", own_lin_out)], count, 2
    )
    cot, w_lin_out = flat(cot), w_lin_out.reshape(128, D)
    part = matmul(o_a, w_lin_out).astype(BF16)
    (h_a, n_a2), (w_up_a, w_down_a) = forward_step(
        part, x_own.astype(F32), g_a2, [Job("zg", mid_a, (ff, ff)), Job("zg", mid_a, (2 * ff, ff))], 3
    )
    n_a2 = flat(n_a2)
    w_a = (whole(w_gate_a), whole(w_up_a), whole(w_down_a))

    def mlp_forward(n, w):
        gate, up = matmul(n, w[0]), matmul(n, w[1])
        hidden = (gate / (1.0 + jnp.exp(-gate)) * up).astype(BF16)
        return gate, up, hidden, matmul_nt(hidden, w[2]).astype(BF16)

    def mlp_backward(n, w, gate, up, hidden, upstream):
        dhidden = matmul(upstream, w[2])
        sig = 1.0 / (1.0 + jnp.exp(-gate))
        dgate = (dhidden * up * sig * (1.0 + gate * (1.0 - sig))).astype(BF16)
        dup = (dhidden * gate * sig).astype(BF16)
        part = (matmul_nt(dgate, w[0]) + matmul_nt(dup, w[1])).astype(BF16)
        both = jnp.concatenate([dgate, dup], axis=1)
        return part, parts(matmul_tn(n, both)), parts(matmul_tn(upstream, hidden))

    gate_a, up_a, hidden_a, part = mlp_forward(n_a2, w_a)
    (out_a, n_b1), (w_win, w_gate_b) = forward_step(
        part, h_a, g_b1, [Job("zg", mid_win), Job("zg", mid_b, (0, ff))], 4
    )
    n_b1, w_win = flat(n_b1), whole(w_win)
    qkv_b = matmul(n_b1, w_win).astype(BF16)
    (o_b, ext), (w_win_out,) = window_forward(qkv_b, seg, [Job("zr", own_win_out)], 5)
    w_win_out = w_win_out.reshape(128, D)
    part = matmul(o_b, w_win_out).astype(BF16)
    (h_b, n_b2), (w_up_b, w_down_b) = forward_step(
        part, out_a, g_b2, [Job("zg", mid_b, (ff, ff)), Job("zg", mid_b, (2 * ff, ff))], 6
    )
    n_b2 = flat(n_b2)
    w_b = (whole(w_gate_b), whole(w_up_b), whole(w_down_b))
    gate_b, up_b, hidden_b, part_out = mlp_forward(n_b2, w_b)

    part, grad_gu_b, grad_down_b = mlp_backward(n_b2, w_b, gate_b, up_b, hidden_b, cot)
    (grad_h_b, gg_b2, up_full), (gu_b,) = backward_step(
        part, h_b, g_b2, cot_own, [Job("zs", grad_gu_b)], 7
    )
    up_full = flat(up_full)
    do_b = matmul_nt(up_full, w_win_out).astype(BF16)
    grad_win_out = matmul_tn(o_b, up_full).astype(BF16).reshape(count, -1, D)
    (dqkv_b, mixed), (down_b,) = window_backward(
        qkv_b, ext, do_b, seg, part_out, h_b, [Job("zs", grad_down_b)], 8
    )
    part = matmul_nt(dqkv_b, w_win).astype(BF16)
    grad_win = parts(matmul_tn(n_b1, dqkv_b))
    (grad_out_a, gg_b1, up_full), (win, win_out_t, gu_b) = backward_step(
        part, out_a, g_b1, grad_h_b,
        [Job("zs", grad_win), Job("zt", grad_win_out), Job("pa", total(gu_b))], 9,
    )
    up_full = flat(up_full)
    part, grad_gu_a, grad_down_a = mlp_backward(n_a2, w_a, gate_a, up_a, hidden_a, up_full)
    (grad_h_a, gg_a2, up_full), (gu_a, down_b) = backward_step(
        part, h_a, g_a2, grad_out_a, [Job("zs", grad_gu_a), Job("pa", total(down_b))], 10
    )
    up_full = flat(up_full)
    do_a = matmul_nt(up_full, w_lin_out).astype(BF16)
    grad_lin_out = matmul_tn(o_a, up_full).astype(BF16).reshape(count, -1, D)
    (dqkv_a,), (down_a, win, gu_a) = taylor_backward(
        qkv_a, do_a, kept, seg, tables,
        [Job("zs", grad_down_a), Job("pa", total(win)), Job("pa", total(gu_a))], count, 11,
    )
    part = matmul_nt(dqkv_a, w_lin).astype(BF16)
    rows_a = flat(x_full).astype(F32)
    rows_a = rows_a * lax.rsqrt(jnp.mean(rows_a * rows_a, axis=-1, keepdims=True) + EPSILON)
    gg_a1 = jnp.sum(part.astype(F32) * rows_a, axis=0, keepdims=True)
    gg = jnp.concatenate([gg_a1, gg_a2, gg_b1, gg_b2, jnp.zeros((60, D), F32)], axis=0).T
    grad_lin = matmul_tn(n_a1, dqkv_a)
    grad_lin = parts(jnp.concatenate([grad_lin[:, :64], gg, grad_lin[:, 128:]], axis=1))
    (grad_input, _), (lin, lin_out_t, down_a) = backward_step(
        part, x_own, g_a1, grad_h_a,
        [Job("zs", grad_lin), Job("zt", grad_lin_out), Job("pa", total(down_a))], 12, last=True,
    )
    _, (lin_g,) = step(
        lambda begin: None, [], [], [], [Job("pa", total(lin))], 7, False, "last", 13, 5
    )

    def joined(a, lo, hi):
        a = a.reshape(NTP, rows, -1)[:, :, lo:hi].astype(F32)
        return a.transpose(1, 0, 2).reshape(rows, -1)

    def unpack_mlp(gate_up, down):
        return (
            joined(gate_up, 0, ff)[:, :hidden_size],
            joined(gate_up, ff, 2 * ff)[:, :hidden_size],
            joined(down, 0, ff)[:, :hidden_size].T,
        )

    gate_b_g, up_b_g, down_b_g = unpack_mlp(gu_b, down_b)
    gate_a_g, up_a_g, down_a_g = unpack_mlp(gu_a, down_a)
    back = [(b, a) for a, b in row_routes()]
    win_out_g = lax.ppermute(total(win_out_t), AXES, back).astype(F32)
    lin_out_g = lax.ppermute(total(lin_out_t), AXES, back).astype(F32)
    gg = jnp.sum(lin_g.reshape(NTP, rows, width)[:, :, 64:68].astype(F32), axis=0)
    return (
        mixed.reshape(128, D),
        grad_input.reshape(128, D),
        gg[:, 0],
        joined(lin_g, 0, 32),
        joined(lin_g, 32, 64),
        joined(lin_g, 128, 256),
        lin_out_g,
        gg[:, 1],
        gate_a_g,
        up_a_g,
        down_a_g,
        gg[:, 2],
        joined(win, 0, 128),
        joined(win, 128, 256),
        joined(win, 256, 384),
        win_out_g,
        gg[:, 3],
        gate_b_g,
        up_b_g,
        down_b_g,
    )


def solution(mesh):
    seq, head = mesh.devices.shape
    fine = Mesh(mesh.devices.reshape(seq // 4, 2, 2, head // 2, 2), AXES)
    row, vec, col = P(AXES, None), P(AXES), P(None, AXES)
    placed = (
        row, P(), vec, row, row, row, row, vec, row, row, col,
        vec, row, row, row, row, vec, row, row, col, row,
    )
    out = (
        row, row, vec, row, row, row, row, vec, row, row, col,
        vec, row, row, row, row, vec, row, row, col,
    )
    return jax.shard_map(on_device, mesh=fine, in_specs=placed, out_specs=out, check_vma=False)
```

```python
import functools

import jax
import jax.numpy as jnp
import numpy as np
from jax import lax
from jax.experimental import pallas as pl
from jax.experimental.pallas import tpu as pltpu
from jax.sharding import Mesh
from jax.sharding import PartitionSpec as P

D = 1024
HEADS = 16
FEAT = 16
WINDOW = 64
NTP = 8
RIM = 64
SROWS = 160
EPSILON = 1e-05
AXES = ("sh", "sy", "sx", "hh", "hl")
TP = ("sy", "sx", "hl")
GROUP = ("sh", "hh")
MESH_ID = pl.DeviceIdType.MESH
F32 = jnp.float32
BF16 = jnp.bfloat16
VM = pltpu.VMEM
LIMIT = 56 * 1024 * 1024


def vmem_specs(count):
    return [pl.BlockSpec(memory_space=pltpu.VMEM)] * count


def matmul(left, right):
    return jnp.dot(left, right, preferred_element_type=F32)


def matmul_tn(left, right):
    return lax.dot_general(left, right, (((0,), (0,)), ((), ())), preferred_element_type=F32)


def matmul_nt(left, right):
    return lax.dot_general(left, right, (((1,), (1,)), ((), ())), preferred_element_type=F32)


def plane_place():
    sy, sx, c = lax.axis_index("sy"), lax.axis_index("sx"), lax.axis_index("hl")
    me = sy * 2 + sx
    xn = sy * 2 + (1 - sx)
    yn = (1 - sy) * 2 + sx
    dg = 3 - me
    return me, xn, yn, dg, c, {"sx": 1 - sx}, {"sy": 1 - sy}, {"hl": 1 - c}


def remote(src, dst, ssem, rsem, target):
    copy = pltpu.make_async_remote_copy(
        src_ref=src, dst_ref=dst, send_sem=ssem, recv_sem=rsem, device_id=target, device_id_type=MESH_ID
    )
    copy.start()
    return copy


AG_COPIES = 13
RS_COPIES = 10


class RowGather:
    def __init__(self, full, ssem, rsem):
        self.full, self.ssem, self.rsem = full, ssem, rsem
        self.place = plane_place()
        self.cps = {}

    def send(self, k, block, half, target):
        view = self.full.at[block, self.place[4], half]
        self.cps[k] = remote(view, view, self.ssem.at[k], self.rsem.at[k], target)

    def start(self):
        me, _, _, _, c, to_x, to_y, to_c = self.place
        self.send(1, me, 0, to_x)
        self.send(3, me, 1, to_y)
        self.send(2, me, 1, to_x)
        self.send(4, me, 0, to_y)
        own = self.full.at[me, c]
        self.cps[0] = remote(own, own, self.ssem.at[0], self.rsem.at[0], to_c)

    def arrived(self, *keys):
        for k in keys:
            self.cps[k].wait_recv()

    def hop1(self):
        _, xn, yn, _, _, to_x, to_y, to_c = self.place
        self.arrived(1)
        self.send(5, xn, 0, to_y)
        self.send(6, xn, 0, to_c)
        self.arrived(3)
        self.send(7, yn, 1, to_x)
        self.send(8, yn, 1, to_c)

    def hop2(self):
        _, xn, yn, _, _, _, _, to_c = self.place
        self.arrived(2)
        self.send(9, xn, 1, to_c)
        self.arrived(4)
        self.send(10, yn, 0, to_c)

    def hop3(self):
        _, _, _, dg, _, _, _, to_c = self.place
        self.arrived(5)
        self.send(11, dg, 0, to_c)
        self.arrived(7)
        self.send(12, dg, 1, to_c)

    def finish(self):
        for k in range(AG_COPIES):
            self.cps[k].wait_send()

    def run(self, consume, spare=()):
        me, xn, yn, dg = self.place[:4]
        spare = list(spare)

        def fill(most):
            for _ in range(min(most, len(spare))):
                spare.pop(0)()

        self.start()
        self.arrived(0)
        consume(me)
        fill(3)
        self.hop1()
        fill(2)
        self.hop2()
        self.arrived(6, 9)
        consume(xn)
        fill(2)
        self.hop3()
        self.arrived(8, 10)
        consume(yn)
        self.arrived(11, 12)
        consume(dg)
        fill(len(spare))
        self.finish()


class RowSum:
    def __init__(self, part, own, cb, sb, keep, r1, r2, ssem, rsem):
        self.part, self.own, self.cb, self.sb, self.keep = part, own, cb, sb, keep
        self.r1, self.r2, self.ssem, self.rsem = r1, r2, ssem, rsem
        self.place = plane_place()
        self.cps = {}

    def block(self, k):
        me, xn, yn, dg = self.place[:4]
        return (dg, xn, yn, me)[k]

    def copy(self, k, src, dst, target):
        self.cps[k] = remote(src, dst, self.ssem.at[k], self.rsem.at[k], target)

    def core(self, k):
        src = self.part.at[self.block(k), 1 - self.place[4]]
        self.copy(k, src, self.cb.at[k], self.place[7])

    def both(self, k, half):
        mine = self.part[self.block(k), self.place[4], half]
        return mine.astype(F32) + self.cb[k, half].astype(F32)

    def push(self, k):
        to_x, to_y = self.place[5:7]
        sb, r1 = self.sb, self.r1
        self.cps[k].wait_recv()
        if k == 0:
            sb[0, 0] = self.both(0, 0).astype(BF16)
            self.copy(4, sb.at[0, 0], r1.at[0, 0], to_x)
            sb[0, 1] = self.both(0, 1).astype(BF16)
            self.copy(5, sb.at[0, 1], r1.at[1, 0], to_y)
        if k == 1:
            sb[1, 0] = self.both(1, 0).astype(BF16)
            self.copy(6, sb.at[1, 0], r1.at[0, 1], to_x)
            self.keep[1] = self.both(1, 1)
        if k == 2:
            sb[2, 1] = self.both(2, 1).astype(BF16)
            self.copy(7, sb.at[2, 1], r1.at[1, 1], to_y)
            self.keep[0] = self.both(2, 0)
        if k == 3:
            self.own[0] = self.both(3, 0)
            self.own[1] = self.both(3, 1)

    def relay(self):
        to_x, to_y = self.place[5:7]
        self.cps[4].wait_recv()
        self.sb[2, 0] = (self.keep[0] + self.r1[0, 0].astype(F32)).astype(BF16)
        self.copy(8, self.sb.at[2, 0], self.r2.at[0], to_y)
        self.cps[5].wait_recv()
        self.sb[1, 1] = (self.keep[1] + self.r1[1, 0].astype(F32)).astype(BF16)
        self.copy(9, self.sb.at[1, 1], self.r2.at[1], to_x)
        self.cps[6].wait_recv()
        self.own[0] += self.r1[0, 1].astype(F32)
        self.cps[7].wait_recv()
        self.own[1] += self.r1[1, 1].astype(F32)

    def finish(self):
        self.cps[8].wait_recv()
        self.own[0] += self.r2[0].astype(F32)
        self.cps[9].wait_recv()
        self.own[1] += self.r2[1].astype(F32)
        for k in range(RS_COPIES):
            self.cps[k].wait_send()

    def run(self, produce, spare=()):
        spare = list(spare)
        for k in range(4):
            produce(self.block(k))
            self.core(k)
        for k in range(4):
            self.push(k)
        for job in spare[: len(spare) // 2]:
            job()
        self.relay()
        for job in spare[len(spare) // 2 :]:
            job()
        self.finish()


def rs_scratch():
    return [
        VM((2, 64, D), F32),
        VM((4, 2, 64, D), BF16),
        VM((3, 2, 64, D), BF16),
        VM((2, 64, D), F32),
        VM((2, 2, 64, D), BF16),
        VM((2, 64, D), BF16),
        pltpu.SemaphoreType.DMA((RS_COPIES,)),
        pltpu.SemaphoreType.DMA((RS_COPIES,)),
    ]


def ag_scratch():
    return [pltpu.SemaphoreType.DMA((AG_COPIES,)), pltpu.SemaphoreType.DMA((AG_COPIES,))]


def cost(micros):
    return pl.CostEstimate(flops=0, bytes_accessed=int(micros * 3.0e6), transcendentals=0)


def group_place():
    return lax.axis_index("sh") * lax.axis_size("hh") + lax.axis_index("hh")


def group_peer(k, count):
    nhh = lax.axis_size("hh")
    other = lax.rem(group_place() + k, count)
    sh, hh = other // nhh, lax.rem(other, nhh)
    return other, sh, hh, {"sh": sh, "hh": hh}


def place_peer(k):
    coords = {}
    for bit, axis in enumerate(("hl", "sx", "sy")):
        here = lax.axis_index(axis)
        coords[axis] = 1 - here if (k >> bit) & 1 else here
    target = {axis: v for bit, (axis, v) in enumerate(coords.items()) if (k >> bit) & 1}
    return coords["sy"] * 2 + coords["sx"], coords["hl"], target


def barrier_of(plane, group, count, column):
    barrier = pltpu.get_barrier_semaphore()
    seen = 0
    if column:
        hh, c = lax.axis_index("hh"), lax.axis_index("hl")
        for k in range(1, 8):
            target = {"hh": lax.rem(hh + k // 2, 4), "hl": 1 - c if k % 2 else c}
            if k == 1 and plane:
                continue
            pl.semaphore_signal(barrier, inc=1, device_id=target, device_id_type=MESH_ID)
            seen += 1
        group = False
    for k in ((1, 2, 4) if plane == 3 else range(1, 8)) if plane else ():
        _, _, target = place_peer(k)
        pl.semaphore_signal(barrier, inc=1, device_id=target, device_id_type=MESH_ID)
        seen += 1
    if group:
        for k in range(1, count):
            target = group_peer(k, count)[3]
            pl.semaphore_signal(barrier, inc=1, device_id=target, device_id_type=MESH_ID)
            seen += 1
    pl.semaphore_wait(barrier, seen)


def chained():
    return lax.axis_size("sh") == 1 and lax.axis_size("hh") == 4


class Job:
    def __init__(self, kind, src, spec=None):
        self.kind, self.src, self.inside = kind, src, isinstance(src, jax.ShapeDtypeStruct)
        self.spec = spec or (VMEM if kind == "zs" else ANY)
        self.src_spec = VMEM if kind == "zs" else ANY

    def out_shape(self):
        nsh, nhh = lax.axis_size("sh"), lax.axis_size("hh")
        shape = list(self.src.shape)
        if self.kind == "zg":
            shape = [nsh * 4, nhh] + shape[1:]
        if self.kind == "zr":
            shape = [nsh * nhh] + shape
        if self.kind == "zo":
            shape = [nsh * nhh, 4] + shape[2:]
        if self.kind == "zs":
            shape = [4] + shape[2:]
        if self.kind == "zw":
            shape = [4] + shape
        return jax.ShapeDtypeStruct(tuple(shape), BF16)


class Transfers:
    def __init__(self, kinds, sources, results, buffers, sems, count, chain):
        self.kinds, self.sources, self.results = kinds, sources, results
        self.buffers, self.sems, self.count, self.chain = buffers, sems, count, chain
        self.state = {}

    def copy(self, i, src, dst, send, recv, target):
        return pltpu.make_async_remote_copy(
            src_ref=src, dst_ref=dst, send_sem=self.sems[0].at[i, send],
            recv_sem=self.sems[1].at[i, recv], device_id=target, device_id_type=MESH_ID,
        )

    early = ()

    def __call__(self):
        for i, src in enumerate(self.sources):
            if src is not None and i not in self.state:
                self.start(i)

    late = __call__

    def slot(self, i, group):
        out, nhh = self.results[i], lax.axis_size("hh")
        if self.kinds[i] == "zg":
            return out.at[pl.ds(group // nhh * 4, 4), lax.rem(group, nhh)]
        return out.at[group]

    def got(self, i, ref, index):
        pltpu.make_async_copy(ref, ref, self.sems[1].at[i, index]).wait()

    def sent(self, i, ref, index):
        pltpu.make_async_copy(ref, ref, self.sems[0].at[i, index]).wait()

    def start(self, i, src=None):
        if src is not None:
            self.sources[i] = src
        self.state[i] = "sent"
        kind, src, out, count = self.kinds[i], self.sources[i], self.results[i], self.count
        hh, g = lax.axis_index("hh"), group_place()
        local = None
        if kind == "pa":
            s, c, _ = place_peer(0)
            for k in range(1, 8):
                ps, pc, target = place_peer(k)
                self.copy(i, src.at[ps, pc], out.at[s, c], k, k, target).start()
            local = (src.at[s, c], out.at[s, c])
        if kind in ("zg", "zr"):
            for k in (1, 3, 2) if self.chain else range(1, count):
                go = self.copy(i, src, self.slot(i, g), k, g, group_peer(k, count)[3]).start
                if self.chain and k != 2:
                    pl.when(hh != (3 if k == 1 else 0))(go)
                else:
                    go()
            local = (src, self.slot(i, g))
        if kind in ("zo", "zt"):
            nhh = lax.axis_size("hh")
            part = lambda p: (
                src.at[p] if kind == "zt" else src.at[pl.ds(p // nhh * 4, 4), lax.rem(p, nhh)]
            )
            for k in range(1, count):
                other, _, _, target = group_peer(k, count)
                self.copy(i, part(other), out.at[g], k, g, target).start()
            local = (part(g), out.at[g])
        if kind == "zs":
            buf = self.buffers[i]
            last, begin = hh == 3, hh == 0
            up = self.copy(
                i, src.at[:, jnp.where(last, 0, hh + 1)], buf.at[jnp.where(last, 4, g)],
                1, jnp.where(last, 4, g), {"hh": jnp.where(last, 2, hh + 1)},
            ).start
            down = self.copy(
                i, src.at[:, jnp.where(begin, 3, hh - 1)], buf.at[jnp.where(begin, 4, g)],
                3, jnp.where(begin, 4, g), {"hh": jnp.where(begin, 1, hh - 1)},
            ).start

            @pl.when(last)
            def _():
                up()
                down()

            @pl.when(jnp.logical_not(last))
            def _():
                down()
                up()

            far = lax.rem(hh + 2, 4)
            pl.when(last | begin)(self.copy(i, src.at[:, far], buf.at[g], 2, g, {"hh": far}).start)
        if kind in ("zw", "zv"):
            for k in range(4):
                mine, target, src_k, at, _ = self.column(kind, k)
                view = src if kind == "zw" else src.at[src_k]
                here = pltpu.make_async_copy(view, out.at[at], self.sems[2].at[i]).start
                pl.when(mine)(here)
                pl.when(jnp.logical_not(mine))(self.copy(i, view, out.at[at], k, at, target).start)
        if local is not None:
            pltpu.make_async_copy(local[0], local[1], self.sems[2].at[i]).start()
            self.local = getattr(self, "local", {})
            self.local[i] = local

    def column(self, kind, k):
        hh, c = lax.axis_index("hh"), lax.axis_index("hl")
        if kind == "zw":
            z, to_c, slot = lax.rem(hh + k, 4), hh // 2, lax.rem(hh, 2) * 2 + c
            own = (2 * c + k // 2 == hh) & (k % 2 == c)
            return (z == hh) & (to_c == c), {"hh": z, "hl": to_c}, 0, slot, own
        j = lax.rem(lax.rem(hh, 2) * 2 + c + k, 4)
        z, to_c = 2 * c + j // 2, lax.rem(j, 2)
        own = (k == hh) & (hh // 2 == c)
        return (z == hh) & (to_c == c), {"hh": z, "hl": to_c}, j, hh, own

    def relay(self, *which):
        for i in which:
            if i not in self.state:
                continue
            kind = self.kinds[i]
            if not self.chain or kind not in ("zg", "zr", "zs") or self.state[i] != "sent":
                continue
            self.state[i] = "relayed"
            hh, g = lax.axis_index("hh"), group_place()
            inner = (hh == 1) | (hh == 2)
            far = lax.rem(hh + 2, 4)

            @pl.when(inner)
            def _(i=i, kind=kind):
                if kind == "zs":
                    buf, src = self.buffers[i], self.sources[i]
                    self.got(i, buf.at[4], 4)
                    buf[4] = (buf[4].astype(F32) + src[:, far].astype(F32)).astype(BF16)
                    self.copy(i, buf.at[4], buf.at[g], 2, g, {"hh": far}).start()
                else:
                    slot = self.slot(i, far)
                    self.got(i, slot, far)
                    self.copy(i, slot, slot, 0, far, {"hh": 3 - far}).start()

    def wait(self, *which):
        self.relay(*which)
        for i in which:
            if self.state[i] == "done":
                continue
            self.state[i] = "done"
            kind, src, out, count = self.kinds[i], self.sources[i], self.results[i], self.count
            hh, g = lax.axis_index("hh"), group_place()
            inner = (hh == 1) | (hh == 2)
            if kind == "pa":
                s, c, _ = place_peer(0)
                for k in range(1, 8):
                    self.copy(i, src.at[s, c], out.at[s, c], k, k, place_peer(k)[2]).wait()
            if kind in ("zg", "zr"):
                for k in range(1, count):
                    other = lax.rem(g + k, count)
                    slot = self.slot(i, other)

                    def arrive(slot=slot, other=other):
                        self.got(i, slot, other)

                    def leave(k=k):
                        self.sent(i, src, k)

                    if not self.chain:
                        arrive()
                        leave()
                    elif k == 2:
                        pl.when(jnp.logical_not(inner))(arrive)
                        leave()
                        pl.when(inner)(functools.partial(leave, 0))
                    else:
                        arrive()
                        pl.when(hh != (3 if k == 1 else 0))(leave)
            if kind in ("zo", "zt"):
                for k in range(1, count):
                    other = lax.rem(g + k, count)
                    self.got(i, out.at[other], other)
                    self.sent(i, out.at[other], k)
            if kind in ("zw", "zv"):
                for k in range(4):
                    mine, _, _, at, own = self.column(kind, k)
                    slot = out.at[k]
                    here = pltpu.make_async_copy(slot, slot, self.sems[2].at[i]).wait
                    pl.when(own)(here)
                    pl.when(jnp.logical_not(own))(functools.partial(self.got, i, slot, k))
                    pl.when(jnp.logical_not(mine))(functools.partial(self.sent, i, slot, k))
            if kind == "zs":
                buf = self.buffers[i]
                one = jnp.where(hh == 0, 2, hh - 1)
                two = jnp.where(hh == 3, 1, hh + 1)
                far = lax.rem(hh + 2, 4)
                self.got(i, buf.at[one], one)
                self.got(i, buf.at[two], two)
                total = lambda: (
                    src[:, g].astype(F32) + buf[one].astype(F32) + buf[two].astype(F32)
                )

                @pl.when(inner)
                def _():
                    self.got(i, buf.at[far], far)
                    out[...] = (total() + buf[far].astype(F32)).astype(BF16)

                @pl.when(jnp.logical_not(inner))
                def _():
                    out[...] = total().astype(BF16)

                for k in (1, 2, 3):
                    self.sent(i, buf.at[g], k)
            if i in getattr(self, "local", {}):
                a, b = self.local[i]
                pltpu.make_async_copy(a, b, self.sems[2].at[i]).wait()

    def rest(self):
        which = [i for i in self.state if self.state[i] != "done"]
        self.relay(*which)
        self.wait(*which)

    def columns(self, i):
        ref = self.results[i]
        return ref[...].reshape(D, ref.shape[-1])


ANY = pl.BlockSpec(memory_space=pl.ANY)
VMEM = pl.BlockSpec(memory_space=pltpu.VMEM)
SMEM = pl.BlockSpec(memory_space=pltpu.SMEM)


def step(body, ins, outs, scratch, jobs, plane, group, name, collective, micros, early=()):
    count = lax.axis_size(GROUP)
    kinds = [job.kind for job in jobs]
    given = [job for job in jobs if not job.inside]
    n_in, n_out, n_job, n_src = len(ins), len(outs), len(jobs), len(given)
    plane = 7 if "pa" in kinds else plane
    group = group or any(kind != "pa" for kind in kinds)
    column = any(kind in ("zw", "zv") for kind in kinds)
    slots = max(count, 8)
    summed = [i for i, kind in enumerate(kinds) if kind == "zs"]

    def kernel(*refs):
        in_refs, refs = refs[:n_in], refs[n_in:]
        given_refs, refs = list(refs[:n_src]), refs[n_src:]
        out_refs, refs = refs[:n_out], refs[n_out:]
        results, refs = refs[:n_job], refs[n_job:]
        extra_refs, own = refs[len(scratch) :], refs[: len(scratch)]
        sources = [None if job.inside else given_refs.pop(0) for job in jobs]
        buffers = dict(zip(summed, extra_refs[3:]))
        barrier_of(plane, group, count, column)
        begin = Transfers(kinds, sources, results, buffers, extra_refs[:3], count, chained())
        begin.early = early
        body(begin, *in_refs, *out_refs, *own)
        if not begin.state:
            begin()
        begin.rest()

    extra = [
        pltpu.SemaphoreType.DMA((n_job, slots)),
        pltpu.SemaphoreType.DMA((n_job, slots)),
        pltpu.SemaphoreType.DMA((n_job,)),
    ] + [VM((5,) + jobs[i].out_shape().shape, BF16) for i in summed]
    result = pl.pallas_call(
        kernel,
        out_shape=tuple(o for o, _ in outs) + tuple(job.out_shape() for job in jobs),
        in_specs=[spec for _, spec in ins] + [job.src_spec for job in given],
        out_specs=tuple(spec for _, spec in outs) + tuple(job.spec for job in jobs),
        scratch_shapes=list(scratch) + (extra if n_job else []),
        compiler_params=pltpu.CompilerParams(
            collective_id=collective, has_side_effects=True, vmem_limit_bytes=LIMIT
        ),
        cost_estimate=cost(micros),
        name=name,
    )(*[v for v, _ in ins], *[job.src for job in given])
    return result[:n_out], result[n_out:]


FULL = jax.ShapeDtypeStruct((4, 2, 2, 64, D), BF16)
OWN = jax.ShapeDtypeStruct((2, 64, D), F32)


def flat(full):
    return full.reshape(1024, D)


def blocks(rows):
    return rows.reshape(4, 2, 2, 64, D)


def vmem(*values):
    return [(v, VMEM) for v in values]


def normed_half(u, gain):
    inv = lax.rsqrt(jnp.mean(u * u, axis=-1, keepdims=True) + EPSILON)
    return (u * inv * gain).astype(BF16)


def first(x, lead, jobs, collective):
    width = lead.shape[-1]

    def body(begin, x_ref, full, norms, proj, weight, gains, s1, r1):
        me, c = plane_place()[0], plane_place()[4]
        begin.start(0)
        full[me, c] = x_ref[...]
        rows = RowGather(full, s1, r1)
        rows.start()
        begin.wait(0)
        begin.start(1, begin.results[0])
        rows.hop1()
        rows.hop2()
        rows.hop3()
        for i in range(2, 2 + len(jobs)):
            begin.start(i)
        begin.relay(1)
        rows.arrived(0, 6, 8, 9, 10, 11, 12)
        rows.finish()
        begin.wait(1)
        weight[...] = begin.columns(1)
        gains[...] = weight[:, :128].astype(F32).T[64:72]
        lane = lanes(D, width)
        weight[...] = jnp.where((lane < 64) | (lane >= 128), weight[...], jnp.zeros((), BF16))

        def project(block, carry):
            n = normed_half(chip_rows(full, block).astype(F32), gains[0:1])
            put_chip(norms, block, n)
            proj[rows_of(block), :] = matmul(n, weight[...]).astype(BF16)
            return carry

        lax.fori_loop(0, 4, project, 0)

    return step(
        body, vmem(x),
        vmem(
            FULL, FULL, jax.ShapeDtypeStruct((1024, width), BF16), jax.ShapeDtypeStruct((D, width), BF16),
            jax.ShapeDtypeStruct((8, D), F32),
        ),
        ag_scratch(),
        [Job("pa", lead), Job("zg", jax.ShapeDtypeStruct(lead.shape, BF16), VMEM)] + jobs,
        7, True, "first", collective, 25,
    )


def chip_rows(ref, block):
    return ref[block].reshape(256, D)


def put_chip(ref, block, value):
    ref[block] = value.astype(BF16).reshape(2, 2, 64, D)


def rows_of(block):
    return pl.ds(block * 256, 256)


def silu_parts(gate):
    sig = 1.0 / (1.0 + jnp.exp(-gate))
    return sig, gate * sig


def forward_layer(o, w_o, u, gain_mid, gain_next, w_gate, w_up, jobs, collective):
    ff, width = w_gate.shape[1], jobs[1].out_shape().shape[-1]

    def body(
        begin, o_ref, wo_ref, u_ref, gm_ref, gn_ref, wg_ref, wu_ref,
        mid_own, end_own, full1, full2, proj, gate_out, up_out, hid_out, part1, part2, *rest
    ):
        me, c = plane_place()[0], plane_place()[4]
        sum1, sum2 = RowSum(part1, *rest[:8]), RowSum(part2, *rest[8:16])
        gather1, gather2 = RowGather(full1, *rest[16:18]), RowGather(full2, *rest[18:20])
        begin.start(0)

        def attended(block):
            put_chip(part1, block, matmul(o_ref[rows_of(block), :], wo_ref[...]))

        sum1.run(attended)
        begin.relay(0)
        begin.start(1)
        for half in range(2):
            u = u_ref[half].astype(F32) + sum1.own[half]
            mid_own[half] = u
            full1[me, c, half] = normed_half(u, gm_ref[...])

        seen = []

        def mlp(block):
            n = chip_rows(full1, block)
            gate, up = matmul(n, wg_ref[...]), matmul(n, wu_ref[...])
            hidden = (silu_parts(gate)[1] * up).astype(BF16)
            rows = rows_of(block)
            gate_out[rows, :] = gate.astype(BF16)
            up_out[rows, :] = up.astype(BF16)
            hid_out[rows, :] = hidden
            if not seen:
                begin.wait(0)
                begin.start(2)
            put_chip(part2, block, matmul_nt(hidden, begin.columns(0)))
            follow(sum2, seen)

        gather1.run(mlp)
        begin.relay(1)
        begin.start(3)
        sum2.relay()
        sum2.finish()
        begin.relay(2)
        for half in range(2):
            u = mid_own[half] + sum2.own[half]
            end_own[half] = u
            full2[me, c, half] = normed_half(u, gn_ref[...])

        begin.wait(1)

        def project(block):
            proj[rows_of(block), :] = matmul(chip_rows(full2, block), begin.columns(1)).astype(BF16)

        gather2.run(project)

    kept = jax.ShapeDtypeStruct((1024, ff), BF16)
    return step(
        body,
        vmem(o, w_o, u, gain_mid, gain_next, w_gate, w_up),
        vmem(OWN, OWN, FULL, FULL, jax.ShapeDtypeStruct((1024, width), BF16), kept, kept, kept),
        [VM(FULL.shape, BF16)] * 2 + rs_scratch() + rs_scratch() + ag_scratch() + ag_scratch(),
        jobs, 3, False, "forward_layer", collective, 60,
    )


def follow(total, seen):
    k = (3, 1, 2, 0)[len(seen)]
    seen.append(k)
    total.core(k)
    if k == 2:
        total.push(1)
    if k == 0:
        total.push(2)
        total.push(3)
        total.push(0)


def norm_back_half(dn, u, gain, upstream):
    inv = lax.rsqrt(jnp.mean(u * u, axis=-1, keepdims=True) + EPSILON)
    gained = dn * gain
    inner = jnp.mean(gained * u, axis=-1, keepdims=True)
    scaled = u * inv
    grad = upstream + inv * gained - scaled * (inv * inv * inner)
    return grad, jnp.sum(dn * scaled, axis=0, keepdims=True)


def back_own(dn, u_ref, gain_ref, up_ref, gnew, ggain, full):
    me, c = plane_place()[0], plane_place()[4]
    total = None
    for half in range(2):
        grad, gain_part = norm_back_half(
            dn[half], u_ref[half].astype(F32), gain_ref[...], up_ref[half].astype(F32)
        )
        gnew[half] = grad
        total = gain_part if total is None else total + gain_part
        if full is not None:
            full[me, c, half] = grad.astype(BF16)
    ggain[...] = total


def weight_grads(left, right, out):
    def piece(i):
        width = D // 4
        lo = i * width
        lhs = left[:, :, :, :, lo : lo + width].reshape(1024, width)
        value = matmul_tn(lhs, right[...]).astype(BF16)
        if len(out.shape) == 5:
            out[i] = value.reshape(out.shape[1:])
        else:
            out[lo : lo + width, :] = value

    return [functools.partial(piece, i) for i in range(4)]


def shipping():
    return chained() and D % (8 * 4 * 16) == 0


def terms_shape(cols):
    nsh, nhh = lax.axis_size("sh"), lax.axis_size("hh")
    if shipping():
        return jax.ShapeDtypeStruct((4, 4, 2, D // 32, cols), BF16)
    return jax.ShapeDtypeStruct((D, cols), BF16)


def apart(arrays, collective):
    nsh, nhh = lax.axis_size("sh"), lax.axis_size("hh")
    rows = D // (8 * nsh * nhh)
    jobs = [Job("zo", a.reshape(nsh * 4, nhh, 2, rows, a.shape[-1])) for a in arrays]
    _, moved = step(lambda begin: None, [], [], [], jobs, 0, True, "apart", collective, 20)
    return [jnp.sum(a.astype(F32), axis=0).astype(BF16) for a in moved]


def turn_layer(o, w_o, u, gain, w_gate, w_up, cot, cot_own, jobs, collective):
    ff = w_gate.shape[1]
    ship = shipping()

    def body(
        begin, o_ref, wo_ref, u_ref, g_ref, wg_ref, wu_ref, cot_ref, cown_ref,
        mid_own, gnew, ggain, full2, do_out, part_out, up_w, gate_w, down_w,
        part1, part2, full1, hid, dgate_out, dup_out, *rest
    ):
        me, c = plane_place()[0], plane_place()[4]
        sum1, sum2 = RowSum(part1, *rest[:8]), RowSum(part2, *rest[8:16])
        gather1, gather2 = RowGather(full1, *rest[16:18]), RowGather(full2, *rest[18:20])
        begin.start(0)

        def attended(block):
            put_chip(part1, block, matmul(o_ref[rows_of(block), :], wo_ref[...]))

        sum1.run(attended)
        for half in range(2):
            u = u_ref[half] + sum1.own[half]
            mid_own[half] = u
            full1[me, c, half] = normed_half(u, g_ref[...])

        seen = []

        def mlp(block):
            rows = rows_of(block)
            n = chip_rows(full1, block)
            gate, up = matmul(n, wg_ref[...]), matmul(n, wu_ref[...])
            sig, act = silu_parts(gate)
            hidden = (act * up).astype(BF16)
            hid[rows, :] = hidden
            if not seen:
                begin.wait(0)
            dhidden = matmul(chip_rows(cot_ref, block), begin.columns(0))
            dgate = (dhidden * up * (sig + act * (1.0 - sig))).astype(BF16)
            dup = (dhidden * act).astype(BF16)
            dgate_out[rows, :] = dgate
            dup_out[rows, :] = dup
            put_chip(part2, block, matmul_nt(dgate, wg_ref[...]) + matmul_nt(dup, wu_ref[...]))
            follow(sum2, seen)
            put_chip(part_out, block, matmul_nt(hidden, begin.columns(0)))

        gather1.run(mlp)
        for job in weight_grads(cot_ref, hid, down_w):
            job()
        if ship:
            begin.start(1, down_w)
        sum2.relay()
        for job in weight_grads(full1, dgate_out, gate_w):
            job()
        if ship:
            begin.start(2, gate_w)
        sum2.finish()
        begin.relay(1)
        back_own(sum2.own, mid_own, g_ref, cown_ref, gnew, ggain, full2)

        def output_grad(block):
            do_out[rows_of(block), :] = matmul_nt(chip_rows(full2, block), wo_ref[...]).astype(BF16)

        gather2.run(output_grad, weight_grads(full1, dup_out, up_w))

    terms = terms_shape(ff)
    outs = vmem(
        OWN, OWN, jax.ShapeDtypeStruct((1, D), F32), FULL,
        jax.ShapeDtypeStruct((1024, 128), BF16), FULL, terms,
    )
    held = [VM(terms.shape, BF16)] * 2 if ship else []
    outs, sums = step(
        body,
        vmem(o, w_o, u, gain, w_gate, w_up, cot, cot_own),
        outs + ([] if ship else vmem(terms, terms)),
        held + [VM(FULL.shape, BF16)] * 3 + [VM((1024, ff), BF16)] * 3
        + rs_scratch() + rs_scratch() + ag_scratch() + ag_scratch(),
        jobs + ([Job("zs", terms)] * 2 if ship else []), 3, False, "turn_layer", collective, 65,
    )
    return outs[:6], outs[6], sums[1:] if ship else outs[7:][::-1]


def backward_layer(
    dproj, w_proj, u_end, gain_next, up_end, n_next, kept, n_mid, w_mlp, u_mid, gain_mid, w_o, jobs, collective
):
    ff, width = w_mlp[0].shape[1], w_proj.shape[1]
    ship = shipping()

    def body(
        begin, dp_ref, wp_ref, ue_ref, ge_ref, upe_ref, nn_ref, gate_ref, up_ref, hid_ref, nm_ref,
        wg_ref, wu_ref, wd_ref, um_ref, gm_ref, wo_ref,
        gend, ggend, gmid, ggmid, full2, do_out, up_w, proj_w, down_w, gate_w,
        part1, part2, full1, dgate_s, dup_s, *rest
    ):
        sum1, sum2 = RowSum(part1, *rest[:8]), RowSum(part2, *rest[8:16])
        gather1, gather2 = RowGather(full1, *rest[16:18]), RowGather(full2, *rest[18:20])
        begin()
        first_sum = len(jobs)

        def projected(block):
            put_chip(part1, block, matmul_nt(dp_ref[rows_of(block), :], wp_ref[...]))

        sum1.run(projected, weight_grads(nn_ref, dp_ref, proj_w))
        if ship:
            begin.start(first_sum, proj_w)
        back_own(sum1.own, ue_ref, ge_ref, upe_ref, gend, ggend, full1)
        seen = []

        def mlp(block):
            rows = rows_of(block)
            sig, act = silu_parts(gate_ref[rows, :].astype(F32))
            dhidden = matmul(chip_rows(full1, block), wd_ref[...])
            dgate = (dhidden * up_ref[rows, :].astype(F32) * (sig + act * (1.0 - sig))).astype(BF16)
            dup = (dhidden * act).astype(BF16)
            dgate_s[rows, :] = dgate
            dup_s[rows, :] = dup
            put_chip(part2, block, matmul_nt(dgate, wg_ref[...]) + matmul_nt(dup, wu_ref[...]))
            follow(sum2, seen)

        gather1.run(mlp)
        for job in weight_grads(full1, hid_ref, down_w):
            job()
        if ship:
            begin.start(first_sum + 1, down_w)
            begin.relay(first_sum)
        sum2.relay()
        gates = weight_grads(nm_ref, dgate_s, gate_w)
        for job in gates:
            job()
        if ship:
            begin.start(first_sum + 2, gate_w)
        sum2.finish()
        if ship:
            begin.relay(first_sum + 1)
        back_own(sum2.own, um_ref, gm_ref, gend, gmid, ggmid, full2)

        def output_grad(block):
            do_out[rows_of(block), :] = matmul_nt(chip_rows(full2, block), wo_ref[...]).astype(BF16)

        gather2.run(output_grad, weight_grads(nm_ref, dup_s, up_w))

    vector = jax.ShapeDtypeStruct((1, D), F32)
    terms, proj_terms = terms_shape(ff), terms_shape(width)
    held = [VM(a.shape, BF16) for a in (proj_terms, terms, terms)] if ship else []
    outs, sums = step(
        body,
        vmem(
            dproj, w_proj, u_end, gain_next, up_end, n_next, *kept, n_mid, *w_mlp, u_mid, gain_mid, w_o
        ),
        vmem(OWN, vector, OWN, vector, FULL, jax.ShapeDtypeStruct((1024, 128), BF16), terms)
        + ([] if ship else vmem(proj_terms, terms, terms)),
        held + [VM(FULL.shape, BF16)] * 3 + [VM((1024, ff), BF16)] * 2
        + rs_scratch() + rs_scratch() + ag_scratch() + ag_scratch(),
        jobs + ([Job("zs", proj_terms), Job("zs", terms), Job("zs", terms)] if ship else []),
        3, False, "backward_layer", collective, 65,
    )
    n = len(jobs)
    return outs[:6], outs[6], sums[:n], sums[n:] if ship else outs[7:]


def last_layer(dproj, w_proj, u, gain, upstream, x_full, n_first, gains, jobs, collective):
    width = w_proj.shape[1]
    ship = shipping()

    def body(
        begin, dp_ref, wp_ref, u_ref, gain_ref, up_ref, xf_ref, nf_ref, gains_ref,
        gnew, ggain, proj_w, part1, mine, *rest
    ):
        sum1 = RowSum(part1, *rest)
        begin()
        mine[...] = jnp.zeros((128, D), F32)
        mine[65:68, :] = gains_ref[...]

        def projected(block):
            part = matmul_nt(dp_ref[rows_of(block), :], wp_ref[...])
            put_chip(part1, block, part)
            u = chip_rows(xf_ref, block).astype(F32)
            u = u * lax.rsqrt(jnp.mean(u * u, axis=-1, keepdims=True) + EPSILON)
            mine[64:65, :] += jnp.sum(part * u, axis=0, keepdims=True)

        def grads():
            turned = mine[...].T
            for i in range(4):
                at = slice(i * 256, i * 256 + 256)
                lhs = nf_ref[:, :, :, :, at].reshape(1024, 256)
                value = matmul_tn(lhs, dp_ref[...])
                keep = lanes(256, 128) < 64
                value = jnp.concatenate(
                    [jnp.where(keep, value[:, :128], turned[at]), value[:, 128:]], axis=1
                ).astype(BF16)
                if ship:
                    proj_w[i] = value.reshape(proj_w.shape[1:])
                else:
                    proj_w[at, :] = value
            if ship:
                begin.start(len(jobs), proj_w)

        for k in range(4):
            projected(sum1.block(k))
            sum1.core(k)
        for k in range(4):
            sum1.push(k)
        grads()
        sum1.relay()
        sum1.finish()
        back_own(sum1.own, u_ref, gain_ref, up_ref, gnew, ggain, None)
        if ship:
            begin.wait(len(jobs))
            begin.start(len(jobs) + 1, begin.results[len(jobs)])

    terms = terms_shape(width)
    summed = jax.ShapeDtypeStruct((4, 2, D // 32, width), BF16)
    n = len(jobs)
    outs, moved = step(
        body, vmem(dproj, w_proj, u, gain, upstream, x_full, n_first, gains),
        vmem(OWN, jax.ShapeDtypeStruct((1, D), F32)) + ([] if ship else vmem(terms)),
        ([VM(terms.shape, BF16)] if ship else []) + [VM(FULL.shape, BF16), VM((128, D), F32)] + rs_scratch(),
        jobs + ([Job("zs", terms), Job("pa", summed)] if ship else []),
        3, False, "last_layer", collective, 25,
    )
    if ship:
        return outs[0], moved[:n], moved[n + 1]
    (lin,) = apart([outs[2]], collective + 1)
    _, (lin,) = step(
        lambda begin: None, [], [], [], [Job("pa", lin)], 7, False, "last", collective + 2, 5
    )
    return outs[0], moved[:n], lin


def taylor_tables():
    pick = np.zeros((4, 2, 128, 256), np.float32)
    coef = np.zeros((8, 256), np.float32)
    pairs = [(i, j) for i in range(FEAT) for j in range(i, FEAT)]
    one = 4 * FEAT
    for x, (i, j) in enumerate(pairs):
        coef[:, x] = (2.0 * FEAT) ** -0.5 if i == j else FEAT**-0.5
        for t in range(4):
            pick[t, 0, t * FEAT + i, x] = 1.0
            pick[t, 1, t * FEAT + j, x] = 1.0
    for i in range(FEAT):
        x = len(pairs) + i
        coef[:, x] = FEAT**-0.25
        for t in range(4):
            pick[t, 0, t * FEAT + i, x] = 1.0
            pick[t, 1, one, x] = 1.0
    x = len(pairs) + FEAT
    coef[:, x] = 1.0
    pick[:, 0, one, x] = 1.0
    pick[:, 1, one, x] = 1.0
    shift = np.zeros((128, 128), np.float32)
    for i in range(2 * FEAT):
        shift[2 * FEAT + i, i] = 1.0
    return jnp.asarray(pick, BF16), jnp.asarray(coef, F32), jnp.asarray(shift, BF16)


def chunk_of(group, s):
    nhh = lax.axis_size("hh")
    return (group // nhh * 4 + s) * nhh + lax.rem(group, nhh)


def segment_of(starts, position):
    total = jnp.where(position >= starts[0], 0, -1)
    for i in range(1, starts.shape[0]):
        total = total + jnp.where(position >= starts[i], 1, 0)
    return total


class Segments:
    def __init__(self, starts, s):
        first = chunk_of(group_place(), s) * 256
        at = lambda shape, dim: first + lax.broadcasted_iota(jnp.int32, shape, dim)
        self.col = segment_of(starts, at((256, 1), 0))
        self.row = segment_of(starts, at((1, 256), 1))
        self.ext = segment_of(starts, at((1, 256 + RIM), 1) - RIM)
        self.last = segment_of(starts, first + 255)
        self.before = segment_of(starts, first - 1)


def carried(starts, s, st, sm, count, back):
    mine = chunk_of(group_place(), s)
    edge = segment_of(starts, mine * 256 + 255 if back else mine * 256 - 1)

    def group(i, both):
        def one(s2, both):
            state, total = both
            other = chunk_of(i, s2)
            reach = segment_of(starts, other * 256 - 1 if back else other * 256 + 255)
            ordered = other > mine if back else other < mine
            m = jnp.where(ordered & (reach == edge), 1.0, 0.0)
            return state + m * st[i, s2].astype(F32), total + m * sm[i, s2]

        return lax.fori_loop(s, 4, one, both) if back else lax.fori_loop(0, s + 1, one, both)

    return lax.fori_loop(
        0, count, group, (jnp.zeros((SROWS, 128), F32), jnp.zeros((8, 256), F32))
    )


def lanes(rows, width):
    return lax.broadcasted_iota(jnp.int32, (rows, width), 1)


class States:
    def __init__(self, count, st, sm, ssem, rsem):
        self.refs, self.ssem, self.rsem, self.count = (st, sm), ssem, rsem, count
        self.chain = count == 4 and chained()

    def copy(self, n, k, group, target):
        view = self.refs[n].at[group]
        return pltpu.make_async_remote_copy(
            src_ref=view, dst_ref=view, send_sem=self.ssem.at[n, k], recv_sem=self.rsem.at[n, group],
            device_id=target, device_id_type=MESH_ID,
        )

    def send(self):
        g, hh = group_place(), lax.axis_index("hh")
        for k in (2, 1, 3) if self.chain else range(1, self.count):
            for n in range(2):
                go = self.copy(n, k, g, group_peer(k, self.count)[3]).start
                if self.chain and k != 2:
                    pl.when(hh != (3 if k == 1 else 0))(go)
                else:
                    go()

    def got(self, n, group):
        view = self.refs[n].at[group]
        pltpu.make_async_copy(view, view, self.rsem.at[n, group]).wait()

    def sent(self, n, k):
        view = self.refs[n].at[0]
        pltpu.make_async_copy(view, view, self.ssem.at[n, k]).wait()

    def relay(self):
        if not self.chain:
            return
        hh = lax.axis_index("hh")
        far = lax.rem(hh + 2, 4)

        @pl.when((hh == 1) | (hh == 2))
        def _():
            for n in range(2):
                self.got(n, far)
                self.copy(n, 0, far, {"hh": 3 - far}).start()

    def arrive(self):
        g, hh = group_place(), lax.axis_index("hh")
        inner = (hh == 1) | (hh == 2)
        for k in range(1, self.count):
            other = lax.rem(g + k, self.count)
            for n in range(2):
                got = functools.partial(self.got, n, other)
                if self.chain and k == 2:
                    pl.when(jnp.logical_not(inner))(got)
                else:
                    got()

    def finish(self):
        hh = lax.axis_index("hh")
        for k in range(1, self.count):
            for n in range(2):
                sent = functools.partial(self.sent, n, k)
                if self.chain and k != 2:
                    pl.when(hh != (3 if k == 1 else 0))(sent)
                else:
                    sent()
                    if self.chain:
                        pl.when((hh == 1) | (hh == 2))(functools.partial(self.sent, n, 0))


def phi_of(x, pick, coef, t):
    left = matmul(x, pick[t, 0])
    right = matmul(x, pick[t, 1])
    return left, right, (left * right * coef).astype(BF16)


def taylor_forward_kernel(
    count, begin, qkv, pick, coef_ref, shift, cot_ref, starts,
    o_ref, y_ref, den_ref, pre_ref, psum_ref, cfull,
    st, sm, phis, ssem, rsem, ags, agr,
):
    g = group_place()
    me, c = plane_place()[0], plane_place()[4]
    cfull[me, c] = cot_ref[...]
    rows_in = RowGather(cfull, ags, agr)
    rows_in.start()
    for i in begin.early:
        begin.start(i)
    coef = coef_ref[0:1, :]
    left_half = lanes(256, 128) < 64

    def states(s, carry):
        rows = pl.ds(s * 256, 256)
        x = jnp.where(lanes(256, 128) == 4 * FEAT, jnp.ones((), BF16), qkv[rows, 0:128])
        v = qkv[rows, 128:256]
        seg = Segments(starts, s)
        tail = seg.col == seg.last
        v_tail = jnp.where(tail, v, jnp.zeros((), BF16))
        state = jnp.zeros((256, 128), F32)
        for h in range(2):
            _, _, phi_k = phi_of(x, pick, coef, 2 + h)
            side = left_half if h == 0 else jnp.logical_not(left_half)
            state += matmul_tn(phi_k, jnp.where(side, v_tail, jnp.zeros((), BF16)))
            total = jnp.sum(jnp.where(tail, phi_k.astype(F32), 0.0), axis=0, keepdims=True)
            sm[g, s, h : h + 1, :] = total
            _, _, phi_q = phi_of(x, pick, coef, h)
            phis[h, rows, :] = phi_q
        st[g, s] = state[:SROWS].astype(BF16)
        return carry

    sm[g] = jnp.zeros((4, 8, 256), F32)
    lax.fori_loop(0, 4, states, 0)
    exchange = States(count, st, sm, ssem, rsem)
    exchange.send()
    begin.late()
    rows_in.hop1()

    def inner(s, carry):
        rows = pl.ds(s * 256, 256)
        x = qkv[rows, 0:128]
        v = qkv[rows, 128:256]
        k = matmul(x, shift[...]).astype(BF16)
        lane = lanes(256, 128)
        order = lax.broadcasted_iota(jnp.int32, (256, 256), 0) >= lanes(256, 256)
        seg = Segments(starts, s)
        allowed = order & (seg.col == seg.row)
        num = jnp.zeros((256, 128), F32)
        dens = []
        for h in range(2):
            q = jnp.where(lane // FEAT == h, x, jnp.zeros((), BF16))
            dot = matmul_nt(q, k)
            score = jnp.where(allowed, 1.0 + dot * FEAT**-0.5 + dot * dot * (0.5 / FEAT), 0.0)
            side = left_half if h == 0 else jnp.logical_not(left_half)
            num += matmul(score.astype(BF16), jnp.where(side, v, jnp.zeros((), BF16)))
            dens.append(jnp.sum(score, axis=1, keepdims=True))
        y_ref[rows, :] = num
        den_ref[rows, :] = jnp.where(left_half, dens[0], dens[1])
        return carry

    lax.fori_loop(0, 4, inner, 0)
    rows_in.hop2()
    rows_in.hop3()
    exchange.relay()
    begin.relay(*begin.early)
    exchange.arrive()

    def finish(s, carry):
        rows = pl.ds(s * 256, 256)

        state, total = carried(starts, s, st, sm, count, False)
        state = state.astype(BF16)
        pre_ref[s] = state
        psum_ref[s] = total
        seg = Segments(starts, s)
        cont = seg.col == seg.before
        num = jnp.zeros((256, 128), F32)
        dens = []
        for h in range(2):
            phi_q = phis[h, rows, :]
            side = left_half if h == 0 else jnp.logical_not(left_half)
            part = matmul(phi_q[:, :SROWS], state)
            num = jnp.where(side, part, num)
            dens.append(jnp.sum(phi_q.astype(F32) * total[h : h + 1], axis=1, keepdims=True))
        num = jnp.where(cont, num, 0.0) + y_ref[rows, :]
        den = jnp.where(cont, jnp.where(left_half, dens[0], dens[1]), 0.0) + den_ref[rows, :]
        y = num / den
        y_ref[rows, :] = y
        den_ref[rows, :] = den
        o_ref[rows, :] = y.astype(BF16)
        return carry

    lax.fori_loop(0, 4, finish, 0)
    rows_in.arrived(0, 6, 8, 9, 10, 11, 12)
    rows_in.finish()
    exchange.finish()


def taylor_forward(qkv, starts, tables, cot, jobs, count, collective):
    return step(
        functools.partial(taylor_forward_kernel, count),
        vmem(qkv, *tables, cot) + [(starts, SMEM)],
        vmem(
            jax.ShapeDtypeStruct((1024, 128), BF16),
            jax.ShapeDtypeStruct((1024, 128), F32),
            jax.ShapeDtypeStruct((1024, 128), F32),
            jax.ShapeDtypeStruct((4, SROWS, 128), BF16),
            jax.ShapeDtypeStruct((4, 8, 256), F32),
            FULL,
        ),
        [
            VM((count, 4, SROWS, 128), BF16),
            VM((count, 4, 8, 256), F32),
            VM((2, 1024, 256), BF16),
            pltpu.SemaphoreType.DMA((2, count)),
            pltpu.SemaphoreType.DMA((2, count)),
        ]
        + ag_scratch(),
        jobs, 3, True, "taylor_forward", collective, 28, early=(0, 1),
    )


def taylor_backward_kernel(
    count, begin, qkv, do_ref, y_ref, den_ref, pre_ref, psum_ref,
    pick, coef_ref, shift, att_ref, up_full, starts,
    out_ref, out_w, st, sm, acc, dnum_ref, ddens, ssem, rsem,
):
    g = group_place()
    for i in begin.early:
        begin.start(i)
    coef = coef_ref[0:1, :]
    left_half = lanes(256, 128) < 64
    zero = jnp.zeros((), BF16)

    def sides(h):
        return left_half if h == 0 else jnp.logical_not(left_half)

    def feature_back(dphi, left, right, t):
        grad = dphi * coef
        return matmul_nt((grad * right).astype(BF16), pick[t, 0]) + matmul_nt(
            (grad * left).astype(BF16), pick[t, 1]
        )

    def states(s, carry):
        rows = pl.ds(s * 256, 256)
        x = jnp.where(lanes(256, 128) == 4 * FEAT, jnp.ones((), BF16), qkv[rows, 0:128])
        do = do_ref[rows, :].astype(F32)
        den = den_ref[rows, :]
        dnum = do / den
        dnum_low = dnum.astype(BF16)
        dnum_ref[rows, :] = dnum_low
        weighted = dnum * y_ref[rows, :]
        seg = Segments(starts, s)
        cont = seg.col == seg.before
        d_cont = jnp.where(cont, dnum_low, zero)
        pre = pre_ref[s]
        state = jnp.zeros((256, 128), F32)
        grad = jnp.zeros((256, 128), F32)
        for h in range(2):
            dden = -jnp.sum(jnp.where(sides(h), weighted, 0.0), axis=1, keepdims=True)
            ddens[h, rows, :] = jnp.broadcast_to(dden, (256, 128))
            left, right, phi_q = phi_of(x, pick, coef, h)
            d_side = jnp.where(sides(h), d_cont, zero)
            state += matmul_tn(phi_q, d_side)
            dden_cont = jnp.where(cont, dden, 0.0)
            sm[g, s, h : h + 1, :] = jnp.sum(
                phi_q.astype(F32) * dden_cont, axis=0, keepdims=True
            )
            dphi = jnp.concatenate(
                [matmul_nt(d_side, pre), jnp.zeros((256, 256 - SROWS), F32)], axis=1
            ) + dden_cont * psum_ref[s, h : h + 1, :]
            grad += feature_back(dphi, left, right, h)
        st[g, s] = state[:SROWS].astype(BF16)
        acc[0, rows, :] = grad
        return carry

    sm[g] = jnp.zeros((4, 8, 256), F32)
    lax.fori_loop(0, 4, states, 0)
    exchange = States(count, st, sm, ssem, rsem)
    exchange.send()
    begin.late()

    def inner(s, carry):
        rows = pl.ds(s * 256, 256)
        x = qkv[rows, 0:128]
        v = qkv[rows, 128:256]
        dnum = dnum_ref[rows, :]
        k_low = matmul(x, shift[...]).astype(BF16)
        lane = lanes(256, 128)
        order = lax.broadcasted_iota(jnp.int32, (256, 256), 0) >= lanes(256, 256)
        seg = Segments(starts, s)
        allowed = order & (seg.col == seg.row)
        dq = jnp.zeros((256, 128), F32)
        dk = jnp.zeros((256, 128), F32)
        dv = jnp.zeros((256, 128), F32)
        for h in range(2):
            mine = lane // FEAT == h
            q = jnp.where(mine, x, zero)
            dot = matmul_nt(q, k_low)
            score = jnp.where(allowed, 1.0 + dot * FEAT**-0.5 + dot * dot * (0.5 / FEAT), 0.0)
            d_side = jnp.where(sides(h), dnum, zero)
            dscore = matmul_nt(d_side, v) + ddens[h, rows, 0:1]
            e = jnp.where(allowed, dscore * (FEAT**-0.5 + dot * (1.0 / FEAT)), 0.0).astype(BF16)
            dq += matmul(e, jnp.where(mine, k_low, zero))
            dk += matmul_tn(e, q)
            dv += matmul_tn(score.astype(BF16), d_side)
        acc[0, rows, :] += dq
        acc[1, rows, :] = dk
        acc[2, rows, :] = dv
        return carry

    lax.fori_loop(0, 4, inner, 0)
    for i in range(4):
        at = slice(i * 256, i * 256 + 256)
        rhs = up_full[:, :, :, :, at].reshape(1024, 256)
        out_w[:, at] = matmul_tn(att_ref[...], rhs).astype(BF16)
    exchange.relay()
    begin.relay(*begin.early)
    exchange.arrive()

    def finish(s, carry):
        rows = pl.ds(s * 256, 256)

        state, total = carried(starts, s, st, sm, count, True)
        state = state.astype(BF16)
        x = jnp.where(lanes(256, 128) == 4 * FEAT, jnp.ones((), BF16), qkv[rows, 0:128])
        seg = Segments(starts, s)
        tail = seg.col == seg.last
        v_tail = jnp.where(tail, qkv[rows, 128:256], zero)
        grad = acc[0, rows, :]
        lane = lanes(256, 128)
        dv = jnp.zeros((256, 128), F32)
        for h in range(2):
            left, right, phi_k = phi_of(x, pick, coef, 2 + h)
            dphi = jnp.concatenate(
                [
                    matmul_nt(jnp.where(sides(h), v_tail, zero), state),
                    jnp.zeros((256, 256 - SROWS), F32),
                ],
                axis=1,
            ) + jnp.where(tail, total[h : h + 1], 0.0)
            grad += feature_back(dphi, left, right, 2 + h)
            dv = jnp.where(sides(h), matmul(phi_k[:, :SROWS], state), dv)
        grad += matmul_nt(acc[1, rows, :].astype(BF16), shift[...])
        dv = jnp.where(tail, dv, 0.0) + acc[2, rows, :]
        out_ref[rows, 0:128] = jnp.where(lane < 4 * FEAT, grad, 0.0).astype(BF16)
        out_ref[rows, 128:256] = dv.astype(BF16)
        return carry

    lax.fori_loop(0, 4, finish, 0)
    exchange.finish()


def taylor_backward(qkv, do, kept, starts, tables, attended, up_full, jobs, count, collective):
    return step(
        functools.partial(taylor_backward_kernel, count),
        vmem(qkv, do, *kept, *tables, attended, up_full) + [(starts, SMEM)],
        vmem(jax.ShapeDtypeStruct((1024, 256), BF16), jax.ShapeDtypeStruct((128, D), BF16)),
        [
            VM((count, 4, SROWS, 128), BF16),
            VM((count, 4, 8, 256), F32),
            VM((3, 1024, 128), F32),
            VM((1024, 128), BF16),
            VM((2, 1024, 128), F32),
            pltpu.SemaphoreType.DMA((2, count)),
            pltpu.SemaphoreType.DMA((2, count)),
        ],
        jobs, 0, True, "taylor_backward", collective, 28, early=(4,) if len(jobs) > 4 else (),
    )


def rim_target(s, forward):
    hh, sh = lax.axis_index("hh"), lax.axis_index("sh")
    nhh, nsh = lax.axis_size("hh"), lax.axis_size("sh")
    if forward:
        wraps = jnp.where(hh == nhh - 1, 1, 0)
        slot = lax.rem(s + wraps, 4)
        leaves = wraps if s == 3 else 0
        return {"sh": lax.rem(sh + leaves, nsh), "hh": lax.rem(hh + 1, nhh)}, slot
    wraps = jnp.where(hh == 0, 1, 0)
    slot = lax.rem(s + 4 - wraps, 4)
    leaves = wraps if s == 0 else 0
    return {"sh": lax.rem(sh + nsh - leaves, nsh), "hh": lax.rem(hh + nhh - 1, nhh)}, slot


def window_mask(starts, s):
    seg = Segments(starts, s)
    i = lax.broadcasted_iota(jnp.int32, (256, 256 + RIM), 0)
    j = lanes(256, 256 + RIM)
    return (j > i) & (j <= i + WINDOW) & (seg.col == seg.ext)


def window_probs(q, k, allowed):
    scores = jnp.where(allowed, matmul_nt(q, k) * 64**-0.5, -1e30)
    peak = jnp.max(scores, axis=1, keepdims=True)
    weights = jnp.exp(scores - peak)
    return weights / jnp.sum(weights, axis=1, keepdims=True)


def window_forward_kernel(begin, qkv, starts, o_ref, ext, rim, ssem, rsem):
    cps = []
    for s in range(4):
        target, slot = rim_target(s, True)
        src = qkv.at[pl.ds(s * 256 + 256 - RIM, RIM), pl.ds(128, 256)]
        cps.append(remote(src, rim.at[slot], ssem.at[s], rsem.at[slot], target))

    begin()

    def fill(s, carry):
        ext[s, RIM:, :] = qkv[pl.ds(s * 256, 256), 128:384]
        return carry

    lax.fori_loop(0, 4, fill, 0)
    for s in range(4):
        pltpu.make_async_copy(rim.at[s], rim.at[s], rsem.at[s]).wait()

    def run(s, carry):
        rows = pl.ds(s * 256, 256)
        ext[s, :RIM, :] = rim[s]
        q = qkv[rows, 0:128]
        k = ext[s, :, 0:128]
        v = ext[s, :, 128:256]
        left_half = lanes(256, 128) < 64
        allowed = window_mask(starts, s)
        out = jnp.zeros((256, 128), F32)
        for h in range(2):
            side = left_half if h == 0 else jnp.logical_not(left_half)
            probs = window_probs(jnp.where(side, q, jnp.zeros((), BF16)), k, allowed)
            out = jnp.where(side, matmul(probs.astype(BF16), v), out)
        o_ref[rows, :] = out.astype(BF16)
        return carry

    lax.fori_loop(0, 4, run, 0)
    for cp in cps:
        cp.wait_send()


def window_forward(qkv, starts, jobs, collective):
    return step(
        window_forward_kernel,
        vmem(qkv) + [(starts, SMEM)],
        vmem(
            jax.ShapeDtypeStruct((1024, 128), BF16),
            jax.ShapeDtypeStruct((4, 256 + RIM, 256), BF16),
        ),
        [
            VM((4, RIM, 256), BF16),
            pltpu.SemaphoreType.DMA((4,)),
            pltpu.SemaphoreType.DMA((4,)),
        ],
        jobs, 0, True, "window_forward", collective, 14,
    )


def window_backward_kernel(
    begin, qkv, ext, do_ref, part, u_ref, att_ref, up_full, starts, out_ref, mixed, out_w,
    acc, back, rim,
    ssem, rsem, own, cb, sb, keep, r1, r2, ss, rs,
):
    total = RowSum(part, own, cb, sb, keep, r1, r2, ss, rs)
    for k in range(4):
        total.core(k)
    begin()
    zero = jnp.zeros((), BF16)

    def run(s, carry):
        rows = pl.ds(s * 256, 256)
        q = qkv[rows, 0:128]
        k = ext[s, :, 0:128]
        v = ext[s, :, 128:256]
        do = do_ref[rows, :]
        left_half = lanes(256, 128) < 64
        left_ext = lanes(256 + RIM, 128) < 64
        allowed = window_mask(starts, s)
        dq = jnp.zeros((256, 128), F32)
        dk = jnp.zeros((256 + RIM, 128), F32)
        dv = jnp.zeros((256 + RIM, 128), F32)
        for h in range(2):
            side = left_half if h == 0 else jnp.logical_not(left_half)
            q_h = jnp.where(side, q, zero)
            do_h = jnp.where(side, do, zero)
            probs = window_probs(q_h, k, allowed)
            dprobs = matmul_nt(do_h, v)
            inner = jnp.sum(probs * dprobs, axis=1, keepdims=True)
            ds = (probs * (dprobs - inner)).astype(BF16)
            dq = jnp.where(side, matmul(ds, k), dq)
            dk += matmul_tn(ds, q_h)
            dv += matmul_tn(probs.astype(BF16), do_h)
        scale = 64**-0.5
        dk = dk * scale
        out_ref[rows, 0:128] = (dq * scale).astype(BF16)
        acc[rows, 0:128] = dk[RIM:]
        acc[rows, 128:256] = dv[RIM:]
        back[s, :, 0:128] = dk[:RIM].astype(BF16)
        back[s, :, 128:256] = dv[:RIM].astype(BF16)
        return carry

    for k in range(4):
        total.push(k)
    lax.fori_loop(0, 4, run, 0)
    cps = []
    for s in range(4):
        target, slot = rim_target(s, False)
        cps.append(remote(back.at[s], rim.at[slot], ssem.at[s], rsem.at[slot], target))
    for i in range(4):
        at = slice(i * 256, i * 256 + 256)
        rhs = up_full[:, :, :, :, at].reshape(1024, 256)
        out_w[:, at] = matmul_tn(att_ref[...], rhs).astype(BF16)
    total.relay()
    begin.relay(*begin.early)
    for s in range(4):
        pltpu.make_async_copy(rim.at[s], rim.at[s], rsem.at[s]).wait()

    def finish(s, carry):
        out_ref[pl.ds(s * 256, 256 - RIM), 128:384] = acc[pl.ds(s * 256, 256 - RIM), :].astype(BF16)
        rows = pl.ds(s * 256 + 256 - RIM, RIM)
        out_ref[rows, 128:384] = (acc[rows, :] + rim[s].astype(F32)).astype(BF16)
        return carry

    lax.fori_loop(0, 4, finish, 0)
    total.finish()
    for half in range(2):
        mixed[half] = (u_ref[half] + own[half]).astype(BF16)
    for cp in cps:
        cp.wait_send()


def window_backward(qkv, ext, do, starts, part, u, attended, up_full, jobs, collective):
    return step(
        window_backward_kernel,
        vmem(qkv, ext, do, part, u, attended, up_full) + [(starts, SMEM)],
        vmem(
            jax.ShapeDtypeStruct((1024, 384), BF16), jax.ShapeDtypeStruct((2, 64, D), BF16),
            jax.ShapeDtypeStruct((128, D), BF16),
        ),
        [
            VM((1024, 256), F32),
            VM((4, RIM, 256), BF16),
            VM((4, RIM, 256), BF16),
            pltpu.SemaphoreType.DMA((4,)),
            pltpu.SemaphoreType.DMA((4,)),
        ]
        + rs_scratch(),
        jobs, 3, True, "window_backward", collective, 22, early=range(len(jobs)),
    )


def row_routes():
    nsh, nhh = lax.axis_size("sh"), lax.axis_size("hh")
    groups = nsh * nhh
    routes = []
    for d in range(8 * groups):
        place, group = d // groups, d % groups
        s, c = place // 2, place % 2
        sh, hh = group // nhh, group % nhh
        routes.append((d, ((sh * 4 + s) * nhh + hh) * 2 + c))
    return routes


def spread_ff(member):
    rows = member.shape[0]
    width = -(-member.shape[1] // (NTP * 128)) * 128
    padded = jnp.pad(member, ((0, 0), (0, NTP * width - member.shape[1])))
    return padded.reshape(rows, NTP, width)


def on_device(
    layer_input, lengths, gain_a1, lin_q, lin_k, lin_v, lin_out, gain_a2, mlp_a_gate, mlp_a_up,
    mlp_a_down, gain_b1, win_q, win_k, win_v, win_out, gain_b2, mlp_b_gate, mlp_b_up, mlp_b_down,
    cotangent,
):
    count = lax.axis_size(GROUP)
    rows = lin_q.shape[0]
    hidden_size = mlp_a_gate.shape[1]
    gains = jnp.pad(jnp.stack([gain_a1, gain_a2, gain_b1, gain_b2], axis=1), ((0, 0), (0, 60)))
    gains = jnp.broadcast_to(gains[:, None, :], (rows, NTP, 64))
    starts = jnp.cumsum(lengths) - lengths
    tables = taylor_tables()

    split = lambda member: member.reshape(rows, NTP, -1)
    bundle_lin = jnp.concatenate(
        [split(lin_q), split(lin_k), gains, split(lin_v)], axis=-1
    ).transpose(1, 0, 2)
    bundle_a = jnp.concatenate(
        [spread_ff(mlp_a_gate), spread_ff(mlp_a_up), spread_ff(mlp_a_down.T)], axis=-1
    ).transpose(1, 0, 2)
    bundle_win = jnp.concatenate([split(win_q), split(win_k), split(win_v)], axis=-1).transpose(
        1, 0, 2
    )
    bundle_b = jnp.concatenate(
        [spread_ff(mlp_b_gate), spread_ff(mlp_b_up), spread_ff(mlp_b_down.T)], axis=-1
    ).transpose(1, 0, 2)
    ff = bundle_a.shape[-1] // 3
    width = bundle_lin.shape[-1]
    nsh, nhh = lax.axis_size("sh"), lax.axis_size("hh")
    places = lambda a: a.reshape(4, 2, rows, a.shape[-1])
    whole = lambda a: a.reshape(D, a.shape[-1])
    total = lambda a: jnp.sum(a.astype(F32), axis=0).astype(BF16)
    ship = shipping()
    if ship:
        own_rows = lambda a: Job("zw", a)
    else:
        own_rows = lambda a: Job("zr", lax.ppermute(a, AXES, row_routes()))

    x_own = layer_input.reshape(2, 64, D)
    cot_own = cotangent.reshape(2, 64, D)
    third = lambda a, i: Job("pa", places(a[:, :, i * ff : i * ff + ff]))
    (x_full, n_a1, qkv_a, w_lin, gains), (_, _, mid_gate_a, mid_up_a, mid_down_a) = first(
        x_own, places(bundle_lin), [third(bundle_a, 0), third(bundle_a, 1), third(bundle_a, 2)], 1
    )
    g_a1, g_a2, g_b1, g_b2 = (gains[i : i + 1] for i in range(4))
    (o_a, *kept, cot), (w_gate_a, w_lin_out, w_up_a, mid_win, mid_gate_b, mid_up_b, mid_down_b) = (
        taylor_forward(
            qkv_a, starts, tables, cot_own,
            [
                Job("zg", mid_gate_a), own_rows(lin_out), Job("zg", mid_up_a), Job("pa", places(bundle_win)),
                third(bundle_b, 0), third(bundle_b, 1), third(bundle_b, 2),
            ],
            count, 2,
        )
    )
    w_lin_out = w_lin_out.reshape(128, D)
    w_gate_a, w_up_a = whole(w_gate_a), whole(w_up_a)
    (h_a, out_a, n_a2, n_b1, qkv_b, *kept_a), (w_down_a, w_win, w_gate_b, w_up_b) = forward_layer(
        o_a, w_lin_out, x_own, g_a2, g_b1, w_gate_a, w_up_a,
        [
            Job("zg", mid_down_a, VMEM), Job("zg", mid_win, VMEM), Job("zg", mid_gate_b),
            Job("zg", mid_up_b),
        ],
        3,
    )
    w_a, w_win = (w_gate_a, w_up_a, whole(w_down_a)), whole(w_win)
    (o_b, ext), (w_win_out,) = window_forward(qkv_b, starts, [own_rows(win_out)], 4)
    w_win_out = w_win_out.reshape(128, D)
    (h_b, grad_h_b, gg_b2, up_full, do_b, part_out), up_b, (down_b, gate_b) = turn_layer(
        o_b, w_win_out, out_a, g_b2, whole(w_gate_b), whole(w_up_b), cot, cot_own,
        [Job("zg", mid_down_b, VMEM)], 5,
    )
    if not ship:
        down_b, gate_b, up_b = apart([down_b, gate_b, up_b], 10)
    (dqkv_b, mixed, grad_win_out), (down_b, gate_b, *more) = window_backward(
        qkv_b, ext, do_b, starts, part_out, h_b, o_b, up_full,
        [Job("pa", down_b), Job("pa", gate_b)] + ([Job("zs", up_b)] if ship else []), 6,
    )
    (up_b,) = more if ship else (up_b,)
    rows_back = lambda a: (
        Job("zv", a.reshape(4, rows, D)) if ship else Job("zt", a.reshape(count, -1, D))
    )
    (_, gg_b1, grad_h_a, gg_a2, up_full, do_a), up_a, (win_out_t,), (win, down_a, gate_a) = (
        backward_layer(
            dqkv_b, w_win, out_a, g_b1, grad_h_b, n_b1, kept_a, n_a2, w_a, h_a, g_a2, w_lin_out,
            [rows_back(grad_win_out)], 7,
        )
    )
    if not ship:
        win, down_a, gate_a, up_a = apart([win, down_a, gate_a, up_a], 11)
    (dqkv_a, grad_lin_out), (up_b, win, down_a, gate_a, *more) = taylor_backward(
        qkv_a, do_a, kept, starts, tables, o_a, up_full,
        [Job("pa", up_b), Job("pa", win), Job("pa", down_a), Job("pa", gate_a)]
        + ([Job("zs", up_a)] if ship else []),
        count, 8,
    )
    (up_a,) = more if ship else (up_a,)
    grad_input, (lin_out_t, up_a), lin_g = last_layer(
        dqkv_a, w_lin, x_own, g_a1, grad_h_a, x_full, n_a1,
        jnp.concatenate([gg_a2, gg_b1, gg_b2], axis=0),
        [rows_back(grad_lin_out), Job("pa", up_a)], 9,
    )

    def joined(a, lo, hi):
        a = a.reshape(NTP, rows, -1)[:, :, lo:hi].astype(F32)
        return a.transpose(1, 0, 2).reshape(rows, -1)

    def unpack_mlp(gate, up, down):
        joined_ff = lambda a: joined(a, 0, ff)[:, :hidden_size]
        return joined_ff(gate), joined_ff(up), joined_ff(down).T

    gate_b_g, up_b_g, down_b_g = unpack_mlp(gate_b, up_b, down_b)
    gate_a_g, up_a_g, down_a_g = unpack_mlp(gate_a, up_a, down_a)
    def own_terms(a):
        if ship:
            return jnp.sum(a.astype(F32), axis=0)
        return lax.ppermute(total(a), AXES, [(d, e) for e, d in row_routes()]).astype(F32)

    win_out_g, lin_out_g = own_terms(win_out_t), own_terms(lin_out_t)
    gg = jnp.sum(lin_g.reshape(NTP, rows, width)[:, :, 64:68].astype(F32), axis=0)
    return (
        mixed.reshape(128, D),
        grad_input.reshape(128, D),
        gg[:, 0],
        joined(lin_g, 0, 32),
        joined(lin_g, 32, 64),
        joined(lin_g, 128, 256),
        lin_out_g,
        gg[:, 1],
        gate_a_g,
        up_a_g,
        down_a_g,
        gg[:, 2],
        joined(win, 0, 128),
        joined(win, 128, 256),
        joined(win, 256, 384),
        win_out_g,
        gg[:, 3],
        gate_b_g,
        up_b_g,
        down_b_g,
    )


def solution(mesh):
    seq, head = mesh.devices.shape
    fine = Mesh(mesh.devices.reshape(seq // 4, 2, 2, head // 2, 2), AXES)
    row, vec, col = P(AXES, None), P(AXES), P(None, AXES)
    placed = (
        row, P(), vec, row, row, row, row, vec, row, row, col,
        vec, row, row, row, row, vec, row, row, col, row,
    )
    out = (
        row, row, vec, row, row, row, row, vec, row, row, col,
        vec, row, row, row, row, vec, row, row, col,
    )
    return jax.shard_map(on_device, mesh=fine, in_specs=placed, out_specs=out, check_vma=False)
```

```python
import functools

import jax
import jax.numpy as jnp
import numpy as np
from jax import lax
from jax.experimental import pallas as pl
from jax.experimental.pallas import tpu as pltpu
from jax.sharding import Mesh
from jax.sharding import PartitionSpec as P

D = 1024
HEADS = 16
FEAT = 16
WINDOW = 64
NTP = 8
RIM = 64
SROWS = 160
EPSILON = 1e-05
AXES = ("sh", "sy", "sx", "hh", "hl")
TP = ("sy", "sx", "hl")
GROUP = ("sh", "hh")
MESH_ID = pl.DeviceIdType.MESH
F32 = jnp.float32
BF16 = jnp.bfloat16
VM = pltpu.VMEM
LIMIT = 60 * 1024 * 1024


def vmem_specs(count):
    return [pl.BlockSpec(memory_space=pltpu.VMEM)] * count


def matmul(left, right):
    return jnp.dot(left, right, preferred_element_type=F32)


def matmul_tn(left, right):
    return lax.dot_general(left, right, (((0,), (0,)), ((), ())), preferred_element_type=F32)


def matmul_nt(left, right):
    return lax.dot_general(left, right, (((1,), (1,)), ((), ())), preferred_element_type=F32)


def plane_place():
    sy, sx, c = lax.axis_index("sy"), lax.axis_index("sx"), lax.axis_index("hl")
    me = sy * 2 + sx
    xn = sy * 2 + (1 - sx)
    yn = (1 - sy) * 2 + sx
    dg = 3 - me
    return me, xn, yn, dg, c, {"sx": 1 - sx}, {"sy": 1 - sy}, {"hl": 1 - c}


def remote(src, dst, ssem, rsem, target):
    copy = pltpu.make_async_remote_copy(
        src_ref=src, dst_ref=dst, send_sem=ssem, recv_sem=rsem, device_id=target, device_id_type=MESH_ID
    )
    copy.start()
    return copy


AG_COPIES = 13
RS_COPIES = 10


class RowGather:
    def __init__(self, full, ssem, rsem):
        self.full, self.ssem, self.rsem = full, ssem, rsem
        self.place = plane_place()
        self.cps = {}

    def send(self, k, block, half, target):
        view = self.full.at[block, self.place[4], half]
        self.cps[k] = remote(view, view, self.ssem.at[k], self.rsem.at[k], target)

    def start(self):
        me, _, _, _, c, to_x, to_y, to_c = self.place
        self.send(1, me, 0, to_x)
        self.send(3, me, 1, to_y)
        self.send(2, me, 1, to_x)
        self.send(4, me, 0, to_y)
        own = self.full.at[me, c]
        self.cps[0] = remote(own, own, self.ssem.at[0], self.rsem.at[0], to_c)

    def arrived(self, *keys):
        for k in keys:
            self.cps[k].wait_recv()

    def hop1(self):
        _, xn, yn, _, _, to_x, to_y, to_c = self.place
        self.arrived(1)
        self.send(5, xn, 0, to_y)
        self.send(6, xn, 0, to_c)
        self.arrived(3)
        self.send(7, yn, 1, to_x)
        self.send(8, yn, 1, to_c)

    def hop2(self):
        _, xn, yn, _, _, _, _, to_c = self.place
        self.arrived(2)
        self.send(9, xn, 1, to_c)
        self.arrived(4)
        self.send(10, yn, 0, to_c)

    def hop3(self):
        _, _, _, dg, _, _, _, to_c = self.place
        self.arrived(5)
        self.send(11, dg, 0, to_c)
        self.arrived(7)
        self.send(12, dg, 1, to_c)

    def finish(self):
        for k in range(AG_COPIES):
            self.cps[k].wait_send()

    def run(self, consume, spare=()):
        me, xn, yn, dg = self.place[:4]
        spare = list(spare)

        def fill(most):
            for _ in range(min(most, len(spare))):
                spare.pop(0)()

        self.start()
        self.arrived(0)
        consume(me)
        fill(3)
        self.hop1()
        fill(2)
        self.hop2()
        self.arrived(6, 9)
        consume(xn)
        fill(2)
        self.hop3()
        self.arrived(8, 10)
        consume(yn)
        self.arrived(11, 12)
        consume(dg)
        fill(len(spare))
        self.finish()


class RowSum:
    def __init__(self, part, own, cb, sb, keep, r1, r2, ssem, rsem):
        self.part, self.own, self.cb, self.sb, self.keep = part, own, cb, sb, keep
        self.r1, self.r2, self.ssem, self.rsem = r1, r2, ssem, rsem
        self.place = plane_place()
        self.cps = {}

    def block(self, k):
        me, xn, yn, dg = self.place[:4]
        return (dg, xn, yn, me)[k]

    def copy(self, k, src, dst, target):
        self.cps[k] = remote(src, dst, self.ssem.at[k], self.rsem.at[k], target)

    def core(self, k):
        src = self.part.at[self.block(k), 1 - self.place[4]]
        self.copy(k, src, self.cb.at[k], self.place[7])

    def both(self, k, half):
        mine = self.part[self.block(k), self.place[4], half]
        return mine.astype(F32) + self.cb[k, half].astype(F32)

    def push(self, k):
        to_x, to_y = self.place[5:7]
        sb, r1 = self.sb, self.r1
        self.cps[k].wait_recv()
        if k == 0:
            sb[0, 0] = self.both(0, 0).astype(BF16)
            self.copy(4, sb.at[0, 0], r1.at[0, 0], to_x)
            sb[0, 1] = self.both(0, 1).astype(BF16)
            self.copy(5, sb.at[0, 1], r1.at[1, 0], to_y)
        if k == 1:
            sb[1, 0] = self.both(1, 0).astype(BF16)
            self.copy(6, sb.at[1, 0], r1.at[0, 1], to_x)
            self.keep[1] = self.both(1, 1)
        if k == 2:
            sb[2, 1] = self.both(2, 1).astype(BF16)
            self.copy(7, sb.at[2, 1], r1.at[1, 1], to_y)
            self.keep[0] = self.both(2, 0)
        if k == 3:
            self.own[0] = self.both(3, 0)
            self.own[1] = self.both(3, 1)

    def relay(self):
        to_x, to_y = self.place[5:7]
        self.cps[4].wait_recv()
        self.sb[2, 0] = (self.keep[0] + self.r1[0, 0].astype(F32)).astype(BF16)
        self.copy(8, self.sb.at[2, 0], self.r2.at[0], to_y)
        self.cps[5].wait_recv()
        self.sb[1, 1] = (self.keep[1] + self.r1[1, 0].astype(F32)).astype(BF16)
        self.copy(9, self.sb.at[1, 1], self.r2.at[1], to_x)
        self.cps[6].wait_recv()
        self.own[0] += self.r1[0, 1].astype(F32)
        self.cps[7].wait_recv()
        self.own[1] += self.r1[1, 1].astype(F32)

    def finish(self):
        self.cps[8].wait_recv()
        self.own[0] += self.r2[0].astype(F32)
        self.cps[9].wait_recv()
        self.own[1] += self.r2[1].astype(F32)
        for k in range(RS_COPIES):
            self.cps[k].wait_send()

    def run(self, produce, spare=()):
        spare = list(spare)
        for k in range(4):
            produce(self.block(k))
            self.core(k)
        for k in range(4):
            self.push(k)
        for job in spare[: len(spare) // 2]:
            job()
        self.relay()
        for job in spare[len(spare) // 2 :]:
            job()
        self.finish()


def rs_scratch():
    return [
        VM((2, 64, D), F32),
        VM((4, 2, 64, D), BF16),
        VM((3, 2, 64, D), BF16),
        VM((2, 64, D), F32),
        VM((2, 2, 64, D), BF16),
        VM((2, 64, D), BF16),
        pltpu.SemaphoreType.DMA((RS_COPIES,)),
        pltpu.SemaphoreType.DMA((RS_COPIES,)),
    ]


def ag_scratch():
    return [pltpu.SemaphoreType.DMA((AG_COPIES,)), pltpu.SemaphoreType.DMA((AG_COPIES,))]


def cost(micros):
    return pl.CostEstimate(flops=0, bytes_accessed=int(micros * 3.0e6), transcendentals=0)


def group_place():
    return lax.axis_index("sh") * lax.axis_size("hh") + lax.axis_index("hh")


def group_peer(k, count):
    nhh = lax.axis_size("hh")
    other = lax.rem(group_place() + k, count)
    sh, hh = other // nhh, lax.rem(other, nhh)
    return other, sh, hh, {"sh": sh, "hh": hh}


def place_peer(k):
    coords = {}
    for bit, axis in enumerate(("hl", "sx", "sy")):
        here = lax.axis_index(axis)
        coords[axis] = 1 - here if (k >> bit) & 1 else here
    target = {axis: v for bit, (axis, v) in enumerate(coords.items()) if (k >> bit) & 1}
    return coords["sy"] * 2 + coords["sx"], coords["hl"], target


def barrier_of(plane, group, count, column):
    barrier = pltpu.get_barrier_semaphore()
    seen = 0
    if column:
        hh, c = lax.axis_index("hh"), lax.axis_index("hl")
        for k in range(1, 8):
            target = {"hh": lax.rem(hh + k // 2, 4), "hl": 1 - c if k % 2 else c}
            if k == 1 and plane:
                continue
            pl.semaphore_signal(barrier, inc=1, device_id=target, device_id_type=MESH_ID)
            seen += 1
        group = False
    for k in ((1, 2, 4) if plane == 3 else range(1, 8)) if plane else ():
        _, _, target = place_peer(k)
        pl.semaphore_signal(barrier, inc=1, device_id=target, device_id_type=MESH_ID)
        seen += 1
    if group:
        for k in range(1, count):
            target = group_peer(k, count)[3]
            pl.semaphore_signal(barrier, inc=1, device_id=target, device_id_type=MESH_ID)
            seen += 1
    pl.semaphore_wait(barrier, seen)


def chained():
    return lax.axis_size("sh") == 1 and lax.axis_size("hh") == 4


class Job:
    def __init__(self, kind, src, spec=None, name=None, held=False, pool=None):
        self.kind, self.src, self.inside = kind, src, isinstance(src, jax.ShapeDtypeStruct)
        self.spec = spec or (VMEM if kind == "zs" else ANY)
        self.src_spec = VMEM if kind == "zs" else ANY
        self.name, self.held, self.pool = name, held, pool

    def out_shape(self):
        nsh, nhh = lax.axis_size("sh"), lax.axis_size("hh")
        shape = list(self.src.shape)
        if self.kind == "zg":
            shape = [nsh * 4, nhh] + shape[1:]
        if self.kind == "zr":
            shape = [nsh * nhh] + shape
        if self.kind == "zo":
            shape = [nsh * nhh, 4] + shape[2:]
        if self.kind == "zs":
            shape = [4] + shape[2:]
        if self.kind == "zw":
            shape = [4] + shape
        return jax.ShapeDtypeStruct(tuple(shape), BF16)


class Transfers:
    def __init__(self, kinds, sources, results, buffers, sems, count, chain):
        self.kinds, self.sources, self.results = kinds, sources, results
        self.buffers, self.sems, self.count, self.chain = buffers, sems, count, chain
        self.state = {}

    def copy(self, i, src, dst, send, recv, target):
        return pltpu.make_async_remote_copy(
            src_ref=src, dst_ref=dst, send_sem=self.sems[0].at[i, send],
            recv_sem=self.sems[1].at[i, recv], device_id=target, device_id_type=MESH_ID,
        )

    early = ()

    def __call__(self):
        for i, src in enumerate(self.sources):
            if src is not None and i not in self.state:
                self.start(i)

    late = __call__

    def slot(self, i, group):
        out, nhh = self.results[i], lax.axis_size("hh")
        if self.kinds[i] == "zg":
            return out.at[pl.ds(group // nhh * 4, 4), lax.rem(group, nhh)]
        return out.at[group]

    def got(self, i, ref, index):
        pltpu.make_async_copy(ref, ref, self.sems[1].at[i, index]).wait()

    def sent(self, i, ref, index):
        pltpu.make_async_copy(ref, ref, self.sems[0].at[i, index]).wait()

    names = {}

    def has(self, i):
        return i in self.names

    def start(self, i, src=None):
        i = self.names.get(i, i)
        if src is not None:
            self.sources[i] = src
        self.state[i] = "sent"
        kind, src, out, count = self.kinds[i], self.sources[i], self.results[i], self.count
        hh, g = lax.axis_index("hh"), group_place()
        local = None
        if kind == "pa":
            s, c, _ = place_peer(0)
            for k in range(1, 8):
                ps, pc, target = place_peer(k)
                self.copy(i, src.at[ps, pc], out.at[s, c], k, k, target).start()
            local = (src.at[s, c], out.at[s, c])
        if kind in ("zg", "zr"):
            for k in (1, 3, 2) if self.chain else range(1, count):
                go = self.copy(i, src, self.slot(i, g), k, g, group_peer(k, count)[3]).start
                if self.chain and k != 2:
                    pl.when(hh != (3 if k == 1 else 0))(go)
                else:
                    go()
            local = (src, self.slot(i, g))
        if kind in ("zo", "zt"):
            nhh = lax.axis_size("hh")
            part = lambda p: (
                src.at[p] if kind == "zt" else src.at[pl.ds(p // nhh * 4, 4), lax.rem(p, nhh)]
            )
            for k in range(1, count):
                other, _, _, target = group_peer(k, count)
                self.copy(i, part(other), out.at[g], k, g, target).start()
            local = (part(g), out.at[g])
        if kind == "zs":
            buf = self.buffers[i]
            last, begin = hh == 3, hh == 0
            up = self.copy(
                i, src.at[:, jnp.where(last, 0, hh + 1)], buf.at[jnp.where(last, 4, g)],
                1, jnp.where(last, 4, g), {"hh": jnp.where(last, 2, hh + 1)},
            ).start
            down = self.copy(
                i, src.at[:, jnp.where(begin, 3, hh - 1)], buf.at[jnp.where(begin, 4, g)],
                3, jnp.where(begin, 4, g), {"hh": jnp.where(begin, 1, hh - 1)},
            ).start

            @pl.when(last)
            def _():
                up()
                down()

            @pl.when(jnp.logical_not(last))
            def _():
                down()
                up()

            far = lax.rem(hh + 2, 4)
            pl.when(last | begin)(self.copy(i, src.at[:, far], buf.at[g], 2, g, {"hh": far}).start)
        if kind in ("zw", "zv"):
            for k in range(4):
                mine, target, src_k, at, _ = self.column(kind, k)
                view = src if kind == "zw" else src.at[src_k]
                here = pltpu.make_async_copy(view, out.at[at], self.sems[2].at[i]).start
                pl.when(mine)(here)
                pl.when(jnp.logical_not(mine))(self.copy(i, view, out.at[at], k, at, target).start)
        if local is not None:
            pltpu.make_async_copy(local[0], local[1], self.sems[2].at[i]).start()
            self.local = getattr(self, "local", {})
            self.local[i] = local

    def column(self, kind, k):
        hh, c = lax.axis_index("hh"), lax.axis_index("hl")
        if kind == "zw":
            z, to_c, slot = lax.rem(hh + k, 4), hh // 2, lax.rem(hh, 2) * 2 + c
            own = (2 * c + k // 2 == hh) & (k % 2 == c)
            return (z == hh) & (to_c == c), {"hh": z, "hl": to_c}, 0, slot, own
        j = lax.rem(lax.rem(hh, 2) * 2 + c + k, 4)
        z, to_c = 2 * c + j // 2, lax.rem(j, 2)
        own = (k == hh) & (hh // 2 == c)
        return (z == hh) & (to_c == c), {"hh": z, "hl": to_c}, j, hh, own

    def relay(self, *which):
        for i in which:
            i = self.names.get(i, i)
            if i not in self.state:
                continue
            kind = self.kinds[i]
            if not self.chain or kind not in ("zg", "zr", "zs") or self.state[i] != "sent":
                continue
            self.state[i] = "relayed"
            hh, g = lax.axis_index("hh"), group_place()
            inner = (hh == 1) | (hh == 2)
            far = lax.rem(hh + 2, 4)

            @pl.when(inner)
            def _(i=i, kind=kind):
                if kind == "zs":
                    buf, src = self.buffers[i], self.sources[i]
                    self.got(i, buf.at[4], 4)
                    buf[4] = (buf[4].astype(F32) + src[:, far].astype(F32)).astype(BF16)
                    self.copy(i, buf.at[4], buf.at[g], 2, g, {"hh": far}).start()
                else:
                    slot = self.slot(i, far)
                    self.got(i, slot, far)
                    self.copy(i, slot, slot, 0, far, {"hh": 3 - far}).start()

    def wait(self, *which):
        self.relay(*which)
        for i in which:
            i = self.names.get(i, i)
            if self.state[i] == "done":
                continue
            self.state[i] = "done"
            kind, src, out, count = self.kinds[i], self.sources[i], self.results[i], self.count
            hh, g = lax.axis_index("hh"), group_place()
            inner = (hh == 1) | (hh == 2)
            if kind == "pa":
                s, c, _ = place_peer(0)
                for k in range(1, 8):
                    self.copy(i, src.at[s, c], out.at[s, c], k, k, place_peer(k)[2]).wait()
            if kind in ("zg", "zr"):
                for k in range(1, count):
                    other = lax.rem(g + k, count)
                    slot = self.slot(i, other)

                    def arrive(slot=slot, other=other):
                        self.got(i, slot, other)

                    def leave(k=k):
                        self.sent(i, src, k)

                    if not self.chain:
                        arrive()
                        leave()
                    elif k == 2:
                        pl.when(jnp.logical_not(inner))(arrive)
                        leave()
                        pl.when(inner)(functools.partial(leave, 0))
                    else:
                        arrive()
                        pl.when(hh != (3 if k == 1 else 0))(leave)
            if kind in ("zo", "zt"):
                for k in range(1, count):
                    other = lax.rem(g + k, count)
                    self.got(i, out.at[other], other)
                    self.sent(i, out.at[other], k)
            if kind in ("zw", "zv"):
                for k in range(4):
                    mine, _, _, at, own = self.column(kind, k)
                    slot = out.at[k]
                    here = pltpu.make_async_copy(slot, slot, self.sems[2].at[i]).wait
                    pl.when(own)(here)
                    pl.when(jnp.logical_not(own))(functools.partial(self.got, i, slot, k))
                    pl.when(jnp.logical_not(mine))(functools.partial(self.sent, i, slot, k))
            if kind == "zs":
                buf = self.buffers[i]
                one = jnp.where(hh == 0, 2, hh - 1)
                two = jnp.where(hh == 3, 1, hh + 1)
                far = lax.rem(hh + 2, 4)
                self.got(i, buf.at[one], one)
                self.got(i, buf.at[two], two)
                total = lambda: (
                    src[:, g].astype(F32) + buf[one].astype(F32) + buf[two].astype(F32)
                )

                @pl.when(inner)
                def _():
                    self.got(i, buf.at[far], far)
                    out[...] = (total() + buf[far].astype(F32)).astype(BF16)

                @pl.when(jnp.logical_not(inner))
                def _():
                    out[...] = total().astype(BF16)

                for k in (1, 2, 3):
                    self.sent(i, buf.at[g], k)
            if i in getattr(self, "local", {}):
                a, b = self.local[i]
                pltpu.make_async_copy(a, b, self.sems[2].at[i]).wait()

    def rest(self):
        which = [i for i in self.state if self.state[i] != "done"]
        self.relay(*which)
        self.wait(*which)

    def result(self, i):
        return self.results[self.names.get(i, i)]

    def columns(self, i):
        ref = self.result(i)
        return ref[...].reshape(D, ref.shape[-1])


ANY = pl.BlockSpec(memory_space=pl.ANY)
VMEM = pl.BlockSpec(memory_space=pltpu.VMEM)
SMEM = pl.BlockSpec(memory_space=pltpu.SMEM)


def step(body, ins, outs, scratch, jobs, plane, group, name, collective, micros, early=()):
    count = lax.axis_size(GROUP)
    kinds = [job.kind for job in jobs]
    given = [job for job in jobs if not job.inside]
    shown = [job for job in jobs if not job.held]
    n_in, n_out, n_job, n_src = len(ins), len(outs), len(jobs), len(given)
    plane = 7 if "pa" in kinds else plane
    group = group or any(kind != "pa" for kind in kinds)
    column = any(kind in ("zw", "zv") for kind in kinds)
    slots = max(count, 8)
    held = [VM(job.out_shape().shape, BF16) for job in jobs if job.held]
    pools = {}
    for i, job in enumerate(jobs):
        if job.kind == "zs":
            key = (job.pool if job.pool is not None else -1 - i, job.out_shape().shape)
            pools.setdefault(key, []).append(i)

    def kernel(*refs):
        in_refs, refs = refs[:n_in], refs[n_in:]
        given_refs, refs = list(refs[:n_src]), refs[n_src:]
        out_refs, refs = refs[:n_out], refs[n_out:]
        shown_refs, refs = list(refs[: len(shown)]), refs[len(shown) :]
        extra_refs, own = list(refs[len(scratch) :]), refs[: len(scratch)]
        held_refs, pool_refs = extra_refs[3 : 3 + len(held)], extra_refs[3 + len(held) :]
        sources = [None if job.inside else given_refs.pop(0) for job in jobs]
        results = [held_refs.pop(0) if job.held else shown_refs.pop(0) for job in jobs]
        buffers = {i: ref for key, ref in zip(pools, pool_refs) for i in pools[key]}
        barrier_of(plane, group, count, column)
        begin = Transfers(kinds, sources, results, buffers, extra_refs[:3], count, chained())
        begin.early = early
        begin.names = {job.name: i for i, job in enumerate(jobs) if job.name}
        body(begin, *in_refs, *out_refs, *own)
        if not begin.state:
            begin()
        begin.rest()

    extra = (
        [
            pltpu.SemaphoreType.DMA((n_job, slots)),
            pltpu.SemaphoreType.DMA((n_job, slots)),
            pltpu.SemaphoreType.DMA((n_job,)),
        ]
        + held
        + [VM((5,) + key[1], BF16) for key in pools]
    )
    result = pl.pallas_call(
        kernel,
        out_shape=tuple(o for o, _ in outs) + tuple(job.out_shape() for job in shown),
        in_specs=[spec for _, spec in ins] + [job.src_spec for job in given],
        out_specs=tuple(spec for _, spec in outs) + tuple(job.spec for job in shown),
        scratch_shapes=list(scratch) + (extra if n_job else []),
        compiler_params=pltpu.CompilerParams(
            collective_id=collective, has_side_effects=True, vmem_limit_bytes=LIMIT
        ),
        cost_estimate=cost(micros),
        name=name,
    )(*[v for v, _ in ins], *[job.src for job in given])
    return result[:n_out], result[n_out:]


FULL = jax.ShapeDtypeStruct((4, 2, 2, 64, D), BF16)
OWN = jax.ShapeDtypeStruct((2, 64, D), F32)


def flat(full):
    return full.reshape(1024, D)


def blocks(rows):
    return rows.reshape(4, 2, 2, 64, D)


def vmem(*values):
    return [(v, VMEM) for v in values]


def normed_half(u, gain):
    inv = lax.rsqrt(jnp.mean(u * u, axis=-1, keepdims=True) + EPSILON)
    return (u * inv * gain).astype(BF16)


def first(x, lead, jobs, collective):
    width = lead.shape[-1]

    def body(begin, x_ref, full, norms, proj, weight, gains, s1, r1):
        me, c = plane_place()[0], plane_place()[4]
        begin.start(0)
        full[me, c] = x_ref[...]
        rows = RowGather(full, s1, r1)
        rows.start()
        begin.wait(0)
        begin.start(1, begin.results[0])
        rows.hop1()
        rows.hop2()
        rows.hop3()
        for i in range(2, 2 + len(jobs)):
            begin.start(i)
        begin.relay(1)
        rows.arrived(0, 6, 8, 9, 10, 11, 12)
        rows.finish()
        begin.wait(1)
        weight[...] = begin.columns(1)
        gains[...] = weight[:, :128].astype(F32).T[64:72]
        lane = lanes(D, width)
        weight[...] = jnp.where((lane < 64) | (lane >= 128), weight[...], jnp.zeros((), BF16))

        def project(block, carry):
            n = normed_half(chip_rows(full, block).astype(F32), gains[0:1])
            put_chip(norms, block, n)
            proj[rows_of(block), :] = matmul(n, weight[...]).astype(BF16)
            return carry

        lax.fori_loop(0, 4, project, 0)

    return step(
        body, vmem(x),
        vmem(
            FULL, FULL, jax.ShapeDtypeStruct((1024, width), BF16), jax.ShapeDtypeStruct((D, width), BF16),
            jax.ShapeDtypeStruct((8, D), F32),
        ),
        ag_scratch(),
        [Job("pa", lead), Job("zg", jax.ShapeDtypeStruct(lead.shape, BF16), VMEM)] + jobs,
        7, True, "first", collective, 25,
    )


def chip_rows(ref, block):
    return ref[block].reshape(256, D)


def put_chip(ref, block, value):
    ref[block] = value.astype(BF16).reshape(2, 2, 64, D)


def rows_of(block):
    return pl.ds(block * 256, 256)


def silu_parts(gate):
    sig = 1.0 / (1.0 + jnp.exp(-gate))
    return sig, gate * sig


def follow(total, seen):
    k = (3, 1, 2, 0)[len(seen)]
    seen.append(k)
    total.core(k)
    if k == 2:
        total.push(1)
    if k == 0:
        total.push(2)
        total.push(3)
        total.push(0)


def norm_back_half(dn, u, gain, upstream):
    inv = lax.rsqrt(jnp.mean(u * u, axis=-1, keepdims=True) + EPSILON)
    gained = dn * gain
    inner = jnp.mean(gained * u, axis=-1, keepdims=True)
    scaled = u * inv
    grad = upstream + inv * gained - scaled * (inv * inv * inner)
    return grad, jnp.sum(dn * scaled, axis=0, keepdims=True)


def back_own(dn, u_ref, gain_ref, up_ref, gnew, ggain, full):
    me, c = plane_place()[0], plane_place()[4]
    total = None
    for half in range(2):
        grad, gain_part = norm_back_half(
            dn[half], u_ref[half].astype(F32), gain_ref[...], up_ref[half].astype(F32)
        )
        gnew[half] = grad
        total = gain_part if total is None else total + gain_part
        if full is not None:
            full[me, c, half] = grad.astype(BF16)
    ggain[...] = total


def weight_grads(left, right, out):
    def piece(i):
        width = D // 4
        lo = i * width
        lhs = left[:, :, :, :, lo : lo + width].reshape(1024, width)
        value = matmul_tn(lhs, right[...]).astype(BF16)
        if len(out.shape) == 5:
            out[i] = value.reshape(out.shape[1:])
        else:
            out[lo : lo + width, :] = value

    return [functools.partial(piece, i) for i in range(4)]


def shipping():
    return chained() and D % (8 * 4 * 16) == 0


def terms_shape(cols):
    nsh, nhh = lax.axis_size("sh"), lax.axis_size("hh")
    if shipping():
        return jax.ShapeDtypeStruct((4, 4, 2, D // 32, cols), BF16)
    return jax.ShapeDtypeStruct((D, cols), BF16)


def apart(arrays, collective):
    nsh, nhh = lax.axis_size("sh"), lax.axis_size("hh")
    rows = D // (8 * nsh * nhh)
    jobs = [Job("zo", a.reshape(nsh * 4, nhh, 2, rows, a.shape[-1])) for a in arrays]
    _, moved = step(lambda begin: None, [], [], [], jobs, 0, True, "apart", collective, 20)
    return [jnp.sum(a.astype(F32), axis=0).astype(BF16) for a in moved]


def last_layer(dproj, w_proj, u, gain, upstream, x_full, n_first, gains, jobs, collective):
    width = w_proj.shape[1]
    ship = shipping()

    def body(
        begin, dp_ref, wp_ref, u_ref, gain_ref, up_ref, xf_ref, nf_ref, gains_ref,
        gnew, ggain, proj_w, part1, mine, *rest
    ):
        sum1 = RowSum(part1, *rest)
        begin()
        mine[...] = jnp.zeros((128, D), F32)
        mine[65:68, :] = gains_ref[...]

        def projected(block):
            part = matmul_nt(dp_ref[rows_of(block), :], wp_ref[...])
            put_chip(part1, block, part)
            u = chip_rows(xf_ref, block).astype(F32)
            u = u * lax.rsqrt(jnp.mean(u * u, axis=-1, keepdims=True) + EPSILON)
            mine[64:65, :] += jnp.sum(part * u, axis=0, keepdims=True)

        def grads():
            turned = mine[...].T
            for i in range(4):
                at = slice(i * 256, i * 256 + 256)
                lhs = nf_ref[:, :, :, :, at].reshape(1024, 256)
                value = matmul_tn(lhs, dp_ref[...])
                keep = lanes(256, 128) < 64
                value = jnp.concatenate(
                    [jnp.where(keep, value[:, :128], turned[at]), value[:, 128:]], axis=1
                ).astype(BF16)
                if ship:
                    proj_w[i] = value.reshape(proj_w.shape[1:])
                else:
                    proj_w[at, :] = value
            if ship:
                begin.start(len(jobs), proj_w)

        for k in range(4):
            projected(sum1.block(k))
            sum1.core(k)
        for k in range(4):
            sum1.push(k)
        grads()
        sum1.relay()
        sum1.finish()
        back_own(sum1.own, u_ref, gain_ref, up_ref, gnew, ggain, None)
        if ship:
            begin.wait(len(jobs))
            begin.start(len(jobs) + 1, begin.results[len(jobs)])

    terms = terms_shape(width)
    summed = jax.ShapeDtypeStruct((4, 2, D // 32, width), BF16)
    n = len(jobs)
    outs, moved = step(
        body, vmem(dproj, w_proj, u, gain, upstream, x_full, n_first, gains),
        vmem(OWN, jax.ShapeDtypeStruct((1, D), F32)) + ([] if ship else vmem(terms)),
        ([VM(terms.shape, BF16)] if ship else []) + [VM(FULL.shape, BF16), VM((128, D), F32)] + rs_scratch(),
        jobs + ([Job("zs", terms), Job("pa", summed)] if ship else []),
        3, False, "last_layer", collective, 25,
    )
    if ship:
        return outs[0], moved[:n], moved[n + 1]
    (lin,) = apart([outs[2]], 12)
    _, (lin,) = step(
        lambda begin: None, [], [], [], [Job("pa", lin)], 7, False, "last", 13, 5
    )
    return outs[0], moved[:n], lin


def taylor_tables():
    pick = np.zeros((4, 2, 128, 256), np.float32)
    coef = np.zeros((8, 256), np.float32)
    pairs = [(i, j) for i in range(FEAT) for j in range(i, FEAT)]
    one = 4 * FEAT
    for x, (i, j) in enumerate(pairs):
        coef[:, x] = (2.0 * FEAT) ** -0.5 if i == j else FEAT**-0.5
        for t in range(4):
            pick[t, 0, t * FEAT + i, x] = 1.0
            pick[t, 1, t * FEAT + j, x] = 1.0
    for i in range(FEAT):
        x = len(pairs) + i
        coef[:, x] = FEAT**-0.25
        for t in range(4):
            pick[t, 0, t * FEAT + i, x] = 1.0
            pick[t, 1, one, x] = 1.0
    x = len(pairs) + FEAT
    coef[:, x] = 1.0
    pick[:, 0, one, x] = 1.0
    pick[:, 1, one, x] = 1.0
    shift = np.zeros((128, 128), np.float32)
    for i in range(2 * FEAT):
        shift[2 * FEAT + i, i] = 1.0
    return jnp.asarray(pick, BF16), jnp.asarray(coef, F32), jnp.asarray(shift, BF16)


def chunk_of(group, s):
    nhh = lax.axis_size("hh")
    return (group // nhh * 4 + s) * nhh + lax.rem(group, nhh)


def segment_of(starts, position):
    total = jnp.where(position >= starts[0], 0, -1)
    for i in range(1, starts.shape[0]):
        total = total + jnp.where(position >= starts[i], 1, 0)
    return total


class Segments:
    def __init__(self, starts, s):
        first = chunk_of(group_place(), s) * 256
        at = lambda shape, dim: first + lax.broadcasted_iota(jnp.int32, shape, dim)
        self.col = segment_of(starts, at((256, 1), 0))
        self.row = segment_of(starts, at((1, 256), 1))
        self.ext = segment_of(starts, at((1, 256 + RIM), 1) - RIM)
        self.last = segment_of(starts, first + 255)
        self.before = segment_of(starts, first - 1)


def carried(starts, s, st, sm, count, back):
    mine = chunk_of(group_place(), s)
    edge = segment_of(starts, mine * 256 + 255 if back else mine * 256 - 1)

    def group(i, both):
        def one(s2, both):
            state, total = both
            other = chunk_of(i, s2)
            reach = segment_of(starts, other * 256 - 1 if back else other * 256 + 255)
            ordered = other > mine if back else other < mine
            m = jnp.where(ordered & (reach == edge), 1.0, 0.0)
            return state + m * st[i, s2].astype(F32), total + m * sm[i, s2]

        return lax.fori_loop(s, 4, one, both) if back else lax.fori_loop(0, s + 1, one, both)

    return lax.fori_loop(
        0, count, group, (jnp.zeros((SROWS, 128), F32), jnp.zeros((8, 256), F32))
    )


def lanes(rows, width):
    return lax.broadcasted_iota(jnp.int32, (rows, width), 1)


class States:
    def __init__(self, count, st, sm, ssem, rsem):
        self.refs, self.ssem, self.rsem, self.count = (st, sm), ssem, rsem, count
        self.chain = count == 4 and chained()

    def copy(self, n, k, group, target):
        view = self.refs[n].at[group]
        return pltpu.make_async_remote_copy(
            src_ref=view, dst_ref=view, send_sem=self.ssem.at[n, k], recv_sem=self.rsem.at[n, group],
            device_id=target, device_id_type=MESH_ID,
        )

    def send(self):
        g, hh = group_place(), lax.axis_index("hh")
        for k in (2, 1, 3) if self.chain else range(1, self.count):
            for n in range(2):
                go = self.copy(n, k, g, group_peer(k, self.count)[3]).start
                if self.chain and k != 2:
                    pl.when(hh != (3 if k == 1 else 0))(go)
                else:
                    go()

    def got(self, n, group):
        view = self.refs[n].at[group]
        pltpu.make_async_copy(view, view, self.rsem.at[n, group]).wait()

    def sent(self, n, k):
        view = self.refs[n].at[0]
        pltpu.make_async_copy(view, view, self.ssem.at[n, k]).wait()

    def relay(self):
        if not self.chain:
            return
        hh = lax.axis_index("hh")
        far = lax.rem(hh + 2, 4)

        @pl.when((hh == 1) | (hh == 2))
        def _():
            for n in range(2):
                self.got(n, far)
                self.copy(n, 0, far, {"hh": 3 - far}).start()

    def arrive(self):
        g, hh = group_place(), lax.axis_index("hh")
        inner = (hh == 1) | (hh == 2)
        for k in range(1, self.count):
            other = lax.rem(g + k, self.count)
            for n in range(2):
                got = functools.partial(self.got, n, other)
                if self.chain and k == 2:
                    pl.when(jnp.logical_not(inner))(got)
                else:
                    got()

    def finish(self):
        hh = lax.axis_index("hh")
        for k in range(1, self.count):
            for n in range(2):
                sent = functools.partial(self.sent, n, k)
                if self.chain and k != 2:
                    pl.when(hh != (3 if k == 1 else 0))(sent)
                else:
                    sent()
                    if self.chain:
                        pl.when((hh == 1) | (hh == 2))(functools.partial(self.sent, n, 0))


def phi_of(x, pick, coef, t):
    left = matmul(x, pick[t, 0])
    right = matmul(x, pick[t, 1])
    return left, right, (left * right * coef).astype(BF16)


def taylor_forward_kernel(
    count, begin, qkv, pick, coef_ref, shift, cot_ref, starts,
    o_ref, y_ref, den_ref, pre_ref, psum_ref, cfull,
    st, sm, phis, ssem, rsem, ags, agr,
):
    g = group_place()
    me, c = plane_place()[0], plane_place()[4]
    cfull[me, c] = cot_ref[...]
    rows_in = RowGather(cfull, ags, agr)
    rows_in.start()
    for i in begin.early:
        begin.start(i)
    coef = coef_ref[0:1, :]
    left_half = lanes(256, 128) < 64

    def states(s, carry):
        rows = pl.ds(s * 256, 256)
        x = jnp.where(lanes(256, 128) == 4 * FEAT, jnp.ones((), BF16), qkv[rows, 0:128])
        v = qkv[rows, 128:256]
        seg = Segments(starts, s)
        tail = seg.col == seg.last
        v_tail = jnp.where(tail, v, jnp.zeros((), BF16))
        state = jnp.zeros((256, 128), F32)
        for h in range(2):
            _, _, phi_k = phi_of(x, pick, coef, 2 + h)
            side = left_half if h == 0 else jnp.logical_not(left_half)
            state += matmul_tn(phi_k, jnp.where(side, v_tail, jnp.zeros((), BF16)))
            total = jnp.sum(jnp.where(tail, phi_k.astype(F32), 0.0), axis=0, keepdims=True)
            sm[g, s, h : h + 1, :] = total
            _, _, phi_q = phi_of(x, pick, coef, h)
            phis[h, rows, :] = phi_q
        st[g, s] = state[:SROWS].astype(BF16)
        return carry

    sm[g] = jnp.zeros((4, 8, 256), F32)
    lax.fori_loop(0, 4, states, 0)
    exchange = States(count, st, sm, ssem, rsem)
    exchange.send()
    begin.late()
    rows_in.hop1()

    def inner(s, carry):
        rows = pl.ds(s * 256, 256)
        x = qkv[rows, 0:128]
        v = qkv[rows, 128:256]
        k = matmul(x, shift[...]).astype(BF16)
        lane = lanes(256, 128)
        order = lax.broadcasted_iota(jnp.int32, (256, 256), 0) >= lanes(256, 256)
        seg = Segments(starts, s)
        allowed = order & (seg.col == seg.row)
        num = jnp.zeros((256, 128), F32)
        dens = []
        for h in range(2):
            q = jnp.where(lane // FEAT == h, x, jnp.zeros((), BF16))
            dot = matmul_nt(q, k)
            score = jnp.where(allowed, 1.0 + dot * FEAT**-0.5 + dot * dot * (0.5 / FEAT), 0.0)
            side = left_half if h == 0 else jnp.logical_not(left_half)
            num += matmul(score.astype(BF16), jnp.where(side, v, jnp.zeros((), BF16)))
            dens.append(jnp.sum(score, axis=1, keepdims=True))
        y_ref[rows, :] = num
        den_ref[rows, :] = jnp.where(left_half, dens[0], dens[1])
        return carry

    lax.fori_loop(0, 4, inner, 0)
    rows_in.hop2()
    rows_in.hop3()
    exchange.relay()
    begin.relay(*begin.early)
    exchange.arrive()

    def finish(s, carry):
        rows = pl.ds(s * 256, 256)

        state, total = carried(starts, s, st, sm, count, False)
        state = state.astype(BF16)
        pre_ref[s] = state
        psum_ref[s] = total
        seg = Segments(starts, s)
        cont = seg.col == seg.before
        num = jnp.zeros((256, 128), F32)
        dens = []
        for h in range(2):
            phi_q = phis[h, rows, :]
            side = left_half if h == 0 else jnp.logical_not(left_half)
            part = matmul(phi_q[:, :SROWS], state)
            num = jnp.where(side, part, num)
            dens.append(jnp.sum(phi_q.astype(F32) * total[h : h + 1], axis=1, keepdims=True))
        num = jnp.where(cont, num, 0.0) + y_ref[rows, :]
        den = jnp.where(cont, jnp.where(left_half, dens[0], dens[1]), 0.0) + den_ref[rows, :]
        y = num / den
        y_ref[rows, :] = y
        den_ref[rows, :] = den
        o_ref[rows, :] = y.astype(BF16)
        return carry

    lax.fori_loop(0, 4, finish, 0)
    rows_in.arrived(0, 6, 8, 9, 10, 11, 12)
    rows_in.finish()
    exchange.finish()


def taylor_forward(qkv, starts, tables, cot, jobs, count, collective):
    return step(
        functools.partial(taylor_forward_kernel, count),
        vmem(qkv, *tables, cot) + [(starts, SMEM)],
        vmem(
            jax.ShapeDtypeStruct((1024, 128), BF16),
            jax.ShapeDtypeStruct((1024, 128), F32),
            jax.ShapeDtypeStruct((1024, 128), F32),
            jax.ShapeDtypeStruct((4, SROWS, 128), BF16),
            jax.ShapeDtypeStruct((4, 8, 256), F32),
            FULL,
        ),
        [
            VM((count, 4, SROWS, 128), BF16),
            VM((count, 4, 8, 256), F32),
            VM((2, 1024, 256), BF16),
            pltpu.SemaphoreType.DMA((2, count)),
            pltpu.SemaphoreType.DMA((2, count)),
        ]
        + ag_scratch(),
        jobs, 3, True, "taylor_forward", collective, 28, early=(0, 1),
    )


def taylor_backward_kernel(
    count, begin, qkv, do_ref, y_ref, den_ref, pre_ref, psum_ref,
    pick, coef_ref, shift, starts,
    out_ref, st, sm, acc, dnum_ref, ddens, ssem, rsem,
):
    g = group_place()
    for i in begin.early:
        begin.start(i)
    coef = coef_ref[0:1, :]
    left_half = lanes(256, 128) < 64
    zero = jnp.zeros((), BF16)

    def sides(h):
        return left_half if h == 0 else jnp.logical_not(left_half)

    def feature_back(dphi, left, right, t):
        grad = dphi * coef
        return matmul_nt((grad * right).astype(BF16), pick[t, 0]) + matmul_nt(
            (grad * left).astype(BF16), pick[t, 1]
        )

    def states(s, carry):
        rows = pl.ds(s * 256, 256)
        x = jnp.where(lanes(256, 128) == 4 * FEAT, jnp.ones((), BF16), qkv[rows, 0:128])
        do = do_ref[rows, :].astype(F32)
        den = den_ref[rows, :]
        dnum = do / den
        dnum_low = dnum.astype(BF16)
        dnum_ref[rows, :] = dnum_low
        weighted = dnum * y_ref[rows, :]
        seg = Segments(starts, s)
        cont = seg.col == seg.before
        d_cont = jnp.where(cont, dnum_low, zero)
        pre = pre_ref[s]
        state = jnp.zeros((256, 128), F32)
        grad = jnp.zeros((256, 128), F32)
        for h in range(2):
            dden = -jnp.sum(jnp.where(sides(h), weighted, 0.0), axis=1, keepdims=True)
            ddens[h, rows, :] = jnp.broadcast_to(dden, (256, 128))
            left, right, phi_q = phi_of(x, pick, coef, h)
            d_side = jnp.where(sides(h), d_cont, zero)
            state += matmul_tn(phi_q, d_side)
            dden_cont = jnp.where(cont, dden, 0.0)
            sm[g, s, h : h + 1, :] = jnp.sum(
                phi_q.astype(F32) * dden_cont, axis=0, keepdims=True
            )
            dphi = jnp.concatenate(
                [matmul_nt(d_side, pre), jnp.zeros((256, 256 - SROWS), F32)], axis=1
            ) + dden_cont * psum_ref[s, h : h + 1, :]
            grad += feature_back(dphi, left, right, h)
        st[g, s] = state[:SROWS].astype(BF16)
        acc[0, rows, :] = grad
        return carry

    sm[g] = jnp.zeros((4, 8, 256), F32)
    lax.fori_loop(0, 4, states, 0)
    exchange = States(count, st, sm, ssem, rsem)
    exchange.send()
    begin.late()

    def inner(s, carry):
        rows = pl.ds(s * 256, 256)
        x = qkv[rows, 0:128]
        v = qkv[rows, 128:256]
        dnum = dnum_ref[rows, :]
        k_low = matmul(x, shift[...]).astype(BF16)
        lane = lanes(256, 128)
        order = lax.broadcasted_iota(jnp.int32, (256, 256), 0) >= lanes(256, 256)
        seg = Segments(starts, s)
        allowed = order & (seg.col == seg.row)
        dq = jnp.zeros((256, 128), F32)
        dk = jnp.zeros((256, 128), F32)
        dv = jnp.zeros((256, 128), F32)
        for h in range(2):
            mine = lane // FEAT == h
            q = jnp.where(mine, x, zero)
            dot = matmul_nt(q, k_low)
            score = jnp.where(allowed, 1.0 + dot * FEAT**-0.5 + dot * dot * (0.5 / FEAT), 0.0)
            d_side = jnp.where(sides(h), dnum, zero)
            dscore = matmul_nt(d_side, v) + ddens[h, rows, 0:1]
            e = jnp.where(allowed, dscore * (FEAT**-0.5 + dot * (1.0 / FEAT)), 0.0).astype(BF16)
            dq += matmul(e, jnp.where(mine, k_low, zero))
            dk += matmul_tn(e, q)
            dv += matmul_tn(score.astype(BF16), d_side)
        acc[0, rows, :] += dq
        acc[1, rows, :] = dk
        acc[2, rows, :] = dv
        return carry

    lax.fori_loop(0, 4, inner, 0)
    exchange.relay()
    begin.relay(*begin.early)
    exchange.arrive()

    def finish(s, carry):
        rows = pl.ds(s * 256, 256)

        state, total = carried(starts, s, st, sm, count, True)
        state = state.astype(BF16)
        x = jnp.where(lanes(256, 128) == 4 * FEAT, jnp.ones((), BF16), qkv[rows, 0:128])
        seg = Segments(starts, s)
        tail = seg.col == seg.last
        v_tail = jnp.where(tail, qkv[rows, 128:256], zero)
        grad = acc[0, rows, :]
        lane = lanes(256, 128)
        dv = jnp.zeros((256, 128), F32)
        for h in range(2):
            left, right, phi_k = phi_of(x, pick, coef, 2 + h)
            dphi = jnp.concatenate(
                [
                    matmul_nt(jnp.where(sides(h), v_tail, zero), state),
                    jnp.zeros((256, 256 - SROWS), F32),
                ],
                axis=1,
            ) + jnp.where(tail, total[h : h + 1], 0.0)
            grad += feature_back(dphi, left, right, 2 + h)
            dv = jnp.where(sides(h), matmul(phi_k[:, :SROWS], state), dv)
        grad += matmul_nt(acc[1, rows, :].astype(BF16), shift[...])
        dv = jnp.where(tail, dv, 0.0) + acc[2, rows, :]
        out_ref[rows, 0:128] = jnp.where(lane < 4 * FEAT, grad, 0.0).astype(BF16)
        out_ref[rows, 128:256] = dv.astype(BF16)
        return carry

    lax.fori_loop(0, 4, finish, 0)
    exchange.finish()


def taylor_backward(qkv, do, kept, starts, tables, jobs, count, collective):
    return step(
        functools.partial(taylor_backward_kernel, count),
        vmem(qkv, do, *kept, *tables) + [(starts, SMEM)],
        vmem(jax.ShapeDtypeStruct((1024, 256), BF16)),
        [
            VM((count, 4, SROWS, 128), BF16),
            VM((count, 4, 8, 256), F32),
            VM((3, 1024, 128), F32),
            VM((1024, 128), BF16),
            VM((2, 1024, 128), F32),
            pltpu.SemaphoreType.DMA((2, count)),
            pltpu.SemaphoreType.DMA((2, count)),
        ],
        jobs, 0, True, "taylor_backward", collective, 28, early=range(len(jobs)),
    )


def rim_target(s, forward):
    hh, sh = lax.axis_index("hh"), lax.axis_index("sh")
    nhh, nsh = lax.axis_size("hh"), lax.axis_size("sh")
    if forward:
        wraps = jnp.where(hh == nhh - 1, 1, 0)
        slot = lax.rem(s + wraps, 4)
        leaves = wraps if s == 3 else 0
        return {"sh": lax.rem(sh + leaves, nsh), "hh": lax.rem(hh + 1, nhh)}, slot
    wraps = jnp.where(hh == 0, 1, 0)
    slot = lax.rem(s + 4 - wraps, 4)
    leaves = wraps if s == 0 else 0
    return {"sh": lax.rem(sh + nsh - leaves, nsh), "hh": lax.rem(hh + nhh - 1, nhh)}, slot


def window_mask(starts, s):
    seg = Segments(starts, s)
    i = lax.broadcasted_iota(jnp.int32, (256, 256 + RIM), 0)
    j = lanes(256, 256 + RIM)
    return (j > i) & (j <= i + WINDOW) & (seg.col == seg.ext)


def window_probs(q, k, allowed):
    scores = jnp.where(allowed, matmul_nt(q, k) * 64**-0.5, -1e30)
    peak = jnp.max(scores, axis=1, keepdims=True)
    weights = jnp.exp(scores - peak)
    return weights / jnp.sum(weights, axis=1, keepdims=True)


def window_forward_kernel(begin, qkv, starts, o_ref, ext, rim, ssem, rsem):
    cps = []
    for s in range(4):
        target, slot = rim_target(s, True)
        src = qkv.at[pl.ds(s * 256 + 256 - RIM, RIM), pl.ds(128, 256)]
        cps.append(remote(src, rim.at[slot], ssem.at[s], rsem.at[slot], target))

    if begin is not None:
        begin()

    def fill(s, carry):
        ext[s, RIM:, :] = qkv[pl.ds(s * 256, 256), 128:384]
        return carry

    lax.fori_loop(0, 4, fill, 0)
    for s in range(4):
        pltpu.make_async_copy(rim.at[s], rim.at[s], rsem.at[s]).wait()

    def run(s, carry):
        rows = pl.ds(s * 256, 256)
        ext[s, :RIM, :] = rim[s]
        q = qkv[rows, 0:128]
        k = ext[s, :, 0:128]
        v = ext[s, :, 128:256]
        left_half = lanes(256, 128) < 64
        allowed = window_mask(starts, s)
        out = jnp.zeros((256, 128), F32)
        for h in range(2):
            side = left_half if h == 0 else jnp.logical_not(left_half)
            probs = window_probs(jnp.where(side, q, jnp.zeros((), BF16)), k, allowed)
            out = jnp.where(side, matmul(probs.astype(BF16), v), out)
        o_ref[rows, :] = out.astype(BF16)
        return carry

    lax.fori_loop(0, 4, run, 0)
    for cp in cps:
        cp.wait_send()


def window_backward_kernel(
    begin, qkv, ext, do_ref, part, u_ref, att_ref, up_full, starts, out_ref, mixed, out_w,
    acc, back, rim,
    ssem, rsem, own, cb, sb, keep, r1, r2, ss, rs,
):
    total = RowSum(part, own, cb, sb, keep, r1, r2, ss, rs)
    for k in range(4):
        total.core(k)
    begin[0]()
    zero = jnp.zeros((), BF16)

    def run(s, carry):
        rows = pl.ds(s * 256, 256)
        q = qkv[rows, 0:128]
        k = ext[s, :, 0:128]
        v = ext[s, :, 128:256]
        do = do_ref[rows, :]
        left_half = lanes(256, 128) < 64
        left_ext = lanes(256 + RIM, 128) < 64
        allowed = window_mask(starts, s)
        dq = jnp.zeros((256, 128), F32)
        dk = jnp.zeros((256 + RIM, 128), F32)
        dv = jnp.zeros((256 + RIM, 128), F32)
        for h in range(2):
            side = left_half if h == 0 else jnp.logical_not(left_half)
            q_h = jnp.where(side, q, zero)
            do_h = jnp.where(side, do, zero)
            probs = window_probs(q_h, k, allowed)
            dprobs = matmul_nt(do_h, v)
            inner = jnp.sum(probs * dprobs, axis=1, keepdims=True)
            ds = (probs * (dprobs - inner)).astype(BF16)
            dq = jnp.where(side, matmul(ds, k), dq)
            dk += matmul_tn(ds, q_h)
            dv += matmul_tn(probs.astype(BF16), do_h)
        scale = 64**-0.5
        dk = dk * scale
        out_ref[rows, 0:128] = (dq * scale).astype(BF16)
        acc[rows, 0:128] = dk[RIM:]
        acc[rows, 128:256] = dv[RIM:]
        back[s, :, 0:128] = dk[:RIM].astype(BF16)
        back[s, :, 128:256] = dv[:RIM].astype(BF16)
        return carry

    for k in range(4):
        total.push(k)
    lax.fori_loop(0, 4, run, 0)
    cps = []
    for s in range(4):
        target, slot = rim_target(s, False)
        cps.append(remote(back.at[s], rim.at[slot], ssem.at[s], rsem.at[slot], target))
    for i in range(4):
        at = slice(i * 256, i * 256 + 256)
        rhs = up_full[:, :, :, :, at].reshape(1024, 256)
        value = matmul_tn(att_ref[...], rhs).astype(BF16)
        if len(out_w.shape) == 3:
            out_w[:, :, at] = value.reshape(out_w.shape[:2] + (256,))
        else:
            out_w[:, at] = value
    total.relay()
    begin[1]()
    for s in range(4):
        pltpu.make_async_copy(rim.at[s], rim.at[s], rsem.at[s]).wait()

    def finish(s, carry):
        out_ref[pl.ds(s * 256, 256 - RIM), 128:384] = acc[pl.ds(s * 256, 256 - RIM), :].astype(BF16)
        rows = pl.ds(s * 256 + 256 - RIM, RIM)
        out_ref[rows, 128:384] = (acc[rows, :] + rim[s].astype(F32)).astype(BF16)
        return carry

    lax.fori_loop(0, 4, finish, 0)
    total.finish()
    for half in range(2):
        mixed[half] = (u_ref[half] + own[half]).astype(BF16)
    for cp in cps:
        cp.wait_send()


def middle(
    o_a, w_lin_out, x_own, gains, w_gate_a, cot, cot_own, starts, jobs, collective
):
    ff = w_gate_a.shape[1]
    ship = shipping()
    terms = terms_shape(ff)
    vector = jax.ShapeDtypeStruct((8, D), F32)
    rowset = jax.ShapeDtypeStruct((4, D // 32, D) if ship else (128, D), BF16)
    makers = ("down_b", "gate_b", "up_b", "win", "down_a", "gate_a", "up_a")

    def body(
        begin, o_a, wlo, x_own, gains, wga, cot, cot_own, starts,
        mixed, g_ha, gg, do_a, lo_w, wo_w, *rest
    ):
        n_terms = 1 + (4 if ship else 6)
        weights, rest = rest[:n_terms], rest[n_terms:]
        made = dict(zip(("up_a",) + makers[:-1], weights))
        if ship:
            made["down_a"], made["gate_a"] = made["down_b"], made["gate_b"]
        h_a, out_a, h_b, g_hb, g_oa = rest[:5]
        na2, nb1, nb2, full1, full2, part1, part2, part3 = rest[5:13]
        qkv, ext, o_b, do_b, dqkv, acc, back, rim1, rim2 = rest[13:22]
        gate_s, up_s, hid_s, hid_t, dgate, dup = rest[22:28]
        rest = rest[28:]
        set1, set2 = rest[:8], rest[8:16]
        ag = [rest[16 + 2 * i : 18 + 2 * i] for i in range(6)]
        rims = rest[28:32]
        me, c = plane_place()[0], plane_place()[4]

        def call(name, *args):
            return functools.partial(getattr(begin, name), *args)

        def ship_terms(name):
            if ship:
                begin.start(name + "_t", made[name])

        def send_on(name):
            if ship:
                begin.wait(name + "_t")
                begin.start(name + "_p", begin.result(name + "_t"))

        def relay(*names):
            if ship:
                begin.relay(*[name + "_t" for name in names])

        def norm_own(total, before, after, full, gain):
            for half in range(2):
                u = before[half].astype(F32) + total.own[half]
                after[half] = u
                full[me, c, half] = normed_half(u, gains[gain : gain + 1])

        begin.start("up_a")
        total = RowSum(part1, *set1)

        def attended_a(block):
            put_chip(part1, block, matmul(o_a[rows_of(block), :], wlo[...]))

        total.run(attended_a, [call("start", "down_a")])
        norm_own(total, x_own, h_a, na2, 1)
        total2, seen = RowSum(part2, *set2), []

        def mlp_a(block):
            n = chip_rows(na2, block)
            gate = matmul(n, wga[...])
            if not seen:
                begin.wait("up_a")
                begin.start("win")
            up = matmul(n, begin.columns("up_a"))
            hidden = (silu_parts(gate)[1] * up).astype(BF16)
            rows = rows_of(block)
            gate_s[rows, :] = gate.astype(BF16)
            up_s[rows, :] = up.astype(BF16)
            hid_s[rows, :] = hidden
            if not seen:
                begin.wait("down_a")
                begin.start("gate_b")
            put_chip(part2, block, matmul_nt(hidden, begin.columns("down_a")))
            follow(total2, seen)

        RowGather(na2, *ag[0]).run(mlp_a)
        total2.relay()
        begin.relay("win")
        begin.start("up_b")
        total2.finish()
        norm_own(total2, h_a, out_a, nb1, 2)

        def project(block):
            if not gotten:
                begin.wait("win")
                gotten.append(1)
            qkv[rows_of(block), :] = matmul(chip_rows(nb1, block), begin.columns("win")).astype(BF16)

        gotten = []
        RowGather(nb1, *ag[1]).run(
            project, [call("relay", "gate_b"), call("start", "win_out"), call("start", "down_b")]
        )
        window_forward_kernel(None, qkv, starts, o_b, ext, rim1, *rims[:2])
        begin.relay("up_b")
        begin.wait("win_out")
        wwo = begin.result("win_out")
        total = RowSum(part1, *set1)

        def attended_b(block):
            put_chip(part1, block, matmul(o_b[rows_of(block), :], wwo[...].reshape(128, D)))

        total.run(attended_b)
        norm_own(total, out_a, h_b, nb2, 3)
        begin.relay("down_b")
        total2, seen_b = RowSum(part2, *set2), []

        def mlp_b(block):
            rows = rows_of(block)
            n = chip_rows(nb2, block)
            if not seen_b:
                begin.wait("gate_b", "up_b", "down_b")
            wg, wu, wd = (begin.columns(name) for name in ("gate_b", "up_b", "down_b"))
            gate, up = matmul(n, wg), matmul(n, wu)
            sig, act = silu_parts(gate)
            hidden = (act * up).astype(BF16)
            hid_t[rows, :] = hidden
            dhidden = matmul(chip_rows(cot, block), wd)
            dg = (dhidden * up * (sig + act * (1.0 - sig))).astype(BF16)
            du = (dhidden * act).astype(BF16)
            dgate[rows, :] = dg
            dup[rows, :] = du
            put_chip(part2, block, matmul_nt(dg, wg) + matmul_nt(du, wu))
            follow(total2, seen_b)
            put_chip(part3, block, matmul_nt(hidden, wd))

        RowGather(nb2, *ag[2]).run(mlp_b)
        for job in weight_grads(cot, hid_t, made["down_b"]):
            job()
        ship_terms("down_b")
        total2.relay()
        for job in weight_grads(nb2, dgate, made["gate_b"]):
            job()
        ship_terms("gate_b")
        total2.finish()
        back_own(total2.own, h_b, gains[3:4], cot_own, g_hb, gg.at[2:3], full1)

        def output_grad_b(block):
            do_b[rows_of(block), :] = matmul_nt(
                chip_rows(full1, block), wwo[...].reshape(128, D)
            ).astype(BF16)

        RowGather(full1, *ag[3]).run(
            output_grad_b,
            weight_grads(nb2, dup, made["up_b"]) + [functools.partial(relay, "down_b")],
        )

        def window_begin():
            ship_terms("up_b")

        def window_mid():
            relay("gate_b")
            send_on("down_b")

        window_backward_kernel(
            (window_begin, window_mid), qkv, ext, do_b, part3, h_b, o_b, full1, starts,
            dqkv, mixed, wo_w, acc, back, rim2, *rims[2:4], *set1,
        )
        relay("up_b")
        if ship:
            begin.start("win_out_v", wo_w)
        total = RowSum(part1, *set2)

        def projected(block):
            put_chip(part1, block, matmul_nt(dqkv[rows_of(block), :], begin.columns("win")))

        total.run(projected, weight_grads(nb1, dqkv, made["win"]))
        ship_terms("win")
        back_own(total.own, out_a, gains[2:3], g_hb, g_oa, gg.at[1:2], full2)
        total2, seen_a = RowSum(part2, *set1), []

        def mlp_back(block):
            rows = rows_of(block)
            sig, act = silu_parts(gate_s[rows, :].astype(F32))
            dhidden = matmul(chip_rows(full2, block), begin.columns("down_a"))
            dg = (dhidden * up_s[rows, :].astype(F32) * (sig + act * (1.0 - sig))).astype(BF16)
            du = (dhidden * act).astype(BF16)
            dgate[rows, :] = dg
            dup[rows, :] = du
            put_chip(part2, block, matmul_nt(dg, wga[...]) + matmul_nt(du, begin.columns("up_a")))
            follow(total2, seen_a)

        RowGather(full2, *ag[4]).run(mlp_back)
        for job in weight_grads(full2, hid_s, made["down_a"]):
            job()
        ship_terms("down_a")
        send_on("gate_b")
        total2.relay()
        for job in weight_grads(na2, dgate, made["gate_a"]):
            job()
        ship_terms("gate_a")
        total2.finish()
        back_own(total2.own, h_a, gains[1:2], g_oa, g_ha, gg.at[0:1], full1)

        def output_grad_a(block):
            do_a[rows_of(block), :] = matmul_nt(chip_rows(full1, block), wlo[...]).astype(BF16)

        def output_weight(i):
            at = slice(i * 256, i * 256 + 256)
            rhs = full1[:, :, :, :, at].reshape(1024, 256)
            lo_w[:, at] = matmul_tn(o_a[...], rhs).astype(BF16)

        RowGather(full1, *ag[5]).run(
            output_grad_a,
            weight_grads(na2, dup, made["up_a"])
            + [functools.partial(send_on, "up_b"), functools.partial(relay, "win", "down_a")],
        )
        for i in range(4):
            output_weight(i)
        send_on("win")
        send_on("down_a")

    rows16 = lambda *shape: VM(shape, BF16)
    n_held = 6
    summed = jax.ShapeDtypeStruct((4, 2, D // (8 * lax.axis_size(GROUP)), ff), BF16)
    late = []
    if ship:
        late = [Job("zs", terms, name=m + "_t", held=m != "gate_a") for m in makers[:-1]]
        late += [Job("pa", summed, name=m + "_p") for m in makers[:-2]] + [Job("zv", rowset, name="win_out_v")]
    sem = lambda n: pltpu.SemaphoreType.DMA((n,))
    weights = [VM(terms.shape, BF16)] * 4 if ship else []
    outs, moved = step(
        body,
        vmem(o_a, w_lin_out, x_own, gains, w_gate_a, cot, cot_own) + [(starts, SMEM)],
        vmem(
            jax.ShapeDtypeStruct((2, 64, D), BF16), OWN, vector, jax.ShapeDtypeStruct((1024, 128), BF16),
            jax.ShapeDtypeStruct((128, D), BF16),
            rowset, terms,
        )
        + ([] if ship else vmem(*[terms] * n_held)),
        weights + [VM((2, 64, D), F32)] * 5 + [VM(FULL.shape, BF16)] * 8
        + [
            rows16(1024, 384), rows16(4, 256 + RIM, 256), rows16(1024, 128), rows16(1024, 128),
            rows16(1024, 384), VM((1024, 256), F32), rows16(4, RIM, 256), rows16(4, RIM, 256),
            rows16(4, RIM, 256),
        ]
        + [rows16(1024, ff)] * 6
        + rs_scratch() + rs_scratch() + ag_scratch() * 6 + [sem(4)] * 4,
        jobs + late, 3, True, "middle", collective, 250,
    )
    return outs, moved


def row_routes():
    nsh, nhh = lax.axis_size("sh"), lax.axis_size("hh")
    groups = nsh * nhh
    routes = []
    for d in range(8 * groups):
        place, group = d // groups, d % groups
        s, c = place // 2, place % 2
        sh, hh = group // nhh, group % nhh
        routes.append((d, ((sh * 4 + s) * nhh + hh) * 2 + c))
    return routes


def spread_ff(member):
    rows = member.shape[0]
    width = -(-member.shape[1] // (NTP * 128)) * 128
    padded = jnp.pad(member, ((0, 0), (0, NTP * width - member.shape[1])))
    return padded.reshape(rows, NTP, width)


def on_device(
    layer_input, lengths, gain_a1, lin_q, lin_k, lin_v, lin_out, gain_a2, mlp_a_gate, mlp_a_up,
    mlp_a_down, gain_b1, win_q, win_k, win_v, win_out, gain_b2, mlp_b_gate, mlp_b_up, mlp_b_down,
    cotangent,
):
    count = lax.axis_size(GROUP)
    rows = lin_q.shape[0]
    hidden_size = mlp_a_gate.shape[1]
    gains = jnp.pad(jnp.stack([gain_a1, gain_a2, gain_b1, gain_b2], axis=1), ((0, 0), (0, 60)))
    gains = jnp.broadcast_to(gains[:, None, :], (rows, NTP, 64))
    starts = jnp.cumsum(lengths) - lengths
    tables = taylor_tables()

    split = lambda member: member.reshape(rows, NTP, -1)
    bundle_lin = jnp.concatenate(
        [split(lin_q), split(lin_k), gains, split(lin_v)], axis=-1
    ).transpose(1, 0, 2)
    bundle_a = jnp.concatenate(
        [spread_ff(mlp_a_gate), spread_ff(mlp_a_up), spread_ff(mlp_a_down.T)], axis=-1
    ).transpose(1, 0, 2)
    bundle_win = jnp.concatenate([split(win_q), split(win_k), split(win_v)], axis=-1).transpose(
        1, 0, 2
    )
    bundle_b = jnp.concatenate(
        [spread_ff(mlp_b_gate), spread_ff(mlp_b_up), spread_ff(mlp_b_down.T)], axis=-1
    ).transpose(1, 0, 2)
    ff = bundle_a.shape[-1] // 3
    width = bundle_lin.shape[-1]
    nsh, nhh = lax.axis_size("sh"), lax.axis_size("hh")
    places = lambda a: a.reshape(4, 2, rows, a.shape[-1])
    whole = lambda a: a.reshape(D, a.shape[-1])
    total = lambda a: jnp.sum(a.astype(F32), axis=0).astype(BF16)
    ship = shipping()
    if ship:
        own_rows = lambda a, **kw: Job("zw", a, **kw)
    else:
        own_rows = lambda a, **kw: Job("zr", lax.ppermute(a, AXES, row_routes()), **kw)

    x_own = layer_input.reshape(2, 64, D)
    cot_own = cotangent.reshape(2, 64, D)
    third = lambda a, i: Job("pa", places(a[:, :, i * ff : i * ff + ff]))
    (x_full, n_a1, qkv_a, w_lin, gains), (_, _, mid_gate_a, mid_up_a, mid_down_a) = first(
        x_own, places(bundle_lin), [third(bundle_a, 0), third(bundle_a, 1), third(bundle_a, 2)], 1
    )
    (o_a, *kept, cot), (w_gate_a, w_lin_out, mid_win, mid_gate_b, mid_up_b, mid_down_b) = taylor_forward(
        qkv_a, starts, tables, cot_own,
        [
            Job("zg", mid_gate_a), own_rows(lin_out), Job("pa", places(bundle_win)),
            third(bundle_b, 0), third(bundle_b, 1), third(bundle_b, 2),
        ],
        count, 2,
    )
    column = lambda name, a: Job("zg", a, VMEM, name, True)
    (mixed, grad_h_a, gg, do_a, grad_lin_out, grad_win_out, up_a, *apart_terms), moved = middle(
        o_a, w_lin_out.reshape(128, D), x_own, gains, whole(w_gate_a), cot, cot_own, starts,
        [
            column("up_a", mid_up_a), column("down_a", mid_down_a), column("win", mid_win),
            column("gate_b", mid_gate_b), column("up_b", mid_up_b), column("down_b", mid_down_b),
            own_rows(win_out, spec=VMEM, name="win_out", held=True),
        ],
        3,
    )
    if ship:
        gate_a, down_b, gate_b, up_b, win, down_a, win_out_t = moved
        late = [Job("pa", gate_a), Job("zs", up_a)]
    else:
        sums = apart(apart_terms, 10)
        _, moved = step(
            lambda begin: None, [], [], [], [Job("pa", a) for a in sums[:5]]
            + [Job("zt", grad_win_out.reshape(count, -1, D))], 7, True, "spread", 11, 20,
        )
        down_b, gate_b, up_b, win, down_a, win_out_t = moved
        late = [Job("pa", sums[5])]
        (up_a,) = apart([up_a], 14)
    (dqkv_a,), (gate_a, *more) = taylor_backward(qkv_a, do_a, kept, starts, tables, late, count, 8)
    (up_a,) = more if ship else (up_a,)
    rows_back = Job("zv", grad_lin_out.reshape(4, rows, D)) if ship else Job(
        "zt", grad_lin_out.reshape(count, -1, D)
    )
    grad_input, (lin_out_t, up_a), lin_g = last_layer(
        dqkv_a, w_lin, x_own, gains[0:1], grad_h_a, x_full, n_a1, gg[0:3], [rows_back, Job("pa", up_a)], 9,
    )

    def joined(a, lo, hi):
        a = a.reshape(NTP, rows, -1)[:, :, lo:hi].astype(F32)
        return a.transpose(1, 0, 2).reshape(rows, -1)

    def unpack_mlp(gate, up, down):
        joined_ff = lambda a: joined(a, 0, ff)[:, :hidden_size]
        return joined_ff(gate), joined_ff(up), joined_ff(down).T

    gate_b_g, up_b_g, down_b_g = unpack_mlp(gate_b, up_b, down_b)
    gate_a_g, up_a_g, down_a_g = unpack_mlp(gate_a, up_a, down_a)
    def own_terms(a):
        if ship:
            return jnp.sum(a.astype(F32), axis=0)
        return lax.ppermute(total(a), AXES, [(d, e) for e, d in row_routes()]).astype(F32)

    win_out_g, lin_out_g = own_terms(win_out_t), own_terms(lin_out_t)
    gg = jnp.sum(lin_g.reshape(NTP, rows, width)[:, :, 64:68].astype(F32), axis=0)
    return (
        mixed.reshape(128, D),
        grad_input.reshape(128, D),
        gg[:, 0],
        joined(lin_g, 0, 32),
        joined(lin_g, 32, 64),
        joined(lin_g, 128, 256),
        lin_out_g,
        gg[:, 1],
        gate_a_g,
        up_a_g,
        down_a_g,
        gg[:, 2],
        joined(win, 0, 128),
        joined(win, 128, 256),
        joined(win, 256, 384),
        win_out_g,
        gg[:, 3],
        gate_b_g,
        up_b_g,
        down_b_g,
    )


def solution(mesh):
    seq, head = mesh.devices.shape
    fine = Mesh(mesh.devices.reshape(seq // 4, 2, 2, head // 2, 2), AXES)
    row, vec, col = P(AXES, None), P(AXES), P(None, AXES)
    placed = (
        row, P(), vec, row, row, row, row, vec, row, row, col,
        vec, row, row, row, row, vec, row, row, col, row,
    )
    out = (
        row, row, vec, row, row, row, row, vec, row, row, col,
        vec, row, row, row, row, vec, row, row, col,
    )
    return jax.shard_map(on_device, mesh=fine, in_specs=placed, out_specs=out, check_vma=False)
```

```python
import functools

import jax
import jax.numpy as jnp
import numpy as np
from jax import lax
from jax.experimental import pallas as pl
from jax.experimental.pallas import tpu as pltpu
from jax.sharding import Mesh
from jax.sharding import PartitionSpec as P

D = 1024
HEADS = 16
FEAT = 16
WINDOW = 64
NTP = 8
RIM = 64
SROWS = 160
EPSILON = 1e-05
AXES = ("sh", "sy", "sx", "hh", "hl")
TP = ("sy", "sx", "hl")
GROUP = ("sh", "hh")
MESH_ID = pl.DeviceIdType.MESH
F32 = jnp.float32
BF16 = jnp.bfloat16
VM = pltpu.VMEM
LIMIT = 60 * 1024 * 1024


def vmem_specs(count):
    return [pl.BlockSpec(memory_space=pltpu.VMEM)] * count


def matmul(left, right):
    return jnp.dot(left, right, preferred_element_type=F32)


def matmul_tn(left, right):
    return lax.dot_general(left, right, (((0,), (0,)), ((), ())), preferred_element_type=F32)


def matmul_nt(left, right):
    return lax.dot_general(left, right, (((1,), (1,)), ((), ())), preferred_element_type=F32)


def plane_place():
    sy, sx, c = lax.axis_index("sy"), lax.axis_index("sx"), lax.axis_index("hl")
    me = sy * 2 + sx
    xn = sy * 2 + (1 - sx)
    yn = (1 - sy) * 2 + sx
    dg = 3 - me
    return me, xn, yn, dg, c, {"sx": 1 - sx}, {"sy": 1 - sy}, {"hl": 1 - c}


def remote(src, dst, ssem, rsem, target):
    copy = pltpu.make_async_remote_copy(
        src_ref=src, dst_ref=dst, send_sem=ssem, recv_sem=rsem, device_id=target, device_id_type=MESH_ID
    )
    copy.start()
    return copy


AG_COPIES = 13
RS_COPIES = 10


class RowGather:
    def __init__(self, full, ssem, rsem):
        self.full, self.ssem, self.rsem = full, ssem, rsem
        self.place = plane_place()
        self.cps = {}

    def send(self, k, block, half, target):
        view = self.full.at[block, self.place[4], half]
        self.cps[k] = remote(view, view, self.ssem.at[k], self.rsem.at[k], target)

    def start(self):
        me, _, _, _, c, to_x, to_y, to_c = self.place
        self.send(1, me, 0, to_x)
        self.send(3, me, 1, to_y)
        self.send(2, me, 1, to_x)
        self.send(4, me, 0, to_y)
        own = self.full.at[me, c]
        self.cps[0] = remote(own, own, self.ssem.at[0], self.rsem.at[0], to_c)

    def arrived(self, *keys):
        for k in keys:
            self.cps[k].wait_recv()

    def hop1(self):
        _, xn, yn, _, _, to_x, to_y, to_c = self.place
        self.arrived(1)
        self.send(5, xn, 0, to_y)
        self.send(6, xn, 0, to_c)
        self.arrived(3)
        self.send(7, yn, 1, to_x)
        self.send(8, yn, 1, to_c)

    def hop2(self):
        _, xn, yn, _, _, _, _, to_c = self.place
        self.arrived(2)
        self.send(9, xn, 1, to_c)
        self.arrived(4)
        self.send(10, yn, 0, to_c)

    def hop3(self):
        _, _, _, dg, _, _, _, to_c = self.place
        self.arrived(5)
        self.send(11, dg, 0, to_c)
        self.arrived(7)
        self.send(12, dg, 1, to_c)

    def finish(self):
        for k in range(AG_COPIES):
            self.cps[k].wait_send()

    def run(self, consume, spare=()):
        me, xn, yn, dg = self.place[:4]
        spare = list(spare)

        def fill(most):
            for _ in range(min(most, len(spare))):
                spare.pop(0)()

        self.start()
        self.arrived(0)
        consume(me)
        fill(3)
        self.hop1()
        fill(2)
        self.hop2()
        self.arrived(6, 9)
        consume(xn)
        fill(2)
        self.hop3()
        self.arrived(8, 10)
        consume(yn)
        self.arrived(11, 12)
        consume(dg)
        fill(len(spare))
        self.finish()


class RowSum:
    def __init__(self, part, own, cb, sb, keep, r1, r2, ssem, rsem):
        self.part, self.own, self.cb, self.sb, self.keep = part, own, cb, sb, keep
        self.r1, self.r2, self.ssem, self.rsem = r1, r2, ssem, rsem
        self.place = plane_place()
        self.cps = {}

    def block(self, k):
        me, xn, yn, dg = self.place[:4]
        return (dg, xn, yn, me)[k]

    def copy(self, k, src, dst, target):
        self.cps[k] = remote(src, dst, self.ssem.at[k], self.rsem.at[k], target)

    def core(self, k):
        src = self.part.at[self.block(k), 1 - self.place[4]]
        self.copy(k, src, self.cb.at[k], self.place[7])

    def both(self, k, half):
        mine = self.part[self.block(k), self.place[4], half]
        return mine.astype(F32) + self.cb[k, half].astype(F32)

    def push(self, k):
        to_x, to_y = self.place[5:7]
        sb, r1 = self.sb, self.r1
        self.cps[k].wait_recv()
        if k == 0:
            sb[0, 0] = self.both(0, 0).astype(BF16)
            self.copy(4, sb.at[0, 0], r1.at[0, 0], to_x)
            sb[0, 1] = self.both(0, 1).astype(BF16)
            self.copy(5, sb.at[0, 1], r1.at[1, 0], to_y)
        if k == 1:
            sb[1, 0] = self.both(1, 0).astype(BF16)
            self.copy(6, sb.at[1, 0], r1.at[0, 1], to_x)
            self.keep[1] = self.both(1, 1)
        if k == 2:
            sb[2, 1] = self.both(2, 1).astype(BF16)
            self.copy(7, sb.at[2, 1], r1.at[1, 1], to_y)
            self.keep[0] = self.both(2, 0)
        if k == 3:
            self.own[0] = self.both(3, 0)
            self.own[1] = self.both(3, 1)

    def relay(self):
        to_x, to_y = self.place[5:7]
        self.cps[4].wait_recv()
        self.sb[2, 0] = (self.keep[0] + self.r1[0, 0].astype(F32)).astype(BF16)
        self.copy(8, self.sb.at[2, 0], self.r2.at[0], to_y)
        self.cps[5].wait_recv()
        self.sb[1, 1] = (self.keep[1] + self.r1[1, 0].astype(F32)).astype(BF16)
        self.copy(9, self.sb.at[1, 1], self.r2.at[1], to_x)
        self.cps[6].wait_recv()
        self.own[0] += self.r1[0, 1].astype(F32)
        self.cps[7].wait_recv()
        self.own[1] += self.r1[1, 1].astype(F32)

    def finish(self):
        self.cps[8].wait_recv()
        self.own[0] += self.r2[0].astype(F32)
        self.cps[9].wait_recv()
        self.own[1] += self.r2[1].astype(F32)
        for k in range(RS_COPIES):
            self.cps[k].wait_send()

    def run(self, produce, spare=()):
        spare = list(spare)
        for k in range(4):
            produce(self.block(k))
            self.core(k)
        for k in range(4):
            self.push(k)
        for job in spare[: len(spare) // 2]:
            job()
        self.relay()
        for job in spare[len(spare) // 2 :]:
            job()
        self.finish()


def rs_scratch():
    return [
        VM((2, 64, D), F32),
        VM((4, 2, 64, D), BF16),
        VM((3, 2, 64, D), BF16),
        VM((2, 64, D), F32),
        VM((2, 2, 64, D), BF16),
        VM((2, 64, D), BF16),
        pltpu.SemaphoreType.DMA((RS_COPIES,)),
        pltpu.SemaphoreType.DMA((RS_COPIES,)),
    ]


def ag_scratch():
    return [pltpu.SemaphoreType.DMA((AG_COPIES,)), pltpu.SemaphoreType.DMA((AG_COPIES,))]


def cost(micros):
    return pl.CostEstimate(flops=0, bytes_accessed=int(micros * 3.0e6), transcendentals=0)


def group_place():
    return lax.axis_index("sh") * lax.axis_size("hh") + lax.axis_index("hh")


def group_peer(k, count):
    nhh = lax.axis_size("hh")
    other = lax.rem(group_place() + k, count)
    sh, hh = other // nhh, lax.rem(other, nhh)
    return other, sh, hh, {"sh": sh, "hh": hh}


def place_peer(k):
    coords = {}
    for bit, axis in enumerate(("hl", "sx", "sy")):
        here = lax.axis_index(axis)
        coords[axis] = 1 - here if (k >> bit) & 1 else here
    target = {axis: v for bit, (axis, v) in enumerate(coords.items()) if (k >> bit) & 1}
    return coords["sy"] * 2 + coords["sx"], coords["hl"], target


def barrier_of(plane, group, count, column):
    barrier = pltpu.get_barrier_semaphore()
    seen = 0
    if column:
        hh, c = lax.axis_index("hh"), lax.axis_index("hl")
        for k in range(1, 8):
            target = {"hh": lax.rem(hh + k // 2, 4), "hl": 1 - c if k % 2 else c}
            if k == 1 and plane:
                continue
            pl.semaphore_signal(barrier, inc=1, device_id=target, device_id_type=MESH_ID)
            seen += 1
        group = False
    for k in ((1, 2, 4) if plane == 3 else range(1, 8)) if plane else ():
        _, _, target = place_peer(k)
        pl.semaphore_signal(barrier, inc=1, device_id=target, device_id_type=MESH_ID)
        seen += 1
    if group:
        for k in range(1, count):
            target = group_peer(k, count)[3]
            pl.semaphore_signal(barrier, inc=1, device_id=target, device_id_type=MESH_ID)
            seen += 1
    pl.semaphore_wait(barrier, seen)


def chained():
    return lax.axis_size("sh") == 1 and lax.axis_size("hh") == 4


class Job:
    def __init__(self, kind, src, spec=None, name=None, held=False, pool=None):
        self.kind, self.src, self.inside = kind, src, isinstance(src, jax.ShapeDtypeStruct)
        self.spec = spec or (VMEM if kind == "zs" else ANY)
        self.src_spec = VMEM if kind == "zs" else ANY
        self.name, self.held, self.pool = name, held, pool

    def out_shape(self):
        nsh, nhh = lax.axis_size("sh"), lax.axis_size("hh")
        shape = list(self.src.shape)
        if self.kind == "zg":
            shape = [nsh * 4, nhh] + shape[1:]
        if self.kind == "zr":
            shape = [nsh * nhh] + shape
        if self.kind == "zo":
            shape = [nsh * nhh, 4] + shape[2:]
        if self.kind == "zs":
            shape = [4] + shape[2:]
        if self.kind == "zw":
            shape = [4] + shape
        return jax.ShapeDtypeStruct(tuple(shape), BF16)


class Transfers:
    def __init__(self, kinds, sources, results, buffers, sems, count, chain):
        self.kinds, self.sources, self.results = kinds, sources, results
        self.buffers, self.sems, self.count, self.chain = buffers, sems, count, chain
        self.state = {}

    def copy(self, i, src, dst, send, recv, target):
        return pltpu.make_async_remote_copy(
            src_ref=src, dst_ref=dst, send_sem=self.sems[0].at[i, send],
            recv_sem=self.sems[1].at[i, recv], device_id=target, device_id_type=MESH_ID,
        )

    early = ()

    def __call__(self):
        for i, src in enumerate(self.sources):
            if src is not None and i not in self.state:
                self.start(i)

    late = __call__

    def slot(self, i, group):
        out, nhh = self.results[i], lax.axis_size("hh")
        if self.kinds[i] == "zg":
            return out.at[pl.ds(group // nhh * 4, 4), lax.rem(group, nhh)]
        return out.at[group]

    def got(self, i, ref, index):
        pltpu.make_async_copy(ref, ref, self.sems[1].at[i, index]).wait()

    def sent(self, i, ref, index):
        pltpu.make_async_copy(ref, ref, self.sems[0].at[i, index]).wait()

    names = {}

    def has(self, i):
        return i in self.names

    def start(self, i, src=None):
        i = self.names.get(i, i)
        if src is not None:
            self.sources[i] = src
        self.state[i] = "sent"
        kind, src, out, count = self.kinds[i], self.sources[i], self.results[i], self.count
        hh, g = lax.axis_index("hh"), group_place()
        local = None
        if kind == "pa":
            s, c, _ = place_peer(0)
            for k in range(1, 8):
                ps, pc, target = place_peer(k)
                self.copy(i, src.at[ps, pc], out.at[s, c], k, k, target).start()
            local = (src.at[s, c], out.at[s, c])
        if kind in ("zg", "zr"):
            for k in (1, 3, 2) if self.chain else range(1, count):
                go = self.copy(i, src, self.slot(i, g), k, g, group_peer(k, count)[3]).start
                if self.chain and k != 2:
                    pl.when(hh != (3 if k == 1 else 0))(go)
                else:
                    go()
            local = (src, self.slot(i, g))
        if kind in ("zo", "zt"):
            nhh = lax.axis_size("hh")
            part = lambda p: (
                src.at[p] if kind == "zt" else src.at[pl.ds(p // nhh * 4, 4), lax.rem(p, nhh)]
            )
            for k in range(1, count):
                other, _, _, target = group_peer(k, count)
                self.copy(i, part(other), out.at[g], k, g, target).start()
            local = (part(g), out.at[g])
        if kind == "zs":
            buf = self.buffers[i]
            last, begin = hh == 3, hh == 0
            up = self.copy(
                i, src.at[:, jnp.where(last, 0, hh + 1)], buf.at[jnp.where(last, 4, g)],
                1, jnp.where(last, 4, g), {"hh": jnp.where(last, 2, hh + 1)},
            ).start
            down = self.copy(
                i, src.at[:, jnp.where(begin, 3, hh - 1)], buf.at[jnp.where(begin, 4, g)],
                3, jnp.where(begin, 4, g), {"hh": jnp.where(begin, 1, hh - 1)},
            ).start

            @pl.when(last)
            def _():
                up()
                down()

            @pl.when(jnp.logical_not(last))
            def _():
                down()
                up()

            far = lax.rem(hh + 2, 4)
            pl.when(last | begin)(self.copy(i, src.at[:, far], buf.at[g], 2, g, {"hh": far}).start)
        if kind in ("zw", "zv"):
            for k in range(4):
                mine, target, src_k, at, _ = self.column(kind, k)
                view = src if kind == "zw" else src.at[src_k]
                here = pltpu.make_async_copy(view, out.at[at], self.sems[2].at[i]).start
                pl.when(mine)(here)
                pl.when(jnp.logical_not(mine))(self.copy(i, view, out.at[at], k, at, target).start)
        if local is not None:
            pltpu.make_async_copy(local[0], local[1], self.sems[2].at[i]).start()
            self.local = getattr(self, "local", {})
            self.local[i] = local

    def column(self, kind, k):
        hh, c = lax.axis_index("hh"), lax.axis_index("hl")
        if kind == "zw":
            z, to_c, slot = lax.rem(hh + k, 4), hh // 2, lax.rem(hh, 2) * 2 + c
            own = (2 * c + k // 2 == hh) & (k % 2 == c)
            return (z == hh) & (to_c == c), {"hh": z, "hl": to_c}, 0, slot, own
        j = lax.rem(lax.rem(hh, 2) * 2 + c + k, 4)
        z, to_c = 2 * c + j // 2, lax.rem(j, 2)
        own = (k == hh) & (hh // 2 == c)
        return (z == hh) & (to_c == c), {"hh": z, "hl": to_c}, j, hh, own

    def relay(self, *which):
        for i in which:
            i = self.names.get(i, i)
            if i not in self.state:
                continue
            kind = self.kinds[i]
            if not self.chain or kind not in ("zg", "zr", "zs") or self.state[i] != "sent":
                continue
            self.state[i] = "relayed"
            hh, g = lax.axis_index("hh"), group_place()
            inner = (hh == 1) | (hh == 2)
            far = lax.rem(hh + 2, 4)

            @pl.when(inner)
            def _(i=i, kind=kind):
                if kind == "zs":
                    buf, src = self.buffers[i], self.sources[i]
                    self.got(i, buf.at[4], 4)
                    buf[4] = (buf[4].astype(F32) + src[:, far].astype(F32)).astype(BF16)
                    self.copy(i, buf.at[4], buf.at[g], 2, g, {"hh": far}).start()
                else:
                    slot = self.slot(i, far)
                    self.got(i, slot, far)
                    self.copy(i, slot, slot, 0, far, {"hh": 3 - far}).start()

    def wait(self, *which):
        self.relay(*which)
        for i in which:
            i = self.names.get(i, i)
            if self.state[i] == "done":
                continue
            self.state[i] = "done"
            kind, src, out, count = self.kinds[i], self.sources[i], self.results[i], self.count
            hh, g = lax.axis_index("hh"), group_place()
            inner = (hh == 1) | (hh == 2)
            if kind == "pa":
                s, c, _ = place_peer(0)
                for k in range(1, 8):
                    self.copy(i, src.at[s, c], out.at[s, c], k, k, place_peer(k)[2]).wait()
            if kind in ("zg", "zr"):
                for k in range(1, count):
                    other = lax.rem(g + k, count)
                    slot = self.slot(i, other)

                    def arrive(slot=slot, other=other):
                        self.got(i, slot, other)

                    def leave(k=k):
                        self.sent(i, src, k)

                    if not self.chain:
                        arrive()
                        leave()
                    elif k == 2:
                        pl.when(jnp.logical_not(inner))(arrive)
                        leave()
                        pl.when(inner)(functools.partial(leave, 0))
                    else:
                        arrive()
                        pl.when(hh != (3 if k == 1 else 0))(leave)
            if kind in ("zo", "zt"):
                for k in range(1, count):
                    other = lax.rem(g + k, count)
                    self.got(i, out.at[other], other)
                    self.sent(i, out.at[other], k)
            if kind in ("zw", "zv"):
                for k in range(4):
                    mine, _, _, at, own = self.column(kind, k)
                    slot = out.at[k]
                    here = pltpu.make_async_copy(slot, slot, self.sems[2].at[i]).wait
                    pl.when(own)(here)
                    pl.when(jnp.logical_not(own))(functools.partial(self.got, i, slot, k))
                    pl.when(jnp.logical_not(mine))(functools.partial(self.sent, i, slot, k))
            if kind == "zs":
                buf = self.buffers[i]
                one = jnp.where(hh == 0, 2, hh - 1)
                two = jnp.where(hh == 3, 1, hh + 1)
                far = lax.rem(hh + 2, 4)
                self.got(i, buf.at[one], one)
                self.got(i, buf.at[two], two)
                total = lambda: (
                    src[:, g].astype(F32) + buf[one].astype(F32) + buf[two].astype(F32)
                )

                @pl.when(inner)
                def _():
                    self.got(i, buf.at[far], far)
                    out[...] = (total() + buf[far].astype(F32)).astype(BF16)

                @pl.when(jnp.logical_not(inner))
                def _():
                    out[...] = total().astype(BF16)

                for k in (1, 2, 3):
                    self.sent(i, buf.at[g], k)
            if i in getattr(self, "local", {}):
                a, b = self.local[i]
                pltpu.make_async_copy(a, b, self.sems[2].at[i]).wait()

    def rest(self):
        which = [i for i in self.state if self.state[i] != "done"]
        self.relay(*which)
        self.wait(*which)

    def result(self, i):
        return self.results[self.names.get(i, i)]

    def columns(self, i):
        ref = self.result(i)
        return ref[...].reshape(D, ref.shape[-1])


ANY = pl.BlockSpec(memory_space=pl.ANY)
VMEM = pl.BlockSpec(memory_space=pltpu.VMEM)
SMEM = pl.BlockSpec(memory_space=pltpu.SMEM)


def step(body, ins, outs, scratch, jobs, plane, group, name, collective, micros, early=()):
    count = lax.axis_size(GROUP)
    kinds = [job.kind for job in jobs]
    given = [job for job in jobs if not job.inside]
    shown = [job for job in jobs if not job.held]
    n_in, n_out, n_job, n_src = len(ins), len(outs), len(jobs), len(given)
    plane = 7 if "pa" in kinds else plane
    group = group or any(kind != "pa" for kind in kinds)
    column = any(kind in ("zw", "zv") for kind in kinds)
    slots = max(count, 8)
    held = [VM(job.out_shape().shape, BF16) for job in jobs if job.held]
    pools = {}
    for i, job in enumerate(jobs):
        if job.kind == "zs":
            key = (job.pool if job.pool is not None else -1 - i, job.out_shape().shape)
            pools.setdefault(key, []).append(i)

    def kernel(*refs):
        in_refs, refs = refs[:n_in], refs[n_in:]
        given_refs, refs = list(refs[:n_src]), refs[n_src:]
        out_refs, refs = refs[:n_out], refs[n_out:]
        shown_refs, refs = list(refs[: len(shown)]), refs[len(shown) :]
        extra_refs, own = list(refs[len(scratch) :]), refs[: len(scratch)]
        held_refs, pool_refs = extra_refs[3 : 3 + len(held)], extra_refs[3 + len(held) :]
        sources = [None if job.inside else given_refs.pop(0) for job in jobs]
        results = [held_refs.pop(0) if job.held else shown_refs.pop(0) for job in jobs]
        buffers = {i: ref for key, ref in zip(pools, pool_refs) for i in pools[key]}
        barrier_of(plane, group, count, column)
        begin = Transfers(kinds, sources, results, buffers, extra_refs[:3], count, chained())
        begin.early = early
        begin.names = {job.name: i for i, job in enumerate(jobs) if job.name}
        body(begin, *in_refs, *out_refs, *own)
        if not begin.state:
            begin()
        begin.rest()

    extra = (
        [
            pltpu.SemaphoreType.DMA((n_job, slots)),
            pltpu.SemaphoreType.DMA((n_job, slots)),
            pltpu.SemaphoreType.DMA((n_job,)),
        ]
        + held
        + [VM((5,) + key[1], BF16) for key in pools]
    )
    result = pl.pallas_call(
        kernel,
        out_shape=tuple(o for o, _ in outs) + tuple(job.out_shape() for job in shown),
        in_specs=[spec for _, spec in ins] + [job.src_spec for job in given],
        out_specs=tuple(spec for _, spec in outs) + tuple(job.spec for job in shown),
        scratch_shapes=list(scratch) + (extra if n_job else []),
        compiler_params=pltpu.CompilerParams(
            collective_id=collective, has_side_effects=True, vmem_limit_bytes=LIMIT
        ),
        cost_estimate=cost(micros),
        name=name,
    )(*[v for v, _ in ins], *[job.src for job in given])
    return result[:n_out], result[n_out:]


FULL = jax.ShapeDtypeStruct((4, 2, 2, 64, D), BF16)
OWN = jax.ShapeDtypeStruct((2, 64, D), F32)


def flat(full):
    return full.reshape(1024, D)


def blocks(rows):
    return rows.reshape(4, 2, 2, 64, D)


def vmem(*values):
    return [(v, VMEM) for v in values]


def normed_half(u, gain):
    inv = lax.rsqrt(jnp.mean(u * u, axis=-1, keepdims=True) + EPSILON)
    return (u * inv * gain).astype(BF16)


def chip_rows(ref, block):
    return ref[block].reshape(256, D)


def put_chip(ref, block, value):
    ref[block] = value.astype(BF16).reshape(2, 2, 64, D)


def rows_of(block):
    return pl.ds(block * 256, 256)


def silu_parts(gate):
    sig = 1.0 / (1.0 + jnp.exp(-gate))
    return sig, gate * sig


def follow(total, seen):
    k = (3, 1, 2, 0)[len(seen)]
    seen.append(k)
    total.core(k)
    if k == 2:
        total.push(1)
    if k == 0:
        total.push(2)
        total.push(3)
        total.push(0)


def norm_back_half(dn, u, gain, upstream):
    inv = lax.rsqrt(jnp.mean(u * u, axis=-1, keepdims=True) + EPSILON)
    gained = dn * gain
    inner = jnp.mean(gained * u, axis=-1, keepdims=True)
    scaled = u * inv
    grad = upstream + inv * gained - scaled * (inv * inv * inner)
    return grad, jnp.sum(dn * scaled, axis=0, keepdims=True)


def back_own(dn, u_ref, gain_ref, up_ref, gnew, ggain, full):
    me, c = plane_place()[0], plane_place()[4]
    total = None
    for half in range(2):
        grad, gain_part = norm_back_half(
            dn[half], u_ref[half].astype(F32), gain_ref[...], up_ref[half].astype(F32)
        )
        gnew[half] = grad
        total = gain_part if total is None else total + gain_part
        if full is not None:
            full[me, c, half] = grad.astype(BF16)
    ggain[...] = total


def weight_grads(left, right, out):
    def piece(i):
        width = D // 4
        lo = i * width
        lhs = left[:, :, :, :, lo : lo + width].reshape(1024, width)
        value = matmul_tn(lhs, right[...]).astype(BF16)
        if len(out.shape) == 5:
            out[i] = value.reshape(out.shape[1:])
        else:
            out[lo : lo + width, :] = value

    return [functools.partial(piece, i) for i in range(4)]


def shipping():
    return chained() and D % (8 * 4 * 16) == 0


def terms_shape(cols):
    nsh, nhh = lax.axis_size("sh"), lax.axis_size("hh")
    if shipping():
        return jax.ShapeDtypeStruct((4, 4, 2, D // 32, cols), BF16)
    return jax.ShapeDtypeStruct((D, cols), BF16)


def apart(arrays, collective):
    nsh, nhh = lax.axis_size("sh"), lax.axis_size("hh")
    rows = D // (8 * nsh * nhh)
    jobs = [Job("zo", a.reshape(nsh * 4, nhh, 2, rows, a.shape[-1])) for a in arrays]
    _, moved = step(lambda begin: None, [], [], [], jobs, 0, True, "apart", collective, 20)
    return [jnp.sum(a.astype(F32), axis=0).astype(BF16) for a in moved]


def last_layer(dproj, w_proj, u, gain, upstream, x_full, n_first, gains, jobs, collective):
    width = w_proj.shape[1]
    ship = shipping()

    def body(
        begin, dp_ref, wp_ref, u_ref, gain_ref, up_ref, xf_ref, nf_ref, gains_ref,
        gnew, ggain, proj_w, part1, mine, *rest
    ):
        sum1 = RowSum(part1, *rest)
        begin()
        mine[...] = jnp.zeros((128, D), F32)
        mine[65:68, :] = gains_ref[...]

        def projected(block):
            part = matmul_nt(dp_ref[rows_of(block), :], wp_ref[...])
            put_chip(part1, block, part)
            u = chip_rows(xf_ref, block).astype(F32)
            u = u * lax.rsqrt(jnp.mean(u * u, axis=-1, keepdims=True) + EPSILON)
            mine[64:65, :] += jnp.sum(part * u, axis=0, keepdims=True)

        def grads():
            turned = mine[...].T
            for i in range(4):
                at = slice(i * 256, i * 256 + 256)
                lhs = nf_ref[:, :, :, :, at].reshape(1024, 256)
                value = matmul_tn(lhs, dp_ref[...])
                keep = lanes(256, 128) < 64
                value = jnp.concatenate(
                    [jnp.where(keep, value[:, :128], turned[at]), value[:, 128:]], axis=1
                ).astype(BF16)
                if ship:
                    proj_w[i] = value.reshape(proj_w.shape[1:])
                else:
                    proj_w[at, :] = value
            if ship:
                begin.start(len(jobs), proj_w)

        for k in range(4):
            projected(sum1.block(k))
            sum1.core(k)
        for k in range(4):
            sum1.push(k)
        grads()
        sum1.relay()
        sum1.finish()
        back_own(sum1.own, u_ref, gain_ref, up_ref, gnew, ggain, None)
        if ship:
            begin.wait(len(jobs))
            begin.start(len(jobs) + 1, begin.results[len(jobs)])

    terms = terms_shape(width)
    summed = jax.ShapeDtypeStruct((4, 2, D // 32, width), BF16)
    n = len(jobs)
    outs, moved = step(
        body, vmem(dproj, w_proj, u, gain, upstream, x_full, n_first, gains),
        vmem(OWN, jax.ShapeDtypeStruct((1, D), F32)) + ([] if ship else vmem(terms)),
        ([VM(terms.shape, BF16)] if ship else []) + [VM(FULL.shape, BF16), VM((128, D), F32)] + rs_scratch(),
        jobs + ([Job("zs", terms), Job("pa", summed)] if ship else []),
        3, False, "last_layer", collective, 25,
    )
    if ship:
        return outs[0], moved[:n], moved[n + 1]
    (lin,) = apart([outs[2]], 12)
    _, (lin,) = step(
        lambda begin: None, [], [], [], [Job("pa", lin)], 7, False, "last", 13, 5
    )
    return outs[0], moved[:n], lin


def taylor_tables():
    pick = np.zeros((4, 2, 128, 256), np.float32)
    coef = np.zeros((8, 256), np.float32)
    pairs = [(i, j) for i in range(FEAT) for j in range(i, FEAT)]
    one = 4 * FEAT
    for x, (i, j) in enumerate(pairs):
        coef[:, x] = (2.0 * FEAT) ** -0.5 if i == j else FEAT**-0.5
        for t in range(4):
            pick[t, 0, t * FEAT + i, x] = 1.0
            pick[t, 1, t * FEAT + j, x] = 1.0
    for i in range(FEAT):
        x = len(pairs) + i
        coef[:, x] = FEAT**-0.25
        for t in range(4):
            pick[t, 0, t * FEAT + i, x] = 1.0
            pick[t, 1, one, x] = 1.0
    x = len(pairs) + FEAT
    coef[:, x] = 1.0
    pick[:, 0, one, x] = 1.0
    pick[:, 1, one, x] = 1.0
    shift = np.zeros((128, 128), np.float32)
    for i in range(2 * FEAT):
        shift[2 * FEAT + i, i] = 1.0
    return jnp.asarray(pick, BF16), jnp.asarray(coef, F32), jnp.asarray(shift, BF16)


def chunk_of(group, s):
    nhh = lax.axis_size("hh")
    return (group // nhh * 4 + s) * nhh + lax.rem(group, nhh)


def segment_of(starts, position):
    total = jnp.where(position >= starts[0], 0, -1)
    for i in range(1, starts.shape[0]):
        total = total + jnp.where(position >= starts[i], 1, 0)
    return total


class Segments:
    def __init__(self, starts, s):
        first = chunk_of(group_place(), s) * 256
        at = lambda shape, dim: first + lax.broadcasted_iota(jnp.int32, shape, dim)
        self.col = segment_of(starts, at((256, 1), 0))
        self.row = segment_of(starts, at((1, 256), 1))
        self.ext = segment_of(starts, at((1, 256 + RIM), 1) - RIM)
        self.last = segment_of(starts, first + 255)
        self.before = segment_of(starts, first - 1)


def carried(starts, s, st, sm, count, back):
    mine = chunk_of(group_place(), s)
    edge = segment_of(starts, mine * 256 + 255 if back else mine * 256 - 1)

    def group(i, both):
        def one(s2, both):
            state, total = both
            other = chunk_of(i, s2)
            reach = segment_of(starts, other * 256 - 1 if back else other * 256 + 255)
            ordered = other > mine if back else other < mine
            m = jnp.where(ordered & (reach == edge), 1.0, 0.0)
            return state + m * st[i, s2].astype(F32), total + m * sm[i, s2]

        return lax.fori_loop(s, 4, one, both) if back else lax.fori_loop(0, s + 1, one, both)

    return lax.fori_loop(
        0, count, group, (jnp.zeros((SROWS, 128), F32), jnp.zeros((8, 256), F32))
    )


def lanes(rows, width):
    return lax.broadcasted_iota(jnp.int32, (rows, width), 1)


class States:
    def __init__(self, count, st, sm, ssem, rsem):
        self.refs, self.ssem, self.rsem, self.count = (st, sm), ssem, rsem, count
        self.chain = count == 4 and chained()

    def copy(self, n, k, group, target):
        view = self.refs[n].at[group]
        return pltpu.make_async_remote_copy(
            src_ref=view, dst_ref=view, send_sem=self.ssem.at[n, k], recv_sem=self.rsem.at[n, group],
            device_id=target, device_id_type=MESH_ID,
        )

    def send(self):
        g, hh = group_place(), lax.axis_index("hh")
        for k in (2, 1, 3) if self.chain else range(1, self.count):
            for n in range(2):
                go = self.copy(n, k, g, group_peer(k, self.count)[3]).start
                if self.chain and k != 2:
                    pl.when(hh != (3 if k == 1 else 0))(go)
                else:
                    go()

    def got(self, n, group):
        view = self.refs[n].at[group]
        pltpu.make_async_copy(view, view, self.rsem.at[n, group]).wait()

    def sent(self, n, k):
        view = self.refs[n].at[0]
        pltpu.make_async_copy(view, view, self.ssem.at[n, k]).wait()

    def relay(self):
        if not self.chain:
            return
        hh = lax.axis_index("hh")
        far = lax.rem(hh + 2, 4)

        @pl.when((hh == 1) | (hh == 2))
        def _():
            for n in range(2):
                self.got(n, far)
                self.copy(n, 0, far, {"hh": 3 - far}).start()

    def arrive(self):
        g, hh = group_place(), lax.axis_index("hh")
        inner = (hh == 1) | (hh == 2)
        for k in range(1, self.count):
            other = lax.rem(g + k, self.count)
            for n in range(2):
                got = functools.partial(self.got, n, other)
                if self.chain and k == 2:
                    pl.when(jnp.logical_not(inner))(got)
                else:
                    got()

    def finish(self):
        hh = lax.axis_index("hh")
        for k in range(1, self.count):
            for n in range(2):
                sent = functools.partial(self.sent, n, k)
                if self.chain and k != 2:
                    pl.when(hh != (3 if k == 1 else 0))(sent)
                else:
                    sent()
                    if self.chain:
                        pl.when((hh == 1) | (hh == 2))(functools.partial(self.sent, n, 0))


def phi_of(x, pick, coef, t):
    left = matmul(x, pick[t, 0])
    right = matmul(x, pick[t, 1])
    return left, right, (left * right * coef).astype(BF16)


def taylor_forward_kernel(
    count, hooks, qkv, pick, coef_ref, shift, starts,
    o_ref, y_ref, den_ref, pre_ref, psum_ref, st, sm, phis, ssem, rsem,
):
    g = group_place()
    coef = coef_ref[0:1, :]
    left_half = lanes(256, 128) < 64

    def states(s, carry):
        rows = pl.ds(s * 256, 256)
        x = jnp.where(lanes(256, 128) == 4 * FEAT, jnp.ones((), BF16), qkv[rows, 0:128])
        v = qkv[rows, 128:256]
        seg = Segments(starts, s)
        tail = seg.col == seg.last
        v_tail = jnp.where(tail, v, jnp.zeros((), BF16))
        state = jnp.zeros((256, 128), F32)
        for h in range(2):
            _, _, phi_k = phi_of(x, pick, coef, 2 + h)
            side = left_half if h == 0 else jnp.logical_not(left_half)
            state += matmul_tn(phi_k, jnp.where(side, v_tail, jnp.zeros((), BF16)))
            total = jnp.sum(jnp.where(tail, phi_k.astype(F32), 0.0), axis=0, keepdims=True)
            sm[g, s, h : h + 1, :] = total
            _, _, phi_q = phi_of(x, pick, coef, h)
            phis[h][rows, 0:256] = phi_q
        st[g, s] = state[:SROWS].astype(BF16)
        return carry

    sm[g] = jnp.zeros((4, 8, 256), F32)
    lax.fori_loop(0, 4, states, 0)
    exchange = States(count, st, sm, ssem, rsem)
    exchange.send()
    hooks[0]()

    def inner(s, carry):
        rows = pl.ds(s * 256, 256)
        x = qkv[rows, 0:128]
        v = qkv[rows, 128:256]
        k = matmul(x, shift[...]).astype(BF16)
        lane = lanes(256, 128)
        order = lax.broadcasted_iota(jnp.int32, (256, 256), 0) >= lanes(256, 256)
        seg = Segments(starts, s)
        allowed = order & (seg.col == seg.row)
        num = jnp.zeros((256, 128), F32)
        dens = []
        for h in range(2):
            q = jnp.where(lane // FEAT == h, x, jnp.zeros((), BF16))
            dot = matmul_nt(q, k)
            score = jnp.where(allowed, 1.0 + dot * FEAT**-0.5 + dot * dot * (0.5 / FEAT), 0.0)
            side = left_half if h == 0 else jnp.logical_not(left_half)
            num += matmul(score.astype(BF16), jnp.where(side, v, jnp.zeros((), BF16)))
            dens.append(jnp.sum(score, axis=1, keepdims=True))
        y_ref[rows, :] = num
        den_ref[rows, :] = jnp.where(left_half, dens[0], dens[1])
        return carry

    lax.fori_loop(0, 4, inner, 0)
    exchange.relay()
    hooks[1]()
    exchange.arrive()

    def finish(s, carry):
        rows = pl.ds(s * 256, 256)

        state, total = carried(starts, s, st, sm, count, False)
        state = state.astype(BF16)
        pre_ref[s] = state
        psum_ref[s] = total
        seg = Segments(starts, s)
        cont = seg.col == seg.before
        num = jnp.zeros((256, 128), F32)
        dens = []
        for h in range(2):
            phi_q = phis[h][rows, 0:256]
            side = left_half if h == 0 else jnp.logical_not(left_half)
            part = matmul(phi_q[:, :SROWS], state)
            num = jnp.where(side, part, num)
            dens.append(jnp.sum(phi_q.astype(F32) * total[h : h + 1], axis=1, keepdims=True))
        num = jnp.where(cont, num, 0.0) + y_ref[rows, :]
        den = jnp.where(cont, jnp.where(left_half, dens[0], dens[1]), 0.0) + den_ref[rows, :]
        y = num / den
        y_ref[rows, :] = y
        den_ref[rows, :] = den
        o_ref[rows, :] = y.astype(BF16)
        return carry

    lax.fori_loop(0, 4, finish, 0)
    hooks[2]()
    exchange.finish()


def taylor_backward_kernel(
    count, begin, qkv, do_ref, y_ref, den_ref, pre_ref, psum_ref,
    pick, coef_ref, shift, starts,
    out_ref, st, sm, acc, dnum_ref, ddens, ssem, rsem,
):
    g = group_place()
    for i in begin.early:
        begin.start(i)
    coef = coef_ref[0:1, :]
    left_half = lanes(256, 128) < 64
    zero = jnp.zeros((), BF16)

    def sides(h):
        return left_half if h == 0 else jnp.logical_not(left_half)

    def feature_back(dphi, left, right, t):
        grad = dphi * coef
        return matmul_nt((grad * right).astype(BF16), pick[t, 0]) + matmul_nt(
            (grad * left).astype(BF16), pick[t, 1]
        )

    def states(s, carry):
        rows = pl.ds(s * 256, 256)
        x = jnp.where(lanes(256, 128) == 4 * FEAT, jnp.ones((), BF16), qkv[rows, 0:128])
        do = do_ref[rows, :].astype(F32)
        den = den_ref[rows, :]
        dnum = do / den
        dnum_low = dnum.astype(BF16)
        dnum_ref[rows, :] = dnum_low
        weighted = dnum * y_ref[rows, :]
        seg = Segments(starts, s)
        cont = seg.col == seg.before
        d_cont = jnp.where(cont, dnum_low, zero)
        pre = pre_ref[s]
        state = jnp.zeros((256, 128), F32)
        grad = jnp.zeros((256, 128), F32)
        for h in range(2):
            dden = -jnp.sum(jnp.where(sides(h), weighted, 0.0), axis=1, keepdims=True)
            ddens[h, rows, :] = jnp.broadcast_to(dden, (256, 128))
            left, right, phi_q = phi_of(x, pick, coef, h)
            d_side = jnp.where(sides(h), d_cont, zero)
            state += matmul_tn(phi_q, d_side)
            dden_cont = jnp.where(cont, dden, 0.0)
            sm[g, s, h : h + 1, :] = jnp.sum(
                phi_q.astype(F32) * dden_cont, axis=0, keepdims=True
            )
            dphi = jnp.concatenate(
                [matmul_nt(d_side, pre), jnp.zeros((256, 256 - SROWS), F32)], axis=1
            ) + dden_cont * psum_ref[s, h : h + 1, :]
            grad += feature_back(dphi, left, right, h)
        st[g, s] = state[:SROWS].astype(BF16)
        acc[0, rows, :] = grad
        return carry

    sm[g] = jnp.zeros((4, 8, 256), F32)
    lax.fori_loop(0, 4, states, 0)
    exchange = States(count, st, sm, ssem, rsem)
    exchange.send()
    begin.late()

    def inner(s, carry):
        rows = pl.ds(s * 256, 256)
        x = qkv[rows, 0:128]
        v = qkv[rows, 128:256]
        dnum = dnum_ref[rows, :]
        k_low = matmul(x, shift[...]).astype(BF16)
        lane = lanes(256, 128)
        order = lax.broadcasted_iota(jnp.int32, (256, 256), 0) >= lanes(256, 256)
        seg = Segments(starts, s)
        allowed = order & (seg.col == seg.row)
        dq = jnp.zeros((256, 128), F32)
        dk = jnp.zeros((256, 128), F32)
        dv = jnp.zeros((256, 128), F32)
        for h in range(2):
            mine = lane // FEAT == h
            q = jnp.where(mine, x, zero)
            dot = matmul_nt(q, k_low)
            score = jnp.where(allowed, 1.0 + dot * FEAT**-0.5 + dot * dot * (0.5 / FEAT), 0.0)
            d_side = jnp.where(sides(h), dnum, zero)
            dscore = matmul_nt(d_side, v) + ddens[h, rows, 0:1]
            e = jnp.where(allowed, dscore * (FEAT**-0.5 + dot * (1.0 / FEAT)), 0.0).astype(BF16)
            dq += matmul(e, jnp.where(mine, k_low, zero))
            dk += matmul_tn(e, q)
            dv += matmul_tn(score.astype(BF16), d_side)
        acc[0, rows, :] += dq
        acc[1, rows, :] = dk
        acc[2, rows, :] = dv
        return carry

    lax.fori_loop(0, 4, inner, 0)
    exchange.relay()
    begin.relay(*begin.early)
    exchange.arrive()

    def finish(s, carry):
        rows = pl.ds(s * 256, 256)

        state, total = carried(starts, s, st, sm, count, True)
        state = state.astype(BF16)
        x = jnp.where(lanes(256, 128) == 4 * FEAT, jnp.ones((), BF16), qkv[rows, 0:128])
        seg = Segments(starts, s)
        tail = seg.col == seg.last
        v_tail = jnp.where(tail, qkv[rows, 128:256], zero)
        grad = acc[0, rows, :]
        lane = lanes(256, 128)
        dv = jnp.zeros((256, 128), F32)
        for h in range(2):
            left, right, phi_k = phi_of(x, pick, coef, 2 + h)
            dphi = jnp.concatenate(
                [
                    matmul_nt(jnp.where(sides(h), v_tail, zero), state),
                    jnp.zeros((256, 256 - SROWS), F32),
                ],
                axis=1,
            ) + jnp.where(tail, total[h : h + 1], 0.0)
            grad += feature_back(dphi, left, right, 2 + h)
            dv = jnp.where(sides(h), matmul(phi_k[:, :SROWS], state), dv)
        grad += matmul_nt(acc[1, rows, :].astype(BF16), shift[...])
        dv = jnp.where(tail, dv, 0.0) + acc[2, rows, :]
        out_ref[rows, 0:128] = jnp.where(lane < 4 * FEAT, grad, 0.0).astype(BF16)
        out_ref[rows, 128:256] = dv.astype(BF16)
        return carry

    lax.fori_loop(0, 4, finish, 0)
    exchange.finish()


def taylor_backward(qkv, do, kept, starts, tables, jobs, count, collective):
    return step(
        functools.partial(taylor_backward_kernel, count),
        vmem(qkv, do, *kept, *tables) + [(starts, SMEM)],
        vmem(jax.ShapeDtypeStruct((1024, 256), BF16)),
        [
            VM((count, 4, SROWS, 128), BF16),
            VM((count, 4, 8, 256), F32),
            VM((3, 1024, 128), F32),
            VM((1024, 128), BF16),
            VM((2, 1024, 128), F32),
            pltpu.SemaphoreType.DMA((2, count)),
            pltpu.SemaphoreType.DMA((2, count)),
        ],
        jobs, 0, True, "taylor_backward", collective, 28, early=range(len(jobs)),
    )


def rim_target(s, forward):
    hh, sh = lax.axis_index("hh"), lax.axis_index("sh")
    nhh, nsh = lax.axis_size("hh"), lax.axis_size("sh")
    if forward:
        wraps = jnp.where(hh == nhh - 1, 1, 0)
        slot = lax.rem(s + wraps, 4)
        leaves = wraps if s == 3 else 0
        return {"sh": lax.rem(sh + leaves, nsh), "hh": lax.rem(hh + 1, nhh)}, slot
    wraps = jnp.where(hh == 0, 1, 0)
    slot = lax.rem(s + 4 - wraps, 4)
    leaves = wraps if s == 0 else 0
    return {"sh": lax.rem(sh + nsh - leaves, nsh), "hh": lax.rem(hh + nhh - 1, nhh)}, slot


def window_mask(starts, s):
    seg = Segments(starts, s)
    i = lax.broadcasted_iota(jnp.int32, (256, 256 + RIM), 0)
    j = lanes(256, 256 + RIM)
    return (j > i) & (j <= i + WINDOW) & (seg.col == seg.ext)


def window_probs(q, k, allowed):
    scores = jnp.where(allowed, matmul_nt(q, k) * 64**-0.5, -1e30)
    peak = jnp.max(scores, axis=1, keepdims=True)
    weights = jnp.exp(scores - peak)
    return weights / jnp.sum(weights, axis=1, keepdims=True)


def window_forward_kernel(begin, qkv, starts, o_ref, ext, rim, ssem, rsem):
    cps = []
    for s in range(4):
        target, slot = rim_target(s, True)
        src = qkv.at[pl.ds(s * 256 + 256 - RIM, RIM), pl.ds(128, 256)]
        cps.append(remote(src, rim.at[slot], ssem.at[s], rsem.at[slot], target))

    def fill(s, carry):
        ext[s, RIM:, :] = qkv[pl.ds(s * 256, 256), 128:384]
        return carry

    lax.fori_loop(0, 4, fill, 0)
    for s in range(4):
        pltpu.make_async_copy(rim.at[s], rim.at[s], rsem.at[s]).wait()
    begin()

    def run(s, carry):
        rows = pl.ds(s * 256, 256)
        ext[s, :RIM, :] = rim[s]
        q = qkv[rows, 0:128]
        k = ext[s, :, 0:128]
        v = ext[s, :, 128:256]
        left_half = lanes(256, 128) < 64
        allowed = window_mask(starts, s)
        out = jnp.zeros((256, 128), F32)
        for h in range(2):
            side = left_half if h == 0 else jnp.logical_not(left_half)
            probs = window_probs(jnp.where(side, q, jnp.zeros((), BF16)), k, allowed)
            out = jnp.where(side, matmul(probs.astype(BF16), v), out)
        o_ref[rows, :] = out.astype(BF16)
        return carry

    lax.fori_loop(0, 4, run, 0)
    for cp in cps:
        cp.wait_send()


def window_backward_kernel(
    begin, qkv, ext, do_ref, part, u_ref, att_ref, up_full, starts, out_ref, mixed, out_w,
    acc, back, rim,
    ssem, rsem, own, cb, sb, keep, r1, r2, ss, rs,
):
    total = RowSum(part, own, cb, sb, keep, r1, r2, ss, rs)
    for k in range(4):
        total.core(k)
    zero = jnp.zeros((), BF16)

    def run(s, carry):
        rows = pl.ds(s * 256, 256)
        q = qkv[rows, 0:128]
        k = ext[s, :, 0:128]
        v = ext[s, :, 128:256]
        do = do_ref[rows, :]
        left_half = lanes(256, 128) < 64
        left_ext = lanes(256 + RIM, 128) < 64
        allowed = window_mask(starts, s)
        dq = jnp.zeros((256, 128), F32)
        dk = jnp.zeros((256 + RIM, 128), F32)
        dv = jnp.zeros((256 + RIM, 128), F32)
        for h in range(2):
            side = left_half if h == 0 else jnp.logical_not(left_half)
            q_h = jnp.where(side, q, zero)
            do_h = jnp.where(side, do, zero)
            probs = window_probs(q_h, k, allowed)
            dprobs = matmul_nt(do_h, v)
            inner = jnp.sum(probs * dprobs, axis=1, keepdims=True)
            ds = (probs * (dprobs - inner)).astype(BF16)
            dq = jnp.where(side, matmul(ds, k), dq)
            dk += matmul_tn(ds, q_h)
            dv += matmul_tn(probs.astype(BF16), do_h)
        scale = 64**-0.5
        dk = dk * scale
        out_ref[rows, 0:128] = (dq * scale).astype(BF16)
        acc[rows, 0:128] = dk[RIM:]
        acc[rows, 128:256] = dv[RIM:]
        back[s, :, 0:128] = dk[:RIM].astype(BF16)
        back[s, :, 128:256] = dv[:RIM].astype(BF16)
        return carry

    for k in range(4):
        total.push(k)
    lax.fori_loop(0, 4, run, 0)
    cps = []
    for s in range(4):
        target, slot = rim_target(s, False)
        cps.append(remote(back.at[s], rim.at[slot], ssem.at[s], rsem.at[slot], target))
    for i in range(4):
        at = slice(i * 256, i * 256 + 256)
        rhs = up_full[:, :, :, :, at].reshape(1024, 256)
        value = matmul_tn(att_ref[...], rhs).astype(BF16)
        if len(out_w.shape) == 3:
            out_w[:, :, at] = value.reshape(out_w.shape[:2] + (256,))
        else:
            out_w[:, at] = value
    total.relay()
    begin[1]()
    for s in range(4):
        pltpu.make_async_copy(rim.at[s], rim.at[s], rsem.at[s]).wait()
    begin[0]()

    def finish(s, carry):
        out_ref[pl.ds(s * 256, 256 - RIM), 128:384] = acc[pl.ds(s * 256, 256 - RIM), :].astype(BF16)
        rows = pl.ds(s * 256 + 256 - RIM, RIM)
        out_ref[rows, 128:384] = (acc[rows, :] + rim[s].astype(F32)).astype(BF16)
        return carry

    lax.fori_loop(0, 4, finish, 0)
    total.finish()
    for half in range(2):
        mixed[half] = (u_ref[half] + own[half]).astype(BF16)
    for cp in cps:
        cp.wait_send()


def front(x_own, cot_own, tables, starts, jobs, count, ff, width, collective):
    ship = shipping()
    terms = terms_shape(ff)
    vector = jax.ShapeDtypeStruct((8, D), F32)
    rowset = jax.ShapeDtypeStruct((4, D // 32, D) if ship else (128, D), BF16)
    makers = ("down_b", "gate_b", "up_b", "win", "down_a", "gate_a", "up_a")

    def body(
        begin, x_own, cot_own, pick, coef, shift, starts,
        mixed, g_ha, gg, do_a, lo_w, wo_w, qkv_a, y_a, den_a, pre, psum, w_lin, gains, x_out, n_out, *rest
    ):
        n_terms = 1 + (4 if ship else 6)
        weights, rest = rest[:n_terms], rest[n_terms:]
        made = dict(zip(("up_a",) + makers[:-1], weights))
        if ship:
            made["down_a"], made["gate_a"] = made["down_b"], made["gate_b"]
        h_a, out_a, h_b, g_hb, g_oa = rest[:5]
        na2, nb1, nb2, full1, part1, part2, cot = rest[5:12]
        full2, part3 = nb2, part1
        qkv, ext, o_b, do_b, dqkv, acc, back, rim1, rim2 = rest[12:21]
        gate_s, up_s, hid_s, hid_t, dgate, dup = rest[21:27]
        o_a, st, sm = rest[27:30]
        rest = rest[30:]
        set1, set2 = rest[:8], rest[8:16]
        ag = [rest[16 + 2 * i : 18 + 2 * i] for i in range(8)]
        rims = rest[32:36]
        states, out_sem = rest[36:38], rest[38]
        me, c = plane_place()[0], plane_place()[4]

        def call(name, *args):
            return functools.partial(getattr(begin, name), *args)

        def ship_terms(name):
            if ship:
                begin.start(name + "_t", made[name])

        def send_on(name):
            if ship:
                begin.wait(name + "_t")
                begin.start(name + "_p", begin.result(name + "_t"))

        def relay(*names):
            if ship:
                begin.relay(*[name + "_t" for name in names])

        def norm_own(total, before, after, full, gain):
            for half in range(2):
                u = before[half].astype(F32) + total.own[half]
                after[half] = u
                full[me, c, half] = normed_half(u, gains[gain : gain + 1])

        def start_all(*names):
            for name in names:
                begin.start(name)

        def spread_on(name):
            begin.wait(name + "_m")
            begin.start(name, begin.result(name + "_m"))

        begin.start("lin_m")
        nb1[me, c] = x_own[...]
        rows_in = RowGather(nb1, *ag[6])
        rows_in.start()
        begin.start("gate_a_m")
        spread_on("lin")
        rows_in.hop1()
        start_all("win_out", "lin_out")
        rows_in.hop2()
        rows_in.hop3()
        start_all("up_a_m", "down_a_m")
        rows_in.arrived(0, 6, 8, 9, 10, 11, 12)
        rows_in.finish()
        begin.relay("lin")
        spread_on("gate_a")
        begin.wait("lin")
        w_lin[...] = begin.columns("lin")
        gains[...] = w_lin[:, :128].astype(F32).T[64:72]
        lane = lanes(D, width)
        w_lin[...] = jnp.where((lane < 64) | (lane >= 128), w_lin[...], jnp.zeros((), BF16))

        def project_a(block, carry):
            n = normed_half(chip_rows(nb1, block).astype(F32), gains[0:1])
            put_chip(part2, block, n)
            qkv_a[rows_of(block), :] = matmul(n, w_lin[...]).astype(BF16)
            return carry

        cot[me, c] = cot_own[...]
        cot_in = RowGather(cot, *ag[7])
        cot_in.start()
        lax.fori_loop(0, 4, project_a, 0)
        kept = [
            pltpu.make_async_copy(nb1, x_out, out_sem.at[0]),
            pltpu.make_async_copy(part2, n_out, out_sem.at[1]),
        ]
        for cp in kept:
            cp.start()

        def states_sent():
            spread_on("up_a")
            cot_in.hop1()
            start_all("win_m", "gate_b_m", "up_b_m", "down_b_m")

        def inner_done():
            cot_in.hop2()
            cot_in.hop3()
            begin.relay("gate_a")

        def taylor_done():
            cot_in.arrived(0, 6, 8, 9, 10, 11, 12)
            cot_in.finish()
            for cp in kept:
                cp.wait()

        taylor_forward_kernel(
            count, (states_sent, inner_done, taylor_done), qkv_a, pick, coef, shift, starts,
            o_a, y_a, den_a, pre, psum, st, sm, (hid_t, dgate), *states,
        )
        begin.relay("up_a")
        begin.wait("lin_out")
        wlo = begin.result("lin_out")
        spread_on("down_a")
        total = RowSum(part1, *set1)

        def attended_a(block):
            put_chip(part1, block, matmul(o_a[rows_of(block), :], wlo[...].reshape(128, D)))

        total.run(attended_a)
        norm_own(total, x_own, h_a, na2, 1)
        begin.wait("gate_a")
        begin.relay("down_a")
        total2, seen = RowSum(part2, *set2), []

        def mlp_a(block):
            n = chip_rows(na2, block)
            if not seen:
                begin.wait("up_a")
            gate, up = matmul(n, begin.columns("gate_a")), matmul(n, begin.columns("up_a"))
            hidden = (silu_parts(gate)[1] * up).astype(BF16)
            rows = rows_of(block)
            gate_s[rows, :] = gate.astype(BF16)
            up_s[rows, :] = up.astype(BF16)
            hid_s[rows, :] = hidden
            if not seen:
                begin.wait("down_a")
                spread_on("win")
            put_chip(part2, block, matmul_nt(hidden, begin.columns("down_a")))
            follow(total2, seen)

        RowGather(na2, *ag[0]).run(mlp_a)
        spread_on("gate_b")
        total2.relay()
        total2.finish()
        norm_own(total2, h_a, out_a, nb1, 2)

        def project(block):
            if not gotten:
                begin.wait("win")
                gotten.append(1)
            qkv[rows_of(block), :] = matmul(chip_rows(nb1, block), begin.columns("win")).astype(BF16)

        gotten = []
        RowGather(nb1, *ag[1]).run(
            project, [functools.partial(spread_on, "up_b")]
        )
        begin.relay("gate_b")

        def rims_in():
            spread_on("down_b")

        window_forward_kernel(rims_in, qkv, starts, o_b, ext, rim1, *rims[:2])
        begin.wait("win_out")
        wwo = begin.result("win_out")
        total = RowSum(part1, *set1)

        def attended_b(block):
            put_chip(part1, block, matmul(o_b[rows_of(block), :], wwo[...].reshape(128, D)))

        total.run(attended_b)
        norm_own(total, out_a, h_b, nb2, 3)
        begin.relay("up_b", "down_b")
        total2, seen_b = RowSum(part2, *set2), []

        def mlp_b(block):
            rows = rows_of(block)
            n = chip_rows(nb2, block)
            if not seen_b:
                begin.wait("gate_b", "up_b", "down_b")
            wg, wu, wd = (begin.columns(name) for name in ("gate_b", "up_b", "down_b"))
            gate, up = matmul(n, wg), matmul(n, wu)
            sig, act = silu_parts(gate)
            hidden = (act * up).astype(BF16)
            hid_t[rows, :] = hidden
            dhidden = matmul(chip_rows(cot, block), wd)
            dg = (dhidden * up * (sig + act * (1.0 - sig))).astype(BF16)
            du = (dhidden * act).astype(BF16)
            dgate[rows, :] = dg
            dup[rows, :] = du
            put_chip(part2, block, matmul_nt(dg, wg) + matmul_nt(du, wu))
            follow(total2, seen_b)
            put_chip(part3, block, matmul_nt(hidden, wd))

        RowGather(nb2, *ag[2]).run(mlp_b)
        for job in weight_grads(cot, hid_t, made["down_b"]):
            job()
        ship_terms("down_b")
        total2.relay()
        for job in weight_grads(nb2, dgate, made["gate_b"]):
            job()
        ship_terms("gate_b")
        total2.finish()
        back_own(total2.own, h_b, gains[3:4], cot_own, g_hb, gg.at[2:3], full1)

        def output_grad_b(block):
            do_b[rows_of(block), :] = matmul_nt(
                chip_rows(full1, block), wwo[...].reshape(128, D)
            ).astype(BF16)

        RowGather(full1, *ag[3]).run(
            output_grad_b,
            weight_grads(nb2, dup, made["up_b"]) + [functools.partial(relay, "down_b")],
        )

        def window_begin():
            ship_terms("up_b")

        def window_mid():
            relay("gate_b")
            send_on("down_b")

        window_backward_kernel(
            (window_begin, window_mid), qkv, ext, do_b, part3, h_b, o_b, full1, starts,
            dqkv, mixed, wo_w, acc, back, rim2, *rims[2:4], *set1,
        )
        relay("up_b")
        if ship:
            begin.start("win_out_v", wo_w)
        total = RowSum(part1, *set2)

        def projected(block):
            put_chip(part1, block, matmul_nt(dqkv[rows_of(block), :], begin.columns("win")))

        total.run(projected, weight_grads(nb1, dqkv, made["win"]))
        ship_terms("win")
        back_own(total.own, out_a, gains[2:3], g_hb, g_oa, gg.at[1:2], full2)
        total2, seen_a = RowSum(part2, *set1), []

        def mlp_back(block):
            rows = rows_of(block)
            sig, act = silu_parts(gate_s[rows, :].astype(F32))
            dhidden = matmul(chip_rows(full2, block), begin.columns("down_a"))
            dg = (dhidden * up_s[rows, :].astype(F32) * (sig + act * (1.0 - sig))).astype(BF16)
            du = (dhidden * act).astype(BF16)
            dgate[rows, :] = dg
            dup[rows, :] = du
            put_chip(part2, block, matmul_nt(dg, begin.columns("gate_a")) + matmul_nt(du, begin.columns("up_a")))
            follow(total2, seen_a)

        RowGather(full2, *ag[4]).run(mlp_back)
        for job in weight_grads(full2, hid_s, made["down_a"]):
            job()
        ship_terms("down_a")
        send_on("gate_b")
        total2.relay()
        for job in weight_grads(na2, dgate, made["gate_a"]):
            job()
        ship_terms("gate_a")
        total2.finish()
        back_own(total2.own, h_a, gains[1:2], g_oa, g_ha, gg.at[0:1], full1)

        def output_grad_a(block):
            do_a[rows_of(block), :] = matmul_nt(
                chip_rows(full1, block), wlo[...].reshape(128, D)
            ).astype(BF16)

        def output_weight(i):
            at = slice(i * 256, i * 256 + 256)
            rhs = full1[:, :, :, :, at].reshape(1024, 256)
            lo_w[:, at] = matmul_tn(o_a[...], rhs).astype(BF16)

        RowGather(full1, *ag[5]).run(
            output_grad_a,
            weight_grads(na2, dup, made["up_a"])
            + [functools.partial(send_on, "up_b"), functools.partial(relay, "win", "down_a")],
        )
        for i in range(4):
            output_weight(i)
        send_on("win")
        send_on("down_a")

    rows16 = lambda *shape: VM(shape, BF16)
    rows16s = lambda *shape: jax.ShapeDtypeStruct(shape, BF16)
    OWN_ROWS = jax.ShapeDtypeStruct((1024, 128), F32)
    n_held = 6
    summed = jax.ShapeDtypeStruct((4, 2, D // (8 * lax.axis_size(GROUP)), ff), BF16)
    late = []
    if ship:
        late = [Job("zs", terms, name=m + "_t", held=m != "gate_a") for m in makers[:-1]]
        late += [Job("pa", summed, name=m + "_p") for m in makers[:-2]] + [Job("zv", rowset, name="win_out_v")]
    sem = lambda n: pltpu.SemaphoreType.DMA((n,))
    weights = [VM(terms.shape, BF16)] * 4 if ship else []
    outs, moved = step(
        body,
        vmem(x_own, cot_own, *tables) + [(starts, SMEM)],
        vmem(
            jax.ShapeDtypeStruct((2, 64, D), BF16), OWN, vector, jax.ShapeDtypeStruct((1024, 128), BF16),
            jax.ShapeDtypeStruct((128, D), BF16),
            rowset, rows16s(1024, width), OWN_ROWS, OWN_ROWS, rows16s(4, SROWS, 128),
            jax.ShapeDtypeStruct((4, 8, 256), F32), rows16s(D, width), jax.ShapeDtypeStruct((8, D), F32),
        )
        + [(FULL, ANY), (FULL, ANY)]
        + vmem(terms)
        + ([] if ship else vmem(*[terms] * n_held)),
        weights + [VM((2, 64, D), F32)] * 5 + [VM(FULL.shape, BF16)] * 7
        + [
            rows16(1024, 384), rows16(4, 256 + RIM, 256), rows16(1024, 128), rows16(1024, 128),
            rows16(1024, 384), VM((1024, 256), F32), rows16(4, RIM, 256), rows16(4, RIM, 256),
            rows16(4, RIM, 256),
        ]
        + [rows16(1024, ff)] * 6
        + [rows16(1024, 128), VM((count, 4, SROWS, 128), BF16), VM((count, 4, 8, 256), F32)]
        + rs_scratch() + rs_scratch() + ag_scratch() * 8 + [sem(4)] * 4
        + [pltpu.SemaphoreType.DMA((2, count + 1))] * 2 + [sem(2)],
        jobs + late, 7, True, "front", collective, 300,
    )
    return outs, moved


def row_routes():
    nsh, nhh = lax.axis_size("sh"), lax.axis_size("hh")
    groups = nsh * nhh
    routes = []
    for d in range(8 * groups):
        place, group = d // groups, d % groups
        s, c = place // 2, place % 2
        sh, hh = group // nhh, group % nhh
        routes.append((d, ((sh * 4 + s) * nhh + hh) * 2 + c))
    return routes


def spread_ff(member):
    rows = member.shape[0]
    width = -(-member.shape[1] // (NTP * 128)) * 128
    padded = jnp.pad(member, ((0, 0), (0, NTP * width - member.shape[1])))
    return padded.reshape(rows, NTP, width)


def on_device(
    layer_input, lengths, gain_a1, lin_q, lin_k, lin_v, lin_out, gain_a2, mlp_a_gate, mlp_a_up,
    mlp_a_down, gain_b1, win_q, win_k, win_v, win_out, gain_b2, mlp_b_gate, mlp_b_up, mlp_b_down,
    cotangent,
):
    count = lax.axis_size(GROUP)
    rows = lin_q.shape[0]
    hidden_size = mlp_a_gate.shape[1]
    gains = jnp.pad(jnp.stack([gain_a1, gain_a2, gain_b1, gain_b2], axis=1), ((0, 0), (0, 60)))
    gains = jnp.broadcast_to(gains[:, None, :], (rows, NTP, 64))
    starts = jnp.cumsum(lengths) - lengths
    tables = taylor_tables()

    split = lambda member: member.reshape(rows, NTP, -1)
    bundle_lin = jnp.concatenate(
        [split(lin_q), split(lin_k), gains, split(lin_v)], axis=-1
    ).transpose(1, 0, 2)
    bundle_a = jnp.concatenate(
        [spread_ff(mlp_a_gate), spread_ff(mlp_a_up), spread_ff(mlp_a_down.T)], axis=-1
    ).transpose(1, 0, 2)
    bundle_win = jnp.concatenate([split(win_q), split(win_k), split(win_v)], axis=-1).transpose(
        1, 0, 2
    )
    bundle_b = jnp.concatenate(
        [spread_ff(mlp_b_gate), spread_ff(mlp_b_up), spread_ff(mlp_b_down.T)], axis=-1
    ).transpose(1, 0, 2)
    ff = bundle_a.shape[-1] // 3
    width = bundle_lin.shape[-1]
    nsh, nhh = lax.axis_size("sh"), lax.axis_size("hh")
    places = lambda a: a.reshape(4, 2, rows, a.shape[-1])
    whole = lambda a: a.reshape(D, a.shape[-1])
    total = lambda a: jnp.sum(a.astype(F32), axis=0).astype(BF16)
    ship = shipping()
    if ship:
        own_rows = lambda a, **kw: Job("zw", a, **kw)
    else:
        own_rows = lambda a, **kw: Job("zr", lax.ppermute(a, AXES, row_routes()), **kw)

    x_own = layer_input.reshape(2, 64, D)
    cot_own = cotangent.reshape(2, 64, D)
    def column(name, a):
        return [
            Job("pa", a, name=name + "_m"),
            Job("zg", jax.ShapeDtypeStruct(a.shape, BF16), VMEM, name, True),
        ]

    third = lambda a, i: places(a[:, :, i * ff : i * ff + ff])
    jobs = [
        column("lin", places(bundle_lin)), column("gate_a", third(bundle_a, 0)),
        column("up_a", third(bundle_a, 1)), column("down_a", third(bundle_a, 2)),
        column("win", places(bundle_win)), column("gate_b", third(bundle_b, 0)),
        column("up_b", third(bundle_b, 1)), column("down_b", third(bundle_b, 2)),
        [own_rows(lin_out, spec=VMEM, name="lin_out", held=True)],
        [own_rows(win_out, spec=VMEM, name="win_out", held=True)],
    ]
    outs, moved = front(x_own, cot_own, tables, starts, sum(jobs, []), count, ff, width, 1)
    mixed, grad_h_a, gg, do_a, grad_lin_out, grad_win_out = outs[:6]
    qkv_a, y_a, den_a, pre, psum, w_lin, gains, x_full, n_a1, up_a = outs[6:16]
    kept, apart_terms, moved = (y_a, den_a, pre, psum), outs[16:], moved[8:]
    if ship:
        gate_a, down_b, gate_b, up_b, win, down_a, win_out_t = moved
        late = [Job("pa", gate_a), Job("zs", up_a)]
    else:
        sums = apart(apart_terms, 10)
        _, moved = step(
            lambda begin: None, [], [], [], [Job("pa", a) for a in sums[:5]]
            + [Job("zt", grad_win_out.reshape(count, -1, D))], 7, True, "spread", 11, 20,
        )
        down_b, gate_b, up_b, win, down_a, win_out_t = moved
        late = [Job("pa", sums[5])]
        (up_a,) = apart([up_a], 14)
    (dqkv_a,), (gate_a, *more) = taylor_backward(qkv_a, do_a, kept, starts, tables, late, count, 8)
    (up_a,) = more if ship else (up_a,)
    rows_back = Job("zv", grad_lin_out.reshape(4, rows, D)) if ship else Job(
        "zt", grad_lin_out.reshape(count, -1, D)
    )
    grad_input, (lin_out_t, up_a), lin_g = last_layer(
        dqkv_a, w_lin, x_own, gains[0:1], grad_h_a, x_full, n_a1, gg[0:3], [rows_back, Job("pa", up_a)], 9,
    )

    def joined(a, lo, hi):
        a = a.reshape(NTP, rows, -1)[:, :, lo:hi].astype(F32)
        return a.transpose(1, 0, 2).reshape(rows, -1)

    def unpack_mlp(gate, up, down):
        joined_ff = lambda a: joined(a, 0, ff)[:, :hidden_size]
        return joined_ff(gate), joined_ff(up), joined_ff(down).T

    gate_b_g, up_b_g, down_b_g = unpack_mlp(gate_b, up_b, down_b)
    gate_a_g, up_a_g, down_a_g = unpack_mlp(gate_a, up_a, down_a)
    def own_terms(a):
        if ship:
            return jnp.sum(a.astype(F32), axis=0)
        return lax.ppermute(total(a), AXES, [(d, e) for e, d in row_routes()]).astype(F32)

    win_out_g, lin_out_g = own_terms(win_out_t), own_terms(lin_out_t)
    gg = jnp.sum(lin_g.reshape(NTP, rows, width)[:, :, 64:68].astype(F32), axis=0)
    return (
        mixed.reshape(128, D),
        grad_input.reshape(128, D),
        gg[:, 0],
        joined(lin_g, 0, 32),
        joined(lin_g, 32, 64),
        joined(lin_g, 128, 256),
        lin_out_g,
        gg[:, 1],
        gate_a_g,
        up_a_g,
        down_a_g,
        gg[:, 2],
        joined(win, 0, 128),
        joined(win, 128, 256),
        joined(win, 256, 384),
        win_out_g,
        gg[:, 3],
        gate_b_g,
        up_b_g,
        down_b_g,
    )


def solution(mesh):
    seq, head = mesh.devices.shape
    fine = Mesh(mesh.devices.reshape(seq // 4, 2, 2, head // 2, 2), AXES)
    row, vec, col = P(AXES, None), P(AXES), P(None, AXES)
    placed = (
        row, P(), vec, row, row, row, row, vec, row, row, col,
        vec, row, row, row, row, vec, row, row, col, row,
    )
    out = (
        row, row, vec, row, row, row, row, vec, row, row, col,
        vec, row, row, row, row, vec, row, row, col,
    )
    return jax.shard_map(on_device, mesh=fine, in_specs=placed, out_specs=out, check_vma=False)
```

```python
import functools

import jax
import jax.numpy as jnp
import numpy as np
from jax import lax
from jax.experimental import pallas as pl
from jax.experimental.pallas import tpu as pltpu
from jax.sharding import Mesh
from jax.sharding import PartitionSpec as P

D = 1024
HEADS = 16
FEAT = 16
WINDOW = 64
NTP = 8
RIM = 64
SROWS = 160
EPSILON = 1e-05
AXES = ("sh", "sy", "sx", "hh", "hl")
TP = ("sy", "sx", "hl")
GROUP = ("sh", "hh")
MESH_ID = pl.DeviceIdType.MESH
F32 = jnp.float32
BF16 = jnp.bfloat16
VM = pltpu.VMEM
LIMIT = 60 * 1024 * 1024


def vmem_specs(count):
    return [pl.BlockSpec(memory_space=pltpu.VMEM)] * count


def matmul(left, right):
    return jnp.dot(left, right, preferred_element_type=F32)


def matmul_tn(left, right):
    return lax.dot_general(left, right, (((0,), (0,)), ((), ())), preferred_element_type=F32)


def matmul_nt(left, right):
    return lax.dot_general(left, right, (((1,), (1,)), ((), ())), preferred_element_type=F32)


def plane_place():
    sy, sx, c = lax.axis_index("sy"), lax.axis_index("sx"), lax.axis_index("hl")
    me = sy * 2 + sx
    xn = sy * 2 + (1 - sx)
    yn = (1 - sy) * 2 + sx
    dg = 3 - me
    return me, xn, yn, dg, c, {"sx": 1 - sx}, {"sy": 1 - sy}, {"hl": 1 - c}


def remote(src, dst, ssem, rsem, target):
    copy = pltpu.make_async_remote_copy(
        src_ref=src, dst_ref=dst, send_sem=ssem, recv_sem=rsem, device_id=target, device_id_type=MESH_ID
    )
    copy.start()
    return copy


AG_COPIES = 13
RS_COPIES = 10


class RowGather:
    def __init__(self, full, ssem, rsem):
        self.full, self.ssem, self.rsem = full, ssem, rsem
        self.place = plane_place()
        self.cps = {}

    def send(self, k, block, half, target):
        view = self.full.at[block, self.place[4], half]
        self.cps[k] = remote(view, view, self.ssem.at[k], self.rsem.at[k], target)

    def start(self):
        me, _, _, _, c, to_x, to_y, to_c = self.place
        self.send(1, me, 0, to_x)
        self.send(3, me, 1, to_y)
        self.send(2, me, 1, to_x)
        self.send(4, me, 0, to_y)
        own = self.full.at[me, c]
        self.cps[0] = remote(own, own, self.ssem.at[0], self.rsem.at[0], to_c)

    def arrived(self, *keys):
        for k in keys:
            self.cps[k].wait_recv()

    def hop1(self):
        _, xn, yn, _, _, to_x, to_y, to_c = self.place
        self.arrived(1)
        self.send(5, xn, 0, to_y)
        self.send(6, xn, 0, to_c)
        self.arrived(3)
        self.send(7, yn, 1, to_x)
        self.send(8, yn, 1, to_c)

    def hop2(self):
        _, xn, yn, _, _, _, _, to_c = self.place
        self.arrived(2)
        self.send(9, xn, 1, to_c)
        self.arrived(4)
        self.send(10, yn, 0, to_c)

    def hop3(self):
        _, _, _, dg, _, _, _, to_c = self.place
        self.arrived(5)
        self.send(11, dg, 0, to_c)
        self.arrived(7)
        self.send(12, dg, 1, to_c)

    def finish(self):
        for k in range(AG_COPIES):
            self.cps[k].wait_send()

    def run(self, consume, spare=()):
        me, xn, yn, dg = self.place[:4]
        spare = list(spare)

        def fill(most):
            for _ in range(min(most, len(spare))):
                spare.pop(0)()

        self.start()
        self.arrived(0)
        consume(me)
        fill(3)
        self.hop1()
        fill(2)
        self.hop2()
        self.arrived(6, 9)
        consume(xn)
        fill(2)
        self.hop3()
        self.arrived(8, 10)
        consume(yn)
        self.arrived(11, 12)
        consume(dg)
        fill(len(spare))
        self.finish()


class RowSum:
    def __init__(self, part, own, cb, sb, keep, r1, r2, ssem, rsem):
        self.part, self.own, self.cb, self.sb, self.keep = part, own, cb, sb, keep
        self.r1, self.r2, self.ssem, self.rsem = r1, r2, ssem, rsem
        self.place = plane_place()
        self.cps = {}

    def block(self, k):
        me, xn, yn, dg = self.place[:4]
        return (dg, xn, yn, me)[k]

    def copy(self, k, src, dst, target):
        self.cps[k] = remote(src, dst, self.ssem.at[k], self.rsem.at[k], target)

    def core(self, k):
        src = self.part.at[self.block(k), 1 - self.place[4]]
        self.copy(k, src, self.cb.at[k], self.place[7])

    def both(self, k, half):
        mine = self.part[self.block(k), self.place[4], half]
        return mine.astype(F32) + self.cb[k, half].astype(F32)

    def push(self, k):
        to_x, to_y = self.place[5:7]
        sb, r1 = self.sb, self.r1
        self.cps[k].wait_recv()
        if k == 0:
            sb[0, 0] = self.both(0, 0).astype(BF16)
            self.copy(4, sb.at[0, 0], r1.at[0, 0], to_x)
            sb[0, 1] = self.both(0, 1).astype(BF16)
            self.copy(5, sb.at[0, 1], r1.at[1, 0], to_y)
        if k == 1:
            sb[1, 0] = self.both(1, 0).astype(BF16)
            self.copy(6, sb.at[1, 0], r1.at[0, 1], to_x)
            self.keep[1] = self.both(1, 1)
        if k == 2:
            sb[2, 1] = self.both(2, 1).astype(BF16)
            self.copy(7, sb.at[2, 1], r1.at[1, 1], to_y)
            self.keep[0] = self.both(2, 0)
        if k == 3:
            self.own[0] = self.both(3, 0)
            self.own[1] = self.both(3, 1)

    def relay(self):
        to_x, to_y = self.place[5:7]
        self.cps[4].wait_recv()
        self.sb[2, 0] = (self.keep[0] + self.r1[0, 0].astype(F32)).astype(BF16)
        self.copy(8, self.sb.at[2, 0], self.r2.at[0], to_y)
        self.cps[5].wait_recv()
        self.sb[1, 1] = (self.keep[1] + self.r1[1, 0].astype(F32)).astype(BF16)
        self.copy(9, self.sb.at[1, 1], self.r2.at[1], to_x)
        self.cps[6].wait_recv()
        self.own[0] += self.r1[0, 1].astype(F32)
        self.cps[7].wait_recv()
        self.own[1] += self.r1[1, 1].astype(F32)

    def finish(self):
        self.cps[8].wait_recv()
        self.own[0] += self.r2[0].astype(F32)
        self.cps[9].wait_recv()
        self.own[1] += self.r2[1].astype(F32)
        for k in range(RS_COPIES):
            self.cps[k].wait_send()

    def run(self, produce, spare=()):
        spare = list(spare)
        for k in range(4):
            produce(self.block(k))
            self.core(k)
        for k in range(4):
            self.push(k)
        for job in spare[: len(spare) // 2]:
            job()
        self.relay()
        for job in spare[len(spare) // 2 :]:
            job()
        self.finish()


def rs_scratch():
    return [
        VM((2, 64, D), F32),
        VM((4, 2, 64, D), BF16),
        VM((3, 2, 64, D), BF16),
        VM((2, 64, D), F32),
        VM((2, 2, 64, D), BF16),
        VM((2, 64, D), BF16),
        pltpu.SemaphoreType.DMA((RS_COPIES,)),
        pltpu.SemaphoreType.DMA((RS_COPIES,)),
    ]


def ag_scratch():
    return [pltpu.SemaphoreType.DMA((AG_COPIES,)), pltpu.SemaphoreType.DMA((AG_COPIES,))]


def cost(micros):
    return pl.CostEstimate(flops=0, bytes_accessed=int(micros * 3.0e6), transcendentals=0)


def group_place():
    return lax.axis_index("sh") * lax.axis_size("hh") + lax.axis_index("hh")


def group_peer(k, count):
    nhh = lax.axis_size("hh")
    other = lax.rem(group_place() + k, count)
    sh, hh = other // nhh, lax.rem(other, nhh)
    return other, sh, hh, {"sh": sh, "hh": hh}


def place_peer(k):
    coords = {}
    for bit, axis in enumerate(("hl", "sx", "sy")):
        here = lax.axis_index(axis)
        coords[axis] = 1 - here if (k >> bit) & 1 else here
    target = {axis: v for bit, (axis, v) in enumerate(coords.items()) if (k >> bit) & 1}
    return coords["sy"] * 2 + coords["sx"], coords["hl"], target


def barrier_of(plane, group, count, column):
    barrier = pltpu.get_barrier_semaphore()
    seen = 0
    if column:
        hh, c = lax.axis_index("hh"), lax.axis_index("hl")
        for k in range(1, 8):
            target = {"hh": lax.rem(hh + k // 2, 4), "hl": 1 - c if k % 2 else c}
            if k == 1 and plane:
                continue
            pl.semaphore_signal(barrier, inc=1, device_id=target, device_id_type=MESH_ID)
            seen += 1
        group = False
    for k in ((1, 2, 4) if plane == 3 else range(1, 8)) if plane else ():
        _, _, target = place_peer(k)
        pl.semaphore_signal(barrier, inc=1, device_id=target, device_id_type=MESH_ID)
        seen += 1
    if group:
        for k in range(1, count):
            target = group_peer(k, count)[3]
            pl.semaphore_signal(barrier, inc=1, device_id=target, device_id_type=MESH_ID)
            seen += 1
    pl.semaphore_wait(barrier, seen)


def chained():
    return lax.axis_size("sh") == 1 and lax.axis_size("hh") == 4


class Job:
    def __init__(self, kind, src, spec=None, name=None, held=False, pool=None):
        self.kind, self.src, self.inside = kind, src, isinstance(src, jax.ShapeDtypeStruct)
        self.spec = spec or (VMEM if kind == "zs" else ANY)
        self.src_spec = VMEM if kind == "zs" else ANY
        self.name, self.held, self.pool = name, held, pool

    def out_shape(self):
        nsh, nhh = lax.axis_size("sh"), lax.axis_size("hh")
        shape = list(self.src.shape)
        if self.kind == "zg":
            shape = [nsh * 4, nhh] + shape[1:]
        if self.kind == "zr":
            shape = [nsh * nhh] + shape
        if self.kind == "zo":
            shape = [nsh * nhh, 4] + shape[2:]
        if self.kind == "zs":
            shape = [4] + shape[2:]
        if self.kind == "zw":
            shape = [4] + shape
        return jax.ShapeDtypeStruct(tuple(shape), BF16)


class Transfers:
    def __init__(self, kinds, sources, results, buffers, sems, count, chain):
        self.kinds, self.sources, self.results = kinds, sources, results
        self.buffers, self.sems, self.count, self.chain = buffers, sems, count, chain
        self.state = {}

    def copy(self, i, src, dst, send, recv, target):
        return pltpu.make_async_remote_copy(
            src_ref=src, dst_ref=dst, send_sem=self.sems[0].at[i, send],
            recv_sem=self.sems[1].at[i, recv], device_id=target, device_id_type=MESH_ID,
        )

    early = ()

    def __call__(self):
        for i, src in enumerate(self.sources):
            if src is not None and i not in self.state:
                self.start(i)

    late = __call__

    def slot(self, i, group):
        out, nhh = self.results[i], lax.axis_size("hh")
        if self.kinds[i] == "zg":
            return out.at[pl.ds(group // nhh * 4, 4), lax.rem(group, nhh)]
        return out.at[group]

    def got(self, i, ref, index):
        pltpu.make_async_copy(ref, ref, self.sems[1].at[i, index]).wait()

    def sent(self, i, ref, index):
        pltpu.make_async_copy(ref, ref, self.sems[0].at[i, index]).wait()

    names = {}

    def has(self, i):
        return i in self.names

    def start(self, i, src=None):
        i = self.names.get(i, i)
        if src is not None:
            self.sources[i] = src
        self.state[i] = "sent"
        kind, src, out, count = self.kinds[i], self.sources[i], self.results[i], self.count
        hh, g = lax.axis_index("hh"), group_place()
        local = None
        if kind == "pa":
            s, c, _ = place_peer(0)
            for k in range(1, 8):
                ps, pc, target = place_peer(k)
                self.copy(i, src.at[ps, pc], out.at[s, c], k, k, target).start()
            local = (src.at[s, c], out.at[s, c])
        if kind in ("zg", "zr"):
            for k in (1, 3, 2) if self.chain else range(1, count):
                go = self.copy(i, src, self.slot(i, g), k, g, group_peer(k, count)[3]).start
                if self.chain and k != 2:
                    pl.when(hh != (3 if k == 1 else 0))(go)
                else:
                    go()
            local = (src, self.slot(i, g))
        if kind in ("zo", "zt"):
            nhh = lax.axis_size("hh")
            part = lambda p: (
                src.at[p] if kind == "zt" else src.at[pl.ds(p // nhh * 4, 4), lax.rem(p, nhh)]
            )
            for k in range(1, count):
                other, _, _, target = group_peer(k, count)
                self.copy(i, part(other), out.at[g], k, g, target).start()
            local = (part(g), out.at[g])
        if kind == "zs":
            buf = self.buffers[i]
            last, begin = hh == 3, hh == 0
            up = self.copy(
                i, src.at[:, jnp.where(last, 0, hh + 1)], buf.at[jnp.where(last, 4, g)],
                1, jnp.where(last, 4, g), {"hh": jnp.where(last, 2, hh + 1)},
            ).start
            down = self.copy(
                i, src.at[:, jnp.where(begin, 3, hh - 1)], buf.at[jnp.where(begin, 4, g)],
                3, jnp.where(begin, 4, g), {"hh": jnp.where(begin, 1, hh - 1)},
            ).start

            @pl.when(last)
            def _():
                up()
                down()

            @pl.when(jnp.logical_not(last))
            def _():
                down()
                up()

            far = lax.rem(hh + 2, 4)
            pl.when(last | begin)(self.copy(i, src.at[:, far], buf.at[g], 2, g, {"hh": far}).start)
        if kind in ("zw", "zv"):
            for k in range(4):
                mine, target, src_k, at, _ = self.column(kind, k)
                view = src if kind == "zw" else src.at[src_k]
                here = pltpu.make_async_copy(view, out.at[at], self.sems[2].at[i]).start
                pl.when(mine)(here)
                pl.when(jnp.logical_not(mine))(self.copy(i, view, out.at[at], k, at, target).start)
        if local is not None:
            pltpu.make_async_copy(local[0], local[1], self.sems[2].at[i]).start()
            self.local = getattr(self, "local", {})
            self.local[i] = local

    def column(self, kind, k):
        hh, c = lax.axis_index("hh"), lax.axis_index("hl")
        if kind == "zw":
            z, to_c, slot = lax.rem(hh + k, 4), hh // 2, lax.rem(hh, 2) * 2 + c
            own = (2 * c + k // 2 == hh) & (k % 2 == c)
            return (z == hh) & (to_c == c), {"hh": z, "hl": to_c}, 0, slot, own
        j = lax.rem(lax.rem(hh, 2) * 2 + c + k, 4)
        z, to_c = 2 * c + j // 2, lax.rem(j, 2)
        own = (k == hh) & (hh // 2 == c)
        return (z == hh) & (to_c == c), {"hh": z, "hl": to_c}, j, hh, own

    def relay(self, *which):
        for i in which:
            i = self.names.get(i, i)
            if i not in self.state:
                continue
            kind = self.kinds[i]
            if not self.chain or kind not in ("zg", "zr", "zs") or self.state[i] != "sent":
                continue
            self.state[i] = "relayed"
            hh, g = lax.axis_index("hh"), group_place()
            inner = (hh == 1) | (hh == 2)
            far = lax.rem(hh + 2, 4)

            @pl.when(inner)
            def _(i=i, kind=kind):
                if kind == "zs":
                    buf, src = self.buffers[i], self.sources[i]
                    self.got(i, buf.at[4], 4)
                    buf[4] = (buf[4].astype(F32) + src[:, far].astype(F32)).astype(BF16)
                    self.copy(i, buf.at[4], buf.at[g], 2, g, {"hh": far}).start()
                else:
                    slot = self.slot(i, far)
                    self.got(i, slot, far)
                    self.copy(i, slot, slot, 0, far, {"hh": 3 - far}).start()

    def wait(self, *which):
        self.relay(*which)
        for i in which:
            i = self.names.get(i, i)
            if self.state[i] == "done":
                continue
            self.state[i] = "done"
            kind, src, out, count = self.kinds[i], self.sources[i], self.results[i], self.count
            hh, g = lax.axis_index("hh"), group_place()
            inner = (hh == 1) | (hh == 2)
            if kind == "pa":
                s, c, _ = place_peer(0)
                for k in range(1, 8):
                    self.copy(i, src.at[s, c], out.at[s, c], k, k, place_peer(k)[2]).wait()
            if kind in ("zg", "zr"):
                for k in range(1, count):
                    other = lax.rem(g + k, count)
                    slot = self.slot(i, other)

                    def arrive(slot=slot, other=other):
                        self.got(i, slot, other)

                    def leave(k=k):
                        self.sent(i, src, k)

                    if not self.chain:
                        arrive()
                        leave()
                    elif k == 2:
                        pl.when(jnp.logical_not(inner))(arrive)
                        leave()
                        pl.when(inner)(functools.partial(leave, 0))
                    else:
                        arrive()
                        pl.when(hh != (3 if k == 1 else 0))(leave)
            if kind in ("zo", "zt"):
                for k in range(1, count):
                    other = lax.rem(g + k, count)
                    self.got(i, out.at[other], other)
                    self.sent(i, out.at[other], k)
            if kind in ("zw", "zv"):
                for k in range(4):
                    mine, _, _, at, own = self.column(kind, k)
                    slot = out.at[k]
                    here = pltpu.make_async_copy(slot, slot, self.sems[2].at[i]).wait
                    pl.when(own)(here)
                    pl.when(jnp.logical_not(own))(functools.partial(self.got, i, slot, k))
                    pl.when(jnp.logical_not(mine))(functools.partial(self.sent, i, slot, k))
            if kind == "zs":
                buf = self.buffers[i]
                one = jnp.where(hh == 0, 2, hh - 1)
                two = jnp.where(hh == 3, 1, hh + 1)
                far = lax.rem(hh + 2, 4)
                self.got(i, buf.at[one], one)
                self.got(i, buf.at[two], two)
                total = lambda: (
                    src[:, g].astype(F32) + buf[one].astype(F32) + buf[two].astype(F32)
                )

                @pl.when(inner)
                def _():
                    self.got(i, buf.at[far], far)
                    out[...] = (total() + buf[far].astype(F32)).astype(BF16)

                @pl.when(jnp.logical_not(inner))
                def _():
                    out[...] = total().astype(BF16)

                for k in (1, 2, 3):
                    self.sent(i, buf.at[g], k)
            if i in getattr(self, "local", {}):
                a, b = self.local[i]
                pltpu.make_async_copy(a, b, self.sems[2].at[i]).wait()

    def rest(self):
        which = [i for i in self.state if self.state[i] != "done"]
        self.relay(*which)
        self.wait(*which)

    def result(self, i):
        return self.results[self.names.get(i, i)]

    def columns(self, i):
        ref = self.result(i)
        return ref[...].reshape(D, ref.shape[-1])


ANY = pl.BlockSpec(memory_space=pl.ANY)
VMEM = pl.BlockSpec(memory_space=pltpu.VMEM)
SMEM = pl.BlockSpec(memory_space=pltpu.SMEM)


def step(body, ins, outs, scratch, jobs, plane, group, name, collective, micros, early=()):
    count = lax.axis_size(GROUP)
    kinds = [job.kind for job in jobs]
    given = [job for job in jobs if not job.inside]
    shown = [job for job in jobs if not job.held]
    n_in, n_out, n_job, n_src = len(ins), len(outs), len(jobs), len(given)
    plane = 7 if "pa" in kinds else plane
    group = group or any(kind != "pa" for kind in kinds)
    column = any(kind in ("zw", "zv") for kind in kinds)
    slots = max(count, 8)
    held = [VM(job.out_shape().shape, BF16) for job in jobs if job.held]
    pools = {}
    for i, job in enumerate(jobs):
        if job.kind == "zs":
            key = (job.pool if job.pool is not None else -1 - i, job.out_shape().shape)
            pools.setdefault(key, []).append(i)

    def kernel(*refs):
        in_refs, refs = refs[:n_in], refs[n_in:]
        given_refs, refs = list(refs[:n_src]), refs[n_src:]
        out_refs, refs = refs[:n_out], refs[n_out:]
        shown_refs, refs = list(refs[: len(shown)]), refs[len(shown) :]
        extra_refs, own = list(refs[len(scratch) :]), refs[: len(scratch)]
        held_refs, pool_refs = extra_refs[3 : 3 + len(held)], extra_refs[3 + len(held) :]
        sources = [None if job.inside else given_refs.pop(0) for job in jobs]
        results = [held_refs.pop(0) if job.held else shown_refs.pop(0) for job in jobs]
        buffers = {i: ref for key, ref in zip(pools, pool_refs) for i in pools[key]}
        barrier_of(plane, group, count, column)
        begin = Transfers(kinds, sources, results, buffers, extra_refs[:3], count, chained())
        begin.early = early
        begin.names = {job.name: i for i, job in enumerate(jobs) if job.name}
        body(begin, *in_refs, *out_refs, *own)
        if not begin.state:
            begin()
        begin.rest()

    extra = (
        [
            pltpu.SemaphoreType.DMA((n_job, slots)),
            pltpu.SemaphoreType.DMA((n_job, slots)),
            pltpu.SemaphoreType.DMA((n_job,)),
        ]
        + held
        + [VM((5,) + key[1], BF16) for key in pools]
    )
    result = pl.pallas_call(
        kernel,
        out_shape=tuple(o for o, _ in outs) + tuple(job.out_shape() for job in shown),
        in_specs=[spec for _, spec in ins] + [job.src_spec for job in given],
        out_specs=tuple(spec for _, spec in outs) + tuple(job.spec for job in shown),
        scratch_shapes=list(scratch) + (extra if n_job else []),
        compiler_params=pltpu.CompilerParams(
            collective_id=collective, has_side_effects=True, vmem_limit_bytes=LIMIT
        ),
        cost_estimate=cost(micros),
        name=name,
    )(*[v for v, _ in ins], *[job.src for job in given])
    return result[:n_out], result[n_out:]


FULL = jax.ShapeDtypeStruct((4, 2, 2, 64, D), BF16)
OWN = jax.ShapeDtypeStruct((2, 64, D), F32)


def flat(full):
    return full.reshape(1024, D)


def blocks(rows):
    return rows.reshape(4, 2, 2, 64, D)


def vmem(*values):
    return [(v, VMEM) for v in values]


def normed_half(u, gain):
    inv = lax.rsqrt(jnp.mean(u * u, axis=-1, keepdims=True) + EPSILON)
    return (u * inv * gain).astype(BF16)


def chip_rows(ref, block):
    return ref[block].reshape(256, D)


def put_chip(ref, block, value):
    ref[block] = value.astype(BF16).reshape(2, 2, 64, D)


def rows_of(block):
    return pl.ds(block * 256, 256)


def silu_parts(gate):
    sig = 1.0 / (1.0 + jnp.exp(-gate))
    return sig, gate * sig


def follow(total, seen):
    k = (3, 1, 2, 0)[len(seen)]
    seen.append(k)
    total.core(k)
    if k == 2:
        total.push(1)
    if k == 0:
        total.push(2)
        total.push(3)
        total.push(0)


def norm_back_half(dn, u, gain, upstream):
    inv = lax.rsqrt(jnp.mean(u * u, axis=-1, keepdims=True) + EPSILON)
    gained = dn * gain
    inner = jnp.mean(gained * u, axis=-1, keepdims=True)
    scaled = u * inv
    grad = upstream + inv * gained - scaled * (inv * inv * inner)
    return grad, jnp.sum(dn * scaled, axis=0, keepdims=True)


def back_own(dn, u_ref, gain_ref, up_ref, gnew, ggain, full):
    me, c = plane_place()[0], plane_place()[4]
    total = None
    for half in range(2):
        grad, gain_part = norm_back_half(
            dn[half], u_ref[half].astype(F32), gain_ref[...], up_ref[half].astype(F32)
        )
        gnew[half] = grad
        total = gain_part if total is None else total + gain_part
        if full is not None:
            full[me, c, half] = grad.astype(BF16)
    ggain[...] = total


def weight_grads(left, right, out):
    def piece(i):
        width = D // 4
        lo = i * width
        lhs = left[:, :, :, :, lo : lo + width].reshape(1024, width)
        value = matmul_tn(lhs, right[...]).astype(BF16)
        if len(out.shape) == 5:
            out[i] = value.reshape(out.shape[1:])
        else:
            out[lo : lo + width, :] = value

    return [functools.partial(piece, i) for i in range(4)]


def shipping():
    return chained() and D % (8 * 4 * 16) == 0


def terms_shape(cols):
    nsh, nhh = lax.axis_size("sh"), lax.axis_size("hh")
    if shipping():
        return jax.ShapeDtypeStruct((4, 4, 2, D // 32, cols), BF16)
    return jax.ShapeDtypeStruct((D, cols), BF16)


def apart(arrays, collective):
    nsh, nhh = lax.axis_size("sh"), lax.axis_size("hh")
    rows = D // (8 * nsh * nhh)
    jobs = [Job("zo", a.reshape(nsh * 4, nhh, 2, rows, a.shape[-1])) for a in arrays]
    _, moved = step(lambda begin: None, [], [], [], jobs, 0, True, "apart", collective, 20)
    return [jnp.sum(a.astype(F32), axis=0).astype(BF16) for a in moved]


def last_layer(dproj, w_proj, u, gain, upstream, x_full, n_first, gains, jobs, collective):
    width = w_proj.shape[1]
    ship = shipping()

    def body(
        begin, dp_ref, wp_ref, u_ref, gain_ref, up_ref, xf_ref, nf_ref, gains_ref,
        gnew, ggain, proj_w, part1, mine, *rest
    ):
        sum1 = RowSum(part1, *rest)
        begin()
        mine[...] = jnp.zeros((128, D), F32)
        mine[65:68, :] = gains_ref[...]

        def projected(block):
            part = matmul_nt(dp_ref[rows_of(block), :], wp_ref[...])
            put_chip(part1, block, part)
            u = chip_rows(xf_ref, block).astype(F32)
            u = u * lax.rsqrt(jnp.mean(u * u, axis=-1, keepdims=True) + EPSILON)
            mine[64:65, :] += jnp.sum(part * u, axis=0, keepdims=True)

        def grads():
            turned = mine[...].T
            for i in range(4):
                at = slice(i * 256, i * 256 + 256)
                lhs = nf_ref[:, :, :, :, at].reshape(1024, 256)
                value = matmul_tn(lhs, dp_ref[...])
                keep = lanes(256, 128) < 64
                value = jnp.concatenate(
                    [jnp.where(keep, value[:, :128], turned[at]), value[:, 128:]], axis=1
                ).astype(BF16)
                if ship:
                    proj_w[i] = value.reshape(proj_w.shape[1:])
                else:
                    proj_w[at, :] = value
            if ship:
                begin.start(len(jobs), proj_w)

        for k in range(4):
            projected(sum1.block(k))
            sum1.core(k)
        grads()
        for k in range(4):
            sum1.push(k)
        sum1.relay()
        sum1.finish()
        begin.relay(len(jobs))
        back_own(sum1.own, u_ref, gain_ref, up_ref, gnew, ggain, None)
        if ship:
            begin.wait(len(jobs))
            begin.start(len(jobs) + 1, begin.results[len(jobs)])

    terms = terms_shape(width)
    summed = jax.ShapeDtypeStruct((4, 2, D // 32, width), BF16)
    n = len(jobs)
    outs, moved = step(
        body, vmem(dproj, w_proj, u, gain, upstream, x_full, n_first, gains),
        vmem(OWN, jax.ShapeDtypeStruct((1, D), F32)) + ([] if ship else vmem(terms)),
        ([VM(terms.shape, BF16)] if ship else []) + [VM(FULL.shape, BF16), VM((128, D), F32)] + rs_scratch(),
        jobs + ([Job("zs", terms), Job("pa", summed)] if ship else []),
        3, False, "last_layer", collective, 25,
    )
    if ship:
        return outs[0], moved[:n], moved[n + 1]
    (lin,) = apart([outs[2]], 12)
    _, (lin,) = step(
        lambda begin: None, [], [], [], [Job("pa", lin)], 7, False, "last", 13, 5
    )
    return outs[0], moved[:n], lin


def taylor_tables():
    pick = np.zeros((4, 2, 128, 256), np.float32)
    coef = np.zeros((8, 256), np.float32)
    pairs = [(i, j) for i in range(FEAT) for j in range(i, FEAT)]
    one = 4 * FEAT
    for x, (i, j) in enumerate(pairs):
        coef[:, x] = (2.0 * FEAT) ** -0.5 if i == j else FEAT**-0.5
        for t in range(4):
            pick[t, 0, t * FEAT + i, x] = 1.0
            pick[t, 1, t * FEAT + j, x] = 1.0
    for i in range(FEAT):
        x = len(pairs) + i
        coef[:, x] = FEAT**-0.25
        for t in range(4):
            pick[t, 0, t * FEAT + i, x] = 1.0
            pick[t, 1, one, x] = 1.0
    x = len(pairs) + FEAT
    coef[:, x] = 1.0
    pick[:, 0, one, x] = 1.0
    pick[:, 1, one, x] = 1.0
    shift = np.zeros((128, 128), np.float32)
    for i in range(2 * FEAT):
        shift[2 * FEAT + i, i] = 1.0
    return jnp.asarray(pick, BF16), jnp.asarray(coef, F32), jnp.asarray(shift, BF16)


def chunk_of(group, s):
    nhh = lax.axis_size("hh")
    return (group // nhh * 4 + s) * nhh + lax.rem(group, nhh)


def segment_of(starts, position):
    total = jnp.where(position >= starts[0], 0, -1)
    for i in range(1, starts.shape[0]):
        total = total + jnp.where(position >= starts[i], 1, 0)
    return total


class Segments:
    def __init__(self, starts, s):
        first = chunk_of(group_place(), s) * 256
        at = lambda shape, dim: first + lax.broadcasted_iota(jnp.int32, shape, dim)
        self.col = segment_of(starts, at((256, 1), 0))
        self.row = segment_of(starts, at((1, 256), 1))
        self.ext = segment_of(starts, at((1, 256 + RIM), 1) - RIM)
        self.last = segment_of(starts, first + 255)
        self.before = segment_of(starts, first - 1)


def carried(starts, s, st, sm, count, back):
    mine = chunk_of(group_place(), s)
    edge = segment_of(starts, mine * 256 + 255 if back else mine * 256 - 1)

    def group(i, both):
        def one(s2, both):
            state, total = both
            other = chunk_of(i, s2)
            reach = segment_of(starts, other * 256 - 1 if back else other * 256 + 255)
            ordered = other > mine if back else other < mine
            m = jnp.where(ordered & (reach == edge), 1.0, 0.0)
            return state + m * st[i, s2].astype(F32), total + m * sm[i, s2]

        return lax.fori_loop(s, 4, one, both) if back else lax.fori_loop(0, s + 1, one, both)

    return lax.fori_loop(
        0, count, group, (jnp.zeros((SROWS, 128), F32), jnp.zeros((8, 256), F32))
    )


def lanes(rows, width):
    return lax.broadcasted_iota(jnp.int32, (rows, width), 1)


class States:
    def __init__(self, count, st, sm, ssem, rsem):
        self.refs, self.ssem, self.rsem, self.count = (st, sm), ssem, rsem, count
        self.chain = count == 4 and chained()

    def copy(self, n, k, group, target):
        view = self.refs[n].at[group]
        return pltpu.make_async_remote_copy(
            src_ref=view, dst_ref=view, send_sem=self.ssem.at[n, k], recv_sem=self.rsem.at[n, group],
            device_id=target, device_id_type=MESH_ID,
        )

    def send(self):
        g, hh = group_place(), lax.axis_index("hh")
        for k in (2, 1, 3) if self.chain else range(1, self.count):
            for n in range(2):
                go = self.copy(n, k, g, group_peer(k, self.count)[3]).start
                if self.chain and k != 2:
                    pl.when(hh != (3 if k == 1 else 0))(go)
                else:
                    go()

    def got(self, n, group):
        view = self.refs[n].at[group]
        pltpu.make_async_copy(view, view, self.rsem.at[n, group]).wait()

    def sent(self, n, k):
        view = self.refs[n].at[0]
        pltpu.make_async_copy(view, view, self.ssem.at[n, k]).wait()

    def relay(self):
        if not self.chain:
            return
        hh = lax.axis_index("hh")
        far = lax.rem(hh + 2, 4)

        @pl.when((hh == 1) | (hh == 2))
        def _():
            for n in range(2):
                self.got(n, far)
                self.copy(n, 0, far, {"hh": 3 - far}).start()

    def arrive(self):
        g, hh = group_place(), lax.axis_index("hh")
        inner = (hh == 1) | (hh == 2)
        for k in range(1, self.count):
            other = lax.rem(g + k, self.count)
            for n in range(2):
                got = functools.partial(self.got, n, other)
                if self.chain and k == 2:
                    pl.when(jnp.logical_not(inner))(got)
                else:
                    got()

    def finish(self):
        hh = lax.axis_index("hh")
        for k in range(1, self.count):
            for n in range(2):
                sent = functools.partial(self.sent, n, k)
                if self.chain and k != 2:
                    pl.when(hh != (3 if k == 1 else 0))(sent)
                else:
                    sent()
                    if self.chain:
                        pl.when((hh == 1) | (hh == 2))(functools.partial(self.sent, n, 0))


def phi_of(x, pick, coef, t):
    left = matmul(x, pick[t, 0])
    right = matmul(x, pick[t, 1])
    return left, right, (left * right * coef).astype(BF16)


def taylor_forward_kernel(
    count, hooks, qkv, pick, coef_ref, shift, starts,
    o_ref, y_ref, den_ref, pre_ref, psum_ref, st, sm, phis, ssem, rsem,
):
    g = group_place()
    coef = coef_ref[0:1, :]
    left_half = lanes(256, 128) < 64

    def states(s, carry):
        rows = pl.ds(s * 256, 256)
        x = jnp.where(lanes(256, 128) == 4 * FEAT, jnp.ones((), BF16), qkv[rows, 0:128])
        v = qkv[rows, 128:256]
        seg = Segments(starts, s)
        tail = seg.col == seg.last
        v_tail = jnp.where(tail, v, jnp.zeros((), BF16))
        state = jnp.zeros((256, 128), F32)
        for h in range(2):
            _, _, phi_k = phi_of(x, pick, coef, 2 + h)
            side = left_half if h == 0 else jnp.logical_not(left_half)
            state += matmul_tn(phi_k, jnp.where(side, v_tail, jnp.zeros((), BF16)))
            total = jnp.sum(jnp.where(tail, phi_k.astype(F32), 0.0), axis=0, keepdims=True)
            sm[g, s, h : h + 1, :] = total
            _, _, phi_q = phi_of(x, pick, coef, h)
            phis[h][rows, 0:256] = phi_q
        st[g, s] = state[:SROWS].astype(BF16)
        return carry

    sm[g] = jnp.zeros((4, 8, 256), F32)
    lax.fori_loop(0, 4, states, 0)
    exchange = States(count, st, sm, ssem, rsem)
    exchange.send()
    hooks[0]()

    def inner(s, carry):
        rows = pl.ds(s * 256, 256)
        x = qkv[rows, 0:128]
        v = qkv[rows, 128:256]
        k = matmul(x, shift[...]).astype(BF16)
        lane = lanes(256, 128)
        order = lax.broadcasted_iota(jnp.int32, (256, 256), 0) >= lanes(256, 256)
        seg = Segments(starts, s)
        allowed = order & (seg.col == seg.row)
        num = jnp.zeros((256, 128), F32)
        dens = []
        for h in range(2):
            q = jnp.where(lane // FEAT == h, x, jnp.zeros((), BF16))
            dot = matmul_nt(q, k)
            score = jnp.where(allowed, 1.0 + dot * FEAT**-0.5 + dot * dot * (0.5 / FEAT), 0.0)
            side = left_half if h == 0 else jnp.logical_not(left_half)
            num += matmul(score.astype(BF16), jnp.where(side, v, jnp.zeros((), BF16)))
            dens.append(jnp.sum(score, axis=1, keepdims=True))
        y_ref[rows, :] = num
        den_ref[rows, :] = jnp.where(left_half, dens[0], dens[1])
        return carry

    lax.fori_loop(0, 4, inner, 0)
    exchange.relay()
    hooks[1]()
    exchange.arrive()
    hooks[2]()

    def finish(s, carry):
        rows = pl.ds(s * 256, 256)

        state, total = carried(starts, s, st, sm, count, False)
        state = state.astype(BF16)
        pre_ref[s] = state
        psum_ref[s] = total
        seg = Segments(starts, s)
        cont = seg.col == seg.before
        num = jnp.zeros((256, 128), F32)
        dens = []
        for h in range(2):
            phi_q = phis[h][rows, 0:256]
            side = left_half if h == 0 else jnp.logical_not(left_half)
            part = matmul(phi_q[:, :SROWS], state)
            num = jnp.where(side, part, num)
            dens.append(jnp.sum(phi_q.astype(F32) * total[h : h + 1], axis=1, keepdims=True))
        num = jnp.where(cont, num, 0.0) + y_ref[rows, :]
        den = jnp.where(cont, jnp.where(left_half, dens[0], dens[1]), 0.0) + den_ref[rows, :]
        y = num / den
        y_ref[rows, :] = y
        den_ref[rows, :] = den
        o_ref[rows, :] = y.astype(BF16)
        return carry

    lax.fori_loop(0, 4, finish, 0)
    hooks[3]()
    exchange.finish()


def taylor_backward_kernel(
    count, begin, qkv, do_ref, y_ref, den_ref, pre_ref, psum_ref,
    pick, coef_ref, shift, starts,
    out_ref, st, sm, acc, dnum_ref, ddens, ssem, rsem,
):
    g = group_place()
    for i in begin.early:
        begin.start(i)
    coef = coef_ref[0:1, :]
    left_half = lanes(256, 128) < 64
    zero = jnp.zeros((), BF16)

    def sides(h):
        return left_half if h == 0 else jnp.logical_not(left_half)

    def feature_back(dphi, left, right, t):
        grad = dphi * coef
        return matmul_nt((grad * right).astype(BF16), pick[t, 0]) + matmul_nt(
            (grad * left).astype(BF16), pick[t, 1]
        )

    def states(s, carry):
        rows = pl.ds(s * 256, 256)
        x = jnp.where(lanes(256, 128) == 4 * FEAT, jnp.ones((), BF16), qkv[rows, 0:128])
        do = do_ref[rows, :].astype(F32)
        den = den_ref[rows, :]
        dnum = do / den
        dnum_low = dnum.astype(BF16)
        dnum_ref[rows, :] = dnum_low
        weighted = dnum * y_ref[rows, :]
        seg = Segments(starts, s)
        cont = seg.col == seg.before
        d_cont = jnp.where(cont, dnum_low, zero)
        pre = pre_ref[s]
        state = jnp.zeros((256, 128), F32)
        grad = jnp.zeros((256, 128), F32)
        for h in range(2):
            dden = -jnp.sum(jnp.where(sides(h), weighted, 0.0), axis=1, keepdims=True)
            ddens[h, rows, :] = jnp.broadcast_to(dden, (256, 128))
            left, right, phi_q = phi_of(x, pick, coef, h)
            d_side = jnp.where(sides(h), d_cont, zero)
            state += matmul_tn(phi_q, d_side)
            dden_cont = jnp.where(cont, dden, 0.0)
            sm[g, s, h : h + 1, :] = jnp.sum(
                phi_q.astype(F32) * dden_cont, axis=0, keepdims=True
            )
            dphi = jnp.concatenate(
                [matmul_nt(d_side, pre), jnp.zeros((256, 256 - SROWS), F32)], axis=1
            ) + dden_cont * psum_ref[s, h : h + 1, :]
            grad += feature_back(dphi, left, right, h)
        st[g, s] = state[:SROWS].astype(BF16)
        acc[0, rows, :] = grad
        return carry

    sm[g] = jnp.zeros((4, 8, 256), F32)
    lax.fori_loop(0, 4, states, 0)
    exchange = States(count, st, sm, ssem, rsem)
    exchange.send()
    begin.late()

    def inner(s, carry):
        rows = pl.ds(s * 256, 256)
        x = qkv[rows, 0:128]
        v = qkv[rows, 128:256]
        dnum = dnum_ref[rows, :]
        k_low = matmul(x, shift[...]).astype(BF16)
        lane = lanes(256, 128)
        order = lax.broadcasted_iota(jnp.int32, (256, 256), 0) >= lanes(256, 256)
        seg = Segments(starts, s)
        allowed = order & (seg.col == seg.row)
        dq = jnp.zeros((256, 128), F32)
        dk = jnp.zeros((256, 128), F32)
        dv = jnp.zeros((256, 128), F32)
        for h in range(2):
            mine = lane // FEAT == h
            q = jnp.where(mine, x, zero)
            dot = matmul_nt(q, k_low)
            score = jnp.where(allowed, 1.0 + dot * FEAT**-0.5 + dot * dot * (0.5 / FEAT), 0.0)
            d_side = jnp.where(sides(h), dnum, zero)
            dscore = matmul_nt(d_side, v) + ddens[h, rows, 0:1]
            e = jnp.where(allowed, dscore * (FEAT**-0.5 + dot * (1.0 / FEAT)), 0.0).astype(BF16)
            dq += matmul(e, jnp.where(mine, k_low, zero))
            dk += matmul_tn(e, q)
            dv += matmul_tn(score.astype(BF16), d_side)
        acc[0, rows, :] += dq
        acc[1, rows, :] = dk
        acc[2, rows, :] = dv
        return carry

    lax.fori_loop(0, 4, inner, 0)
    exchange.relay()
    begin.relay(*begin.early)
    exchange.arrive()

    def finish(s, carry):
        rows = pl.ds(s * 256, 256)

        state, total = carried(starts, s, st, sm, count, True)
        state = state.astype(BF16)
        x = jnp.where(lanes(256, 128) == 4 * FEAT, jnp.ones((), BF16), qkv[rows, 0:128])
        seg = Segments(starts, s)
        tail = seg.col == seg.last
        v_tail = jnp.where(tail, qkv[rows, 128:256], zero)
        grad = acc[0, rows, :]
        lane = lanes(256, 128)
        dv = jnp.zeros((256, 128), F32)
        for h in range(2):
            left, right, phi_k = phi_of(x, pick, coef, 2 + h)
            dphi = jnp.concatenate(
                [
                    matmul_nt(jnp.where(sides(h), v_tail, zero), state),
                    jnp.zeros((256, 256 - SROWS), F32),
                ],
                axis=1,
            ) + jnp.where(tail, total[h : h + 1], 0.0)
            grad += feature_back(dphi, left, right, 2 + h)
            dv = jnp.where(sides(h), matmul(phi_k[:, :SROWS], state), dv)
        grad += matmul_nt(acc[1, rows, :].astype(BF16), shift[...])
        dv = jnp.where(tail, dv, 0.0) + acc[2, rows, :]
        out_ref[rows, 0:128] = jnp.where(lane < 4 * FEAT, grad, 0.0).astype(BF16)
        out_ref[rows, 128:256] = dv.astype(BF16)
        return carry

    lax.fori_loop(0, 4, finish, 0)
    exchange.finish()


def taylor_backward(qkv, do, kept, starts, tables, jobs, count, collective):
    return step(
        functools.partial(taylor_backward_kernel, count),
        vmem(qkv, do, *kept, *tables) + [(starts, SMEM)],
        vmem(jax.ShapeDtypeStruct((1024, 256), BF16)),
        [
            VM((count, 4, SROWS, 128), BF16),
            VM((count, 4, 8, 256), F32),
            VM((3, 1024, 128), F32),
            VM((1024, 128), BF16),
            VM((2, 1024, 128), F32),
            pltpu.SemaphoreType.DMA((2, count)),
            pltpu.SemaphoreType.DMA((2, count)),
        ],
        jobs, 0, True, "taylor_backward", collective, 28, early=range(len(jobs)),
    )


def rim_target(s, forward):
    hh, sh = lax.axis_index("hh"), lax.axis_index("sh")
    nhh, nsh = lax.axis_size("hh"), lax.axis_size("sh")
    if forward:
        wraps = jnp.where(hh == nhh - 1, 1, 0)
        slot = lax.rem(s + wraps, 4)
        leaves = wraps if s == 3 else 0
        return {"sh": lax.rem(sh + leaves, nsh), "hh": lax.rem(hh + 1, nhh)}, slot
    wraps = jnp.where(hh == 0, 1, 0)
    slot = lax.rem(s + 4 - wraps, 4)
    leaves = wraps if s == 0 else 0
    return {"sh": lax.rem(sh + nsh - leaves, nsh), "hh": lax.rem(hh + nhh - 1, nhh)}, slot


def window_mask(starts, s):
    seg = Segments(starts, s)
    i = lax.broadcasted_iota(jnp.int32, (256, 256 + RIM), 0)
    j = lanes(256, 256 + RIM)
    return (j > i) & (j <= i + WINDOW) & (seg.col == seg.ext)


def window_probs(q, k, allowed):
    scores = jnp.where(allowed, matmul_nt(q, k) * 64**-0.5, -1e30)
    peak = jnp.max(scores, axis=1, keepdims=True)
    weights = jnp.exp(scores - peak)
    return weights / jnp.sum(weights, axis=1, keepdims=True)


def window_forward_kernel(begin, qkv, starts, o_ref, ext, rim, ssem, rsem):
    cps = []
    for s in range(4):
        target, slot = rim_target(s, True)
        src = qkv.at[pl.ds(s * 256 + 256 - RIM, RIM), pl.ds(128, 256)]
        cps.append(remote(src, rim.at[slot], ssem.at[s], rsem.at[slot], target))

    def fill(s, carry):
        ext[s, RIM:, :] = qkv[pl.ds(s * 256, 256), 128:384]
        return carry

    lax.fori_loop(0, 4, fill, 0)
    for s in range(4):
        pltpu.make_async_copy(rim.at[s], rim.at[s], rsem.at[s]).wait()
    begin()

    def run(s, carry):
        rows = pl.ds(s * 256, 256)
        ext[s, :RIM, :] = rim[s]
        q = qkv[rows, 0:128]
        k = ext[s, :, 0:128]
        v = ext[s, :, 128:256]
        left_half = lanes(256, 128) < 64
        allowed = window_mask(starts, s)
        out = jnp.zeros((256, 128), F32)
        for h in range(2):
            side = left_half if h == 0 else jnp.logical_not(left_half)
            probs = window_probs(jnp.where(side, q, jnp.zeros((), BF16)), k, allowed)
            out = jnp.where(side, matmul(probs.astype(BF16), v), out)
        o_ref[rows, :] = out.astype(BF16)
        return carry

    lax.fori_loop(0, 4, run, 0)
    for cp in cps:
        cp.wait_send()


def window_backward_kernel(
    begin, qkv, ext, do_ref, part, u_ref, att_ref, up_full, starts, out_ref, mixed, out_w,
    acc, back, rim,
    ssem, rsem, own, cb, sb, keep, r1, r2, ss, rs,
):
    total = RowSum(part, own, cb, sb, keep, r1, r2, ss, rs)
    for k in range(4):
        total.core(k)
    zero = jnp.zeros((), BF16)

    def run(s, carry):
        rows = pl.ds(s * 256, 256)
        q = qkv[rows, 0:128]
        k = ext[s, :, 0:128]
        v = ext[s, :, 128:256]
        do = do_ref[rows, :]
        left_half = lanes(256, 128) < 64
        left_ext = lanes(256 + RIM, 128) < 64
        allowed = window_mask(starts, s)
        dq = jnp.zeros((256, 128), F32)
        dk = jnp.zeros((256 + RIM, 128), F32)
        dv = jnp.zeros((256 + RIM, 128), F32)
        for h in range(2):
            side = left_half if h == 0 else jnp.logical_not(left_half)
            q_h = jnp.where(side, q, zero)
            do_h = jnp.where(side, do, zero)
            probs = window_probs(q_h, k, allowed)
            dprobs = matmul_nt(do_h, v)
            inner = jnp.sum(probs * dprobs, axis=1, keepdims=True)
            ds = (probs * (dprobs - inner)).astype(BF16)
            dq = jnp.where(side, matmul(ds, k), dq)
            dk += matmul_tn(ds, q_h)
            dv += matmul_tn(probs.astype(BF16), do_h)
        scale = 64**-0.5
        dk = dk * scale
        out_ref[rows, 0:128] = (dq * scale).astype(BF16)
        acc[rows, 0:128] = dk[RIM:]
        acc[rows, 128:256] = dv[RIM:]
        back[s, :, 0:128] = dk[:RIM].astype(BF16)
        back[s, :, 128:256] = dv[:RIM].astype(BF16)
        return carry

    for k in range(4):
        total.push(k)
    lax.fori_loop(0, 4, run, 0)
    cps = []
    for s in range(4):
        target, slot = rim_target(s, False)
        cps.append(remote(back.at[s], rim.at[slot], ssem.at[s], rsem.at[slot], target))
    for i in range(4):
        at = slice(i * 256, i * 256 + 256)
        rhs = up_full[:, :, :, :, at].reshape(1024, 256)
        value = matmul_tn(att_ref[...], rhs).astype(BF16)
        if len(out_w.shape) == 3:
            out_w[:, :, at] = value.reshape(out_w.shape[:2] + (256,))
        else:
            out_w[:, at] = value
    total.relay()
    begin[1]()
    for s in range(4):
        pltpu.make_async_copy(rim.at[s], rim.at[s], rsem.at[s]).wait()
    begin[0]()

    def finish(s, carry):
        out_ref[pl.ds(s * 256, 256 - RIM), 128:384] = acc[pl.ds(s * 256, 256 - RIM), :].astype(BF16)
        rows = pl.ds(s * 256 + 256 - RIM, RIM)
        out_ref[rows, 128:384] = (acc[rows, :] + rim[s].astype(F32)).astype(BF16)
        return carry

    lax.fori_loop(0, 4, finish, 0)
    total.finish()
    for half in range(2):
        mixed[half] = (u_ref[half] + own[half]).astype(BF16)
    for cp in cps:
        cp.wait_send()


def front(x_own, cot_own, tables, starts, jobs, count, ff, width, collective):
    ship = shipping()
    terms = terms_shape(ff)
    vector = jax.ShapeDtypeStruct((8, D), F32)
    rowset = jax.ShapeDtypeStruct((4, D // 32, D) if ship else (128, D), BF16)
    makers = ("down_b", "gate_b", "up_b", "win", "down_a", "gate_a", "up_a")

    def body(
        begin, x_own, cot_own, pick, coef, shift, starts,
        mixed, g_ha, gg, do_a, lo_w, wo_w, qkv_a, y_a, den_a, pre, psum, w_lin, gains, x_out, n_out, *rest
    ):
        n_terms = 1 + (4 if ship else 6)
        weights, rest = rest[:n_terms], rest[n_terms:]
        made = dict(zip(("up_a",) + makers[:-1], weights))
        if ship:
            made["down_a"], made["gate_a"] = made["down_b"], made["gate_b"]
        h_a, out_a, h_b, g_hb, g_oa = rest[:5]
        na2, nb1, nb2, full1, part1, part2, cot = rest[5:12]
        full2, part3 = nb2, part1
        qkv, ext, o_b, do_b, dqkv, acc, back, rim1, rim2 = rest[12:21]
        gate_s, up_s, hid_s, hid_t, dgate, dup = rest[21:27]
        o_a, st, sm = rest[27:30]
        rest = rest[30:]
        set1, set2 = rest[:8], rest[8:16]
        ag = [rest[16 + 2 * i : 18 + 2 * i] for i in range(8)]
        rims = rest[32:36]
        states, out_sem = rest[36:38], rest[38]
        me, c = plane_place()[0], plane_place()[4]

        def call(name, *args):
            return functools.partial(getattr(begin, name), *args)

        def ship_terms(name):
            if ship:
                begin.start(name + "_t", made[name])

        def send_on(name):
            if ship:
                begin.wait(name + "_t")
                begin.start(name + "_p", begin.result(name + "_t"))

        def relay(*names):
            if ship:
                begin.relay(*[name + "_t" for name in names])

        def norm_own(total, before, after, full, gain):
            for half in range(2):
                u = before[half].astype(F32) + total.own[half]
                after[half] = u
                full[me, c, half] = normed_half(u, gains[gain : gain + 1])

        def start_all(*names):
            for name in names:
                begin.start(name)

        def spread_on(name):
            begin.wait(name + "_m")
            begin.start(name, begin.result(name + "_m"))

        begin.start("lin_m")
        start_all("lin_out", "win_out")
        nb1[me, c] = x_own[...]
        rows_in = RowGather(nb1, *ag[6])
        rows_in.start()
        begin.start("gate_a_m")
        spread_on("lin")
        rows_in.hop1()
        rows_in.hop2()
        rows_in.hop3()
        start_all("up_a_m", "down_a_m")
        rows_in.arrived(0, 6, 8, 9, 10, 11, 12)
        rows_in.finish()
        begin.relay("lin")
        spread_on("gate_a")
        begin.wait("lin")
        w_lin[...] = begin.columns("lin")
        gains[...] = w_lin[:, :128].astype(F32).T[64:72]
        lane = lanes(D, width)
        w_lin[...] = jnp.where((lane < 64) | (lane >= 128), w_lin[...], jnp.zeros((), BF16))

        def project_a(block, carry):
            n = normed_half(chip_rows(nb1, block).astype(F32), gains[0:1])
            put_chip(part2, block, n)
            qkv_a[rows_of(block), :] = matmul(n, w_lin[...]).astype(BF16)
            return carry

        cot[me, c] = cot_own[...]
        cot_in = RowGather(cot, *ag[7])
        cot_in.start()
        lax.fori_loop(0, 4, project_a, 0)
        kept = [
            pltpu.make_async_copy(nb1, x_out, out_sem.at[0]),
            pltpu.make_async_copy(part2, n_out, out_sem.at[1]),
        ]
        for cp in kept:
            cp.start()

        def states_sent():
            spread_on("up_a")
            cot_in.hop1()
            start_all("win_m", "gate_b_m", "up_b_m", "down_b_m")

        def inner_done():
            cot_in.hop2()
            cot_in.hop3()
            begin.relay("gate_a")

        def states_in():
            spread_on("down_a")

        def taylor_done():
            cot_in.arrived(0, 6, 8, 9, 10, 11, 12)
            cot_in.finish()
            for cp in kept:
                cp.wait()

        taylor_forward_kernel(
            count, (states_sent, inner_done, states_in, taylor_done), qkv_a, pick, coef, shift, starts,
            o_a, y_a, den_a, pre, psum, st, sm, (hid_t, dgate), *states,
        )
        begin.relay("up_a")
        begin.wait("lin_out")
        wlo = begin.result("lin_out")
        total = RowSum(part1, *set1)

        def attended_a(block):
            put_chip(part1, block, matmul(o_a[rows_of(block), :], wlo[...].reshape(128, D)))

        total.run(attended_a)
        norm_own(total, x_own, h_a, na2, 1)
        begin.wait("gate_a")
        begin.relay("down_a")
        total2, seen = RowSum(part2, *set2), []

        def mlp_a(block):
            n = chip_rows(na2, block)
            if not seen:
                begin.wait("up_a")
            gate, up = matmul(n, begin.columns("gate_a")), matmul(n, begin.columns("up_a"))
            hidden = (silu_parts(gate)[1] * up).astype(BF16)
            rows = rows_of(block)
            gate_s[rows, :] = gate.astype(BF16)
            up_s[rows, :] = up.astype(BF16)
            hid_s[rows, :] = hidden
            if not seen:
                begin.wait("down_a")
                spread_on("win")
                spread_on("gate_b")
            put_chip(part2, block, matmul_nt(hidden, begin.columns("down_a")))
            follow(total2, seen)

        RowGather(na2, *ag[0]).run(mlp_a)
        spread_on("up_b")
        total2.relay()
        total2.finish()
        norm_own(total2, h_a, out_a, nb1, 2)

        def project(block):
            if not gotten:
                begin.wait("win")
                gotten.append(1)
            qkv[rows_of(block), :] = matmul(chip_rows(nb1, block), begin.columns("win")).astype(BF16)

        gotten = []
        RowGather(nb1, *ag[1]).run(project)
        begin.relay("gate_b")

        def rims_in():
            spread_on("down_b")

        window_forward_kernel(rims_in, qkv, starts, o_b, ext, rim1, *rims[:2])
        begin.wait("win_out")
        wwo = begin.result("win_out")
        total = RowSum(part1, *set1)

        def attended_b(block):
            put_chip(part1, block, matmul(o_b[rows_of(block), :], wwo[...].reshape(128, D)))

        total.run(attended_b)
        norm_own(total, out_a, h_b, nb2, 3)
        begin.relay("up_b", "down_b")
        total2, seen_b = RowSum(part2, *set2), []

        def mlp_b(block):
            rows = rows_of(block)
            n = chip_rows(nb2, block)
            if not seen_b:
                begin.wait("gate_b", "up_b", "down_b")
            wg, wu, wd = (begin.columns(name) for name in ("gate_b", "up_b", "down_b"))
            gate, up = matmul(n, wg), matmul(n, wu)
            sig, act = silu_parts(gate)
            hidden = (act * up).astype(BF16)
            hid_t[rows, :] = hidden
            dhidden = matmul(chip_rows(cot, block), wd)
            dg = (dhidden * up * (sig + act * (1.0 - sig))).astype(BF16)
            du = (dhidden * act).astype(BF16)
            dgate[rows, :] = dg
            dup[rows, :] = du
            put_chip(part2, block, matmul_nt(dg, wg) + matmul_nt(du, wu))
            follow(total2, seen_b)
            put_chip(part3, block, matmul_nt(hidden, wd))

        RowGather(nb2, *ag[2]).run(mlp_b)
        for job in weight_grads(cot, hid_t, made["down_b"]):
            job()
        ship_terms("down_b")
        total2.relay()
        for job in weight_grads(nb2, dgate, made["gate_b"]):
            job()
        ship_terms("gate_b")
        total2.finish()
        back_own(total2.own, h_b, gains[3:4], cot_own, g_hb, gg.at[2:3], full1)

        def output_grad_b(block):
            do_b[rows_of(block), :] = matmul_nt(
                chip_rows(full1, block), wwo[...].reshape(128, D)
            ).astype(BF16)

        RowGather(full1, *ag[3]).run(
            output_grad_b,
            weight_grads(nb2, dup, made["up_b"]) + [functools.partial(relay, "down_b")],
        )

        def window_begin():
            ship_terms("up_b")

        def window_mid():
            relay("gate_b")
            send_on("down_b")

        window_backward_kernel(
            (window_begin, window_mid), qkv, ext, do_b, part3, h_b, o_b, full1, starts,
            dqkv, mixed, wo_w, acc, back, rim2, *rims[2:4], *set1,
        )
        relay("up_b")
        if ship:
            begin.start("win_out_v", wo_w)
        total = RowSum(part1, *set2)

        def projected(block):
            put_chip(part1, block, matmul_nt(dqkv[rows_of(block), :], begin.columns("win")))

        total.run(projected, weight_grads(nb1, dqkv, made["win"]))
        ship_terms("win")
        back_own(total.own, out_a, gains[2:3], g_hb, g_oa, gg.at[1:2], full2)
        total2, seen_a = RowSum(part2, *set1), []

        def mlp_back(block):
            rows = rows_of(block)
            sig, act = silu_parts(gate_s[rows, :].astype(F32))
            dhidden = matmul(chip_rows(full2, block), begin.columns("down_a"))
            dg = (dhidden * up_s[rows, :].astype(F32) * (sig + act * (1.0 - sig))).astype(BF16)
            du = (dhidden * act).astype(BF16)
            dgate[rows, :] = dg
            dup[rows, :] = du
            put_chip(part2, block, matmul_nt(dg, begin.columns("gate_a")) + matmul_nt(du, begin.columns("up_a")))
            follow(total2, seen_a)

        RowGather(full2, *ag[4]).run(mlp_back)
        for job in weight_grads(full2, hid_s, made["down_a"]):
            job()
        ship_terms("down_a")
        send_on("gate_b")
        total2.relay()
        for job in weight_grads(na2, dgate, made["gate_a"]):
            job()
        ship_terms("gate_a")
        total2.finish()
        back_own(total2.own, h_a, gains[1:2], g_oa, g_ha, gg.at[0:1], full1)

        def output_grad_a(block):
            do_a[rows_of(block), :] = matmul_nt(
                chip_rows(full1, block), wlo[...].reshape(128, D)
            ).astype(BF16)

        def output_weight(i):
            at = slice(i * 256, i * 256 + 256)
            rhs = full1[:, :, :, :, at].reshape(1024, 256)
            lo_w[:, at] = matmul_tn(o_a[...], rhs).astype(BF16)

        RowGather(full1, *ag[5]).run(
            output_grad_a,
            weight_grads(na2, dup, made["up_a"])
            + [functools.partial(send_on, "up_b"), functools.partial(relay, "win", "down_a")],
        )
        for i in range(4):
            output_weight(i)
        send_on("win")
        send_on("down_a")

    rows16 = lambda *shape: VM(shape, BF16)
    rows16s = lambda *shape: jax.ShapeDtypeStruct(shape, BF16)
    OWN_ROWS = jax.ShapeDtypeStruct((1024, 128), F32)
    n_held = 6
    summed = jax.ShapeDtypeStruct((4, 2, D // (8 * lax.axis_size(GROUP)), ff), BF16)
    late = []
    if ship:
        late = [Job("zs", terms, name=m + "_t", held=m != "gate_a") for m in makers[:-1]]
        late += [Job("pa", summed, name=m + "_p") for m in makers[:-2]] + [Job("zv", rowset, name="win_out_v")]
    sem = lambda n: pltpu.SemaphoreType.DMA((n,))
    weights = [VM(terms.shape, BF16)] * 4 if ship else []
    outs, moved = step(
        body,
        vmem(x_own, cot_own, *tables) + [(starts, SMEM)],
        vmem(
            jax.ShapeDtypeStruct((2, 64, D), BF16), OWN, vector, jax.ShapeDtypeStruct((1024, 128), BF16),
            jax.ShapeDtypeStruct((128, D), BF16),
            rowset, rows16s(1024, width), OWN_ROWS, OWN_ROWS, rows16s(4, SROWS, 128),
            jax.ShapeDtypeStruct((4, 8, 256), F32), rows16s(D, width), jax.ShapeDtypeStruct((8, D), F32),
        )
        + [(FULL, ANY), (FULL, ANY)]
        + vmem(terms)
        + ([] if ship else vmem(*[terms] * n_held)),
        weights + [VM((2, 64, D), F32)] * 5 + [VM(FULL.shape, BF16)] * 7
        + [
            rows16(1024, 384), rows16(4, 256 + RIM, 256), rows16(1024, 128), rows16(1024, 128),
            rows16(1024, 384), VM((1024, 256), F32), rows16(4, RIM, 256), rows16(4, RIM, 256),
            rows16(4, RIM, 256),
        ]
        + [rows16(1024, ff)] * 6
        + [rows16(1024, 128), VM((count, 4, SROWS, 128), BF16), VM((count, 4, 8, 256), F32)]
        + rs_scratch() + rs_scratch() + ag_scratch() * 8 + [sem(4)] * 4
        + [pltpu.SemaphoreType.DMA((2, count + 1))] * 2 + [sem(2)],
        jobs + late, 7, True, "front", collective, 300,
    )
    return outs, moved


def row_routes():
    nsh, nhh = lax.axis_size("sh"), lax.axis_size("hh")
    groups = nsh * nhh
    routes = []
    for d in range(8 * groups):
        place, group = d // groups, d % groups
        s, c = place // 2, place % 2
        sh, hh = group // nhh, group % nhh
        routes.append((d, ((sh * 4 + s) * nhh + hh) * 2 + c))
    return routes


def spread_ff(member):
    rows = member.shape[0]
    width = -(-member.shape[1] // (NTP * 128)) * 128
    padded = jnp.pad(member, ((0, 0), (0, NTP * width - member.shape[1])))
    return padded.reshape(rows, NTP, width)


def on_device(
    layer_input, lengths, gain_a1, lin_q, lin_k, lin_v, lin_out, gain_a2, mlp_a_gate, mlp_a_up,
    mlp_a_down, gain_b1, win_q, win_k, win_v, win_out, gain_b2, mlp_b_gate, mlp_b_up, mlp_b_down,
    cotangent,
):
    count = lax.axis_size(GROUP)
    rows = lin_q.shape[0]
    hidden_size = mlp_a_gate.shape[1]
    gains = jnp.pad(jnp.stack([gain_a1, gain_a2, gain_b1, gain_b2], axis=1), ((0, 0), (0, 60)))
    gains = jnp.broadcast_to(gains[:, None, :], (rows, NTP, 64))
    starts = jnp.cumsum(lengths) - lengths
    tables = taylor_tables()

    split = lambda member: member.reshape(rows, NTP, -1)
    bundle_lin = jnp.concatenate(
        [split(lin_q), split(lin_k), gains, split(lin_v)], axis=-1
    ).transpose(1, 0, 2)
    bundle_a = jnp.concatenate(
        [spread_ff(mlp_a_gate), spread_ff(mlp_a_up), spread_ff(mlp_a_down.T)], axis=-1
    ).transpose(1, 0, 2)
    bundle_win = jnp.concatenate([split(win_q), split(win_k), split(win_v)], axis=-1).transpose(
        1, 0, 2
    )
    bundle_b = jnp.concatenate(
        [spread_ff(mlp_b_gate), spread_ff(mlp_b_up), spread_ff(mlp_b_down.T)], axis=-1
    ).transpose(1, 0, 2)
    ff = bundle_a.shape[-1] // 3
    width = bundle_lin.shape[-1]
    nsh, nhh = lax.axis_size("sh"), lax.axis_size("hh")
    places = lambda a: a.reshape(4, 2, rows, a.shape[-1])
    whole = lambda a: a.reshape(D, a.shape[-1])
    total = lambda a: jnp.sum(a.astype(F32), axis=0).astype(BF16)
    ship = shipping()
    if ship:
        own_rows = lambda a, **kw: Job("zw", a, **kw)
    else:
        own_rows = lambda a, **kw: Job("zr", lax.ppermute(a, AXES, row_routes()), **kw)

    x_own = layer_input.reshape(2, 64, D)
    cot_own = cotangent.reshape(2, 64, D)
    def column(name, a):
        return [
            Job("pa", a, name=name + "_m"),
            Job("zg", jax.ShapeDtypeStruct(a.shape, BF16), VMEM, name, True),
        ]

    third = lambda a, i: places(a[:, :, i * ff : i * ff + ff])
    jobs = [
        column("lin", places(bundle_lin)), column("gate_a", third(bundle_a, 0)),
        column("up_a", third(bundle_a, 1)), column("down_a", third(bundle_a, 2)),
        column("win", places(bundle_win)), column("gate_b", third(bundle_b, 0)),
        column("up_b", third(bundle_b, 1)), column("down_b", third(bundle_b, 2)),
        [own_rows(lin_out, spec=VMEM, name="lin_out", held=True)],
        [own_rows(win_out, spec=VMEM, name="win_out", held=True)],
    ]
    outs, moved = front(x_own, cot_own, tables, starts, sum(jobs, []), count, ff, width, 1)
    mixed, grad_h_a, gg, do_a, grad_lin_out, grad_win_out = outs[:6]
    qkv_a, y_a, den_a, pre, psum, w_lin, gains, x_full, n_a1, up_a = outs[6:16]
    kept, apart_terms, moved = (y_a, den_a, pre, psum), outs[16:], moved[8:]
    if ship:
        gate_a, down_b, gate_b, up_b, win, down_a, win_out_t = moved
        late = [Job("pa", gate_a), Job("zs", up_a)]
    else:
        sums = apart(apart_terms, 10)
        _, moved = step(
            lambda begin: None, [], [], [], [Job("pa", a) for a in sums[:5]]
            + [Job("zt", grad_win_out.reshape(count, -1, D))], 7, True, "spread", 11, 20,
        )
        down_b, gate_b, up_b, win, down_a, win_out_t = moved
        late = [Job("pa", sums[5])]
        (up_a,) = apart([up_a], 14)
    (dqkv_a,), (gate_a, *more) = taylor_backward(qkv_a, do_a, kept, starts, tables, late, count, 8)
    (up_a,) = more if ship else (up_a,)
    rows_back = Job("zv", grad_lin_out.reshape(4, rows, D)) if ship else Job(
        "zt", grad_lin_out.reshape(count, -1, D)
    )
    grad_input, (lin_out_t, up_a), lin_g = last_layer(
        dqkv_a, w_lin, x_own, gains[0:1], grad_h_a, x_full, n_a1, gg[0:3], [rows_back, Job("pa", up_a)], 9,
    )

    def joined(a, lo, hi):
        a = a.reshape(NTP, rows, -1)[:, :, lo:hi].astype(F32)
        return a.transpose(1, 0, 2).reshape(rows, -1)

    def unpack_mlp(gate, up, down):
        joined_ff = lambda a: joined(a, 0, ff)[:, :hidden_size]
        return joined_ff(gate), joined_ff(up), joined_ff(down).T

    gate_b_g, up_b_g, down_b_g = unpack_mlp(gate_b, up_b, down_b)
    gate_a_g, up_a_g, down_a_g = unpack_mlp(gate_a, up_a, down_a)
    def own_terms(a):
        if ship:
            return jnp.sum(a.astype(F32), axis=0)
        return lax.ppermute(total(a), AXES, [(d, e) for e, d in row_routes()]).astype(F32)

    win_out_g, lin_out_g = own_terms(win_out_t), own_terms(lin_out_t)
    gg = jnp.sum(lin_g.reshape(NTP, rows, width)[:, :, 64:68].astype(F32), axis=0)
    return (
        mixed.reshape(128, D),
        grad_input.reshape(128, D),
        gg[:, 0],
        joined(lin_g, 0, 32),
        joined(lin_g, 32, 64),
        joined(lin_g, 128, 256),
        lin_out_g,
        gg[:, 1],
        gate_a_g,
        up_a_g,
        down_a_g,
        gg[:, 2],
        joined(win, 0, 128),
        joined(win, 128, 256),
        joined(win, 256, 384),
        win_out_g,
        gg[:, 3],
        gate_b_g,
        up_b_g,
        down_b_g,
    )


def solution(mesh):
    seq, head = mesh.devices.shape
    fine = Mesh(mesh.devices.reshape(seq // 4, 2, 2, head // 2, 2), AXES)
    row, vec, col = P(AXES, None), P(AXES), P(None, AXES)
    placed = (
        row, P(), vec, row, row, row, row, vec, row, row, col,
        vec, row, row, row, row, vec, row, row, col, row,
    )
    out = (
        row, row, vec, row, row, row, row, vec, row, row, col,
        vec, row, row, row, row, vec, row, row, col,
    )
    return jax.shard_map(on_device, mesh=fine, in_specs=placed, out_specs=out, check_vma=False)
```

```python
import functools

import jax
import jax.numpy as jnp
import numpy as np
from jax import lax
from jax.experimental import pallas as pl
from jax.experimental.pallas import tpu as pltpu
from jax.sharding import Mesh
from jax.sharding import PartitionSpec as P

D = 1024
HEADS = 16
FEAT = 16
WINDOW = 64
NTP = 8
RIM = 64
SROWS = 160
EPSILON = 1e-05
AXES = ("sh", "sy", "sx", "hh", "hl")
TP = ("sy", "sx", "hl")
GROUP = ("sh", "hh")
MESH_ID = pl.DeviceIdType.MESH
F32 = jnp.float32
BF16 = jnp.bfloat16
VM = pltpu.VMEM
LIMIT = 60 * 1024 * 1024


def vmem_specs(count):
    return [pl.BlockSpec(memory_space=pltpu.VMEM)] * count


def matmul(left, right):
    return jnp.dot(left, right, preferred_element_type=F32)


def matmul_tn(left, right):
    return lax.dot_general(left, right, (((0,), (0,)), ((), ())), preferred_element_type=F32)


def matmul_nt(left, right):
    return lax.dot_general(left, right, (((1,), (1,)), ((), ())), preferred_element_type=F32)


def plane_place():
    sy, sx, c = lax.axis_index("sy"), lax.axis_index("sx"), lax.axis_index("hl")
    me = sy * 2 + sx
    xn = sy * 2 + (1 - sx)
    yn = (1 - sy) * 2 + sx
    dg = 3 - me
    return me, xn, yn, dg, c, {"sx": 1 - sx}, {"sy": 1 - sy}, {"hl": 1 - c}


def remote(src, dst, ssem, rsem, target):
    copy = pltpu.make_async_remote_copy(
        src_ref=src, dst_ref=dst, send_sem=ssem, recv_sem=rsem, device_id=target, device_id_type=MESH_ID
    )
    copy.start()
    return copy


AG_COPIES = 13
RS_COPIES = 10


class RowGather:
    def __init__(self, full, ssem, rsem):
        self.full, self.ssem, self.rsem = full, ssem, rsem
        self.place = plane_place()
        self.cps = {}

    def send(self, k, block, half, target):
        view = self.full.at[block, self.place[4], half]
        self.cps[k] = remote(view, view, self.ssem.at[k], self.rsem.at[k], target)

    def start(self):
        me, _, _, _, c, to_x, to_y, to_c = self.place
        self.send(1, me, 0, to_x)
        self.send(3, me, 1, to_y)
        self.send(2, me, 1, to_x)
        self.send(4, me, 0, to_y)
        own = self.full.at[me, c]
        self.cps[0] = remote(own, own, self.ssem.at[0], self.rsem.at[0], to_c)

    def arrived(self, *keys):
        for k in keys:
            self.cps[k].wait_recv()

    def hop1(self):
        _, xn, yn, _, _, to_x, to_y, to_c = self.place
        self.arrived(1)
        self.send(5, xn, 0, to_y)
        self.send(6, xn, 0, to_c)
        self.arrived(3)
        self.send(7, yn, 1, to_x)
        self.send(8, yn, 1, to_c)

    def hop2(self):
        _, xn, yn, _, _, _, _, to_c = self.place
        self.arrived(2)
        self.send(9, xn, 1, to_c)
        self.arrived(4)
        self.send(10, yn, 0, to_c)

    def hop3(self):
        _, _, _, dg, _, _, _, to_c = self.place
        self.arrived(5)
        self.send(11, dg, 0, to_c)
        self.arrived(7)
        self.send(12, dg, 1, to_c)

    def finish(self):
        for k in range(AG_COPIES):
            self.cps[k].wait_send()

    def run(self, consume, spare=()):
        me, xn, yn, dg = self.place[:4]
        spare = list(spare)

        def fill(most):
            for _ in range(min(most, len(spare))):
                spare.pop(0)()

        self.start()
        self.arrived(0)
        consume(me)
        fill(3)
        self.hop1()
        fill(2)
        self.hop2()
        self.arrived(6, 9)
        consume(xn)
        fill(2)
        self.hop3()
        self.arrived(8, 10)
        consume(yn)
        self.arrived(11, 12)
        consume(dg)
        fill(len(spare))
        self.finish()


class RowSum:
    def __init__(self, part, own, cb, sb, keep, r1, r2, ssem, rsem):
        self.part, self.own, self.cb, self.sb, self.keep = part, own, cb, sb, keep
        self.r1, self.r2, self.ssem, self.rsem = r1, r2, ssem, rsem
        self.place = plane_place()
        self.cps = {}

    def block(self, k):
        me, xn, yn, dg = self.place[:4]
        return (dg, xn, yn, me)[k]

    def copy(self, k, src, dst, target):
        self.cps[k] = remote(src, dst, self.ssem.at[k], self.rsem.at[k], target)

    def core(self, k):
        src = self.part.at[self.block(k), 1 - self.place[4]]
        self.copy(k, src, self.cb.at[k], self.place[7])

    def both(self, k, half):
        mine = self.part[self.block(k), self.place[4], half]
        return mine.astype(F32) + self.cb[k, half].astype(F32)

    def push(self, k):
        to_x, to_y = self.place[5:7]
        sb, r1 = self.sb, self.r1
        self.cps[k].wait_recv()
        if k == 0:
            sb[0, 0] = self.both(0, 0).astype(BF16)
            self.copy(4, sb.at[0, 0], r1.at[0, 0], to_x)
            sb[0, 1] = self.both(0, 1).astype(BF16)
            self.copy(5, sb.at[0, 1], r1.at[1, 0], to_y)
        if k == 1:
            sb[1, 0] = self.both(1, 0).astype(BF16)
            self.copy(6, sb.at[1, 0], r1.at[0, 1], to_x)
            self.keep[1] = self.both(1, 1)
        if k == 2:
            sb[2, 1] = self.both(2, 1).astype(BF16)
            self.copy(7, sb.at[2, 1], r1.at[1, 1], to_y)
            self.keep[0] = self.both(2, 0)
        if k == 3:
            self.own[0] = self.both(3, 0)
            self.own[1] = self.both(3, 1)

    def relay(self):
        to_x, to_y = self.place[5:7]
        self.cps[4].wait_recv()
        self.sb[2, 0] = (self.keep[0] + self.r1[0, 0].astype(F32)).astype(BF16)
        self.copy(8, self.sb.at[2, 0], self.r2.at[0], to_y)
        self.cps[5].wait_recv()
        self.sb[1, 1] = (self.keep[1] + self.r1[1, 0].astype(F32)).astype(BF16)
        self.copy(9, self.sb.at[1, 1], self.r2.at[1], to_x)
        self.cps[6].wait_recv()
        self.own[0] += self.r1[0, 1].astype(F32)
        self.cps[7].wait_recv()
        self.own[1] += self.r1[1, 1].astype(F32)

    def finish(self):
        self.cps[8].wait_recv()
        self.own[0] += self.r2[0].astype(F32)
        self.cps[9].wait_recv()
        self.own[1] += self.r2[1].astype(F32)
        for k in range(RS_COPIES):
            self.cps[k].wait_send()

    def run(self, produce, spare=()):
        spare = list(spare)
        for k in range(4):
            produce(self.block(k))
            self.core(k)
        for k in range(4):
            self.push(k)
        for job in spare[: len(spare) // 2]:
            job()
        self.relay()
        for job in spare[len(spare) // 2 :]:
            job()
        self.finish()


def rs_scratch():
    return [
        VM((2, 64, D), F32),
        VM((4, 2, 64, D), BF16),
        VM((3, 2, 64, D), BF16),
        VM((2, 64, D), F32),
        VM((2, 2, 64, D), BF16),
        VM((2, 64, D), BF16),
        pltpu.SemaphoreType.DMA((RS_COPIES,)),
        pltpu.SemaphoreType.DMA((RS_COPIES,)),
    ]


def ag_scratch():
    return [pltpu.SemaphoreType.DMA((AG_COPIES,)), pltpu.SemaphoreType.DMA((AG_COPIES,))]


def cost(micros):
    return pl.CostEstimate(flops=0, bytes_accessed=int(micros * 3.0e6), transcendentals=0)


def group_place():
    return lax.axis_index("sh") * lax.axis_size("hh") + lax.axis_index("hh")


def group_peer(k, count):
    nhh = lax.axis_size("hh")
    other = lax.rem(group_place() + k, count)
    sh, hh = other // nhh, lax.rem(other, nhh)
    return other, sh, hh, {"sh": sh, "hh": hh}


def place_peer(k):
    coords = {}
    for bit, axis in enumerate(("hl", "sx", "sy")):
        here = lax.axis_index(axis)
        coords[axis] = 1 - here if (k >> bit) & 1 else here
    target = {axis: v for bit, (axis, v) in enumerate(coords.items()) if (k >> bit) & 1}
    return coords["sy"] * 2 + coords["sx"], coords["hl"], target


def barrier_of(plane, group, count, column):
    barrier = pltpu.get_barrier_semaphore()
    seen = 0
    if column:
        hh, c = lax.axis_index("hh"), lax.axis_index("hl")
        for k in range(1, 8):
            target = {"hh": lax.rem(hh + k // 2, 4), "hl": 1 - c if k % 2 else c}
            if k == 1 and plane:
                continue
            pl.semaphore_signal(barrier, inc=1, device_id=target, device_id_type=MESH_ID)
            seen += 1
        group = False
    for k in ((1, 2, 4) if plane == 3 else range(1, 8)) if plane else ():
        _, _, target = place_peer(k)
        pl.semaphore_signal(barrier, inc=1, device_id=target, device_id_type=MESH_ID)
        seen += 1
    if group:
        for k in range(1, count):
            target = group_peer(k, count)[3]
            pl.semaphore_signal(barrier, inc=1, device_id=target, device_id_type=MESH_ID)
            seen += 1
    pl.semaphore_wait(barrier, seen)


def chained():
    return lax.axis_size("sh") == 1 and lax.axis_size("hh") == 4


class Job:
    def __init__(self, kind, src, spec=None, name=None, held=False, pool=None):
        self.kind, self.src, self.inside = kind, src, isinstance(src, jax.ShapeDtypeStruct)
        self.spec = spec or (VMEM if kind == "zs" else ANY)
        self.src_spec = VMEM if kind == "zs" else ANY
        self.name, self.held, self.pool = name, held, pool

    def out_shape(self):
        nsh, nhh = lax.axis_size("sh"), lax.axis_size("hh")
        shape = list(self.src.shape)
        if self.kind == "zg":
            shape = [nsh * 4, nhh] + shape[1:]
        if self.kind == "zr":
            shape = [nsh * nhh] + shape
        if self.kind == "zo":
            shape = [nsh * nhh, 4] + shape[2:]
        if self.kind == "zs":
            shape = [4] + shape[2:]
        if self.kind == "zw":
            shape = [4] + shape
        return jax.ShapeDtypeStruct(tuple(shape), BF16)


class Transfers:
    def __init__(self, kinds, sources, results, buffers, sems, count, chain):
        self.kinds, self.sources, self.results = kinds, sources, results
        self.buffers, self.sems, self.count, self.chain = buffers, sems, count, chain
        self.state = {}

    def copy(self, i, src, dst, send, recv, target):
        return pltpu.make_async_remote_copy(
            src_ref=src, dst_ref=dst, send_sem=self.sems[0].at[i, send],
            recv_sem=self.sems[1].at[i, recv], device_id=target, device_id_type=MESH_ID,
        )

    early = ()

    def __call__(self):
        for i, src in enumerate(self.sources):
            if src is not None and i not in self.state:
                self.start(i)

    late = __call__

    def slot(self, i, group):
        out, nhh = self.results[i], lax.axis_size("hh")
        if self.kinds[i] == "zg":
            return out.at[pl.ds(group // nhh * 4, 4), lax.rem(group, nhh)]
        return out.at[group]

    def got(self, i, ref, index):
        pltpu.make_async_copy(ref, ref, self.sems[1].at[i, index]).wait()

    def sent(self, i, ref, index):
        pltpu.make_async_copy(ref, ref, self.sems[0].at[i, index]).wait()

    names = {}

    def has(self, i):
        return i in self.names

    def start(self, i, src=None):
        i = self.names.get(i, i)
        if src is not None:
            self.sources[i] = src
        self.state[i] = "sent"
        kind, src, out, count = self.kinds[i], self.sources[i], self.results[i], self.count
        hh, g = lax.axis_index("hh"), group_place()
        local = None
        if kind == "pa":
            s, c, _ = place_peer(0)
            for k in range(1, 8):
                ps, pc, target = place_peer(k)
                self.copy(i, src.at[ps, pc], out.at[s, c], k, k, target).start()
            local = (src.at[s, c], out.at[s, c])
        if kind in ("zg", "zr"):
            for k in (1, 3, 2) if self.chain else range(1, count):
                go = self.copy(i, src, self.slot(i, g), k, g, group_peer(k, count)[3]).start
                if self.chain and k != 2:
                    pl.when(hh != (3 if k == 1 else 0))(go)
                else:
                    go()
            local = (src, self.slot(i, g))
        if kind in ("zo", "zt"):
            nhh = lax.axis_size("hh")
            part = lambda p: (
                src.at[p] if kind == "zt" else src.at[pl.ds(p // nhh * 4, 4), lax.rem(p, nhh)]
            )
            for k in range(1, count):
                other, _, _, target = group_peer(k, count)
                self.copy(i, part(other), out.at[g], k, g, target).start()
            local = (part(g), out.at[g])
        if kind == "zs":
            buf = self.buffers[i]
            last, begin = hh == 3, hh == 0
            up = self.copy(
                i, src.at[:, jnp.where(last, 0, hh + 1)], buf.at[jnp.where(last, 4, g)],
                1, jnp.where(last, 4, g), {"hh": jnp.where(last, 2, hh + 1)},
            ).start
            down = self.copy(
                i, src.at[:, jnp.where(begin, 3, hh - 1)], buf.at[jnp.where(begin, 4, g)],
                3, jnp.where(begin, 4, g), {"hh": jnp.where(begin, 1, hh - 1)},
            ).start

            @pl.when(last)
            def _():
                up()
                down()

            @pl.when(jnp.logical_not(last))
            def _():
                down()
                up()

            far = lax.rem(hh + 2, 4)
            pl.when(last | begin)(self.copy(i, src.at[:, far], buf.at[g], 2, g, {"hh": far}).start)
        if kind in ("zw", "zv"):
            for k in range(4):
                mine, target, src_k, at, _ = self.column(kind, k)
                view = src if kind == "zw" else src.at[src_k]
                here = pltpu.make_async_copy(view, out.at[at], self.sems[2].at[i]).start
                pl.when(mine)(here)
                pl.when(jnp.logical_not(mine))(self.copy(i, view, out.at[at], k, at, target).start)
        if local is not None:
            pltpu.make_async_copy(local[0], local[1], self.sems[2].at[i]).start()
            self.local = getattr(self, "local", {})
            self.local[i] = local

    def column(self, kind, k):
        hh, c = lax.axis_index("hh"), lax.axis_index("hl")
        if kind == "zw":
            z, to_c, slot = lax.rem(hh + k, 4), hh // 2, lax.rem(hh, 2) * 2 + c
            own = (2 * c + k // 2 == hh) & (k % 2 == c)
            return (z == hh) & (to_c == c), {"hh": z, "hl": to_c}, 0, slot, own
        j = lax.rem(lax.rem(hh, 2) * 2 + c + k, 4)
        z, to_c = 2 * c + j // 2, lax.rem(j, 2)
        own = (k == hh) & (hh // 2 == c)
        return (z == hh) & (to_c == c), {"hh": z, "hl": to_c}, j, hh, own

    def relay(self, *which):
        for i in which:
            i = self.names.get(i, i)
            if i not in self.state:
                continue
            kind = self.kinds[i]
            if not self.chain or kind not in ("zg", "zr", "zs") or self.state[i] != "sent":
                continue
            self.state[i] = "relayed"
            hh, g = lax.axis_index("hh"), group_place()
            inner = (hh == 1) | (hh == 2)
            far = lax.rem(hh + 2, 4)

            @pl.when(inner)
            def _(i=i, kind=kind):
                if kind == "zs":
                    buf, src = self.buffers[i], self.sources[i]
                    self.got(i, buf.at[4], 4)
                    buf[4] = (buf[4].astype(F32) + src[:, far].astype(F32)).astype(BF16)
                    self.copy(i, buf.at[4], buf.at[g], 2, g, {"hh": far}).start()
                else:
                    slot = self.slot(i, far)
                    self.got(i, slot, far)
                    self.copy(i, slot, slot, 0, far, {"hh": 3 - far}).start()

    def wait(self, *which):
        self.relay(*which)
        for i in which:
            i = self.names.get(i, i)
            if self.state[i] == "done":
                continue
            self.state[i] = "done"
            kind, src, out, count = self.kinds[i], self.sources[i], self.results[i], self.count
            hh, g = lax.axis_index("hh"), group_place()
            inner = (hh == 1) | (hh == 2)
            if kind == "pa":
                s, c, _ = place_peer(0)
                for k in range(1, 8):
                    self.copy(i, src.at[s, c], out.at[s, c], k, k, place_peer(k)[2]).wait()
            if kind in ("zg", "zr"):
                for k in range(1, count):
                    other = lax.rem(g + k, count)
                    slot = self.slot(i, other)

                    def arrive(slot=slot, other=other):
                        self.got(i, slot, other)

                    def leave(k=k):
                        self.sent(i, src, k)

                    if not self.chain:
                        arrive()
                        leave()
                    elif k == 2:
                        pl.when(jnp.logical_not(inner))(arrive)
                        leave()
                        pl.when(inner)(functools.partial(leave, 0))
                    else:
                        arrive()
                        pl.when(hh != (3 if k == 1 else 0))(leave)
            if kind in ("zo", "zt"):
                for k in range(1, count):
                    other = lax.rem(g + k, count)
                    self.got(i, out.at[other], other)
                    self.sent(i, out.at[other], k)
            if kind in ("zw", "zv"):
                for k in range(4):
                    mine, _, _, at, own = self.column(kind, k)
                    slot = out.at[k]
                    here = pltpu.make_async_copy(slot, slot, self.sems[2].at[i]).wait
                    pl.when(own)(here)
                    pl.when(jnp.logical_not(own))(functools.partial(self.got, i, slot, k))
                    pl.when(jnp.logical_not(mine))(functools.partial(self.sent, i, slot, k))
            if kind == "zs":
                buf = self.buffers[i]
                one = jnp.where(hh == 0, 2, hh - 1)
                two = jnp.where(hh == 3, 1, hh + 1)
                far = lax.rem(hh + 2, 4)
                self.got(i, buf.at[one], one)
                self.got(i, buf.at[two], two)
                total = lambda: (
                    src[:, g].astype(F32) + buf[one].astype(F32) + buf[two].astype(F32)
                )

                @pl.when(inner)
                def _():
                    self.got(i, buf.at[far], far)
                    out[...] = (total() + buf[far].astype(F32)).astype(BF16)

                @pl.when(jnp.logical_not(inner))
                def _():
                    out[...] = total().astype(BF16)

                for k in (1, 2, 3):
                    self.sent(i, buf.at[g], k)
            if i in getattr(self, "local", {}):
                a, b = self.local[i]
                pltpu.make_async_copy(a, b, self.sems[2].at[i]).wait()

    def rest(self):
        which = [i for i in self.state if self.state[i] != "done"]
        self.relay(*which)
        self.wait(*which)

    def result(self, i):
        return self.results[self.names.get(i, i)]

    def columns(self, i):
        ref = self.result(i)
        return ref[...].reshape(D, ref.shape[-1])


ANY = pl.BlockSpec(memory_space=pl.ANY)
VMEM = pl.BlockSpec(memory_space=pltpu.VMEM)
SMEM = pl.BlockSpec(memory_space=pltpu.SMEM)


def step(body, ins, outs, scratch, jobs, plane, group, name, collective, micros, early=()):
    count = lax.axis_size(GROUP)
    kinds = [job.kind for job in jobs]
    given = [job for job in jobs if not job.inside]
    shown = [job for job in jobs if not job.held]
    n_in, n_out, n_job, n_src = len(ins), len(outs), len(jobs), len(given)
    plane = 7 if "pa" in kinds else plane
    group = group or any(kind != "pa" for kind in kinds)
    column = any(kind in ("zw", "zv") for kind in kinds)
    slots = max(count, 8)
    held = [VM(job.out_shape().shape, BF16) for job in jobs if job.held]
    pools = {}
    for i, job in enumerate(jobs):
        if job.kind == "zs":
            key = (job.pool if job.pool is not None else -1 - i, job.out_shape().shape)
            pools.setdefault(key, []).append(i)

    def kernel(*refs):
        in_refs, refs = refs[:n_in], refs[n_in:]
        given_refs, refs = list(refs[:n_src]), refs[n_src:]
        out_refs, refs = refs[:n_out], refs[n_out:]
        shown_refs, refs = list(refs[: len(shown)]), refs[len(shown) :]
        extra_refs, own = list(refs[len(scratch) :]), refs[: len(scratch)]
        held_refs, pool_refs = extra_refs[3 : 3 + len(held)], extra_refs[3 + len(held) :]
        sources = [None if job.inside else given_refs.pop(0) for job in jobs]
        results = [held_refs.pop(0) if job.held else shown_refs.pop(0) for job in jobs]
        buffers = {i: ref for key, ref in zip(pools, pool_refs) for i in pools[key]}
        barrier_of(plane, group, count, column)
        begin = Transfers(kinds, sources, results, buffers, extra_refs[:3], count, chained())
        begin.early = early
        begin.names = {job.name: i for i, job in enumerate(jobs) if job.name}
        body(begin, *in_refs, *out_refs, *own)
        if not begin.state:
            begin()
        begin.rest()

    extra = (
        [
            pltpu.SemaphoreType.DMA((n_job, slots)),
            pltpu.SemaphoreType.DMA((n_job, slots)),
            pltpu.SemaphoreType.DMA((n_job,)),
        ]
        + held
        + [VM((5,) + key[1], BF16) for key in pools]
    )
    result = pl.pallas_call(
        kernel,
        out_shape=tuple(o for o, _ in outs) + tuple(job.out_shape() for job in shown),
        in_specs=[spec for _, spec in ins] + [job.src_spec for job in given],
        out_specs=tuple(spec for _, spec in outs) + tuple(job.spec for job in shown),
        scratch_shapes=list(scratch) + (extra if n_job else []),
        compiler_params=pltpu.CompilerParams(
            collective_id=collective, has_side_effects=True, vmem_limit_bytes=LIMIT
        ),
        cost_estimate=cost(micros),
        name=name,
    )(*[v for v, _ in ins], *[job.src for job in given])
    return result[:n_out], result[n_out:]


FULL = jax.ShapeDtypeStruct((4, 2, 2, 64, D), BF16)
OWN = jax.ShapeDtypeStruct((2, 64, D), F32)


def flat(full):
    return full.reshape(1024, D)


def blocks(rows):
    return rows.reshape(4, 2, 2, 64, D)


def vmem(*values):
    return [(v, VMEM) for v in values]


def normed_half(u, gain):
    inv = lax.rsqrt(jnp.mean(u * u, axis=-1, keepdims=True) + EPSILON)
    return (u * inv * gain).astype(BF16)


def chip_rows(ref, block):
    return ref[block].reshape(256, D)


def put_chip(ref, block, value):
    ref[block] = value.astype(BF16).reshape(2, 2, 64, D)


def rows_of(block):
    return pl.ds(block * 256, 256)


def silu_parts(gate):
    sig = 1.0 / (1.0 + jnp.exp(-gate))
    return sig, gate * sig


def follow(total, seen):
    k = (3, 1, 2, 0)[len(seen)]
    seen.append(k)
    total.core(k)
    if k == 2:
        total.push(1)
    if k == 0:
        total.push(2)
        total.push(3)
        total.push(0)


def norm_back_half(dn, u, gain, upstream):
    inv = lax.rsqrt(jnp.mean(u * u, axis=-1, keepdims=True) + EPSILON)
    gained = dn * gain
    inner = jnp.mean(gained * u, axis=-1, keepdims=True)
    scaled = u * inv
    grad = upstream + inv * gained - scaled * (inv * inv * inner)
    return grad, jnp.sum(dn * scaled, axis=0, keepdims=True)


def back_own(dn, u_ref, gain_ref, up_ref, gnew, ggain, full):
    me, c = plane_place()[0], plane_place()[4]
    total = None
    for half in range(2):
        grad, gain_part = norm_back_half(
            dn[half], u_ref[half].astype(F32), gain_ref[...], up_ref[half].astype(F32)
        )
        gnew[half] = grad
        total = gain_part if total is None else total + gain_part
        if full is not None:
            full[me, c, half] = grad.astype(BF16)
    ggain[...] = total


def weight_grads(left, right, out):
    def piece(i):
        width = D // 4
        lo = i * width
        lhs = left[:, :, :, :, lo : lo + width].reshape(1024, width)
        value = matmul_tn(lhs, right[...]).astype(BF16)
        if len(out.shape) == 5:
            out[i] = value.reshape(out.shape[1:])
        else:
            out[lo : lo + width, :] = value

    return [functools.partial(piece, i) for i in range(4)]


def shipping():
    return chained() and D % (8 * 4 * 16) == 0


def terms_shape(cols):
    nsh, nhh = lax.axis_size("sh"), lax.axis_size("hh")
    if shipping():
        return jax.ShapeDtypeStruct((4, 4, 2, D // 32, cols), BF16)
    return jax.ShapeDtypeStruct((D, cols), BF16)


def apart(arrays, collective):
    nsh, nhh = lax.axis_size("sh"), lax.axis_size("hh")
    rows = D // (8 * nsh * nhh)
    jobs = [Job("zo", a.reshape(nsh * 4, nhh, 2, rows, a.shape[-1])) for a in arrays]
    _, moved = step(lambda begin: None, [], [], [], jobs, 0, True, "apart", collective, 20)
    return [jnp.sum(a.astype(F32), axis=0).astype(BF16) for a in moved]


def last_layer(dproj, w_proj, u, gain, upstream, x_full, n_first, gains, jobs, collective):
    width = w_proj.shape[1]
    ship = shipping()

    def body(
        begin, dp_ref, wp_ref, u_ref, gain_ref, up_ref, xf_ref, nf_ref, gains_ref,
        gnew, ggain, proj_w, part1, mine, *rest
    ):
        sum1 = RowSum(part1, *rest)
        begin()
        mine[...] = jnp.zeros((128, D), F32)
        mine[65:68, :] = gains_ref[...]

        def projected(block):
            part = matmul_nt(dp_ref[rows_of(block), :], wp_ref[...])
            put_chip(part1, block, part)
            u = chip_rows(xf_ref, block).astype(F32)
            u = u * lax.rsqrt(jnp.mean(u * u, axis=-1, keepdims=True) + EPSILON)
            mine[64:65, :] += jnp.sum(part * u, axis=0, keepdims=True)

        def grads():
            turned = mine[...].T
            for i in range(4):
                at = slice(i * 256, i * 256 + 256)
                lhs = nf_ref[:, :, :, :, at].reshape(1024, 256)
                value = matmul_tn(lhs, dp_ref[...])
                keep = lanes(256, 128) < 64
                value = jnp.concatenate(
                    [jnp.where(keep, value[:, :128], turned[at]), value[:, 128:]], axis=1
                ).astype(BF16)
                if ship:
                    proj_w[i] = value.reshape(proj_w.shape[1:])
                else:
                    proj_w[at, :] = value
            if ship:
                begin.start(len(jobs), proj_w)

        for k in range(4):
            projected(sum1.block(k))
            sum1.core(k)
        grads()
        for k in range(4):
            sum1.push(k)
        sum1.relay()
        sum1.finish()
        begin.relay(len(jobs))
        back_own(sum1.own, u_ref, gain_ref, up_ref, gnew, ggain, None)
        if ship:
            begin.wait(len(jobs))
            begin.start(len(jobs) + 1, begin.results[len(jobs)])

    terms = terms_shape(width)
    summed = jax.ShapeDtypeStruct((4, 2, D // 32, width), BF16)
    n = len(jobs)
    outs, moved = step(
        body, vmem(dproj, w_proj, u, gain, upstream, x_full, n_first, gains),
        vmem(OWN, jax.ShapeDtypeStruct((1, D), F32)) + ([] if ship else vmem(terms)),
        ([VM(terms.shape, BF16)] if ship else []) + [VM(FULL.shape, BF16), VM((128, D), F32)] + rs_scratch(),
        jobs + ([Job("zs", terms), Job("pa", summed)] if ship else []),
        3, False, "last_layer", collective, 25,
    )
    if ship:
        return outs[0], moved[:n], moved[n + 1]
    (lin,) = apart([outs[2]], 12)
    _, (lin,) = step(
        lambda begin: None, [], [], [], [Job("pa", lin)], 7, False, "last", 13, 5
    )
    return outs[0], moved[:n], lin


def taylor_tables():
    pick = np.zeros((4, 2, 128, 256), np.float32)
    coef = np.zeros((8, 256), np.float32)
    pairs = [(i, j) for i in range(FEAT) for j in range(i, FEAT)]
    one = 4 * FEAT
    for x, (i, j) in enumerate(pairs):
        coef[:, x] = (2.0 * FEAT) ** -0.5 if i == j else FEAT**-0.5
        for t in range(4):
            pick[t, 0, t * FEAT + i, x] = 1.0
            pick[t, 1, t * FEAT + j, x] = 1.0
    for i in range(FEAT):
        x = len(pairs) + i
        coef[:, x] = FEAT**-0.25
        for t in range(4):
            pick[t, 0, t * FEAT + i, x] = 1.0
            pick[t, 1, one, x] = 1.0
    x = len(pairs) + FEAT
    coef[:, x] = 1.0
    pick[:, 0, one, x] = 1.0
    pick[:, 1, one, x] = 1.0
    shift = np.zeros((128, 128), np.float32)
    for i in range(2 * FEAT):
        shift[2 * FEAT + i, i] = 1.0
    return jnp.asarray(pick, BF16), jnp.asarray(coef, F32), jnp.asarray(shift, BF16)


def chunk_of(group, s):
    nhh = lax.axis_size("hh")
    return (group // nhh * 4 + s) * nhh + lax.rem(group, nhh)


def segment_of(starts, position):
    total = jnp.where(position >= starts[0], 0, -1)
    for i in range(1, starts.shape[0]):
        total = total + jnp.where(position >= starts[i], 1, 0)
    return total


class Segments:
    def __init__(self, starts, s):
        first = chunk_of(group_place(), s) * 256
        at = lambda shape, dim: first + lax.broadcasted_iota(jnp.int32, shape, dim)
        self.col = segment_of(starts, at((256, 1), 0))
        self.row = segment_of(starts, at((1, 256), 1))
        self.ext = segment_of(starts, at((1, 256 + RIM), 1) - RIM)
        self.last = segment_of(starts, first + 255)
        self.before = segment_of(starts, first - 1)


def carried(starts, s, st, sm, count, back):
    mine = chunk_of(group_place(), s)
    edge = segment_of(starts, mine * 256 + 255 if back else mine * 256 - 1)

    def group(i, both):
        def one(s2, both):
            state, total = both
            other = chunk_of(i, s2)
            reach = segment_of(starts, other * 256 - 1 if back else other * 256 + 255)
            ordered = other > mine if back else other < mine
            m = jnp.where(ordered & (reach == edge), 1.0, 0.0)
            return state + m * st[i, s2].astype(F32), total + m * sm[i, s2]

        return lax.fori_loop(s, 4, one, both) if back else lax.fori_loop(0, s + 1, one, both)

    return lax.fori_loop(
        0, count, group, (jnp.zeros((SROWS, 128), F32), jnp.zeros((8, 256), F32))
    )


def lanes(rows, width):
    return lax.broadcasted_iota(jnp.int32, (rows, width), 1)


class States:
    def __init__(self, count, st, sm, ssem, rsem):
        self.refs, self.ssem, self.rsem, self.count = (st, sm), ssem, rsem, count
        self.chain = count == 4 and chained()

    def copy(self, n, k, group, target):
        view = self.refs[n].at[group]
        return pltpu.make_async_remote_copy(
            src_ref=view, dst_ref=view, send_sem=self.ssem.at[n, k], recv_sem=self.rsem.at[n, group],
            device_id=target, device_id_type=MESH_ID,
        )

    def send(self):
        g, hh = group_place(), lax.axis_index("hh")
        for k in (2, 1, 3) if self.chain else range(1, self.count):
            for n in range(2):
                go = self.copy(n, k, g, group_peer(k, self.count)[3]).start
                if self.chain and k != 2:
                    pl.when(hh != (3 if k == 1 else 0))(go)
                else:
                    go()

    def got(self, n, group):
        view = self.refs[n].at[group]
        pltpu.make_async_copy(view, view, self.rsem.at[n, group]).wait()

    def sent(self, n, k):
        view = self.refs[n].at[0]
        pltpu.make_async_copy(view, view, self.ssem.at[n, k]).wait()

    def relay(self):
        if not self.chain:
            return
        hh = lax.axis_index("hh")
        far = lax.rem(hh + 2, 4)

        @pl.when((hh == 1) | (hh == 2))
        def _():
            for n in range(2):
                self.got(n, far)
                self.copy(n, 0, far, {"hh": 3 - far}).start()

    def arrive(self):
        g, hh = group_place(), lax.axis_index("hh")
        inner = (hh == 1) | (hh == 2)
        for k in range(1, self.count):
            other = lax.rem(g + k, self.count)
            for n in range(2):
                got = functools.partial(self.got, n, other)
                if self.chain and k == 2:
                    pl.when(jnp.logical_not(inner))(got)
                else:
                    got()

    def finish(self):
        hh = lax.axis_index("hh")
        for k in range(1, self.count):
            for n in range(2):
                sent = functools.partial(self.sent, n, k)
                if self.chain and k != 2:
                    pl.when(hh != (3 if k == 1 else 0))(sent)
                else:
                    sent()
                    if self.chain:
                        pl.when((hh == 1) | (hh == 2))(functools.partial(self.sent, n, 0))


def phi_of(x, pick, coef, t):
    left = matmul(x, pick[t, 0])
    right = matmul(x, pick[t, 1])
    return left, right, (left * right * coef).astype(BF16)


def taylor_forward_kernel(
    count, hooks, qkv, pick, coef_ref, shift, starts,
    o_ref, y_ref, den_ref, pre_ref, psum_ref, st, sm, phis, ssem, rsem,
):
    g = group_place()
    coef = coef_ref[0:1, :]
    left_half = lanes(256, 128) < 64

    def states(s, carry):
        rows = pl.ds(s * 256, 256)
        x = jnp.where(lanes(256, 128) == 4 * FEAT, jnp.ones((), BF16), qkv[rows, 0:128])
        v = qkv[rows, 128:256]
        seg = Segments(starts, s)
        tail = seg.col == seg.last
        v_tail = jnp.where(tail, v, jnp.zeros((), BF16))
        state = jnp.zeros((256, 128), F32)
        for h in range(2):
            _, _, phi_k = phi_of(x, pick, coef, 2 + h)
            side = left_half if h == 0 else jnp.logical_not(left_half)
            state += matmul_tn(phi_k, jnp.where(side, v_tail, jnp.zeros((), BF16)))
            total = jnp.sum(jnp.where(tail, phi_k.astype(F32), 0.0), axis=0, keepdims=True)
            sm[g, s, h : h + 1, :] = total
            _, _, phi_q = phi_of(x, pick, coef, h)
            phis[h][rows, 0:256] = phi_q
        st[g, s] = state[:SROWS].astype(BF16)
        return carry

    sm[g] = jnp.zeros((4, 8, 256), F32)
    lax.fori_loop(0, 4, states, 0)
    exchange = States(count, st, sm, ssem, rsem)
    exchange.send()
    hooks[0]()

    def inner(s, carry):
        rows = pl.ds(s * 256, 256)
        x = qkv[rows, 0:128]
        v = qkv[rows, 128:256]
        k = matmul(x, shift[...]).astype(BF16)
        lane = lanes(256, 128)
        order = lax.broadcasted_iota(jnp.int32, (256, 256), 0) >= lanes(256, 256)
        seg = Segments(starts, s)
        allowed = order & (seg.col == seg.row)
        num = jnp.zeros((256, 128), F32)
        dens = []
        for h in range(2):
            q = jnp.where(lane // FEAT == h, x, jnp.zeros((), BF16))
            dot = matmul_nt(q, k)
            score = jnp.where(allowed, 1.0 + dot * FEAT**-0.5 + dot * dot * (0.5 / FEAT), 0.0)
            side = left_half if h == 0 else jnp.logical_not(left_half)
            num += matmul(score.astype(BF16), jnp.where(side, v, jnp.zeros((), BF16)))
            dens.append(jnp.sum(score, axis=1, keepdims=True))
        y_ref[rows, :] = num
        den_ref[rows, :] = jnp.where(left_half, dens[0], dens[1])
        return carry

    lax.fori_loop(0, 4, inner, 0)
    exchange.relay()
    hooks[1]()
    exchange.arrive()
    hooks[2]()

    def finish(s, carry):
        rows = pl.ds(s * 256, 256)

        state, total = carried(starts, s, st, sm, count, False)
        state = state.astype(BF16)
        pre_ref[s] = state
        psum_ref[s] = total
        seg = Segments(starts, s)
        cont = seg.col == seg.before
        num = jnp.zeros((256, 128), F32)
        dens = []
        for h in range(2):
            phi_q = phis[h][rows, 0:256]
            side = left_half if h == 0 else jnp.logical_not(left_half)
            part = matmul(phi_q[:, :SROWS], state)
            num = jnp.where(side, part, num)
            dens.append(jnp.sum(phi_q.astype(F32) * total[h : h + 1], axis=1, keepdims=True))
        num = jnp.where(cont, num, 0.0) + y_ref[rows, :]
        den = jnp.where(cont, jnp.where(left_half, dens[0], dens[1]), 0.0) + den_ref[rows, :]
        y = num / den
        y_ref[rows, :] = y
        den_ref[rows, :] = den
        o_ref[rows, :] = y.astype(BF16)
        return carry

    lax.fori_loop(0, 4, finish, 0)
    hooks[3]()
    exchange.finish()


def taylor_backward_kernel(
    count, begin, qkv, do_ref, y_ref, den_ref, pre_ref, psum_ref,
    pick, coef_ref, shift, starts,
    out_ref, st, sm, acc, dnum_ref, ddens, ssem, rsem,
):
    g = group_place()
    for i in begin.early:
        begin.start(i)
    coef = coef_ref[0:1, :]
    left_half = lanes(256, 128) < 64
    zero = jnp.zeros((), BF16)

    def sides(h):
        return left_half if h == 0 else jnp.logical_not(left_half)

    def feature_back(dphi, left, right, t):
        grad = dphi * coef
        return matmul_nt((grad * right).astype(BF16), pick[t, 0]) + matmul_nt(
            (grad * left).astype(BF16), pick[t, 1]
        )

    def states(s, carry):
        rows = pl.ds(s * 256, 256)
        x = jnp.where(lanes(256, 128) == 4 * FEAT, jnp.ones((), BF16), qkv[rows, 0:128])
        do = do_ref[rows, :].astype(F32)
        den = den_ref[rows, :]
        dnum = do / den
        dnum_low = dnum.astype(BF16)
        dnum_ref[rows, :] = dnum_low
        weighted = dnum * y_ref[rows, :]
        seg = Segments(starts, s)
        cont = seg.col == seg.before
        d_cont = jnp.where(cont, dnum_low, zero)
        pre = pre_ref[s]
        state = jnp.zeros((256, 128), F32)
        grad = jnp.zeros((256, 128), F32)
        for h in range(2):
            dden = -jnp.sum(jnp.where(sides(h), weighted, 0.0), axis=1, keepdims=True)
            ddens[h, rows, :] = jnp.broadcast_to(dden, (256, 128))
            left, right, phi_q = phi_of(x, pick, coef, h)
            d_side = jnp.where(sides(h), d_cont, zero)
            state += matmul_tn(phi_q, d_side)
            dden_cont = jnp.where(cont, dden, 0.0)
            sm[g, s, h : h + 1, :] = jnp.sum(
                phi_q.astype(F32) * dden_cont, axis=0, keepdims=True
            )
            dphi = jnp.concatenate(
                [matmul_nt(d_side, pre), jnp.zeros((256, 256 - SROWS), F32)], axis=1
            ) + dden_cont * psum_ref[s, h : h + 1, :]
            grad += feature_back(dphi, left, right, h)
        st[g, s] = state[:SROWS].astype(BF16)
        acc[0, rows, :] = grad
        return carry

    sm[g] = jnp.zeros((4, 8, 256), F32)
    lax.fori_loop(0, 4, states, 0)
    exchange = States(count, st, sm, ssem, rsem)
    exchange.send()
    begin.late()

    def inner(s, carry):
        rows = pl.ds(s * 256, 256)
        x = qkv[rows, 0:128]
        v = qkv[rows, 128:256]
        dnum = dnum_ref[rows, :]
        k_low = matmul(x, shift[...]).astype(BF16)
        lane = lanes(256, 128)
        order = lax.broadcasted_iota(jnp.int32, (256, 256), 0) >= lanes(256, 256)
        seg = Segments(starts, s)
        allowed = order & (seg.col == seg.row)
        dq = jnp.zeros((256, 128), F32)
        dk = jnp.zeros((256, 128), F32)
        dv = jnp.zeros((256, 128), F32)
        for h in range(2):
            mine = lane // FEAT == h
            q = jnp.where(mine, x, zero)
            dot = matmul_nt(q, k_low)
            score = jnp.where(allowed, 1.0 + dot * FEAT**-0.5 + dot * dot * (0.5 / FEAT), 0.0)
            d_side = jnp.where(sides(h), dnum, zero)
            dscore = matmul_nt(d_side, v) + ddens[h, rows, 0:1]
            e = jnp.where(allowed, dscore * (FEAT**-0.5 + dot * (1.0 / FEAT)), 0.0).astype(BF16)
            dq += matmul(e, jnp.where(mine, k_low, zero))
            dk += matmul_tn(e, q)
            dv += matmul_tn(score.astype(BF16), d_side)
        acc[0, rows, :] += dq
        acc[1, rows, :] = dk
        acc[2, rows, :] = dv
        return carry

    lax.fori_loop(0, 4, inner, 0)
    exchange.relay()
    begin.relay(*begin.early)
    exchange.arrive()

    def finish(s, carry):
        rows = pl.ds(s * 256, 256)

        state, total = carried(starts, s, st, sm, count, True)
        state = state.astype(BF16)
        x = jnp.where(lanes(256, 128) == 4 * FEAT, jnp.ones((), BF16), qkv[rows, 0:128])
        seg = Segments(starts, s)
        tail = seg.col == seg.last
        v_tail = jnp.where(tail, qkv[rows, 128:256], zero)
        grad = acc[0, rows, :]
        lane = lanes(256, 128)
        dv = jnp.zeros((256, 128), F32)
        for h in range(2):
            left, right, phi_k = phi_of(x, pick, coef, 2 + h)
            dphi = jnp.concatenate(
                [
                    matmul_nt(jnp.where(sides(h), v_tail, zero), state),
                    jnp.zeros((256, 256 - SROWS), F32),
                ],
                axis=1,
            ) + jnp.where(tail, total[h : h + 1], 0.0)
            grad += feature_back(dphi, left, right, 2 + h)
            dv = jnp.where(sides(h), matmul(phi_k[:, :SROWS], state), dv)
        grad += matmul_nt(acc[1, rows, :].astype(BF16), shift[...])
        dv = jnp.where(tail, dv, 0.0) + acc[2, rows, :]
        out_ref[rows, 0:128] = jnp.where(lane < 4 * FEAT, grad, 0.0).astype(BF16)
        out_ref[rows, 128:256] = dv.astype(BF16)
        return carry

    lax.fori_loop(0, 4, finish, 0)
    exchange.finish()


def taylor_backward(qkv, do, kept, starts, tables, jobs, count, collective):
    return step(
        functools.partial(taylor_backward_kernel, count),
        vmem(qkv, do, *kept, *tables) + [(starts, SMEM)],
        vmem(jax.ShapeDtypeStruct((1024, 256), BF16)),
        [
            VM((count, 4, SROWS, 128), BF16),
            VM((count, 4, 8, 256), F32),
            VM((3, 1024, 128), F32),
            VM((1024, 128), BF16),
            VM((2, 1024, 128), F32),
            pltpu.SemaphoreType.DMA((2, count)),
            pltpu.SemaphoreType.DMA((2, count)),
        ],
        jobs, 0, True, "taylor_backward", collective, 28, early=range(len(jobs)),
    )


def rim_target(s, forward):
    hh, sh = lax.axis_index("hh"), lax.axis_index("sh")
    nhh, nsh = lax.axis_size("hh"), lax.axis_size("sh")
    if forward:
        wraps = jnp.where(hh == nhh - 1, 1, 0)
        slot = lax.rem(s + wraps, 4)
        leaves = wraps if s == 3 else 0
        return {"sh": lax.rem(sh + leaves, nsh), "hh": lax.rem(hh + 1, nhh)}, slot
    wraps = jnp.where(hh == 0, 1, 0)
    slot = lax.rem(s + 4 - wraps, 4)
    leaves = wraps if s == 0 else 0
    return {"sh": lax.rem(sh + nsh - leaves, nsh), "hh": lax.rem(hh + nhh - 1, nhh)}, slot


def window_mask(starts, s):
    seg = Segments(starts, s)
    i = lax.broadcasted_iota(jnp.int32, (256, 256 + RIM), 0)
    j = lanes(256, 256 + RIM)
    return (j > i) & (j <= i + WINDOW) & (seg.col == seg.ext)


def window_probs(q, k, allowed):
    scores = jnp.where(allowed, matmul_nt(q, k) * 64**-0.5, -1e30)
    peak = jnp.max(scores, axis=1, keepdims=True)
    weights = jnp.exp(scores - peak)
    return weights / jnp.sum(weights, axis=1, keepdims=True)


def window_forward_kernel(begin, qkv, starts, o_ref, ext, rim, ssem, rsem):
    cps = []
    for s in range(4):
        target, slot = rim_target(s, True)
        src = qkv.at[pl.ds(s * 256 + 256 - RIM, RIM), pl.ds(128, 256)]
        cps.append(remote(src, rim.at[slot], ssem.at[s], rsem.at[slot], target))

    def fill(s, carry):
        ext[s, RIM:, :] = qkv[pl.ds(s * 256, 256), 128:384]
        return carry

    lax.fori_loop(0, 4, fill, 0)
    for s in range(4):
        pltpu.make_async_copy(rim.at[s], rim.at[s], rsem.at[s]).wait()
    begin()

    def run(s, carry):
        rows = pl.ds(s * 256, 256)
        ext[s, :RIM, :] = rim[s]
        q = qkv[rows, 0:128]
        k = ext[s, :, 0:128]
        v = ext[s, :, 128:256]
        left_half = lanes(256, 128) < 64
        allowed = window_mask(starts, s)
        out = jnp.zeros((256, 128), F32)
        for h in range(2):
            side = left_half if h == 0 else jnp.logical_not(left_half)
            probs = window_probs(jnp.where(side, q, jnp.zeros((), BF16)), k, allowed)
            out = jnp.where(side, matmul(probs.astype(BF16), v), out)
        o_ref[rows, :] = out.astype(BF16)
        return carry

    lax.fori_loop(0, 4, run, 0)
    for cp in cps:
        cp.wait_send()


def window_backward_kernel(
    begin, qkv, ext, do_ref, part, u_ref, att_ref, up_full, starts, out_ref, mixed, out_w,
    acc, back, rim,
    ssem, rsem, own, cb, sb, keep, r1, r2, ss, rs,
):
    total = RowSum(part, own, cb, sb, keep, r1, r2, ss, rs)
    for k in range(4):
        total.core(k)
    zero = jnp.zeros((), BF16)

    def run(s, carry):
        rows = pl.ds(s * 256, 256)
        q = qkv[rows, 0:128]
        k = ext[s, :, 0:128]
        v = ext[s, :, 128:256]
        do = do_ref[rows, :]
        left_half = lanes(256, 128) < 64
        left_ext = lanes(256 + RIM, 128) < 64
        allowed = window_mask(starts, s)
        dq = jnp.zeros((256, 128), F32)
        dk = jnp.zeros((256 + RIM, 128), F32)
        dv = jnp.zeros((256 + RIM, 128), F32)
        for h in range(2):
            side = left_half if h == 0 else jnp.logical_not(left_half)
            q_h = jnp.where(side, q, zero)
            do_h = jnp.where(side, do, zero)
            probs = window_probs(q_h, k, allowed)
            dprobs = matmul_nt(do_h, v)
            inner = jnp.sum(probs * dprobs, axis=1, keepdims=True)
            ds = (probs * (dprobs - inner)).astype(BF16)
            dq = jnp.where(side, matmul(ds, k), dq)
            dk += matmul_tn(ds, q_h)
            dv += matmul_tn(probs.astype(BF16), do_h)
        scale = 64**-0.5
        dk = dk * scale
        out_ref[rows, 0:128] = (dq * scale).astype(BF16)
        acc[rows, 0:128] = dk[RIM:]
        acc[rows, 128:256] = dv[RIM:]
        back[s, :, 0:128] = dk[:RIM].astype(BF16)
        back[s, :, 128:256] = dv[:RIM].astype(BF16)
        return carry

    for k in range(4):
        total.push(k)
    lax.fori_loop(0, 4, run, 0)
    cps = []
    for s in range(4):
        target, slot = rim_target(s, False)
        cps.append(remote(back.at[s], rim.at[slot], ssem.at[s], rsem.at[slot], target))
    for i in range(4):
        at = slice(i * 256, i * 256 + 256)
        rhs = up_full[:, :, :, :, at].reshape(1024, 256)
        value = matmul_tn(att_ref[...], rhs).astype(BF16)
        if len(out_w.shape) == 3:
            out_w[:, :, at] = value.reshape(out_w.shape[:2] + (256,))
        else:
            out_w[:, at] = value
    total.relay()
    begin[1]()
    for s in range(4):
        pltpu.make_async_copy(rim.at[s], rim.at[s], rsem.at[s]).wait()
    begin[0]()

    def finish(s, carry):
        out_ref[pl.ds(s * 256, 256 - RIM), 128:384] = acc[pl.ds(s * 256, 256 - RIM), :].astype(BF16)
        rows = pl.ds(s * 256 + 256 - RIM, RIM)
        out_ref[rows, 128:384] = (acc[rows, :] + rim[s].astype(F32)).astype(BF16)
        return carry

    lax.fori_loop(0, 4, finish, 0)
    total.finish()
    for half in range(2):
        mixed[half] = (u_ref[half] + own[half]).astype(BF16)
    for cp in cps:
        cp.wait_send()


def front(x_own, cot_own, tables, starts, jobs, count, ff, width, collective):
    ship = shipping()
    terms = terms_shape(ff)
    vector = jax.ShapeDtypeStruct((8, D), F32)
    rowset = jax.ShapeDtypeStruct((4, D // 32, D) if ship else (128, D), BF16)
    makers = ("down_b", "gate_b", "up_b", "win", "down_a", "gate_a", "up_a")

    def body(
        begin, x_own, cot_own, pick, coef, shift, starts,
        mixed, g_ha, gg, do_a, lo_w, wo_w, qkv_a, y_a, den_a, pre, psum, w_lin, gains, x_out, n_out, *rest
    ):
        n_terms = 1 + (4 if ship else 6)
        weights, rest = rest[:n_terms], rest[n_terms:]
        made = dict(zip(("up_a",) + makers[:-1], weights))
        if ship:
            made["down_a"], made["gate_a"] = made["down_b"], made["gate_b"]
        h_a, out_a, h_b, g_hb, g_oa = rest[:5]
        na2, nb1, nb2, full1, part1, part2, cot = rest[5:12]
        full2, part3 = nb2, part1
        qkv, ext, o_b, do_b, dqkv, acc, back, rim1, rim2 = rest[12:21]
        gate_s, up_s, hid_s, hid_t, dgate, dup = rest[21:27]
        o_a, st, sm = rest[27:30]
        rest = rest[30:]
        set1, set2 = rest[:8], rest[8:16]
        ag = [rest[16 + 2 * i : 18 + 2 * i] for i in range(8)]
        rims = rest[32:36]
        states, out_sem = rest[36:38], rest[38]
        me, c = plane_place()[0], plane_place()[4]

        def call(name, *args):
            return functools.partial(getattr(begin, name), *args)

        def ship_terms(name):
            if ship:
                begin.start(name + "_t", made[name])

        def send_on(name):
            if ship:
                begin.wait(name + "_t")
                begin.start(name + "_p", begin.result(name + "_t"))

        def relay(*names):
            if ship:
                begin.relay(*[name + "_t" for name in names])

        def norm_own(total, before, after, full, gain):
            for half in range(2):
                u = before[half].astype(F32) + total.own[half]
                after[half] = u
                full[me, c, half] = normed_half(u, gains[gain : gain + 1])

        def start_all(*names):
            for name in names:
                begin.start(name)

        def spread_on(name):
            begin.wait(name + "_m")
            begin.start(name, begin.result(name + "_m"))

        begin.start("lin_m")
        start_all("lin_out", "win_out")
        nb1[me, c] = x_own[...]
        rows_in = RowGather(nb1, *ag[6])
        rows_in.start()
        begin.start("gate_a_m")
        spread_on("lin")
        rows_in.hop1()
        rows_in.hop2()
        rows_in.hop3()
        start_all("up_a_m", "down_a_m")
        rows_in.arrived(0, 6, 8, 9, 10, 11, 12)
        rows_in.finish()
        begin.relay("lin")
        spread_on("gate_a")
        begin.wait("lin")
        w_lin[...] = begin.columns("lin")
        gains[...] = w_lin[:, :128].astype(F32).T[64:72]
        lane = lanes(D, width)
        w_lin[...] = jnp.where((lane < 64) | (lane >= 128), w_lin[...], jnp.zeros((), BF16))

        def project_a(block, carry):
            n = normed_half(chip_rows(nb1, block).astype(F32), gains[0:1])
            put_chip(part2, block, n)
            qkv_a[rows_of(block), :] = matmul(n, w_lin[...]).astype(BF16)
            return carry

        cot[me, c] = cot_own[...]
        cot_in = RowGather(cot, *ag[7])
        cot_in.start()
        lax.fori_loop(0, 4, project_a, 0)
        kept = [
            pltpu.make_async_copy(nb1, x_out, out_sem.at[0]),
            pltpu.make_async_copy(part2, n_out, out_sem.at[1]),
        ]
        for cp in kept:
            cp.start()

        def states_sent():
            spread_on("up_a")
            cot_in.hop1()
            start_all("win_m", "gate_b_m", "up_b_m", "down_b_m")

        def inner_done():
            cot_in.hop2()
            cot_in.hop3()
            begin.relay("gate_a")

        def states_in():
            spread_on("down_a")

        def taylor_done():
            cot_in.arrived(0, 6, 8, 9, 10, 11, 12)
            cot_in.finish()
            for cp in kept:
                cp.wait()

        taylor_forward_kernel(
            count, (states_sent, inner_done, states_in, taylor_done), qkv_a, pick, coef, shift, starts,
            o_a, y_a, den_a, pre, psum, st, sm, (hid_t, dgate), *states,
        )
        begin.relay("up_a")
        begin.wait("lin_out")
        wlo = begin.result("lin_out")
        total = RowSum(part1, *set1)

        def attended_a(block):
            put_chip(part1, block, matmul(o_a[rows_of(block), :], wlo[...].reshape(128, D)))

        total.run(attended_a)
        norm_own(total, x_own, h_a, na2, 1)
        begin.wait("gate_a")
        begin.relay("down_a")
        total2, seen = RowSum(part2, *set2), []

        def mlp_a(block):
            n = chip_rows(na2, block)
            if not seen:
                begin.wait("up_a")
            gate, up = matmul(n, begin.columns("gate_a")), matmul(n, begin.columns("up_a"))
            hidden = (silu_parts(gate)[1] * up).astype(BF16)
            rows = rows_of(block)
            gate_s[rows, :] = gate.astype(BF16)
            up_s[rows, :] = up.astype(BF16)
            hid_s[rows, :] = hidden
            if not seen:
                begin.wait("down_a")
                spread_on("win")
                spread_on("gate_b")
            put_chip(part2, block, matmul_nt(hidden, begin.columns("down_a")))
            follow(total2, seen)

        RowGather(na2, *ag[0]).run(mlp_a)
        spread_on("up_b")
        total2.relay()
        total2.finish()
        norm_own(total2, h_a, out_a, nb1, 2)

        def project(block):
            if not gotten:
                begin.wait("win")
                gotten.append(1)
            qkv[rows_of(block), :] = matmul(chip_rows(nb1, block), begin.columns("win")).astype(BF16)

        gotten = []
        RowGather(nb1, *ag[1]).run(project)
        begin.relay("gate_b")

        def rims_in():
            spread_on("down_b")

        window_forward_kernel(rims_in, qkv, starts, o_b, ext, rim1, *rims[:2])
        begin.wait("win_out")
        wwo = begin.result("win_out")
        total = RowSum(part1, *set1)

        def attended_b(block):
            put_chip(part1, block, matmul(o_b[rows_of(block), :], wwo[...].reshape(128, D)))

        total.run(attended_b)
        norm_own(total, out_a, h_b, nb2, 3)
        begin.relay("up_b", "down_b")
        total2, seen_b = RowSum(part2, *set2), []

        def mlp_b(block):
            rows = rows_of(block)
            n = chip_rows(nb2, block)
            if not seen_b:
                begin.wait("gate_b", "up_b", "down_b")
            wg, wu, wd = (begin.columns(name) for name in ("gate_b", "up_b", "down_b"))
            gate, up = matmul(n, wg), matmul(n, wu)
            sig, act = silu_parts(gate)
            hidden = (act * up).astype(BF16)
            hid_t[rows, :] = hidden
            dhidden = matmul(chip_rows(cot, block), wd)
            dg = (dhidden * up * (sig + act * (1.0 - sig))).astype(BF16)
            du = (dhidden * act).astype(BF16)
            dgate[rows, :] = dg
            dup[rows, :] = du
            put_chip(part2, block, matmul_nt(dg, wg) + matmul_nt(du, wu))
            follow(total2, seen_b)
            put_chip(part3, block, matmul_nt(hidden, wd))

        RowGather(nb2, *ag[2]).run(mlp_b)
        for job in weight_grads(cot, hid_t, made["down_b"]):
            job()
        ship_terms("down_b")
        total2.relay()
        for job in weight_grads(nb2, dgate, made["gate_b"]):
            job()
        ship_terms("gate_b")
        total2.finish()
        back_own(total2.own, h_b, gains[3:4], cot_own, g_hb, gg.at[2:3], full1)

        def output_grad_b(block):
            do_b[rows_of(block), :] = matmul_nt(
                chip_rows(full1, block), wwo[...].reshape(128, D)
            ).astype(BF16)

        RowGather(full1, *ag[3]).run(
            output_grad_b,
            weight_grads(nb2, dup, made["up_b"]) + [functools.partial(relay, "down_b")],
        )

        def window_begin():
            ship_terms("up_b")

        def window_mid():
            relay("gate_b")
            send_on("down_b")

        window_backward_kernel(
            (window_begin, window_mid), qkv, ext, do_b, part3, h_b, o_b, full1, starts,
            dqkv, mixed, wo_w, acc, back, rim2, *rims[2:4], *set1,
        )
        relay("up_b")
        if ship:
            begin.start("win_out_v", wo_w)
        total = RowSum(part1, *set2)

        def projected(block):
            put_chip(part1, block, matmul_nt(dqkv[rows_of(block), :], begin.columns("win")))

        total.run(projected, weight_grads(nb1, dqkv, made["win"]))
        ship_terms("win")
        back_own(total.own, out_a, gains[2:3], g_hb, g_oa, gg.at[1:2], full2)
        total2, seen_a = RowSum(part2, *set1), []

        def mlp_back(block):
            rows = rows_of(block)
            sig, act = silu_parts(gate_s[rows, :].astype(F32))
            dhidden = matmul(chip_rows(full2, block), begin.columns("down_a"))
            dg = (dhidden * up_s[rows, :].astype(F32) * (sig + act * (1.0 - sig))).astype(BF16)
            du = (dhidden * act).astype(BF16)
            dgate[rows, :] = dg
            dup[rows, :] = du
            put_chip(part2, block, matmul_nt(dg, begin.columns("gate_a")) + matmul_nt(du, begin.columns("up_a")))
            follow(total2, seen_a)

        RowGather(full2, *ag[4]).run(mlp_back)
        for job in weight_grads(full2, hid_s, made["down_a"]):
            job()
        ship_terms("down_a")
        send_on("gate_b")
        total2.relay()
        for job in weight_grads(na2, dgate, made["gate_a"]):
            job()
        ship_terms("gate_a")
        total2.finish()
        back_own(total2.own, h_a, gains[1:2], g_oa, g_ha, gg.at[0:1], full1)

        def output_grad_a(block):
            do_a[rows_of(block), :] = matmul_nt(
                chip_rows(full1, block), wlo[...].reshape(128, D)
            ).astype(BF16)

        def output_weight(i):
            at = slice(i * 256, i * 256 + 256)
            rhs = full1[:, :, :, :, at].reshape(1024, 256)
            lo_w[:, at] = matmul_tn(o_a[...], rhs).astype(BF16)

        RowGather(full1, *ag[5]).run(
            output_grad_a,
            weight_grads(na2, dup, made["up_a"])
            + [functools.partial(send_on, "up_b"), functools.partial(relay, "win", "down_a")],
        )
        send_on("win")
        send_on("down_a")
        for i in range(4):
            output_weight(i)

    rows16 = lambda *shape: VM(shape, BF16)
    rows16s = lambda *shape: jax.ShapeDtypeStruct(shape, BF16)
    OWN_ROWS = jax.ShapeDtypeStruct((1024, 128), F32)
    n_held = 6
    summed = jax.ShapeDtypeStruct((4, 2, D // (8 * lax.axis_size(GROUP)), ff), BF16)
    late = []
    if ship:
        late = [Job("zs", terms, name=m + "_t", held=m != "gate_a") for m in makers[:-1]]
        late += [Job("pa", summed, name=m + "_p") for m in makers[:-2]] + [Job("zv", rowset, name="win_out_v")]
    sem = lambda n: pltpu.SemaphoreType.DMA((n,))
    weights = [VM(terms.shape, BF16)] * 4 if ship else []
    outs, moved = step(
        body,
        vmem(x_own, cot_own, *tables) + [(starts, SMEM)],
        vmem(
            jax.ShapeDtypeStruct((2, 64, D), BF16), OWN, vector, jax.ShapeDtypeStruct((1024, 128), BF16),
            jax.ShapeDtypeStruct((128, D), BF16),
            rowset, rows16s(1024, width), OWN_ROWS, OWN_ROWS, rows16s(4, SROWS, 128),
            jax.ShapeDtypeStruct((4, 8, 256), F32), rows16s(D, width), jax.ShapeDtypeStruct((8, D), F32),
        )
        + [(FULL, ANY), (FULL, ANY)]
        + vmem(terms)
        + ([] if ship else vmem(*[terms] * n_held)),
        weights + [VM((2, 64, D), F32)] * 5 + [VM(FULL.shape, BF16)] * 7
        + [
            rows16(1024, 384), rows16(4, 256 + RIM, 256), rows16(1024, 128), rows16(1024, 128),
            rows16(1024, 384), VM((1024, 256), F32), rows16(4, RIM, 256), rows16(4, RIM, 256),
            rows16(4, RIM, 256),
        ]
        + [rows16(1024, ff)] * 6
        + [rows16(1024, 128), VM((count, 4, SROWS, 128), BF16), VM((count, 4, 8, 256), F32)]
        + rs_scratch() + rs_scratch() + ag_scratch() * 8 + [sem(4)] * 4
        + [pltpu.SemaphoreType.DMA((2, count + 1))] * 2 + [sem(2)],
        jobs + late, 7, True, "front", collective, 300,
    )
    return outs, moved


def row_routes():
    nsh, nhh = lax.axis_size("sh"), lax.axis_size("hh")
    groups = nsh * nhh
    routes = []
    for d in range(8 * groups):
        place, group = d // groups, d % groups
        s, c = place // 2, place % 2
        sh, hh = group // nhh, group % nhh
        routes.append((d, ((sh * 4 + s) * nhh + hh) * 2 + c))
    return routes


def spread_ff(member):
    rows = member.shape[0]
    width = -(-member.shape[1] // (NTP * 128)) * 128
    padded = jnp.pad(member, ((0, 0), (0, NTP * width - member.shape[1])))
    return padded.reshape(rows, NTP, width)


def on_device(
    layer_input, lengths, gain_a1, lin_q, lin_k, lin_v, lin_out, gain_a2, mlp_a_gate, mlp_a_up,
    mlp_a_down, gain_b1, win_q, win_k, win_v, win_out, gain_b2, mlp_b_gate, mlp_b_up, mlp_b_down,
    cotangent,
):
    count = lax.axis_size(GROUP)
    rows = lin_q.shape[0]
    hidden_size = mlp_a_gate.shape[1]
    gains = jnp.pad(jnp.stack([gain_a1, gain_a2, gain_b1, gain_b2], axis=1), ((0, 0), (0, 60)))
    gains = jnp.broadcast_to(gains[:, None, :], (rows, NTP, 64))
    starts = jnp.cumsum(lengths) - lengths
    tables = taylor_tables()

    split = lambda member: member.reshape(rows, NTP, -1)
    bundle_lin = jnp.concatenate(
        [split(lin_q), split(lin_k), gains, split(lin_v)], axis=-1
    ).transpose(1, 0, 2)
    bundle_a = jnp.concatenate(
        [spread_ff(mlp_a_gate), spread_ff(mlp_a_up), spread_ff(mlp_a_down.T)], axis=-1
    ).transpose(1, 0, 2)
    bundle_win = jnp.concatenate([split(win_q), split(win_k), split(win_v)], axis=-1).transpose(
        1, 0, 2
    )
    bundle_b = jnp.concatenate(
        [spread_ff(mlp_b_gate), spread_ff(mlp_b_up), spread_ff(mlp_b_down.T)], axis=-1
    ).transpose(1, 0, 2)
    ff = bundle_a.shape[-1] // 3
    width = bundle_lin.shape[-1]
    nsh, nhh = lax.axis_size("sh"), lax.axis_size("hh")
    places = lambda a: a.reshape(4, 2, rows, a.shape[-1])
    whole = lambda a: a.reshape(D, a.shape[-1])
    total = lambda a: jnp.sum(a.astype(F32), axis=0).astype(BF16)
    ship = shipping()
    if ship:
        own_rows = lambda a, **kw: Job("zw", a, **kw)
    else:
        own_rows = lambda a, **kw: Job("zr", lax.ppermute(a, AXES, row_routes()), **kw)

    x_own = layer_input.reshape(2, 64, D)
    cot_own = cotangent.reshape(2, 64, D)
    def column(name, a):
        return [
            Job("pa", a, name=name + "_m"),
            Job("zg", jax.ShapeDtypeStruct(a.shape, BF16), VMEM, name, True),
        ]

    third = lambda a, i: places(a[:, :, i * ff : i * ff + ff])
    jobs = [
        column("lin", places(bundle_lin)), column("gate_a", third(bundle_a, 0)),
        column("up_a", third(bundle_a, 1)), column("down_a", third(bundle_a, 2)),
        column("win", places(bundle_win)), column("gate_b", third(bundle_b, 0)),
        column("up_b", third(bundle_b, 1)), column("down_b", third(bundle_b, 2)),
        [own_rows(lin_out, spec=VMEM, name="lin_out", held=True)],
        [own_rows(win_out, spec=VMEM, name="win_out", held=True)],
    ]
    outs, moved = front(x_own, cot_own, tables, starts, sum(jobs, []), count, ff, width, 1)
    mixed, grad_h_a, gg, do_a, grad_lin_out, grad_win_out = outs[:6]
    qkv_a, y_a, den_a, pre, psum, w_lin, gains, x_full, n_a1, up_a = outs[6:16]
    kept, apart_terms, moved = (y_a, den_a, pre, psum), outs[16:], moved[8:]
    if ship:
        gate_a, down_b, gate_b, up_b, win, down_a, win_out_t = moved
        late = [Job("pa", gate_a), Job("zs", up_a)]
    else:
        sums = apart(apart_terms, 10)
        _, moved = step(
            lambda begin: None, [], [], [], [Job("pa", a) for a in sums[:5]]
            + [Job("zt", grad_win_out.reshape(count, -1, D))], 7, True, "spread", 11, 20,
        )
        down_b, gate_b, up_b, win, down_a, win_out_t = moved
        late = [Job("pa", sums[5])]
        (up_a,) = apart([up_a], 14)
    (dqkv_a,), (gate_a, *more) = taylor_backward(qkv_a, do_a, kept, starts, tables, late, count, 8)
    (up_a,) = more if ship else (up_a,)
    rows_back = Job("zv", grad_lin_out.reshape(4, rows, D)) if ship else Job(
        "zt", grad_lin_out.reshape(count, -1, D)
    )
    grad_input, (lin_out_t, up_a), lin_g = last_layer(
        dqkv_a, w_lin, x_own, gains[0:1], grad_h_a, x_full, n_a1, gg[0:3], [rows_back, Job("pa", up_a)], 9,
    )

    def joined(a, lo, hi):
        a = a.reshape(NTP, rows, -1)[:, :, lo:hi].astype(F32)
        return a.transpose(1, 0, 2).reshape(rows, -1)

    def unpack_mlp(gate, up, down):
        joined_ff = lambda a: joined(a, 0, ff)[:, :hidden_size]
        return joined_ff(gate), joined_ff(up), joined_ff(down).T

    gate_b_g, up_b_g, down_b_g = unpack_mlp(gate_b, up_b, down_b)
    gate_a_g, up_a_g, down_a_g = unpack_mlp(gate_a, up_a, down_a)
    def own_terms(a):
        if ship:
            return jnp.sum(a.astype(F32), axis=0)
        return lax.ppermute(total(a), AXES, [(d, e) for e, d in row_routes()]).astype(F32)

    win_out_g, lin_out_g = own_terms(win_out_t), own_terms(lin_out_t)
    gg = jnp.sum(lin_g.reshape(NTP, rows, width)[:, :, 64:68].astype(F32), axis=0)
    return (
        mixed.reshape(128, D),
        grad_input.reshape(128, D),
        gg[:, 0],
        joined(lin_g, 0, 32),
        joined(lin_g, 32, 64),
        joined(lin_g, 128, 256),
        lin_out_g,
        gg[:, 1],
        gate_a_g,
        up_a_g,
        down_a_g,
        gg[:, 2],
        joined(win, 0, 128),
        joined(win, 128, 256),
        joined(win, 256, 384),
        win_out_g,
        gg[:, 3],
        gate_b_g,
        up_b_g,
        down_b_g,
    )


def solution(mesh):
    seq, head = mesh.devices.shape
    fine = Mesh(mesh.devices.reshape(seq // 4, 2, 2, head // 2, 2), AXES)
    row, vec, col = P(AXES, None), P(AXES), P(None, AXES)
    placed = (
        row, P(), vec, row, row, row, row, vec, row, row, col,
        vec, row, row, row, row, vec, row, row, col, row,
    )
    out = (
        row, row, vec, row, row, row, row, vec, row, row, col,
        vec, row, row, row, row, vec, row, row, col,
    )
    return jax.shard_map(on_device, mesh=fine, in_specs=placed, out_specs=out, check_vma=False)
```
